32 devices in a mesh: parts: 2 (over x), dp: 16 (over z, y, core).
Axes of the slice: x: 2, y: 2, z: 4, core: 2. Of those that a mesh axis runs over, the one named last changes fastest.
Arguments:
- hidden_state_input: bfloat16 [8192, 5120], P(('parts', 'dp')), parts along dimension 0, may hold values from -6 to 6
- attention_mixed_state: bfloat16 [8192, 5120], P(('parts', 'dp')), parts along dimension 0, may hold values from -6 to 6
- hidden_state_adjoint: bfloat16 [8192, 5120], P(('parts', 'dp')), parts along dimension 0, may hold values from -6 to 6
- attention_values_adjoint: bfloat16 [8192, 2560], P(('parts', 'dp')), parts along dimension 0, may hold values from -6 to 6
- sequence_token_counts: int32 [32, 2], P(('parts', 'dp')), parts along dimension 0, may hold values from 64 to 192, as said below
- heldout_sketched_signals: bfloat16 [128, 8192], P('dp'), may hold values from -6 to 6
- benchmark_labels: int32 [128, 1], P('dp'), may hold values from 0 to 2
- top_rmsnorm_weights: float32 [5120], replicated, may hold values from 0.5 to 1.5
- top_reducer_matrix: bfloat16 [5120, 128], P('dp'), may hold values from -0.078125 to 0.078125
- top_expander_matrix: bfloat16 [128, 2560], P(None, 'dp'), may hold values from -0.5 to 0.5
- bottom_reducer_matrix: bfloat16 [5120, 128], P('dp'), may hold values from -0.078125 to 0.078125
- bottom_expander_matrix: bfloat16 [128, 5120], P(None, 'dp'), may hold values from -0.5 to 0.5
- source_sketch: bfloat16 [5120, 64], replicated, may hold values from -0.078125 to 0.078125
- top_reducer_sketch: bfloat16 [128, 128], replicated, may hold values from -0.5 to 0.5
- top_expander_sketch: bfloat16 [128, 64], replicated, may hold values from -0.5 to 0.5
- top_target_sketch: bfloat16 [2560, 128], replicated, may hold values from -0.125 to 0.125
- bottom_reducer_sketch: bfloat16 [128, 128], replicated, may hold values from -0.5 to 0.5
- bottom_expander_sketch: bfloat16 [128, 64], replicated, may hold values from -0.5 to 0.5
- bottom_target_sketch: bfloat16 [5120, 128], replicated, may hold values from -0.078125 to 0.078125
Outputs:
- scores: float32 [64], P(('parts', 'dp')), parts along dimension 0
- task_best: float32 [64, 3], P(('parts', 'dp')), parts along dimension 0
The draws below stay inside these ranges and needn't reach their ends.
There are 2 independent parts, one for each index of `parts`. The reference program is written for one: setup_inputs(seed, part) draws one part's arguments, and reference() takes and returns one part's arrays. A program takes and returns all parts, laid end to end along the dimension named above; an argument that names none is the same for every part. Nothing has to cross between parts.
Inputs may be any that keep to these rules, and one draw needn't show every extreme that they name: `sequence_token_counts`: each row sums to 256, and one entry of each row, at a drawn place, is 192. `benchmark_labels`: every task is named by some validation example.
All inputs are finite; a program needn't handle non-finite values.
Results may differ from the reference program's by a relative error of at most 0.0033.
Values may be sent and summed in bfloat16 or wider, within the bound.
No kernel may reach another device: no remote copies, remote signals or barrier semaphores. Data moves between devices by JAX's collectives and lax.ppermute only.
A program may use at most 128 MiB of HBM per device.

```python
import jax
import jax.numpy as jnp
from jax import lax

HIDDEN_SIZE = 5120
HV = 2560
BOTTLENECK = 128
K1 = 64
K2 = 128
K = 8192
TASKS = 3
EX_DEV = 2
TOK_DEV = 256
MOST = 192
TOKENS = 4096
EXAMPLES = 32
VAL = 128
N_DP = 16


def draw_sequence_token_counts(key, part):
    key = jax.random.fold_in(key, 11)
    rest = TOK_DEV - MOST
    others = EX_DEV - 1
    base = rest // others
    extra = rest - base * others
    slots = jnp.arange(EX_DEV, dtype=jnp.int32)[None, :]
    where_long = jax.random.randint(key, (N_DP, 1), 0, EX_DEV).astype(jnp.int32)
    order = jnp.where(slots > where_long, slots - 1, slots)
    filled = base + jnp.where(order == 0, extra, 0)
    return jnp.where(slots == where_long, MOST, filled).astype(jnp.int32)


def shard_levels(key, dims, cuts, smallest, high):
    level = 1.0
    for dim, blocks in cuts:
        draws = jax.random.uniform(jax.random.fold_in(jax.random.fold_in(key, 6), dim), (blocks,), jnp.float32, smallest / len(cuts), high / len(cuts))
        level = level * jnp.repeat(jnp.exp(draws), dims[dim] // blocks).reshape((-1,) + (1,) * (len(dims) - 1 - dim))
    return level


def different_ones(stream_key, rows, amount, top, lift):
    order = jax.random.permutation(jax.random.fold_in(stream_key, 1), amount)
    boost = order
    for power in range(3):
        boost = boost * boost // amount
    boost = boost * lift // amount
    chance = jax.random.randint(jax.random.fold_in(stream_key, 2), (rows, amount), 0, 4096) + boost
    holders = jax.random.permutation(jax.random.fold_in(stream_key, 3), rows)[jnp.arange(amount) % rows]
    chance = jnp.where(jnp.arange(rows)[:, None] == holders[None, :], 1 << 14, chance)
    priority = chance * amount + jnp.arange(amount)
    return lax.top_k(priority.astype(jnp.int32), top)[1].astype(jnp.int32)


def bell_draw(stream_key, extent, scale, reach, pieces=(), kind=jnp.bfloat16):
    drawn = jax.random.normal(stream_key, extent, jnp.float32) * scale
    if len(pieces) > 0:
        drawn = shard_levels(stream_key, extent, pieces, -0.22, 0.18) * drawn
    return jnp.clip(drawn, min=-reach, max=reach).astype(kind)


def setup_inputs(seed: int = 0, part: int = 0) -> dict:
    keys = jax.random.split(jax.random.key(seed), 20)
    part_keys = jax.random.split(jax.random.fold_in(keys[19], part), 20)
    hidden_state_input = bell_draw(part_keys[0], (TOKENS, HIDDEN_SIZE), 1.0, 6.0, ((0, 16),))
    attention_mixed_state = bell_draw(part_keys[1], (TOKENS, HIDDEN_SIZE), 1.0, 6.0, ((0, 16),))
    hidden_state_adjoint = bell_draw(part_keys[2], (TOKENS, HIDDEN_SIZE), 1.0, 6.0, ((0, 16),))
    attention_values_adjoint = bell_draw(part_keys[3], (TOKENS, HV), 1.0, 6.0, ((0, 16),))
    sequence_token_counts = draw_sequence_token_counts(jax.random.fold_in(jax.random.fold_in(keys[19], part), 71), part)
    heldout_sketched_signals = bell_draw(keys[5], (VAL, K), 1.0, 6.0, ((0, 16),))
    benchmark_labels = different_ones(keys[6], VAL, TASKS, 1, 2730)
    top_rmsnorm_weights = jnp.clip(1.0 + 0.1 * jax.random.normal(keys[7], (HIDDEN_SIZE,), jnp.float32), 0.5, 1.5)
    top_reducer_matrix = bell_draw(keys[8], (HIDDEN_SIZE, BOTTLENECK), HIDDEN_SIZE ** -0.5, 0.078125, ((0, 16),))
    top_expander_matrix = bell_draw(keys[9], (BOTTLENECK, HV), BOTTLENECK ** -0.5, 0.5, ((1, 16),))
    bottom_reducer_matrix = bell_draw(keys[10], (HIDDEN_SIZE, BOTTLENECK), HIDDEN_SIZE ** -0.5, 0.078125, ((0, 16),))
    bottom_expander_matrix = bell_draw(keys[11], (BOTTLENECK, HIDDEN_SIZE), BOTTLENECK ** -0.5, 0.5, ((1, 16),))
    source_sketch = bell_draw(keys[12], (HIDDEN_SIZE, K1), HIDDEN_SIZE ** -0.5, 0.078125)
    top_reducer_sketch = bell_draw(keys[13], (BOTTLENECK, K2), BOTTLENECK ** -0.5, 0.5)
    top_expander_sketch = bell_draw(keys[14], (BOTTLENECK, K1), BOTTLENECK ** -0.5, 0.5)
    top_target_sketch = bell_draw(keys[15], (HV, K2), HV ** -0.5, 0.125)
    bottom_reducer_sketch = bell_draw(keys[16], (BOTTLENECK, K2), BOTTLENECK ** -0.5, 0.5)
    bottom_expander_sketch = bell_draw(keys[17], (BOTTLENECK, K1), BOTTLENECK ** -0.5, 0.5)
    bottom_target_sketch = bell_draw(keys[18], (HIDDEN_SIZE, K2), HIDDEN_SIZE ** -0.5, 0.078125)
    return {"hidden_state_input": hidden_state_input, "attention_mixed_state": attention_mixed_state, "hidden_state_adjoint": hidden_state_adjoint, "attention_values_adjoint": attention_values_adjoint, "sequence_token_counts": sequence_token_counts, "heldout_sketched_signals": heldout_sketched_signals, "benchmark_labels": benchmark_labels, "top_rmsnorm_weights": top_rmsnorm_weights, "top_reducer_matrix": top_reducer_matrix, "top_expander_matrix": top_expander_matrix, "bottom_reducer_matrix": bottom_reducer_matrix, "bottom_expander_matrix": bottom_expander_matrix, "source_sketch": source_sketch, "top_reducer_sketch": top_reducer_sketch, "top_expander_sketch": top_expander_sketch, "top_target_sketch": top_target_sketch, "bottom_reducer_sketch": bottom_reducer_sketch, "bottom_expander_sketch": bottom_expander_sketch, "bottom_target_sketch": bottom_target_sketch}


alpha_multiplier = 4.0

def sketch_summands(inputs, gradient_list, down, up_factor, proj_left, adapter_rank_down, rank_b, projection_output):
    reduced = jnp.dot(inputs, down, preferred_element_type=jnp.float32).astype(jnp.bfloat16)
    returned_gradient = lax.dot_general(gradient_list, up_factor, (((1,), (1,)), ((), ())), preferred_element_type=jnp.float32).astype(jnp.bfloat16)
    first_a = jnp.dot(inputs, proj_left, preferred_element_type=jnp.float32)
    first_b = jnp.dot(reduced, rank_b, preferred_element_type=jnp.float32)
    second_layer_down = alpha_multiplier * jnp.dot(returned_gradient, adapter_rank_down, preferred_element_type=jnp.float32)
    second_layer_up = alpha_multiplier * jnp.dot(gradient_list, projection_output, preferred_element_type=jnp.float32)
    return (returned_gradient, first_a, first_b, second_layer_down, second_layer_up)

def example_features(lefts, rights, token_count_vector):
    tokens_count = lefts[0].shape[0]
    left_stack = jnp.stack(lefts, axis=1).astype(jnp.bfloat16)
    right_stack = jnp.stack(rights, axis=1).astype(jnp.bfloat16)
    ends = jnp.cumsum(token_count_vector).astype(jnp.int32)
    starts = ends - token_count_vector
    places = jnp.arange(tokens_count, dtype=jnp.int32)[:, None]
    member = ((places >= starts[None, :]) & (places < ends[None, :])).astype(jnp.bfloat16)
    count_ex = member.shape[1]
    width_left = left_stack.shape[2]
    spread = (member[:, None, :, None] * left_stack[:, :, None, :]).reshape(tokens_count * 4, count_ex * width_left)
    rights_flat = right_stack.reshape(tokens_count * 4, right_stack.shape[2])
    feats = lax.dot_general(spread, rights_flat, (((0,), (0,)), ((), ())), preferred_element_type=jnp.float32)
    feats = feats.reshape(count_ex, -1)
    squares = lax.optimization_barrier(jnp.sum(feats * feats, axis=1, keepdims=True))
    return (feats * lax.rsqrt(squares + 1e-06)).astype(jnp.bfloat16)

def shard_descriptors(hidden_state_input, attention_mixed_state, hidden_state_adjoint, attention_values_adjoint, token_count_vector, top_rmsnorm_weights, top_reducer_matrix, top_expander_matrix, bottom_reducer_matrix, bottom_expander_matrix, source_sketch, top_reducer_sketch, top_expander_sketch, top_target_sketch, bottom_reducer_sketch, bottom_expander_sketch, bottom_target_sketch):
    wide = hidden_state_input.astype(jnp.float32)
    inverse = lax.rsqrt(lax.optimization_barrier(jnp.mean(wide * wide, axis=1, keepdims=True)) + 1e-05)
    unit_stream = wide * inverse
    rescaled_hidden = (unit_stream * top_rmsnorm_weights[None, :]).astype(jnp.bfloat16)
    top_branch_adjoint, initial_left_operand, latter_left_operand, initial_right_operand, latter_right_operand = sketch_summands(rescaled_hidden, attention_values_adjoint, top_reducer_matrix, top_expander_matrix, source_sketch, top_reducer_sketch, top_expander_sketch, top_target_sketch)
    branch_sensitivity = alpha_multiplier * lax.dot_general(top_branch_adjoint, top_reducer_matrix, (((1,), (1,)), ((), ())), preferred_element_type=jnp.float32)
    gain_applied = branch_sensitivity * top_rmsnorm_weights[None, :]
    along = lax.optimization_barrier(jnp.mean(gain_applied * unit_stream, axis=1, keepdims=True))
    lower_grad = (hidden_state_adjoint.astype(jnp.float32) + inverse * (gain_applied - unit_stream * along)).astype(jnp.bfloat16)
    returned_lower, left_three, left_four, right_three, right_four = sketch_summands(attention_mixed_state, lower_grad, bottom_reducer_matrix, bottom_expander_matrix, source_sketch, bottom_reducer_sketch, bottom_expander_sketch, bottom_target_sketch)
    return example_features((initial_left_operand, latter_left_operand, left_three, left_four), (initial_right_operand, latter_right_operand, right_three, right_four), token_count_vector)

def reference(hidden_state_input, attention_mixed_state, hidden_state_adjoint, attention_values_adjoint, sequence_token_counts, heldout_sketched_signals, benchmark_labels, top_rmsnorm_weights, top_reducer_matrix, top_expander_matrix, bottom_reducer_matrix, bottom_expander_matrix, source_sketch, top_reducer_sketch, top_expander_sketch, top_target_sketch, bottom_reducer_sketch, bottom_expander_sketch, bottom_target_sketch):

    def one_block(index):
        first = (index * TOK_DEV).astype(jnp.int32)
        component_terms = [lax.dynamic_slice_in_dim(array, first, TOK_DEV, 0) for array in (hidden_state_input, attention_mixed_state, hidden_state_adjoint, attention_values_adjoint)]
        token_count_vector = lax.dynamic_index_in_dim(sequence_token_counts, index, 0, keepdims=False)
        return shard_descriptors(component_terms[0], component_terms[1], component_terms[2], component_terms[3], token_count_vector, top_rmsnorm_weights, top_reducer_matrix, top_expander_matrix, bottom_reducer_matrix, bottom_expander_matrix, source_sketch, top_reducer_sketch, top_expander_sketch, top_target_sketch, bottom_reducer_sketch, bottom_expander_sketch, bottom_target_sketch)
    pool_unit = lax.map(one_block, jnp.arange(N_DP, dtype=jnp.int32)).reshape(EXAMPLES, K)
    val_wide = heldout_sketched_signals.astype(jnp.float32)
    val_unit = (val_wide * lax.rsqrt(lax.optimization_barrier(jnp.sum(val_wide * val_wide, axis=1, keepdims=True)) + 1e-06)).astype(jnp.bfloat16)
    score_scale = float(K) ** 0.5
    similar = score_scale * lax.dot_general(pool_unit, val_unit, (((1,), (1,)), ((), ())), preferred_element_type=jnp.float32)
    task_mask = benchmark_labels == jnp.arange(TASKS, dtype=jnp.int32)[None, :]
    task_best = lax.optimization_barrier(jnp.max(jnp.where(task_mask[None, :, :], similar[:, :, None], -2.0 * score_scale), axis=1))
    scores = lax.optimization_barrier(jnp.mean(task_best, axis=1))
    return (scores, task_best)
```

```python
import jax
import jax.numpy as jnp
from jax import lax
from jax.sharding import PartitionSpec as P

TASKS = 3
ALPHA = 4.0
F32 = jnp.float32
BF16 = jnp.bfloat16
MOST_RING_CHIPS = 8


def mm(a, b):
    return jnp.dot(a, b, preferred_element_type=F32)


def mm_rows(a, b):
    return lax.dot_general(a, b, (((1,), (1,)), ((), ())), preferred_element_type=F32)


def mm_cols(a, b):
    return lax.dot_general(a, b, (((0,), (0,)), ((), ())), preferred_element_type=F32)


def ring_chip(pos, chips):
    half = chips // 2
    return jnp.where(pos < half, 2 * pos, 2 * (chips - 1 - pos) + 1)


def gather_blocks(block, n):
    chips = n // 2
    if chips > MOST_RING_CHIPS:
        return lax.all_gather(block, "dp")
    half = chips // 2
    place = [2 * q if q < half else 2 * (chips - 1 - q) + 1 for q in range(chips)]

    def hop(value, step):
        pairs = [
            (2 * place[q] + c, 2 * place[(q + step) % chips] + c)
            for q in range(chips)
            for c in range(2)
        ]
        return lax.ppermute(value, "dp", pairs)

    def other_core(value):
        return lax.ppermute(value, "dp", [(d, d ^ 1) for d in range(n)])

    me = lax.axis_index("dp")
    chip, core = me // 2, me % 2
    row, side = chip // 2, chip % 2
    pos = jnp.where(side == 0, row, chips - 1 - row)
    pieces = [(0, block, 0)]
    up, down = block, block
    middle = (block.shape[0] // 2) // 16 * 16
    for k in range(1, half):
        up, down = hop(up, 1), hop(down, -1)
        pieces += [(-k, up, 0), (k, down, 0)]
    pieces += [(-half, hop(up[:middle], 1), 0), (half, hop(down[middle:], -1), middle)]
    out = jnp.zeros((n,) + block.shape, block.dtype)
    for away, piece, first in pieces:
        base = 2 * ring_chip((pos + away + chips) % chips, chips)
        out = lax.dynamic_update_slice(out, piece[None], (base + core, first, 0))
        out = lax.dynamic_update_slice(out, other_core(piece)[None], (base + 1 - core, first, 0))
    return out


def shards(
    hidden_state_input,
    attention_mixed_state,
    hidden_state_adjoint,
    attention_values_adjoint,
    sequence_token_counts,
    heldout_sketched_signals,
    benchmark_labels,
    top_rmsnorm_weights,
    top_reducer_matrix,
    top_expander_matrix,
    bottom_reducer_matrix,
    bottom_expander_matrix,
    source_sketch,
    top_reducer_sketch,
    top_expander_sketch,
    top_target_sketch,
    bottom_reducer_sketch,
    bottom_expander_sketch,
    bottom_target_sketch,
    n,
):
    me = lax.axis_index("dp")
    x, mixed, adjoint, values = (
        hidden_state_input,
        attention_mixed_state,
        hidden_state_adjoint,
        attention_values_adjoint,
    )
    tokens, width = x.shape
    rows = top_reducer_matrix.shape[0]
    up_rows = top_expander_matrix.shape[1]
    rank = top_reducer_matrix.shape[1]
    k1 = source_sketch.shape[1]
    gain = top_rmsnorm_weights
    own_gain = lax.dynamic_slice_in_dim(gain, me * rows, rows)

    down_upper = (own_gain[:, None] * top_reducer_matrix.astype(F32)).astype(BF16)
    up_lower = mm(bottom_expander_matrix.T, bottom_reducer_sketch).astype(BF16)
    down_lower = mm(bottom_reducer_matrix, bottom_expander_sketch).astype(BF16)
    packed_lower = jnp.concatenate([down_lower[: rows // 2], down_lower[rows // 2 :]], axis=1)
    factors = jnp.concatenate([down_upper, up_lower, top_expander_matrix.T, packed_lower], axis=0)
    factors = gather_blocks(factors, n)

    val_wide = heldout_sketched_signals.astype(F32)
    val_unit = (
        val_wide * lax.rsqrt(jnp.sum(val_wide * val_wide, axis=1, keepdims=True) + 1e-06)
    ).astype(BF16)
    labels = jnp.broadcast_to(benchmark_labels.astype(BF16), (val_unit.shape[0], 128))
    panel = jnp.concatenate([val_unit.reshape(-1, 128), labels], axis=0)
    panel = gather_blocks(panel, n)
    val_rows = val_unit.shape[0]
    cut = panel.shape[1] - val_rows
    panel_tasks = panel[:, cut:, 0].reshape(n * val_rows, 1).astype(jnp.int32)
    panel = panel[:, :cut].reshape(n * val_rows, val_unit.shape[1])

    wide = x.astype(F32)
    inverse = lax.rsqrt(jnp.mean(wide * wide, axis=1, keepdims=True) + 1e-05)
    gained_sketch = (gain[:, None] * source_sketch.astype(F32)).astype(BF16)
    left_one = inverse * mm(x, gained_sketch)
    left_three = mm(mixed, source_sketch)
    right_two = ALPHA * mm(values, top_target_sketch)

    at = 0
    down_upper = factors[:, at : at + rows].reshape(width, rank)
    at += rows
    up_lower = factors[:, at : at + rows].reshape(width, -1)
    at += rows
    up_upper = factors[:, at : at + up_rows].reshape(-1, rank)
    at += up_rows
    down_lower = factors[:, at:]
    down_lower = jnp.concatenate([down_lower[:, :, :k1], down_lower[:, :, k1:]], axis=1)
    down_lower = down_lower.reshape(width, k1)

    reduced = inverse * mm(x, down_upper)
    left_two = mm(reduced.astype(BF16), top_expander_sketch)
    left_four = mm(mixed, down_lower)
    returned = mm(values, up_upper).astype(BF16)
    right_one = ALPHA * mm(returned, top_reducer_sketch)
    along = (ALPHA / width) * jnp.sum(returned.astype(F32) * reduced, axis=1, keepdims=True)
    targets = jnp.concatenate([up_lower, bottom_target_sketch], axis=1)
    bridge = mm_cols(down_upper, targets).astype(BF16)
    rights_low = mm(adjoint, targets) + inverse * (
        ALPHA * mm(returned, bridge) - (along * inverse) * mm(x, targets)
    )
    rights_low = ALPHA * rights_low
    k2 = up_lower.shape[1]
    lefts = (left_one, left_two, left_three, left_four)
    rights = (right_one, right_two, rights_low[:, :k2], rights_low[:, k2:])

    counts = sequence_token_counts[0]
    ends = jnp.cumsum(counts)
    starts = ends - counts
    places = jnp.arange(tokens, dtype=jnp.int32)[:, None]
    member = (places >= starts[None, :]) & (places < ends[None, :])
    count_ex = counts.shape[0]
    spread = jnp.concatenate(lefts, axis=0).astype(BF16)
    member = jnp.tile(member, (4, 1))
    spread = jnp.concatenate(
        [jnp.where(member[:, e : e + 1], spread, 0) for e in range(count_ex)], axis=1
    )
    feats = mm_cols(spread, jnp.concatenate(rights, axis=0).astype(BF16))
    feats = feats.reshape(count_ex, -1)
    squares = jnp.sum(feats * feats, axis=1, keepdims=True)
    unit_rows = (feats * lax.rsqrt(squares + 1e-06)).astype(BF16)

    score_scale = float(unit_rows.shape[1]) ** 0.5
    similar = score_scale * mm_rows(unit_rows, panel)
    task_mask = panel_tasks == jnp.arange(TASKS, dtype=jnp.int32)[None, :]
    task_best = jnp.max(
        jnp.where(task_mask[None, :, :], similar[:, :, None], -2.0 * score_scale), axis=1
    )
    return (jnp.mean(task_best, axis=1), task_best)


def solution(mesh):
    n = mesh.shape["dp"]
    split = P(("parts", "dp"), None)
    by_row, by_column, whole = P("dp", None), P(None, "dp"), P()
    placed = (
        (split,) * 5
        + (by_row, by_row, whole)
        + (by_row, by_column, by_row, by_column)
        + (whole,) * 7
    )
    return jax.shard_map(
        lambda *arrays: shards(*arrays, n),
        mesh=mesh,
        in_specs=placed,
        out_specs=(P(("parts", "dp")), split),
        check_vma=False,
    )
```

```python
import functools

import jax
import jax.numpy as jnp
from jax import lax
from jax.experimental import pallas as pl
from jax.experimental.pallas import tpu as pltpu
from jax.sharding import PartitionSpec as P

TASKS = 3
ALPHA = 4.0
F32 = jnp.float32
BF16 = jnp.bfloat16
RING_CHIPS = 8
LANES = 128
STEPS = 4
MIB = 1 << 20


def mm(a, b):
    return jnp.dot(a, b, preferred_element_type=F32)


def mm_rows(a, b):
    return lax.dot_general(a, b, (((1,), (1,)), ((), ())), preferred_element_type=F32)


def mm_cols(a, b):
    return lax.dot_general(a, b, (((0,), (0,)), ((), ())), preferred_element_type=F32)


def ring_chip(pos):
    half = RING_CHIPS // 2
    return jnp.where(pos < half, 2 * pos, 2 * (RING_CHIPS - 1 - pos) + 1)


def ring_pos(chip):
    row, side = chip // 2, chip % 2
    return jnp.where(side == 0, row, RING_CHIPS - 1 - row)


def hop(value, step):
    half = RING_CHIPS // 2
    place = [2 * q if q < half else 2 * (RING_CHIPS - 1 - q) + 1 for q in range(RING_CHIPS)]
    pairs = [
        (2 * place[q] + c, 2 * place[(q + step) % RING_CHIPS] + c)
        for q in range(RING_CHIPS)
        for c in range(2)
    ]
    return lax.ppermute(value, "dp", pairs)


def other_core(value):
    return lax.ppermute(value, "dp", [(d, d ^ 1) for d in range(2 * RING_CHIPS)])


def ring(block, ups, downs):
    pieces = [(0, block)]
    up, down = block, block
    for k in range(1, max(ups, downs) + 1):
        if k <= ups:
            up = hop(up, 1)
            pieces.append((-k, up))
        if k <= downs:
            down = hop(down, -1)
            pieces.append((k, down))
    return pieces


def half_lanes(shape):
    return lax.broadcasted_iota(jnp.int32, shape, 1) < LANES // 2


def diagonal_column(row, first, count):
    shape = (count, row.shape[1])
    lane = lax.broadcasted_iota(jnp.int32, shape, 1)
    at = lax.broadcasted_iota(jnp.int32, shape, 0)
    return jnp.sum(jnp.where(lane == at + first, row, 0.0), axis=1, keepdims=True)


def factor_kernel(me_ref, gain_ref, down_up_ref, up_low_ref, sketch_ref, up_up_ref, down_low_ref, expand_ref, out_ref):
    rows = down_up_ref.shape[0]
    half = LANES // 2
    for b in range(rows // half):
        place = me_ref[0] * (rows // half) + b
        row = gain_ref[pl.ds(place // 2, 1), :]
        column = diagonal_column(row, (place % 2) * half, half)
        part = down_up_ref[pl.ds(b * half, half), :].astype(F32)
        out_ref[pl.ds(b * half, half), :] = (column * part).astype(BF16)
    at = rows
    out_ref[pl.ds(at, rows), :] = mm(up_low_ref[...], sketch_ref[...]).astype(BF16)
    at += rows
    out_ref[pl.ds(at, rows // 2), :] = up_up_ref[...]
    at += rows // 2
    expand = expand_ref[...]
    low = mm_rows(down_low_ref[...], jnp.concatenate([expand, expand], axis=0))
    first, second = low[: rows // 2], low[rows // 2 :]
    out_ref[pl.ds(at, rows // 2), :] = jnp.where(half_lanes(first.shape), first, second).astype(BF16)


def panel_kernel(val_ref, label_ref, out_ref):
    wide = val_ref[...].astype(F32)
    count, width = wide.shape
    scale = lax.rsqrt(jnp.sum(wide * wide, axis=1, keepdims=True) + 1e-06)
    unit = wide * scale
    blocks = [unit[:, i * LANES : (i + 1) * LANES] for i in range(width // LANES)]
    row = label_ref[...].astype(F32)
    labels = jnp.broadcast_to(diagonal_column(row, 0, count), (count, LANES))
    blocks += [labels, labels]
    for i in range(0, len(blocks), 2):
        pair = jnp.concatenate(blocks[i : i + 2], axis=0)
        out_ref[pl.ds(i * count, 2 * count), :] = pair.astype(BF16)


def local_kernel(
    x_ref, mixed_ref, adjoint_ref, values_ref, gain_ref, source_ref, low_target_ref, top_target_ref,
    lefts_ref, right_ref, x_target_ref, adjoint_target_ref, inverse_ref,
    squares, x_source, mixed_source, values_target, width,
):
    step = pl.program_id(0)

    @pl.when(step == 0)
    def _():
        for ref in (squares, x_source, mixed_source, values_target, x_target_ref, adjoint_target_ref):
            ref[...] = jnp.zeros_like(ref)

    x = x_ref[...]
    wide = x.astype(F32)
    square = wide * wide
    total = squares[...]
    for i in range(square.shape[1] // LANES):
        total = total + square[:, i * LANES : (i + 1) * LANES]
    squares[...] = total
    source = source_ref[...]
    gained = (source.astype(F32) * gain_ref[...]).astype(BF16)
    x_source[...] += mm_rows(x, jnp.concatenate([gained, gained], axis=0))
    mixed_source[...] += mm_rows(mixed_ref[...], jnp.concatenate([source, source], axis=0))
    low_target = low_target_ref[...]
    x_target_ref[...] += mm(x, low_target)
    adjoint_target_ref[...] += mm(adjoint_ref[...], low_target)
    values_target[...] += mm(values_ref[...], top_target_ref[...])

    @pl.when(step == STEPS - 1)
    def _():
        mean = jnp.sum(squares[...], axis=1, keepdims=True) * (1.0 / width)
        inverse = jnp.broadcast_to(lax.rsqrt(mean + 1e-05), squares.shape)
        inverse_ref[...] = inverse
        tokens = x_ref.shape[0]
        lefts_ref[pl.ds(0, tokens), :] = (inverse * x_source[...]).astype(BF16)
        lefts_ref[pl.ds(tokens, tokens), :] = mixed_source[...].astype(BF16)
        right_ref[...] = (ALPHA * values_target[...]).astype(BF16)


def feature_kernel(pieces, slots_ref, counts_ref, *refs):
    piece_refs = refs[:pieces]
    (
        x_hbm, mixed_hbm, adjoint_hbm, values_hbm, target_hbm,
        lefts_ref, right_ref, x_target_ref, adjoint_target_ref, inverse_ref, expand_ref, sketch_ref,
        out_ref,
        factors, x_ref, mixed_ref, adjoint_ref, values_ref, target_ref, piece_sems, sems,
    ) = refs[pieces:]
    rows = factors.shape[1] // 3
    tokens, width = x_ref.shape
    span = width // STEPS
    per_step = span // rows
    value_span = values_ref.shape[1] // STEPS

    copies = []
    for i, piece in enumerate(piece_refs):
        copy = pltpu.make_async_copy(piece, factors.at[slots_ref[i]], piece_sems.at[i])
        copy.start()
        copies.append(copy)
    parts = []
    for j in range(STEPS):
        part = []
        for k, (hbm, ref, size) in enumerate(
            (
                (x_hbm, x_ref, span),
                (mixed_hbm, mixed_ref, span),
                (adjoint_hbm, adjoint_ref, span),
                (values_hbm, values_ref, value_span),
            )
        ):
            window = pl.ds(j * size, size)
            part.append(pltpu.make_async_copy(hbm.at[:, window], ref.at[:, window], sems.at[j, k]))
        window = pl.ds(j * span, span)
        part.append(pltpu.make_async_copy(target_hbm.at[window], target_ref.at[window], sems.at[j, 4]))
        for copy in part:
            copy.start()
        parts.append(part)
    for copy in copies:
        copy.wait()

    x_both = jnp.zeros((tokens, 2 * LANES), F32)
    bridge = jnp.zeros((LANES, 2 * LANES), F32)
    adjoint_low = jnp.zeros((tokens, LANES), F32)
    mixed_low = jnp.zeros((tokens, LANES), F32)
    returned = jnp.zeros((tokens, LANES), F32)
    for j in range(STEPS):
        for copy in parts[j]:
            copy.wait()
        held = [factors[j * per_step + s] for s in range(per_step)]
        down_up = jnp.concatenate([f[:rows] for f in held], axis=0)
        up_low = jnp.concatenate([f[rows : 2 * rows] for f in held], axis=0)
        up_up = jnp.concatenate([f[2 * rows : 2 * rows + rows // 2] for f in held], axis=0)
        down_low = []
        for f in held:
            packed = f[2 * rows + rows // 2 :].astype(F32)
            turned = pltpu.roll(packed, LANES // 2, 1)
            lower = half_lanes(packed.shape)
            down_low += [jnp.where(lower, packed, turned), jnp.where(lower, turned, packed)]
        down_low = jnp.concatenate(down_low, axis=0).astype(BF16)
        window = slice(j * span, (j + 1) * span)
        x_both = x_both + mm(x_ref[:, window], jnp.concatenate([down_up, up_low], axis=1))
        adjoint_low = adjoint_low + mm(adjoint_ref[:, window], up_low)
        mixed_low = mixed_low + mm(mixed_ref[:, window], down_low)
        returned = returned + mm(values_ref[:, j * value_span : (j + 1) * value_span], up_up)
        bridge = bridge + mm_cols(down_up, jnp.concatenate([up_low, target_ref[window, :]], axis=1))

    inverse = inverse_ref[...]
    reduced = inverse * x_both[:, :LANES]
    expand = expand_ref[...]
    left_two = mm_rows(reduced.astype(BF16), jnp.concatenate([expand, expand], axis=0))
    returned = returned.astype(BF16)
    right_one = ALPHA * mm(returned, sketch_ref[...])
    along = (ALPHA / width) * jnp.sum(returned.astype(F32) * reduced, axis=1, keepdims=True)
    bridged = mm(returned, bridge.astype(BF16))
    along = along * inverse
    right_three = adjoint_low + inverse * (ALPHA * bridged[:, :LANES] - along * x_both[:, LANES:])
    right_four = adjoint_target_ref[...] + inverse * (
        ALPHA * bridged[:, LANES:] - along * x_target_ref[...]
    )
    rights = (
        right_one.astype(BF16),
        right_ref[...],
        (ALPHA * right_three).astype(BF16),
        (ALPHA * right_four).astype(BF16),
    )
    place = lax.broadcasted_iota(jnp.int32, (tokens, LANES), 0)
    first, second = counts_ref[0, 0], counts_ref[0, 1]
    lower = half_lanes((tokens, LANES))
    start = jnp.where(lower, 0, first)
    end = jnp.where(lower, first, first + second)
    member = (place >= start) & (place < end)
    lefts = (
        lefts_ref[pl.ds(0, tokens), :].astype(F32),
        left_two,
        lefts_ref[pl.ds(tokens, tokens), :].astype(F32),
        mixed_low,
    )
    spread = jnp.concatenate([jnp.where(member, left, 0.0).astype(BF16) for left in lefts], axis=0)
    feats = mm_cols(spread, jnp.concatenate(rights, axis=0))
    half = LANES // 2
    for e in range(2):
        own = feats[e * half : (e + 1) * half]
        squares = jnp.sum(own * own, keepdims=True)
        out_ref[pl.ds(e * half, half), :] = (own * lax.rsqrt(squares + 1e-06)).astype(BF16)


def score_kernel(pieces, count, unit_ref, *refs):
    piece_refs = refs[:pieces]
    best_ref, mean_ref, spread = refs[pieces:]
    half = LANES // 2
    scale = float(half * LANES) ** 0.5
    for e in range(2):
        for i in range(half):
            row = unit_ref[pl.ds(e * half + i, 1), :].astype(F32)
            spread[e, pl.ds(i * count, count), :] = jnp.broadcast_to(row, (count, LANES))
    best = [[jnp.full((count, LANES), -2.0 * scale, F32) for _ in range(TASKS)] for _ in range(2)]
    for piece in piece_refs:
        wide = piece[pl.ds(0, half * count), :].astype(F32)
        labels = piece[pl.ds(half * count, 2 * count), :].astype(F32)[:count]
        for e in range(2):
            products = wide * spread[e]
            total = jnp.sum(products.reshape(half, count, LANES), axis=0)
            similar = scale * jnp.sum(total, axis=1, keepdims=True)
            for t in range(TASKS):
                here = jnp.where(labels == float(t), similar, -2.0 * scale)
                best[e][t] = jnp.maximum(best[e][t], here)
    for e in range(2):
        values = [jnp.max(best[e][t]) for t in range(TASKS)]
        for t in range(TASKS):
            best_ref[e, t] = values[t]
        mean_ref[e] = (values[0] + values[1] + values[2]) * (1.0 / TASKS)


VMEM = pl.BlockSpec(memory_space=pltpu.VMEM)
SMEM = pl.BlockSpec(memory_space=pltpu.SMEM)
ANY = pl.BlockSpec(memory_space=pl.ANY)


def params(mib):
    return pltpu.CompilerParams(vmem_limit_bytes=mib * MIB)


def cost(flops, nbytes):
    return pl.CostEstimate(flops=flops, bytes_accessed=nbytes, transcendentals=0)


def shards(
    hidden_state_input,
    attention_mixed_state,
    hidden_state_adjoint,
    attention_values_adjoint,
    sequence_token_counts,
    heldout_sketched_signals,
    benchmark_labels,
    top_rmsnorm_weights,
    top_reducer_matrix,
    top_expander_matrix,
    bottom_reducer_matrix,
    bottom_expander_matrix,
    source_sketch,
    top_reducer_sketch,
    top_expander_sketch,
    top_target_sketch,
    bottom_reducer_sketch,
    bottom_expander_sketch,
    bottom_target_sketch,
):
    me = lax.axis_index("dp").astype(jnp.int32)
    x, mixed, adjoint, values = (
        hidden_state_input,
        attention_mixed_state,
        hidden_state_adjoint,
        attention_values_adjoint,
    )
    tokens, width = x.shape
    value_width = values.shape[1]
    rows = top_reducer_matrix.shape[0]
    count = heldout_sketched_signals.shape[0]

    factors = pl.pallas_call(
        factor_kernel,
        out_shape=jax.ShapeDtypeStruct((3 * rows, LANES), BF16),
        in_specs=[SMEM] + [VMEM] * 7,
        out_specs=VMEM,
        compiler_params=params(16),
        name="factors",
    )(
        me.reshape(1),
        top_rmsnorm_weights.reshape(width // LANES, LANES),
        top_reducer_matrix,
        bottom_expander_matrix.T,
        bottom_reducer_sketch,
        top_expander_matrix.T,
        bottom_reducer_matrix,
        bottom_expander_sketch.T,
    )
    panel = pl.pallas_call(
        panel_kernel,
        out_shape=jax.ShapeDtypeStruct(((LANES // 2 + 2) * count, LANES), BF16),
        in_specs=[VMEM] * 2,
        out_specs=VMEM,
        compiler_params=params(16),
        name="panel",
    )(heldout_sketched_signals, benchmark_labels.T)

    half = RING_CHIPS // 2
    pos, core = ring_pos(me // 2), me % 2
    pieces, slots = [], []
    for away, piece in ring(factors, half, half - 1):
        base = 2 * ring_chip((pos + away + RING_CHIPS) % RING_CHIPS)
        pieces += [piece, other_core(piece)]
        slots += [base + core, base + 1 - core]
    panels = []
    for _, piece in ring(panel, half - 1, half):
        panels += [piece, other_core(piece)]

    span, value_span = width // STEPS, value_width // STEPS
    by_column = lambda i: (0, i)
    by_row = lambda i: (i, 0)
    whole = lambda i: (0, 0)
    square = (tokens, LANES)
    lefts, right, x_target, adjoint_target, inverse = pl.pallas_call(
        functools.partial(local_kernel, width=width),
        grid=(STEPS,),
        out_shape=(
            jax.ShapeDtypeStruct((2 * tokens, LANES), BF16),
            jax.ShapeDtypeStruct(square, BF16),
            jax.ShapeDtypeStruct(square, F32),
            jax.ShapeDtypeStruct(square, F32),
            jax.ShapeDtypeStruct(square, F32),
        ),
        in_specs=[
            pl.BlockSpec((tokens, span), by_column),
            pl.BlockSpec((tokens, span), by_column),
            pl.BlockSpec((tokens, span), by_column),
            pl.BlockSpec((tokens, value_span), by_column),
            pl.BlockSpec((1, span), by_column),
            pl.BlockSpec((LANES // 2, span), by_column),
            pl.BlockSpec((span, LANES), by_row),
            pl.BlockSpec((value_span, LANES), by_row),
        ],
        out_specs=(
            pl.BlockSpec((2 * tokens, LANES), whole),
            pl.BlockSpec(square, whole),
            pl.BlockSpec(square, whole),
            pl.BlockSpec(square, whole),
            pl.BlockSpec(square, whole),
        ),
        scratch_shapes=[pltpu.VMEM(square, F32)] * 4,
        compiler_params=params(24),
        cost_estimate=cost(tokens * width * LANES * 12, 12 * MIB),
        name="local_products",
    )(
        x,
        mixed,
        adjoint,
        values,
        top_rmsnorm_weights.reshape(1, width),
        source_sketch.T,
        bottom_target_sketch,
        top_target_sketch,
    )

    unit = pl.pallas_call(
        functools.partial(feature_kernel, len(pieces)),
        out_shape=jax.ShapeDtypeStruct((LANES, LANES), BF16),
        in_specs=[SMEM, SMEM] + [ANY] * (len(pieces) + 5) + [VMEM] * 7,
        out_specs=VMEM,
        scratch_shapes=[
            pltpu.VMEM((len(pieces), 3 * rows, LANES), BF16),
            pltpu.VMEM(x.shape, BF16),
            pltpu.VMEM(x.shape, BF16),
            pltpu.VMEM(x.shape, BF16),
            pltpu.VMEM(values.shape, BF16),
            pltpu.VMEM(bottom_target_sketch.shape, BF16),
            pltpu.SemaphoreType.DMA((len(pieces),)),
            pltpu.SemaphoreType.DMA((STEPS, 5)),
        ],
        compiler_params=params(32),
        cost_estimate=cost(tokens * width * LANES * 12, 16 * MIB),
        name="features",
    )(
        jnp.stack(slots),
        sequence_token_counts,
        *pieces,
        x,
        mixed,
        adjoint,
        values,
        bottom_target_sketch,
        lefts,
        right,
        x_target,
        adjoint_target,
        inverse,
        top_expander_sketch.T,
        top_reducer_sketch,
    )

    task_best, scores = pl.pallas_call(
        functools.partial(score_kernel, len(panels), count),
        out_shape=(jax.ShapeDtypeStruct((2, TASKS), F32), jax.ShapeDtypeStruct((2,), F32)),
        in_specs=[VMEM] * (1 + len(panels)),
        out_specs=(SMEM, SMEM),
        scratch_shapes=[pltpu.VMEM((2, LANES // 2 * count, LANES), F32)],
        compiler_params=params(16),
        cost_estimate=cost(4 * MIB, 2 * MIB),
        name="scores",
    )(unit, *panels)
    return (scores, task_best)


def shards_of_any_slice(
    hidden_state_input,
    attention_mixed_state,
    hidden_state_adjoint,
    attention_values_adjoint,
    sequence_token_counts,
    heldout_sketched_signals,
    benchmark_labels,
    top_rmsnorm_weights,
    top_reducer_matrix,
    top_expander_matrix,
    bottom_reducer_matrix,
    bottom_expander_matrix,
    source_sketch,
    top_reducer_sketch,
    top_expander_sketch,
    top_target_sketch,
    bottom_reducer_sketch,
    bottom_expander_sketch,
    bottom_target_sketch,
    n,
):
    me = lax.axis_index("dp")
    x, mixed, adjoint, values = (
        hidden_state_input,
        attention_mixed_state,
        hidden_state_adjoint,
        attention_values_adjoint,
    )
    tokens, width = x.shape
    rows = top_reducer_matrix.shape[0]
    up_rows = top_expander_matrix.shape[1]
    rank = top_reducer_matrix.shape[1]
    k1 = source_sketch.shape[1]
    gain = top_rmsnorm_weights
    own_gain = lax.dynamic_slice_in_dim(gain, me * rows, rows)

    down_upper = (own_gain[:, None] * top_reducer_matrix.astype(F32)).astype(BF16)
    up_lower = mm(bottom_expander_matrix.T, bottom_reducer_sketch).astype(BF16)
    down_lower = mm(bottom_reducer_matrix, bottom_expander_sketch).astype(BF16)
    packed_lower = jnp.concatenate([down_lower[: rows // 2], down_lower[rows // 2 :]], axis=1)
    factors = jnp.concatenate([down_upper, up_lower, top_expander_matrix.T, packed_lower], axis=0)
    factors = lax.all_gather(factors, "dp")

    val_wide = heldout_sketched_signals.astype(F32)
    val_unit = (
        val_wide * lax.rsqrt(jnp.sum(val_wide * val_wide, axis=1, keepdims=True) + 1e-06)
    ).astype(BF16)
    labels = jnp.broadcast_to(benchmark_labels.astype(BF16), (val_unit.shape[0], 128))
    panel = jnp.concatenate([val_unit.reshape(-1, 128), labels], axis=0)
    panel = lax.all_gather(panel, "dp")
    val_rows = val_unit.shape[0]
    cut = panel.shape[1] - val_rows
    panel_tasks = panel[:, cut:, 0].reshape(n * val_rows, 1).astype(jnp.int32)
    panel = panel[:, :cut].reshape(n * val_rows, val_unit.shape[1])

    wide = x.astype(F32)
    inverse = lax.rsqrt(jnp.mean(wide * wide, axis=1, keepdims=True) + 1e-05)
    gained_sketch = (gain[:, None] * source_sketch.astype(F32)).astype(BF16)
    left_one = inverse * mm(x, gained_sketch)
    left_three = mm(mixed, source_sketch)
    right_two = ALPHA * mm(values, top_target_sketch)

    at = 0
    down_upper = factors[:, at : at + rows].reshape(width, rank)
    at += rows
    up_lower = factors[:, at : at + rows].reshape(width, -1)
    at += rows
    up_upper = factors[:, at : at + up_rows].reshape(-1, rank)
    at += up_rows
    down_lower = factors[:, at:]
    down_lower = jnp.concatenate([down_lower[:, :, :k1], down_lower[:, :, k1:]], axis=1)
    down_lower = down_lower.reshape(width, k1)

    reduced = inverse * mm(x, down_upper)
    left_two = mm(reduced.astype(BF16), top_expander_sketch)
    left_four = mm(mixed, down_lower)
    returned = mm(values, up_upper).astype(BF16)
    right_one = ALPHA * mm(returned, top_reducer_sketch)
    along = (ALPHA / width) * jnp.sum(returned.astype(F32) * reduced, axis=1, keepdims=True)
    targets = jnp.concatenate([up_lower, bottom_target_sketch], axis=1)
    bridge = mm_cols(down_upper, targets).astype(BF16)
    rights_low = mm(adjoint, targets) + inverse * (
        ALPHA * mm(returned, bridge) - (along * inverse) * mm(x, targets)
    )
    rights_low = ALPHA * rights_low
    k2 = up_lower.shape[1]
    lefts = (left_one, left_two, left_three, left_four)
    rights = (right_one, right_two, rights_low[:, :k2], rights_low[:, k2:])

    counts = sequence_token_counts[0]
    ends = jnp.cumsum(counts)
    starts = ends - counts
    places = jnp.arange(tokens, dtype=jnp.int32)[:, None]
    member = (places >= starts[None, :]) & (places < ends[None, :])
    count_ex = counts.shape[0]
    spread = jnp.concatenate(lefts, axis=0).astype(BF16)
    member = jnp.tile(member, (4, 1))
    spread = jnp.concatenate(
        [jnp.where(member[:, e : e + 1], spread, 0) for e in range(count_ex)], axis=1
    )
    feats = mm_cols(spread, jnp.concatenate(rights, axis=0).astype(BF16))
    feats = feats.reshape(count_ex, -1)
    squares = jnp.sum(feats * feats, axis=1, keepdims=True)
    unit_rows = (feats * lax.rsqrt(squares + 1e-06)).astype(BF16)

    score_scale = float(unit_rows.shape[1]) ** 0.5
    similar = score_scale * mm_rows(unit_rows, panel)
    task_mask = panel_tasks == jnp.arange(TASKS, dtype=jnp.int32)[None, :]
    task_best = jnp.max(
        jnp.where(task_mask[None, :, :], similar[:, :, None], -2.0 * score_scale), axis=1
    )
    return (jnp.mean(task_best, axis=1), task_best)


def solution(mesh):
    n = mesh.shape["dp"]
    split = P(("parts", "dp"), None)
    by_row, by_column, whole = P("dp", None), P(None, "dp"), P()
    placed = (
        (split,) * 5
        + (by_row, by_row, whole)
        + (by_row, by_column, by_row, by_column)
        + (whole,) * 7
    )
    ours = shards if n == 2 * RING_CHIPS else functools.partial(shards_of_any_slice, n=n)
    return jax.shard_map(
        ours,
        mesh=mesh,
        in_specs=placed,
        out_specs=(P(("parts", "dp")), split),
        check_vma=False,
    )
```

```python
import functools

import jax
import jax.numpy as jnp
from jax import lax
from jax.experimental import pallas as pl
from jax.experimental.pallas import tpu as pltpu
from jax.sharding import PartitionSpec as P

TASKS = 3
ALPHA = 4.0
F32 = jnp.float32
BF16 = jnp.bfloat16
RING_CHIPS = 8
LANES = 128
MIB = 1 << 20


def mm(a, b):
    return jnp.dot(a, b, preferred_element_type=F32)


def mm_rows(a, b):
    return lax.dot_general(a, b, (((1,), (1,)), ((), ())), preferred_element_type=F32)


def mm_cols(a, b):
    return lax.dot_general(a, b, (((0,), (0,)), ((), ())), preferred_element_type=F32)


def ring_chip(pos):
    half = RING_CHIPS // 2
    return jnp.where(pos < half, 2 * pos, 2 * (RING_CHIPS - 1 - pos) + 1)


def ring_pos(chip):
    row, side = chip // 2, chip % 2
    return jnp.where(side == 0, row, RING_CHIPS - 1 - row)


def hop(value, step):
    half = RING_CHIPS // 2
    place = [2 * q if q < half else 2 * (RING_CHIPS - 1 - q) + 1 for q in range(RING_CHIPS)]
    pairs = [
        (2 * place[q] + c, 2 * place[(q + step) % RING_CHIPS] + c)
        for q in range(RING_CHIPS)
        for c in range(2)
    ]
    return lax.ppermute(value, "dp", pairs)


def other_core(value):
    return lax.ppermute(value, "dp", [(d, d ^ 1) for d in range(2 * RING_CHIPS)])


def half_lanes(shape):
    return lax.broadcasted_iota(jnp.int32, shape, 1) < LANES // 2


def diagonal_column(row, first, count):
    shape = (count, row.shape[1])
    lane = lax.broadcasted_iota(jnp.int32, shape, 1)
    at = lax.broadcasted_iota(jnp.int32, shape, 0)
    return jnp.sum(jnp.where(lane == at + first, row, 0.0), axis=1, keepdims=True)


def load(pairs, sems):
    copies = [pltpu.make_async_copy(src, dst, sems.at[i]) for i, (src, dst) in enumerate(pairs)]
    for copy in copies:
        copy.start()
    return copies


def factor_kernel(me_ref, *refs):
    hbm, out_ref, held, sems = refs[:7], refs[7], refs[8:15], refs[15]
    gain_ref, down_up_ref, up_low_ref, sketch_ref, up_up_ref, down_low_ref, expand_ref = held
    copies = load(zip(hbm, held), sems)
    rows = down_up_ref.shape[0]
    half = LANES // 2
    copies[0].wait()
    copies[1].wait()
    for b in range(rows // half):
        place = me_ref[0] * (rows // half) + b
        row = gain_ref[pl.ds(place // 2, 1), :]
        column = diagonal_column(row, (place % 2) * half, half)
        part = down_up_ref[pl.ds(b * half, half), :].astype(F32)
        out_ref[pl.ds(b * half, half), :] = (column * part).astype(BF16)
    for copy in copies[2:]:
        copy.wait()
    at = rows
    out_ref[pl.ds(at, rows), :] = mm(up_low_ref[...], sketch_ref[...]).astype(BF16)
    at += rows
    out_ref[pl.ds(at, rows // 2), :] = up_up_ref[...]
    at += rows // 2
    expand = expand_ref[...]
    low = mm_rows(down_low_ref[...], jnp.concatenate([expand, expand], axis=0))
    first, second = low[: rows // 2], low[rows // 2 :]
    out_ref[pl.ds(at, rows // 2), :] = jnp.where(half_lanes(first.shape), first, second).astype(BF16)


def panel_kernel(val_hbm, label_hbm, out_ref, val_ref, label_ref, sems):
    for copy in load(((val_hbm, val_ref), (label_hbm, label_ref)), sems):
        copy.wait()
    wide = val_ref[...].astype(F32)
    count, width = wide.shape
    scale = lax.rsqrt(jnp.sum(wide * wide, axis=1, keepdims=True) + 1e-06)
    unit = wide * scale
    blocks = [unit[:, i * LANES : (i + 1) * LANES] for i in range(width // LANES)]
    row = label_ref[...].astype(F32)
    labels = jnp.broadcast_to(diagonal_column(row, 0, count), (count, LANES))
    blocks += [labels, labels]
    for i in range(0, len(blocks), 2):
        pair = jnp.concatenate(blocks[i : i + 2], axis=0)
        out_ref[pl.ds(i * count, 2 * count), :] = pair.astype(BF16)


X_LOW, X_DOWN, X_SOURCE, SQUARES, J_LOW, M_DOWN, M_SOURCE, VALUES, SUMS = 0, 2, 3, 4, 5, 7, 8, 9, 11


def stage_kernel(aways, first, last, me_ref, *refs):
    refs = list(refs)
    take = lambda k: [refs.pop(0) for _ in range(k)]
    counts_ref = take(1)[0] if last else None
    pieces = take(2 * len(aways))
    x_hbm, mixed_hbm, adjoint_hbm, values_hbm, gain_hbm, source_hbm, target_hbm, top_target_hbm = take(8)
    old_sums, old_bridge = (None, None) if first else take(2)
    expand_hbm, sketch_hbm = take(2) if last else (None, None)
    if last:
        (out_ref,) = take(1)
    else:
        new_sums, new_bridge = take(2)
    xs, ms, js, vs, gains, sources, low, down, up, packed, expand_ref, sketch_ref, sems = refs
    rows = down.shape[1] // 2
    half = rows // 2
    tokens, span = xs.shape[1:]
    pad = LANES // 2
    me = me_ref[0]
    pos, core = ring_pos(me // 2), me % 2

    copies = []
    for k, away in enumerate(aways):
        chip = ring_chip((pos + (away + RING_CHIPS)) % RING_CHIPS)
        odd = chip % 2
        mine = pl.ds(pl.multiple_of(chip * span, LANES), span)
        values_start = (chip // 2) * span + odd * (span // 2 - pad)
        values_window = pl.ds(pl.multiple_of(values_start, LANES), vs.shape[2])
        shift = odd * pad
        up[k, pl.ds(pl.multiple_of((1 - odd) * rows, 16), pad), :] = jnp.zeros((pad, 2 * LANES), BF16)
        pairs = []
        for piece, c in ((pieces[2 * k], core), (pieces[2 * k + 1], 1 - core)):
            one = pl.ds(pl.multiple_of(c * rows, 16), rows)
            part = pl.ds(pl.multiple_of(c * half, 16), half)
            up_part = pl.ds(pl.multiple_of(shift + c * half, 16), half)
            pairs += [
                (piece.at[pl.ds(0, rows)], down.at[k, one]),
                (piece.at[pl.ds(rows, rows)], low.at[k, one, pl.ds(0, LANES)]),
                (piece.at[pl.ds(2 * rows, half)], up.at[k, up_part, pl.ds(0, LANES)]),
                (piece.at[pl.ds(2 * rows + half, half)], packed.at[k, part]),
            ]
        pairs += [
            (target_hbm.at[mine], low.at[k, :, pl.ds(LANES, LANES)]),
            (
                top_target_hbm.at[pl.ds(pl.multiple_of(chip * rows, 16), rows)],
                up.at[k, pl.ds(pl.multiple_of(shift, 16), rows), pl.ds(LANES, LANES)],
            ),
            (source_hbm.at[:, mine], sources.at[k]),
            (gain_hbm.at[:, mine], gains.at[k]),
            (x_hbm.at[:, mine], xs.at[k]),
            (adjoint_hbm.at[:, mine], js.at[k]),
            (mixed_hbm.at[:, mine], ms.at[k]),
            (values_hbm.at[:, values_window], vs.at[k]),
        ]
        copies.append(load(pairs, sems.at[k]))
    if last:
        more = load(((expand_hbm, expand_ref), (sketch_hbm, sketch_ref)), sems.at[len(aways)])

    total = [None if first else old_sums[:, i * LANES : (i + 1) * LANES] for i in range(SUMS)]
    bridged = None if first else old_bridge[...]

    def add(column, value):
        for i in range(value.shape[1] // LANES):
            part = value[:, i * LANES : (i + 1) * LANES]
            total[column + i] = part if total[column + i] is None else total[column + i] + part

    for k in range(len(aways)):
        for copy in copies[k]:
            copy.wait()
        x, mixed = xs[k], ms[k]
        add(X_LOW, mm(x, low[k]))
        add(X_DOWN, mm(x, down[k]))
        source = sources[k]
        gained = (source.astype(F32) * gains[k]).astype(BF16)
        add(X_SOURCE, mm_rows(x, jnp.concatenate([gained, gained], axis=0)))
        square = jnp.zeros((tokens, LANES), F32)
        for i in range(span // LANES):
            wide = x[:, i * LANES : (i + 1) * LANES].astype(F32)
            square = square + wide * wide
        add(SQUARES, square)
        add(J_LOW, mm(js[k], low[k]))
        unpacked = []
        for c in range(2):
            both = packed[k, pl.ds(c * half, half), :].astype(F32)
            turned = pltpu.roll(both, LANES // 2, 1)
            lower = half_lanes(both.shape)
            unpacked += [jnp.where(lower, both, turned), jnp.where(lower, turned, both)]
        add(M_DOWN, mm(mixed, jnp.concatenate(unpacked, axis=0).astype(BF16)))
        add(M_SOURCE, mm_rows(mixed, jnp.concatenate([source, source], axis=0)))
        add(VALUES, mm(vs[k], up[k]))
        product = mm_cols(down[k], low[k])
        bridged = product if bridged is None else bridged + product

    if not last:
        for i in range(SUMS):
            new_sums[:, i * LANES : (i + 1) * LANES] = total[i]
        new_bridge[...] = bridged
        return

    for copy in more:
        copy.wait()
    width = x_hbm.shape[1]
    mean = jnp.sum(total[SQUARES], axis=1, keepdims=True) * (1.0 / width)
    inverse = lax.rsqrt(mean + 1e-05)
    reduced = inverse * total[X_DOWN]
    expand = expand_ref[...]
    left_two = mm_rows(reduced.astype(BF16), jnp.concatenate([expand, expand], axis=0))
    returned = total[VALUES].astype(BF16)
    right_one = ALPHA * mm(returned, sketch_ref[...])
    along = (ALPHA / width) * jnp.sum(returned.astype(F32) * reduced, axis=1, keepdims=True)
    back = mm(returned, bridged.astype(BF16))
    along = along * inverse
    lows = [
        total[J_LOW + i]
        + inverse * (ALPHA * back[:, i * LANES : (i + 1) * LANES] - along * total[X_LOW + i])
        for i in range(2)
    ]
    rights = (right_one, ALPHA * total[VALUES + 1], ALPHA * lows[0], ALPHA * lows[1])
    lefts = (inverse * total[X_SOURCE], left_two, total[M_SOURCE], total[M_DOWN])
    place = lax.broadcasted_iota(jnp.int32, (tokens, LANES), 0)
    one, two = counts_ref[0, 0], counts_ref[0, 1]
    lower = half_lanes((tokens, LANES))
    member = (place >= jnp.where(lower, 0, one)) & (place < jnp.where(lower, one, one + two))
    spread = jnp.concatenate([jnp.where(member, left, 0.0).astype(BF16) for left in lefts], axis=0)
    feats = mm_cols(spread, jnp.concatenate([right.astype(BF16) for right in rights], axis=0))
    for e in range(2):
        own = feats[e * pad : (e + 1) * pad]
        squares = jnp.sum(own * own, keepdims=True)
        out_ref[pl.ds(e * pad, pad), :] = (own * lax.rsqrt(squares + 1e-06)).astype(BF16)


def score_kernel(pieces, count, unit_ref, *refs):
    piece_refs = refs[:pieces]
    best_ref, mean_ref, spread = refs[pieces:]
    half = LANES // 2
    scale = float(half * LANES) ** 0.5
    for e in range(2):
        for i in range(half):
            row = unit_ref[pl.ds(e * half + i, 1), :].astype(F32)
            spread[e, pl.ds(i * count, count), :] = jnp.broadcast_to(row, (count, LANES))
    best = [[jnp.full((count, LANES), -2.0 * scale, F32) for _ in range(TASKS)] for _ in range(2)]
    for piece in piece_refs:
        wide = piece[pl.ds(0, half * count), :].astype(F32)
        labels = piece[pl.ds(half * count, 2 * count), :].astype(F32)[:count]
        for e in range(2):
            products = wide * spread[e]
            total = jnp.sum(products.reshape(half, count, LANES), axis=0)
            similar = scale * jnp.sum(total, axis=1, keepdims=True)
            for t in range(TASKS):
                here = jnp.where(labels == float(t), similar, -2.0 * scale)
                best[e][t] = jnp.maximum(best[e][t], here)
    for e in range(2):
        values = [jnp.max(best[e][t]) for t in range(TASKS)]
        for t in range(TASKS):
            best_ref[e, t] = values[t]
        mean_ref[e] = (values[0] + values[1] + values[2]) * (1.0 / TASKS)


VMEM = pl.BlockSpec(memory_space=pltpu.VMEM)
SMEM = pl.BlockSpec(memory_space=pltpu.SMEM)
ANY = pl.BlockSpec(memory_space=pl.ANY)
HBM = pl.BlockSpec(memory_space=pltpu.HBM)


def params(mib):
    return pltpu.CompilerParams(vmem_limit_bytes=mib * MIB)


def cost(flops, nbytes):
    return pl.CostEstimate(flops=flops, bytes_accessed=nbytes, transcendentals=0)


def shards(
    hidden_state_input,
    attention_mixed_state,
    hidden_state_adjoint,
    attention_values_adjoint,
    sequence_token_counts,
    heldout_sketched_signals,
    benchmark_labels,
    top_rmsnorm_weights,
    top_reducer_matrix,
    top_expander_matrix,
    bottom_reducer_matrix,
    bottom_expander_matrix,
    source_sketch,
    top_reducer_sketch,
    top_expander_sketch,
    top_target_sketch,
    bottom_reducer_sketch,
    bottom_expander_sketch,
    bottom_target_sketch,
):
    me = lax.axis_index("dp").astype(jnp.int32)
    x, mixed, adjoint, values = (
        hidden_state_input,
        attention_mixed_state,
        hidden_state_adjoint,
        attention_values_adjoint,
    )
    tokens, width = x.shape
    rows = top_reducer_matrix.shape[0]
    count = heldout_sketched_signals.shape[0]

    inputs = (
        top_rmsnorm_weights.reshape(width // LANES, LANES),
        top_reducer_matrix,
        bottom_expander_matrix.T,
        bottom_reducer_sketch,
        top_expander_matrix.T,
        bottom_reducer_matrix,
        bottom_expander_sketch.T,
    )
    factors = pl.pallas_call(
        factor_kernel,
        out_shape=jax.ShapeDtypeStruct((3 * rows, LANES), BF16),
        in_specs=[SMEM] + [HBM] * len(inputs),
        out_specs=VMEM,
        scratch_shapes=[pltpu.VMEM(a.shape, a.dtype) for a in inputs]
        + [pltpu.SemaphoreType.DMA((len(inputs),))],
        compiler_params=params(8),
        name="factors",
    )(me.reshape(1), *inputs)
    inputs = (heldout_sketched_signals, benchmark_labels.T)
    panel = pl.pallas_call(
        panel_kernel,
        out_shape=jax.ShapeDtypeStruct(((LANES // 2 + 2) * count, LANES), BF16),
        in_specs=[HBM] * len(inputs),
        out_specs=VMEM,
        scratch_shapes=[pltpu.VMEM(a.shape, a.dtype) for a in inputs]
        + [pltpu.SemaphoreType.DMA((len(inputs),))],
        compiler_params=params(8),
        name="panel",
    )(*inputs)

    span = 2 * rows
    activations = (
        x,
        mixed,
        adjoint,
        values,
        top_rmsnorm_weights.reshape(1, width),
        source_sketch.T,
        bottom_target_sketch,
        top_target_sketch,
    )

    def stage(aways, pieces, sums=(), last=False):
        first, n = not sums, len(aways)
        sums_shape, bridge_shape = (tokens, SUMS * LANES), (LANES, 2 * LANES)
        small = (top_expander_sketch.T, top_reducer_sketch)
        head = [me.reshape(1)] + ([sequence_token_counts] if last else [])
        start = len(head) + len(pieces) + len(activations)
        return pl.pallas_call(
            functools.partial(stage_kernel, aways, first, last),
            out_shape=jax.ShapeDtypeStruct((LANES, LANES), BF16)
            if last
            else (jax.ShapeDtypeStruct(sums_shape, F32), jax.ShapeDtypeStruct(bridge_shape, F32)),
            in_specs=[SMEM] * len(head)
            + [ANY] * len(pieces)
            + [HBM] * len(activations)
            + [VMEM] * len(sums)
            + ([HBM] * 2 if last else []),
            out_specs=VMEM if last else (VMEM, VMEM),
            scratch_shapes=[
                pltpu.VMEM((n, tokens, span), BF16),
                pltpu.VMEM((n, tokens, span), BF16),
                pltpu.VMEM((n, tokens, span), BF16),
                pltpu.VMEM((n, tokens, rows + LANES // 2), BF16),
                pltpu.VMEM((n, 1, span), F32),
                pltpu.VMEM((n, LANES // 2, span), BF16),
                pltpu.VMEM((n, span, 2 * LANES), BF16),
                pltpu.VMEM((n, span, LANES), BF16),
                pltpu.VMEM((n, rows + LANES // 2, 2 * LANES), BF16),
                pltpu.VMEM((n, rows, LANES), BF16),
                pltpu.VMEM(small[0].shape, BF16),
                pltpu.VMEM(small[1].shape, BF16),
                pltpu.SemaphoreType.DMA((n + 1, 16)),
            ],
            input_output_aliases={} if first or last else {start: 0, start + 1: 1},
            compiler_params=params(16),
            cost_estimate=cost(n * tokens * span * LANES * 24, 3 * n * MIB),
            name="features" if last else "stage",
        )(*head, *pieces, *activations, *sums, *(small if last else ()))

    tie = lax.optimization_barrier
    half = RING_CHIPS // 2
    up = down = factors
    panel_up = panel_down = panel
    sums = ()
    held = [factors, other_core(factors)]
    aways = (0,)
    panels = [panel, other_core(panel)]
    for k in range(1, half + 1):
        up = hop(up, 1)
        down = hop(down, -1) if k < half else down
        panel_up = hop(panel_up, 1) if k < half else panel_up
        panel_down = hop(panel_down, -1)
        sums = stage(aways, held, sums)
        up, down = tie((up, down))
        panel_up, panel_down, _, _ = tie((panel_up, panel_down, up, down))
        aways = (-k, k) if k < half else (-half,)
        held = [up, other_core(up)]
        if k < half:
            held += [down, other_core(down)]
            panels += [panel_up, other_core(panel_up)]
        panels += [panel_down, other_core(panel_down)]
    unit = stage(aways, held, sums, last=True)

    task_best, scores = pl.pallas_call(
        functools.partial(score_kernel, len(panels), count),
        out_shape=(jax.ShapeDtypeStruct((2, TASKS), F32), jax.ShapeDtypeStruct((2,), F32)),
        in_specs=[VMEM] * (1 + len(panels)),
        out_specs=(SMEM, SMEM),
        scratch_shapes=[pltpu.VMEM((2, LANES // 2 * count, LANES), F32)],
        compiler_params=params(16),
        cost_estimate=cost(4 * MIB, 2 * MIB),
        name="scores",
    )(unit, *panels)
    return (scores, task_best)


def shards_of_any_slice(
    hidden_state_input,
    attention_mixed_state,
    hidden_state_adjoint,
    attention_values_adjoint,
    sequence_token_counts,
    heldout_sketched_signals,
    benchmark_labels,
    top_rmsnorm_weights,
    top_reducer_matrix,
    top_expander_matrix,
    bottom_reducer_matrix,
    bottom_expander_matrix,
    source_sketch,
    top_reducer_sketch,
    top_expander_sketch,
    top_target_sketch,
    bottom_reducer_sketch,
    bottom_expander_sketch,
    bottom_target_sketch,
    n,
):
    me = lax.axis_index("dp")
    x, mixed, adjoint, values = (
        hidden_state_input,
        attention_mixed_state,
        hidden_state_adjoint,
        attention_values_adjoint,
    )
    tokens, width = x.shape
    rows = top_reducer_matrix.shape[0]
    up_rows = top_expander_matrix.shape[1]
    rank = top_reducer_matrix.shape[1]
    k1 = source_sketch.shape[1]
    gain = top_rmsnorm_weights
    own_gain = lax.dynamic_slice_in_dim(gain, me * rows, rows)

    down_upper = (own_gain[:, None] * top_reducer_matrix.astype(F32)).astype(BF16)
    up_lower = mm(bottom_expander_matrix.T, bottom_reducer_sketch).astype(BF16)
    down_lower = mm(bottom_reducer_matrix, bottom_expander_sketch).astype(BF16)
    packed_lower = jnp.concatenate([down_lower[: rows // 2], down_lower[rows // 2 :]], axis=1)
    factors = jnp.concatenate([down_upper, up_lower, top_expander_matrix.T, packed_lower], axis=0)
    factors = lax.all_gather(factors, "dp")

    val_wide = heldout_sketched_signals.astype(F32)
    val_unit = (
        val_wide * lax.rsqrt(jnp.sum(val_wide * val_wide, axis=1, keepdims=True) + 1e-06)
    ).astype(BF16)
    labels = jnp.broadcast_to(benchmark_labels.astype(BF16), (val_unit.shape[0], 128))
    panel = jnp.concatenate([val_unit.reshape(-1, 128), labels], axis=0)
    panel = lax.all_gather(panel, "dp")
    val_rows = val_unit.shape[0]
    cut = panel.shape[1] - val_rows
    panel_tasks = panel[:, cut:, 0].reshape(n * val_rows, 1).astype(jnp.int32)
    panel = panel[:, :cut].reshape(n * val_rows, val_unit.shape[1])

    wide = x.astype(F32)
    inverse = lax.rsqrt(jnp.mean(wide * wide, axis=1, keepdims=True) + 1e-05)
    gained_sketch = (gain[:, None] * source_sketch.astype(F32)).astype(BF16)
    left_one = inverse * mm(x, gained_sketch)
    left_three = mm(mixed, source_sketch)
    right_two = ALPHA * mm(values, top_target_sketch)

    at = 0
    down_upper = factors[:, at : at + rows].reshape(width, rank)
    at += rows
    up_lower = factors[:, at : at + rows].reshape(width, -1)
    at += rows
    up_upper = factors[:, at : at + up_rows].reshape(-1, rank)
    at += up_rows
    down_lower = factors[:, at:]
    down_lower = jnp.concatenate([down_lower[:, :, :k1], down_lower[:, :, k1:]], axis=1)
    down_lower = down_lower.reshape(width, k1)

    reduced = inverse * mm(x, down_upper)
    left_two = mm(reduced.astype(BF16), top_expander_sketch)
    left_four = mm(mixed, down_lower)
    returned = mm(values, up_upper).astype(BF16)
    right_one = ALPHA * mm(returned, top_reducer_sketch)
    along = (ALPHA / width) * jnp.sum(returned.astype(F32) * reduced, axis=1, keepdims=True)
    targets = jnp.concatenate([up_lower, bottom_target_sketch], axis=1)
    bridge = mm_cols(down_upper, targets).astype(BF16)
    rights_low = mm(adjoint, targets) + inverse * (
        ALPHA * mm(returned, bridge) - (along * inverse) * mm(x, targets)
    )
    rights_low = ALPHA * rights_low
    k2 = up_lower.shape[1]
    lefts = (left_one, left_two, left_three, left_four)
    rights = (right_one, right_two, rights_low[:, :k2], rights_low[:, k2:])

    counts = sequence_token_counts[0]
    ends = jnp.cumsum(counts)
    starts = ends - counts
    places = jnp.arange(tokens, dtype=jnp.int32)[:, None]
    member = (places >= starts[None, :]) & (places < ends[None, :])
    count_ex = counts.shape[0]
    spread = jnp.concatenate(lefts, axis=0).astype(BF16)
    member = jnp.tile(member, (4, 1))
    spread = jnp.concatenate(
        [jnp.where(member[:, e : e + 1], spread, 0) for e in range(count_ex)], axis=1
    )
    feats = mm_cols(spread, jnp.concatenate(rights, axis=0).astype(BF16))
    feats = feats.reshape(count_ex, -1)
    squares = jnp.sum(feats * feats, axis=1, keepdims=True)
    unit_rows = (feats * lax.rsqrt(squares + 1e-06)).astype(BF16)

    score_scale = float(unit_rows.shape[1]) ** 0.5
    similar = score_scale * mm_rows(unit_rows, panel)
    task_mask = panel_tasks == jnp.arange(TASKS, dtype=jnp.int32)[None, :]
    task_best = jnp.max(
        jnp.where(task_mask[None, :, :], similar[:, :, None], -2.0 * score_scale), axis=1
    )
    return (jnp.mean(task_best, axis=1), task_best)


def solution(mesh):
    n = mesh.shape["dp"]
    split = P(("parts", "dp"), None)
    by_row, by_column, whole = P("dp", None), P(None, "dp"), P()
    placed = (
        (split,) * 5
        + (by_row, by_row, whole)
        + (by_row, by_column, by_row, by_column)
        + (whole,) * 7
    )
    ours = shards if n == 2 * RING_CHIPS else functools.partial(shards_of_any_slice, n=n)
    return jax.shard_map(
        ours,
        mesh=mesh,
        in_specs=placed,
        out_specs=(P(("parts", "dp")), split),
        check_vma=False,
    )
```

```python
import functools

import jax
import jax.numpy as jnp
from jax import lax
from jax.experimental import pallas as pl
from jax.experimental.pallas import tpu as pltpu
from jax.sharding import PartitionSpec as P

TASKS = 3
ALPHA = 4.0
F32 = jnp.float32
BF16 = jnp.bfloat16
RING_CHIPS = 8
LANES = 128
MIB = 1 << 20


def mm(a, b):
    return jnp.dot(a, b, preferred_element_type=F32)


def mm_rows(a, b):
    return lax.dot_general(a, b, (((1,), (1,)), ((), ())), preferred_element_type=F32)


def mm_cols(a, b):
    return lax.dot_general(a, b, (((0,), (0,)), ((), ())), preferred_element_type=F32)


def ring_chip(pos):
    half = RING_CHIPS // 2
    return jnp.where(pos < half, 2 * pos, 2 * (RING_CHIPS - 1 - pos) + 1)


def ring_pos(chip):
    row, side = chip // 2, chip % 2
    return jnp.where(side == 0, row, RING_CHIPS - 1 - row)


def hop(value):
    half = RING_CHIPS // 2
    place = [2 * q if q < half else 2 * (RING_CHIPS - 1 - q) + 1 for q in range(RING_CHIPS)]
    pairs = []
    for q in range(RING_CHIPS):
        pairs.append((2 * place[q], 2 * place[(q + 1) % RING_CHIPS]))
        pairs.append((2 * place[q] + 1, 2 * place[(q - 1) % RING_CHIPS] + 1))
    return lax.ppermute(value, "dp", pairs)


def other_core(value):
    return lax.ppermute(value, "dp", [(d, d ^ 1) for d in range(2 * RING_CHIPS)])


def half_lanes(shape):
    return lax.broadcasted_iota(jnp.int32, shape, 1) < LANES // 2


def diagonal_column(row, first, count):
    shape = (count, row.shape[1])
    lane = lax.broadcasted_iota(jnp.int32, shape, 1)
    at = lax.broadcasted_iota(jnp.int32, shape, 0)
    return jnp.sum(jnp.where(lane == at + first, row, 0.0), axis=1, keepdims=True)


def load(pairs, sems):
    copies = [pltpu.make_async_copy(src, dst, sems.at[i]) for i, (src, dst) in enumerate(pairs)]
    for copy in copies:
        copy.start()
    return copies


def pack_kernel(me_ref, *refs):
    hbm, out_ref, held, sems = refs[:9], refs[9], refs[10:19], refs[19]
    gain_ref, down_up_ref, up_low_ref, sketch_ref, up_up_ref, down_low_ref, expand_ref, val_ref, label_ref = held
    copies = load(zip(hbm, held), sems)
    rows = down_up_ref.shape[0]
    half = LANES // 2
    for copy in copies:
        copy.wait()
    for b in range(rows // half):
        place = me_ref[0] * (rows // half) + b
        row = gain_ref[pl.ds(place // 2, 1), :]
        column = diagonal_column(row, (place % 2) * half, half)
        part = down_up_ref[pl.ds(b * half, half), :].astype(F32)
        out_ref[pl.ds(b * half, half), :] = (column * part).astype(BF16)
    at = rows
    out_ref[pl.ds(at, rows), :] = mm(up_low_ref[...], sketch_ref[...]).astype(BF16)
    at += rows
    out_ref[pl.ds(at, rows // 2), :] = up_up_ref[...]
    at += rows // 2
    expand = expand_ref[...]
    low = mm_rows(down_low_ref[...], jnp.concatenate([expand, expand], axis=0))
    first, second = low[: rows // 2], low[rows // 2 :]
    out_ref[pl.ds(at, rows // 2), :] = jnp.where(half_lanes(first.shape), first, second).astype(BF16)
    at += rows // 2
    wide = val_ref[...].astype(F32)
    count, width = wide.shape
    scale = lax.rsqrt(jnp.sum(wide * wide, axis=1, keepdims=True) + 1e-06)
    unit = wide * scale
    blocks = [unit[:, i * LANES : (i + 1) * LANES] for i in range(width // LANES)]
    row = label_ref[...].astype(F32)
    labels = jnp.broadcast_to(diagonal_column(row, 0, count), (count, LANES))
    blocks += [labels, labels]
    for i in range(0, len(blocks), 2):
        pair = jnp.concatenate(blocks[i : i + 2], axis=0)
        out_ref[pl.ds(at + i * count, 2 * count), :] = pair.astype(BF16)


X_LOW, X_DOWN, X_SOURCE, SQUARES, J_LOW, M_DOWN, M_SOURCE, VALUES, SUMS = 0, 2, 3, 4, 5, 7, 8, 9, 11


def stage_kernel(aways, first, last, me_ref, *refs):
    refs = list(refs)
    take = lambda k: [refs.pop(0) for _ in range(k)]
    counts_ref = take(1)[0] if last else None
    pieces = take(2 * len(aways))
    x_hbm, mixed_hbm, adjoint_hbm, values_hbm, gain_hbm, source_hbm, target_hbm, top_target_hbm = take(8)
    old_sums, old_bridge = (None, None) if first else take(2)
    expand_hbm, sketch_hbm = take(2) if last else (None, None)
    if last:
        (out_ref,) = take(1)
    else:
        new_sums, new_bridge = take(2)
    xs, ms, js, vs, gains, sources, low, down, up, packed, expand_ref, sketch_ref, sems = refs
    rows = down.shape[1] // 2
    half = rows // 2
    tokens, span = xs.shape[1:]
    pad = LANES // 2
    me = me_ref[0]
    pos, core = ring_pos(me // 2), me % 2

    copies = []
    for k, away in enumerate(aways):
        chip = ring_chip((pos + away * (2 * core - 1) + RING_CHIPS) % RING_CHIPS)
        odd = chip % 2
        mine = pl.ds(pl.multiple_of(chip * span, LANES), span)
        values_start = (chip // 2) * span + odd * (span // 2 - pad)
        values_window = pl.ds(pl.multiple_of(values_start, LANES), vs.shape[2])
        shift = odd * pad
        up[k, pl.ds(pl.multiple_of((1 - odd) * rows, 16), pad), :] = jnp.zeros((pad, 2 * LANES), BF16)
        pairs = []
        side = core if away >= 0 else 1 - core
        for piece, c in ((pieces[2 * k], side), (pieces[2 * k + 1], 1 - side)):
            one = pl.ds(pl.multiple_of(c * rows, 16), rows)
            part = pl.ds(pl.multiple_of(c * half, 16), half)
            up_part = pl.ds(pl.multiple_of(shift + c * half, 16), half)
            pairs += [
                (piece.at[pl.ds(0, rows)], down.at[k, one]),
                (piece.at[pl.ds(rows, rows)], low.at[k, one, pl.ds(0, LANES)]),
                (piece.at[pl.ds(2 * rows, half)], up.at[k, up_part, pl.ds(0, LANES)]),
                (piece.at[pl.ds(2 * rows + half, half)], packed.at[k, part]),
            ]
        pairs += [
            (target_hbm.at[mine], low.at[k, :, pl.ds(LANES, LANES)]),
            (
                top_target_hbm.at[pl.ds(pl.multiple_of(chip * rows, 16), rows)],
                up.at[k, pl.ds(pl.multiple_of(shift, 16), rows), pl.ds(LANES, LANES)],
            ),
            (source_hbm.at[:, mine], sources.at[k]),
            (gain_hbm.at[:, mine], gains.at[k]),
            (x_hbm.at[:, mine], xs.at[k]),
            (adjoint_hbm.at[:, mine], js.at[k]),
            (mixed_hbm.at[:, mine], ms.at[k]),
            (values_hbm.at[:, values_window], vs.at[k]),
        ]
        copies.append(load(pairs, sems.at[k]))
    if last:
        more = load(((expand_hbm, expand_ref), (sketch_hbm, sketch_ref)), sems.at[len(aways)])

    total = [None if first else old_sums[:, i * LANES : (i + 1) * LANES] for i in range(SUMS)]
    bridged = None if first else old_bridge[...]

    def add(column, value):
        for i in range(value.shape[1] // LANES):
            part = value[:, i * LANES : (i + 1) * LANES]
            total[column + i] = part if total[column + i] is None else total[column + i] + part

    for k in range(len(aways)):
        for copy in copies[k]:
            copy.wait()
        x, mixed = xs[k], ms[k]
        add(X_LOW, mm(x, low[k]))
        add(X_DOWN, mm(x, down[k]))
        source = sources[k]
        gained = (source.astype(F32) * gains[k]).astype(BF16)
        add(X_SOURCE, mm_rows(x, jnp.concatenate([gained, gained], axis=0)))
        square = jnp.zeros((tokens, LANES), F32)
        for i in range(span // LANES):
            wide = x[:, i * LANES : (i + 1) * LANES].astype(F32)
            square = square + wide * wide
        add(SQUARES, square)
        add(J_LOW, mm(js[k], low[k]))
        unpacked = []
        for c in range(2):
            both = packed[k, pl.ds(c * half, half), :].astype(F32)
            turned = pltpu.roll(both, LANES // 2, 1)
            lower = half_lanes(both.shape)
            unpacked += [jnp.where(lower, both, turned), jnp.where(lower, turned, both)]
        add(M_DOWN, mm(mixed, jnp.concatenate(unpacked, axis=0).astype(BF16)))
        add(M_SOURCE, mm_rows(mixed, jnp.concatenate([source, source], axis=0)))
        add(VALUES, mm(vs[k], up[k]))
        product = mm_cols(down[k], low[k])
        bridged = product if bridged is None else bridged + product

    if not last:
        for i in range(SUMS):
            new_sums[:, i * LANES : (i + 1) * LANES] = total[i]
        new_bridge[...] = bridged
        return

    for copy in more:
        copy.wait()
    width = x_hbm.shape[1]
    mean = jnp.sum(total[SQUARES], axis=1, keepdims=True) * (1.0 / width)
    inverse = lax.rsqrt(mean + 1e-05)
    reduced = inverse * total[X_DOWN]
    expand = expand_ref[...]
    left_two = mm_rows(reduced.astype(BF16), jnp.concatenate([expand, expand], axis=0))
    returned = total[VALUES].astype(BF16)
    right_one = ALPHA * mm(returned, sketch_ref[...])
    along = (ALPHA / width) * jnp.sum(returned.astype(F32) * reduced, axis=1, keepdims=True)
    back = mm(returned, bridged.astype(BF16))
    along = along * inverse
    lows = [
        total[J_LOW + i]
        + inverse * (ALPHA * back[:, i * LANES : (i + 1) * LANES] - along * total[X_LOW + i])
        for i in range(2)
    ]
    rights = (right_one, ALPHA * total[VALUES + 1], ALPHA * lows[0], ALPHA * lows[1])
    lefts = (inverse * total[X_SOURCE], left_two, total[M_SOURCE], total[M_DOWN])
    place = lax.broadcasted_iota(jnp.int32, (tokens, LANES), 0)
    one, two = counts_ref[0, 0], counts_ref[0, 1]
    lower = half_lanes((tokens, LANES))
    member = (place >= jnp.where(lower, 0, one)) & (place < jnp.where(lower, one, one + two))
    spread = jnp.concatenate([jnp.where(member, left, 0.0).astype(BF16) for left in lefts], axis=0)
    feats = mm_cols(spread, jnp.concatenate([right.astype(BF16) for right in rights], axis=0))
    for e in range(2):
        own = feats[e * pad : (e + 1) * pad]
        squares = jnp.sum(own * own, keepdims=True)
        out_ref[pl.ds(e * pad, pad), :] = (own * lax.rsqrt(squares + 1e-06)).astype(BF16)


def score_kernel(pieces, count, start, unit_ref, *refs):
    piece_refs = refs[:pieces]
    best_ref, mean_ref, spread = refs[pieces:]
    half = LANES // 2
    scale = float(half * LANES) ** 0.5
    for e in range(2):
        for i in range(half):
            row = unit_ref[pl.ds(e * half + i, 1), :].astype(F32)
            spread[e, pl.ds(i * count, count), :] = jnp.broadcast_to(row, (count, LANES))
    best = [[jnp.full((count, LANES), -2.0 * scale, F32) for _ in range(TASKS)] for _ in range(2)]
    for piece in piece_refs:
        wide = piece[pl.ds(start, half * count), :].astype(F32)
        labels = piece[pl.ds(start + half * count, 2 * count), :].astype(F32)[:count]
        for e in range(2):
            products = wide * spread[e]
            total = jnp.sum(products.reshape(half, count, LANES), axis=0)
            similar = scale * jnp.sum(total, axis=1, keepdims=True)
            for t in range(TASKS):
                here = jnp.where(labels == float(t), similar, -2.0 * scale)
                best[e][t] = jnp.maximum(best[e][t], here)
    for e in range(2):
        values = [jnp.max(best[e][t]) for t in range(TASKS)]
        for t in range(TASKS):
            best_ref[e, t] = values[t]
        mean_ref[e] = (values[0] + values[1] + values[2]) * (1.0 / TASKS)


VMEM = pl.BlockSpec(memory_space=pltpu.VMEM)
SMEM = pl.BlockSpec(memory_space=pltpu.SMEM)
ANY = pl.BlockSpec(memory_space=pl.ANY)
HBM = pl.BlockSpec(memory_space=pltpu.HBM)


def in_hbm(arrays):
    return [pltpu.with_memory_space_constraint(a, pltpu.HBM) for a in arrays]


def params(mib):
    return pltpu.CompilerParams(vmem_limit_bytes=mib * MIB)


def cost(flops, nbytes):
    return pl.CostEstimate(flops=flops, bytes_accessed=nbytes, transcendentals=0)


def shards(
    hidden_state_input,
    attention_mixed_state,
    hidden_state_adjoint,
    attention_values_adjoint,
    sequence_token_counts,
    heldout_sketched_signals,
    benchmark_labels,
    top_rmsnorm_weights,
    top_reducer_matrix,
    top_expander_matrix,
    bottom_reducer_matrix,
    bottom_expander_matrix,
    source_sketch,
    top_reducer_sketch,
    top_expander_sketch,
    top_target_sketch,
    bottom_reducer_sketch,
    bottom_expander_sketch,
    bottom_target_sketch,
):
    me = lax.axis_index("dp").astype(jnp.int32)
    x, mixed, adjoint, values = (
        hidden_state_input,
        attention_mixed_state,
        hidden_state_adjoint,
        attention_values_adjoint,
    )
    tokens, width = x.shape
    rows = top_reducer_matrix.shape[0]
    count = heldout_sketched_signals.shape[0]

    inputs = (
        top_rmsnorm_weights.reshape(width // LANES, LANES),
        top_reducer_matrix,
        bottom_expander_matrix.T,
        bottom_reducer_sketch,
        top_expander_matrix.T,
        bottom_reducer_matrix,
        bottom_expander_sketch.T,
        heldout_sketched_signals,
        benchmark_labels.T,
    )
    own = pl.pallas_call(
        pack_kernel,
        out_shape=jax.ShapeDtypeStruct((3 * rows + (LANES // 2 + 2) * count, LANES), BF16),
        in_specs=[SMEM] + [HBM] * len(inputs),
        out_specs=VMEM,
        scratch_shapes=[pltpu.VMEM(a.shape, a.dtype) for a in inputs]
        + [pltpu.SemaphoreType.DMA((len(inputs),))],
        compiler_params=params(8),
        name="pack",
    )(me.reshape(1), *in_hbm(inputs))

    span = 2 * rows
    activations = (
        x,
        mixed,
        adjoint,
        values,
        top_rmsnorm_weights.reshape(1, width),
        source_sketch.T,
        bottom_target_sketch,
        top_target_sketch,
    )

    def stage(aways, pieces, sums=(), last=False):
        first, n = not sums, len(aways)
        sums_shape, bridge_shape = (tokens, SUMS * LANES), (LANES, 2 * LANES)
        small = (top_expander_sketch.T, top_reducer_sketch)
        head = [me.reshape(1)] + ([sequence_token_counts] if last else [])
        start = len(head) + len(pieces) + len(activations)
        return pl.pallas_call(
            functools.partial(stage_kernel, aways, first, last),
            out_shape=jax.ShapeDtypeStruct((LANES, LANES), BF16)
            if last
            else (jax.ShapeDtypeStruct(sums_shape, F32), jax.ShapeDtypeStruct(bridge_shape, F32)),
            in_specs=[SMEM] * len(head)
            + [ANY] * len(pieces)
            + [HBM] * len(activations)
            + [VMEM] * len(sums)
            + ([HBM] * 2 if last else []),
            out_specs=VMEM if last else (VMEM, VMEM),
            scratch_shapes=[
                pltpu.VMEM((n, tokens, span), BF16),
                pltpu.VMEM((n, tokens, span), BF16),
                pltpu.VMEM((n, tokens, span), BF16),
                pltpu.VMEM((n, tokens, rows + LANES // 2), BF16),
                pltpu.VMEM((n, 1, span), F32),
                pltpu.VMEM((n, LANES // 2, span), BF16),
                pltpu.VMEM((n, span, 2 * LANES), BF16),
                pltpu.VMEM((n, span, LANES), BF16),
                pltpu.VMEM((n, rows + LANES // 2, 2 * LANES), BF16),
                pltpu.VMEM((n, rows, LANES), BF16),
                pltpu.VMEM(small[0].shape, BF16),
                pltpu.VMEM(small[1].shape, BF16),
                pltpu.SemaphoreType.DMA((n + 1, 16)),
            ],
            input_output_aliases={} if first or last else {start: 0, start + 1: 1},
            compiler_params=params(16),
            cost_estimate=cost(n * tokens * span * LANES * 24, 3 * n * MIB),
            name="features" if last else "stage",
        )(*head, *pieces, *in_hbm(activations), *sums, *in_hbm(small if last else ()))

    tie = lax.optimization_barrier
    half = RING_CHIPS // 2
    first, second = own, other_core(own)
    held, aways, sums = [first, second], (0,), ()
    blocks = list(held)
    for k in range(1, half + 1):
        first = hop(first)
        if k == half:
            held, aways, sums = [first, other_core(first)], (half,), stage(aways, held, sums)
        else:
            second = hop(second)
            old, held = held, [first, second, other_core(first), other_core(second)]
            sums = stage(aways, old, sums)
            second, sums = tie((second, sums))
            aways = (k, -k)
        blocks += held
    unit = stage(aways, held, sums, last=True)

    task_best, scores = pl.pallas_call(
        functools.partial(score_kernel, len(blocks), count, 3 * rows),
        out_shape=(jax.ShapeDtypeStruct((2, TASKS), F32), jax.ShapeDtypeStruct((2,), F32)),
        in_specs=[VMEM] * (1 + len(blocks)),
        out_specs=(SMEM, SMEM),
        scratch_shapes=[pltpu.VMEM((2, LANES // 2 * count, LANES), F32)],
        compiler_params=params(16),
        cost_estimate=cost(4 * MIB, 2 * MIB),
        name="scores",
    )(unit, *blocks)
    return (scores, task_best)


def shards_of_any_slice(
    hidden_state_input,
    attention_mixed_state,
    hidden_state_adjoint,
    attention_values_adjoint,
    sequence_token_counts,
    heldout_sketched_signals,
    benchmark_labels,
    top_rmsnorm_weights,
    top_reducer_matrix,
    top_expander_matrix,
    bottom_reducer_matrix,
    bottom_expander_matrix,
    source_sketch,
    top_reducer_sketch,
    top_expander_sketch,
    top_target_sketch,
    bottom_reducer_sketch,
    bottom_expander_sketch,
    bottom_target_sketch,
    n,
):
    me = lax.axis_index("dp")
    x, mixed, adjoint, values = (
        hidden_state_input,
        attention_mixed_state,
        hidden_state_adjoint,
        attention_values_adjoint,
    )
    tokens, width = x.shape
    rows = top_reducer_matrix.shape[0]
    up_rows = top_expander_matrix.shape[1]
    rank = top_reducer_matrix.shape[1]
    k1 = source_sketch.shape[1]
    gain = top_rmsnorm_weights
    own_gain = lax.dynamic_slice_in_dim(gain, me * rows, rows)

    down_upper = (own_gain[:, None] * top_reducer_matrix.astype(F32)).astype(BF16)
    up_lower = mm(bottom_expander_matrix.T, bottom_reducer_sketch).astype(BF16)
    down_lower = mm(bottom_reducer_matrix, bottom_expander_sketch).astype(BF16)
    packed_lower = jnp.concatenate([down_lower[: rows // 2], down_lower[rows // 2 :]], axis=1)
    factors = jnp.concatenate([down_upper, up_lower, top_expander_matrix.T, packed_lower], axis=0)
    factors = lax.all_gather(factors, "dp")

    val_wide = heldout_sketched_signals.astype(F32)
    val_unit = (
        val_wide * lax.rsqrt(jnp.sum(val_wide * val_wide, axis=1, keepdims=True) + 1e-06)
    ).astype(BF16)
    labels = jnp.broadcast_to(benchmark_labels.astype(BF16), (val_unit.shape[0], 128))
    panel = jnp.concatenate([val_unit.reshape(-1, 128), labels], axis=0)
    panel = lax.all_gather(panel, "dp")
    val_rows = val_unit.shape[0]
    cut = panel.shape[1] - val_rows
    panel_tasks = panel[:, cut:, 0].reshape(n * val_rows, 1).astype(jnp.int32)
    panel = panel[:, :cut].reshape(n * val_rows, val_unit.shape[1])

    wide = x.astype(F32)
    inverse = lax.rsqrt(jnp.mean(wide * wide, axis=1, keepdims=True) + 1e-05)
    gained_sketch = (gain[:, None] * source_sketch.astype(F32)).astype(BF16)
    left_one = inverse * mm(x, gained_sketch)
    left_three = mm(mixed, source_sketch)
    right_two = ALPHA * mm(values, top_target_sketch)

    at = 0
    down_upper = factors[:, at : at + rows].reshape(width, rank)
    at += rows
    up_lower = factors[:, at : at + rows].reshape(width, -1)
    at += rows
    up_upper = factors[:, at : at + up_rows].reshape(-1, rank)
    at += up_rows
    down_lower = factors[:, at:]
    down_lower = jnp.concatenate([down_lower[:, :, :k1], down_lower[:, :, k1:]], axis=1)
    down_lower = down_lower.reshape(width, k1)

    reduced = inverse * mm(x, down_upper)
    left_two = mm(reduced.astype(BF16), top_expander_sketch)
    left_four = mm(mixed, down_lower)
    returned = mm(values, up_upper).astype(BF16)
    right_one = ALPHA * mm(returned, top_reducer_sketch)
    along = (ALPHA / width) * jnp.sum(returned.astype(F32) * reduced, axis=1, keepdims=True)
    targets = jnp.concatenate([up_lower, bottom_target_sketch], axis=1)
    bridge = mm_cols(down_upper, targets).astype(BF16)
    rights_low = mm(adjoint, targets) + inverse * (
        ALPHA * mm(returned, bridge) - (along * inverse) * mm(x, targets)
    )
    rights_low = ALPHA * rights_low
    k2 = up_lower.shape[1]
    lefts = (left_one, left_two, left_three, left_four)
    rights = (right_one, right_two, rights_low[:, :k2], rights_low[:, k2:])

    counts = sequence_token_counts[0]
    ends = jnp.cumsum(counts)
    starts = ends - counts
    places = jnp.arange(tokens, dtype=jnp.int32)[:, None]
    member = (places >= starts[None, :]) & (places < ends[None, :])
    count_ex = counts.shape[0]
    spread = jnp.concatenate(lefts, axis=0).astype(BF16)
    member = jnp.tile(member, (4, 1))
    spread = jnp.concatenate(
        [jnp.where(member[:, e : e + 1], spread, 0) for e in range(count_ex)], axis=1
    )
    feats = mm_cols(spread, jnp.concatenate(rights, axis=0).astype(BF16))
    feats = feats.reshape(count_ex, -1)
    squares = jnp.sum(feats * feats, axis=1, keepdims=True)
    unit_rows = (feats * lax.rsqrt(squares + 1e-06)).astype(BF16)

    score_scale = float(unit_rows.shape[1]) ** 0.5
    similar = score_scale * mm_rows(unit_rows, panel)
    task_mask = panel_tasks == jnp.arange(TASKS, dtype=jnp.int32)[None, :]
    task_best = jnp.max(
        jnp.where(task_mask[None, :, :], similar[:, :, None], -2.0 * score_scale), axis=1
    )
    return (jnp.mean(task_best, axis=1), task_best)


def solution(mesh):
    n = mesh.shape["dp"]
    split = P(("parts", "dp"), None)
    by_row, by_column, whole = P("dp", None), P(None, "dp"), P()
    placed = (
        (split,) * 5
        + (by_row, by_row, whole)
        + (by_row, by_column, by_row, by_column)
        + (whole,) * 7
    )
    ours = shards if n == 2 * RING_CHIPS else functools.partial(shards_of_any_slice, n=n)
    return jax.shard_map(
        ours,
        mesh=mesh,
        in_specs=placed,
        out_specs=(P(("parts", "dp")), split),
        check_vma=False,
    )
```

```python
import functools

import jax
import jax.numpy as jnp
from jax import lax
from jax.experimental import pallas as pl
from jax.experimental.pallas import tpu as pltpu
from jax.sharding import PartitionSpec as P

TASKS = 3
ALPHA = 4.0
F32 = jnp.float32
BF16 = jnp.bfloat16
RING_CHIPS = 8
LANES = 128
STEPS = 4
X_DOWN, X_LOW, J_LOW, M_DOWN, VALUES, SUMS = range(6)
X_SOURCE, X_TARGET, SQUARES, M_SOURCE, J_TARGET, V_TARGET, LOCAL_SUMS = range(7)
MIB = 1 << 20


def mm(a, b):
    return jnp.dot(a, b, preferred_element_type=F32)


def mm_rows(a, b):
    return lax.dot_general(a, b, (((1,), (1,)), ((), ())), preferred_element_type=F32)


def mm_cols(a, b):
    return lax.dot_general(a, b, (((0,), (0,)), ((), ())), preferred_element_type=F32)


def ring_chip(pos):
    half = RING_CHIPS // 2
    return jnp.where(pos < half, 2 * pos, 2 * (RING_CHIPS - 1 - pos) + 1)


def ring_pos(chip):
    row, side = chip // 2, chip % 2
    return jnp.where(side == 0, row, RING_CHIPS - 1 - row)


def hop(value):
    half = RING_CHIPS // 2
    place = [2 * q if q < half else 2 * (RING_CHIPS - 1 - q) + 1 for q in range(RING_CHIPS)]
    pairs = []
    for q in range(RING_CHIPS):
        pairs.append((2 * place[q], 2 * place[(q + 1) % RING_CHIPS]))
        pairs.append((2 * place[q] + 1, 2 * place[(q - 1) % RING_CHIPS] + 1))
    return lax.ppermute(value, "dp", pairs)


def other_core(value):
    return lax.ppermute(value, "dp", [(d, d ^ 1) for d in range(2 * RING_CHIPS)])


def half_lanes(shape):
    return lax.broadcasted_iota(jnp.int32, shape, 1) < LANES // 2


def diagonal_column(row, first, count):
    shape = (count, row.shape[1])
    lane = lax.broadcasted_iota(jnp.int32, shape, 1)
    at = lax.broadcasted_iota(jnp.int32, shape, 0)
    return jnp.sum(jnp.where(lane == at + first, row, 0.0), axis=1, keepdims=True)


def load(pairs, sems):
    copies = [pltpu.make_async_copy(src, dst, sems.at[i]) for i, (src, dst) in enumerate(pairs)]
    for copy in copies:
        copy.start()
    return copies


def pack_kernel(me_ref, *refs):
    hbm, out_ref, held, sems = refs[:9], refs[9], refs[10:19], refs[19]
    gain_ref, down_up_ref, up_low_ref, sketch_ref, up_up_ref, down_low_ref, expand_ref, val_ref, label_ref = held
    copies = load(zip(hbm, held), sems)
    rows = down_up_ref.shape[0]
    half = LANES // 2
    for copy in copies:
        copy.wait()
    for b in range(rows // half):
        place = me_ref[0] * (rows // half) + b
        row = gain_ref[pl.ds(place // 2, 1), :]
        column = diagonal_column(row, (place % 2) * half, half)
        part = down_up_ref[pl.ds(b * half, half), :].astype(F32)
        out_ref[pl.ds(b * half, half), :] = (column * part).astype(BF16)
    at = rows
    out_ref[pl.ds(at, rows), :] = mm(up_low_ref[...], sketch_ref[...]).astype(BF16)
    at += rows
    out_ref[pl.ds(at, rows // 2), :] = up_up_ref[...]
    at += rows // 2
    expand = expand_ref[...]
    low = mm_rows(down_low_ref[...], jnp.concatenate([expand, expand], axis=0))
    first, second = low[: rows // 2], low[rows // 2 :]
    out_ref[pl.ds(at, rows // 2), :] = jnp.where(half_lanes(first.shape), first, second).astype(BF16)
    at += rows // 2
    wide = val_ref[...].astype(F32)
    count, width = wide.shape
    scale = lax.rsqrt(jnp.sum(wide * wide, axis=1, keepdims=True) + 1e-06)
    unit = wide * scale
    blocks = [unit[:, i * LANES : (i + 1) * LANES] for i in range(width // LANES)]
    row = label_ref[...].astype(F32)
    labels = jnp.broadcast_to(diagonal_column(row, 0, count), (count, LANES))
    blocks += [labels, labels]
    for i in range(0, len(blocks), 2):
        pair = jnp.concatenate(blocks[i : i + 2], axis=0)
        out_ref[pl.ds(at + i * count, 2 * count), :] = pair.astype(BF16)


def local_kernel(*refs):
    x_hbm, mixed_hbm, adjoint_hbm, values_hbm, target_hbm, gain_hbm, source_hbm, top_target_hbm = refs[:8]
    x_ref, mixed_ref, adjoint_ref, values_ref, target_ref, sums_ref = refs[8:14]
    gain_ref, source_ref, top_target_ref, sems = refs[14:]
    width, value_width = x_ref.shape[1], values_ref.shape[1]
    span, value_span = width // STEPS, value_width // STEPS
    copies = []
    for j in range(STEPS):
        part, value_part = pl.ds(j * span, span), pl.ds(j * value_span, value_span)
        pairs = (
            (gain_hbm.at[:, part], gain_ref.at[:, part]),
            (source_hbm.at[:, part], source_ref.at[:, part]),
            (x_hbm.at[:, part], x_ref.at[:, part]),
            (target_hbm.at[part], target_ref.at[part]),
            (mixed_hbm.at[:, part], mixed_ref.at[:, part]),
            (adjoint_hbm.at[:, part], adjoint_ref.at[:, part]),
            (values_hbm.at[:, value_part], values_ref.at[:, value_part]),
            (top_target_hbm.at[value_part], top_target_ref.at[value_part]),
        )
        copies.append(load(pairs, sems.at[j]))
    total = [None] * LOCAL_SUMS

    def add(column, value):
        total[column] = value if total[column] is None else total[column] + value

    for j in range(STEPS):
        for copy in copies[j]:
            copy.wait()
        part, value_part = slice(j * span, (j + 1) * span), slice(j * value_span, (j + 1) * value_span)
        x, target, source = x_ref[:, part], target_ref[part, :], source_ref[:, part]
        gained = (source.astype(F32) * gain_ref[:, part]).astype(BF16)
        add(X_SOURCE, mm_rows(x, jnp.concatenate([gained, gained], axis=0)))
        add(X_TARGET, mm(x, target))
        for i in range(span // LANES):
            wide = x[:, i * LANES : (i + 1) * LANES].astype(F32)
            add(SQUARES, wide * wide)
        add(M_SOURCE, mm_rows(mixed_ref[:, part], jnp.concatenate([source, source], axis=0)))
        add(J_TARGET, mm(adjoint_ref[:, part], target))
        add(V_TARGET, mm(values_ref[:, value_part], top_target_ref[value_part, :]))
    for i in range(LOCAL_SUMS):
        sums_ref[:, i * LANES : (i + 1) * LANES] = total[i]


def stage_kernel(away, first, last, me_ref, *refs):
    refs = list(refs)
    take = lambda k: [refs.pop(0) for _ in range(k)]
    counts_ref = take(1)[0] if last else None
    pieces = take(2)
    x_ref, mixed_ref, adjoint_ref, values_ref, target_ref = take(5)
    old_sums, old_bridge = (None, None) if first else take(2)
    local_ref, expand_hbm, sketch_hbm = take(3) if last else (None, None, None)
    if last:
        (out_ref,) = take(1)
    else:
        new_sums, new_bridge = take(2)
    both, up, down, expand_ref, sketch_ref, sems = refs
    rows = both.shape[0] // 2
    half, pad = rows // 2, LANES // 2
    tokens, width = x_ref.shape
    span = 2 * rows
    if last:
        more = load(((expand_hbm, expand_ref), (sketch_hbm, sketch_ref)), sems)

    me = me_ref[0]
    pos, core = ring_pos(me // 2), me % 2
    chip = ring_chip((pos + away * (2 * core - 1) + RING_CHIPS) % RING_CHIPS)
    odd = chip % 2
    mine = pl.ds(pl.multiple_of(chip * span, LANES), span)
    values_start = (chip // 2) * span + odd * (rows - pad)
    values_part = pl.ds(pl.multiple_of(values_start, LANES), rows + pad)
    side = core if away >= 0 else 1 - core
    up[pl.ds(pl.multiple_of((1 - odd) * rows, 16), pad), :] = jnp.zeros((pad, LANES), BF16)
    for piece, c in ((pieces[0], side), (pieces[1], 1 - side)):
        one = pl.ds(pl.multiple_of(c * rows, 16), rows)
        both[one, pl.ds(0, LANES)] = piece[pl.ds(0, rows), :]
        both[one, pl.ds(LANES, LANES)] = piece[pl.ds(rows, rows), :]
        up[pl.ds(pl.multiple_of(odd * pad + c * half, 16), half), :] = piece[pl.ds(2 * rows, half), :]
        packed = piece[pl.ds(2 * rows + half, half), :].astype(F32)
        turned = pltpu.roll(packed, pad, 1)
        lower = half_lanes(packed.shape)
        down[pl.ds(pl.multiple_of(c * rows, 16), half), :] = jnp.where(lower, packed, turned).astype(BF16)
        down[pl.ds(pl.multiple_of(c * rows + half, 16), half), :] = jnp.where(lower, turned, packed).astype(BF16)

    weights = both[...]
    products = [None] * SUMS
    x_both = mm(x_ref[:, mine], weights)
    products[X_DOWN], products[X_LOW] = x_both[:, :LANES], x_both[:, LANES:]
    products[J_LOW] = mm(adjoint_ref[:, mine], weights[:, LANES:])
    products[M_DOWN] = mm(mixed_ref[:, mine], down[...])
    products[VALUES] = mm(values_ref[:, values_part], up[...])
    bridge = mm_cols(
        weights[:, :LANES], jnp.concatenate([weights[:, LANES:], target_ref[mine, :]], axis=1)
    )
    if not first:
        products = [p + old_sums[:, i * LANES : (i + 1) * LANES] for i, p in enumerate(products)]
        bridge = bridge + old_bridge[...]
    if not last:
        for i in range(SUMS):
            new_sums[:, i * LANES : (i + 1) * LANES] = products[i]
        new_bridge[...] = bridge
        return

    for copy in more:
        copy.wait()
    local = [local_ref[:, i * LANES : (i + 1) * LANES] for i in range(LOCAL_SUMS)]
    mean = jnp.sum(local[SQUARES], axis=1, keepdims=True) * (1.0 / width)
    inverse = lax.rsqrt(mean + 1e-05)
    reduced = inverse * products[X_DOWN]
    expand = expand_ref[...]
    left_two = mm_rows(reduced.astype(BF16), jnp.concatenate([expand, expand], axis=0))
    returned = products[VALUES].astype(BF16)
    right_one = ALPHA * mm(returned, sketch_ref[...])
    along = (ALPHA / width) * jnp.sum(returned.astype(F32) * reduced, axis=1, keepdims=True)
    back = mm(returned, bridge.astype(BF16))
    along = along * inverse
    right_three = products[J_LOW] + inverse * (ALPHA * back[:, :LANES] - along * products[X_LOW])
    right_four = local[J_TARGET] + inverse * (ALPHA * back[:, LANES:] - along * local[X_TARGET])
    rights = (right_one, ALPHA * local[V_TARGET], ALPHA * right_three, ALPHA * right_four)
    lefts = (inverse * local[X_SOURCE], left_two, local[M_SOURCE], products[M_DOWN])
    place = lax.broadcasted_iota(jnp.int32, (tokens, LANES), 0)
    one, two = counts_ref[0, 0], counts_ref[0, 1]
    lower = half_lanes((tokens, LANES))
    member = (place >= jnp.where(lower, 0, one)) & (place < jnp.where(lower, one, one + two))
    spread = jnp.concatenate([jnp.where(member, left, 0.0).astype(BF16) for left in lefts], axis=0)
    feats = mm_cols(spread, jnp.concatenate([right.astype(BF16) for right in rights], axis=0))
    for e in range(2):
        own = feats[e * pad : (e + 1) * pad]
        squares = jnp.sum(own * own, keepdims=True)
        out_ref[pl.ds(e * pad, pad), :] = (own * lax.rsqrt(squares + 1e-06)).astype(BF16)


def score_kernel(pieces, count, start, unit_ref, *refs):
    piece_refs = refs[:pieces]
    best_ref, mean_ref, spread = refs[pieces:]
    half = LANES // 2
    scale = float(half * LANES) ** 0.5
    for e in range(2):
        for i in range(half):
            row = unit_ref[pl.ds(e * half + i, 1), :].astype(F32)
            spread[e, pl.ds(i * count, count), :] = jnp.broadcast_to(row, (count, LANES))
    best = [[jnp.full((count, LANES), -2.0 * scale, F32) for _ in range(TASKS)] for _ in range(2)]
    for piece in piece_refs:
        wide = piece[pl.ds(start, half * count), :].astype(F32)
        labels = piece[pl.ds(start + half * count, 2 * count), :].astype(F32)[:count]
        for e in range(2):
            products = wide * spread[e]
            total = jnp.sum(products.reshape(half, count, LANES), axis=0)
            similar = scale * jnp.sum(total, axis=1, keepdims=True)
            for t in range(TASKS):
                here = jnp.where(labels == float(t), similar, -2.0 * scale)
                best[e][t] = jnp.maximum(best[e][t], here)
    for e in range(2):
        values = [jnp.max(best[e][t]) for t in range(TASKS)]
        for t in range(TASKS):
            best_ref[e, t] = values[t]
        mean_ref[e] = (values[0] + values[1] + values[2]) * (1.0 / TASKS)


VMEM = pl.BlockSpec(memory_space=pltpu.VMEM)
SMEM = pl.BlockSpec(memory_space=pltpu.SMEM)
ANY = pl.BlockSpec(memory_space=pl.ANY)
HBM = pl.BlockSpec(memory_space=pltpu.HBM)


def in_hbm(arrays):
    return [pltpu.with_memory_space_constraint(a, pltpu.HBM) for a in arrays]


def params(mib):
    return pltpu.CompilerParams(vmem_limit_bytes=mib * MIB)


def cost(flops, nbytes):
    return pl.CostEstimate(flops=flops, bytes_accessed=nbytes, transcendentals=0)


def shards(
    hidden_state_input,
    attention_mixed_state,
    hidden_state_adjoint,
    attention_values_adjoint,
    sequence_token_counts,
    heldout_sketched_signals,
    benchmark_labels,
    top_rmsnorm_weights,
    top_reducer_matrix,
    top_expander_matrix,
    bottom_reducer_matrix,
    bottom_expander_matrix,
    source_sketch,
    top_reducer_sketch,
    top_expander_sketch,
    top_target_sketch,
    bottom_reducer_sketch,
    bottom_expander_sketch,
    bottom_target_sketch,
):
    me = lax.axis_index("dp").astype(jnp.int32)
    x, mixed, adjoint, values = (
        hidden_state_input,
        attention_mixed_state,
        hidden_state_adjoint,
        attention_values_adjoint,
    )
    tokens, width = x.shape
    rows = top_reducer_matrix.shape[0]
    count = heldout_sketched_signals.shape[0]

    inputs = (
        top_rmsnorm_weights.reshape(width // LANES, LANES),
        top_reducer_matrix,
        bottom_expander_matrix.T,
        bottom_reducer_sketch,
        top_expander_matrix.T,
        bottom_reducer_matrix,
        bottom_expander_sketch.T,
        heldout_sketched_signals,
        benchmark_labels.T,
    )
    own = pl.pallas_call(
        pack_kernel,
        out_shape=jax.ShapeDtypeStruct((3 * rows + (LANES // 2 + 2) * count, LANES), BF16),
        in_specs=[SMEM] + [HBM] * len(inputs),
        out_specs=VMEM,
        scratch_shapes=[pltpu.VMEM(a.shape, a.dtype) for a in inputs]
        + [pltpu.SemaphoreType.DMA((len(inputs),))],
        compiler_params=params(8),
        name="pack",
    )(me.reshape(1), *in_hbm(inputs))

    inputs = (
        x,
        mixed,
        adjoint,
        values,
        bottom_target_sketch,
        top_rmsnorm_weights.reshape(1, width),
        source_sketch.T,
        top_target_sketch,
    )
    *activations, local = pl.pallas_call(
        local_kernel,
        out_shape=[jax.ShapeDtypeStruct(a.shape, a.dtype) for a in inputs[:5]]
        + [jax.ShapeDtypeStruct((tokens, LOCAL_SUMS * LANES), F32)],
        in_specs=[HBM] * len(inputs),
        out_specs=[VMEM] * 6,
        scratch_shapes=[pltpu.VMEM(a.shape, a.dtype) for a in inputs[5:]]
        + [pltpu.SemaphoreType.DMA((STEPS, len(inputs)))],
        compiler_params=params(24),
        cost_estimate=cost(tokens * width * LANES * 12, 14 * MIB),
        name="local_products",
    )(*in_hbm(inputs))

    def stage(away, pieces, sums, local=None):
        first, last = not sums, local is not None
        sums_shape, bridge_shape = (tokens, SUMS * LANES), (LANES, 2 * LANES)
        small = (top_expander_sketch.T, top_reducer_sketch)
        head = [me.reshape(1)] + ([sequence_token_counts] if last else [])
        start = len(head) + len(pieces) + len(activations)
        return pl.pallas_call(
            functools.partial(stage_kernel, away, first, last),
            out_shape=jax.ShapeDtypeStruct((LANES, LANES), BF16)
            if last
            else [jax.ShapeDtypeStruct(sums_shape, F32), jax.ShapeDtypeStruct(bridge_shape, F32)],
            in_specs=[SMEM] * len(head)
            + [VMEM] * (len(pieces) + len(activations) + len(sums))
            + ([VMEM, HBM, HBM] if last else []),
            out_specs=VMEM if last else [VMEM, VMEM],
            scratch_shapes=[
                pltpu.VMEM((2 * rows, 2 * LANES), BF16),
                pltpu.VMEM((rows + LANES // 2, LANES), BF16),
                pltpu.VMEM((2 * rows, LANES), BF16),
                pltpu.VMEM(small[0].shape, BF16),
                pltpu.VMEM(small[1].shape, BF16),
                pltpu.SemaphoreType.DMA((2,)),
            ],
            input_output_aliases={} if first or last else {start: 0, start + 1: 1},
            compiler_params=params(16),
            cost_estimate=cost(tokens * rows * LANES * 16, 2 * MIB),
            name="features" if last else "stage",
        )(*head, *pieces, *activations, *sums, *((local, *in_hbm(small)) if last else ()))

    tie = lax.optimization_barrier
    half = RING_CHIPS // 2
    first, second = own, other_core(own)
    blocks = [first, second]
    held = [first, second]
    first, second = hop(first), hop(second)
    first, activations = tie((first, activations))
    sums = stage(0, held, [])
    second, sums = tie((second, sums))
    for k in range(1, half):
        held = [first, second]
        crossed = [other_core(first), other_core(second)]
        blocks += held + crossed
        first = hop(first)
        sums = stage(k, held, sums)
        first, sums = tie((first, sums))
        if k < half - 1:
            second = hop(second)
        sums = stage(-k, crossed, sums)
        if k < half - 1:
            second, sums = tie((second, sums))
    held = [first, other_core(first)]
    blocks += held
    unit = stage(half, held, sums, local)

    task_best, scores = pl.pallas_call(
        functools.partial(score_kernel, len(blocks), count, 3 * rows),
        out_shape=(jax.ShapeDtypeStruct((2, TASKS), F32), jax.ShapeDtypeStruct((2,), F32)),
        in_specs=[VMEM] * (1 + len(blocks)),
        out_specs=(SMEM, SMEM),
        scratch_shapes=[pltpu.VMEM((2, LANES // 2 * count, LANES), F32)],
        compiler_params=params(16),
        cost_estimate=cost(4 * MIB, 2 * MIB),
        name="scores",
    )(unit, *blocks)
    return (scores, task_best)


def shards_of_any_slice(
    hidden_state_input,
    attention_mixed_state,
    hidden_state_adjoint,
    attention_values_adjoint,
    sequence_token_counts,
    heldout_sketched_signals,
    benchmark_labels,
    top_rmsnorm_weights,
    top_reducer_matrix,
    top_expander_matrix,
    bottom_reducer_matrix,
    bottom_expander_matrix,
    source_sketch,
    top_reducer_sketch,
    top_expander_sketch,
    top_target_sketch,
    bottom_reducer_sketch,
    bottom_expander_sketch,
    bottom_target_sketch,
    n,
):
    me = lax.axis_index("dp")
    x, mixed, adjoint, values = (
        hidden_state_input,
        attention_mixed_state,
        hidden_state_adjoint,
        attention_values_adjoint,
    )
    tokens, width = x.shape
    rows = top_reducer_matrix.shape[0]
    up_rows = top_expander_matrix.shape[1]
    rank = top_reducer_matrix.shape[1]
    k1 = source_sketch.shape[1]
    gain = top_rmsnorm_weights
    own_gain = lax.dynamic_slice_in_dim(gain, me * rows, rows)

    down_upper = (own_gain[:, None] * top_reducer_matrix.astype(F32)).astype(BF16)
    up_lower = mm(bottom_expander_matrix.T, bottom_reducer_sketch).astype(BF16)
    down_lower = mm(bottom_reducer_matrix, bottom_expander_sketch).astype(BF16)
    packed_lower = jnp.concatenate([down_lower[: rows // 2], down_lower[rows // 2 :]], axis=1)
    factors = jnp.concatenate([down_upper, up_lower, top_expander_matrix.T, packed_lower], axis=0)
    factors = lax.all_gather(factors, "dp")

    val_wide = heldout_sketched_signals.astype(F32)
    val_unit = (
        val_wide * lax.rsqrt(jnp.sum(val_wide * val_wide, axis=1, keepdims=True) + 1e-06)
    ).astype(BF16)
    labels = jnp.broadcast_to(benchmark_labels.astype(BF16), (val_unit.shape[0], 128))
    panel = jnp.concatenate([val_unit.reshape(-1, 128), labels], axis=0)
    panel = lax.all_gather(panel, "dp")
    val_rows = val_unit.shape[0]
    cut = panel.shape[1] - val_rows
    panel_tasks = panel[:, cut:, 0].reshape(n * val_rows, 1).astype(jnp.int32)
    panel = panel[:, :cut].reshape(n * val_rows, val_unit.shape[1])

    wide = x.astype(F32)
    inverse = lax.rsqrt(jnp.mean(wide * wide, axis=1, keepdims=True) + 1e-05)
    gained_sketch = (gain[:, None] * source_sketch.astype(F32)).astype(BF16)
    left_one = inverse * mm(x, gained_sketch)
    left_three = mm(mixed, source_sketch)
    right_two = ALPHA * mm(values, top_target_sketch)

    at = 0
    down_upper = factors[:, at : at + rows].reshape(width, rank)
    at += rows
    up_lower = factors[:, at : at + rows].reshape(width, -1)
    at += rows
    up_upper = factors[:, at : at + up_rows].reshape(-1, rank)
    at += up_rows
    down_lower = factors[:, at:]
    down_lower = jnp.concatenate([down_lower[:, :, :k1], down_lower[:, :, k1:]], axis=1)
    down_lower = down_lower.reshape(width, k1)

    reduced = inverse * mm(x, down_upper)
    left_two = mm(reduced.astype(BF16), top_expander_sketch)
    left_four = mm(mixed, down_lower)
    returned = mm(values, up_upper).astype(BF16)
    right_one = ALPHA * mm(returned, top_reducer_sketch)
    along = (ALPHA / width) * jnp.sum(returned.astype(F32) * reduced, axis=1, keepdims=True)
    targets = jnp.concatenate([up_lower, bottom_target_sketch], axis=1)
    bridge = mm_cols(down_upper, targets).astype(BF16)
    rights_low = mm(adjoint, targets) + inverse * (
        ALPHA * mm(returned, bridge) - (along * inverse) * mm(x, targets)
    )
    rights_low = ALPHA * rights_low
    k2 = up_lower.shape[1]
    lefts = (left_one, left_two, left_three, left_four)
    rights = (right_one, right_two, rights_low[:, :k2], rights_low[:, k2:])

    counts = sequence_token_counts[0]
    ends = jnp.cumsum(counts)
    starts = ends - counts
    places = jnp.arange(tokens, dtype=jnp.int32)[:, None]
    member = (places >= starts[None, :]) & (places < ends[None, :])
    count_ex = counts.shape[0]
    spread = jnp.concatenate(lefts, axis=0).astype(BF16)
    member = jnp.tile(member, (4, 1))
    spread = jnp.concatenate(
        [jnp.where(member[:, e : e + 1], spread, 0) for e in range(count_ex)], axis=1
    )
    feats = mm_cols(spread, jnp.concatenate(rights, axis=0).astype(BF16))
    feats = feats.reshape(count_ex, -1)
    squares = jnp.sum(feats * feats, axis=1, keepdims=True)
    unit_rows = (feats * lax.rsqrt(squares + 1e-06)).astype(BF16)

    score_scale = float(unit_rows.shape[1]) ** 0.5
    similar = score_scale * mm_rows(unit_rows, panel)
    task_mask = panel_tasks == jnp.arange(TASKS, dtype=jnp.int32)[None, :]
    task_best = jnp.max(
        jnp.where(task_mask[None, :, :], similar[:, :, None], -2.0 * score_scale), axis=1
    )
    return (jnp.mean(task_best, axis=1), task_best)


def solution(mesh):
    n = mesh.shape["dp"]
    split = P(("parts", "dp"), None)
    by_row, by_column, whole = P("dp", None), P(None, "dp"), P()
    placed = (
        (split,) * 5
        + (by_row, by_row, whole)
        + (by_row, by_column, by_row, by_column)
        + (whole,) * 7
    )
    ours = shards if n == 2 * RING_CHIPS else functools.partial(shards_of_any_slice, n=n)
    return jax.shard_map(
        ours,
        mesh=mesh,
        in_specs=placed,
        out_specs=(P(("parts", "dp")), split),
        check_vma=False,
    )
```

```python
import functools

import jax
import jax.numpy as jnp
from jax import lax
from jax.experimental import pallas as pl
from jax.experimental.pallas import tpu as pltpu
from jax.sharding import PartitionSpec as P

TASKS = 3
ALPHA = 4.0
F32 = jnp.float32
BF16 = jnp.bfloat16
RING_CHIPS = 8
LANES = 128
STEPS = 4
X_DOWN, X_LOW, J_LOW, J_TARGET, M_DOWN, M_SOURCE, VALUES, V_TARGET, SUMS = range(9)
INVERSE, LEFT_ONE, X_TARGET, LOCAL_SUMS = range(4)
MIB = 1 << 20


def mm(a, b):
    return jnp.dot(a, b, preferred_element_type=F32)


def mm_rows(a, b):
    return lax.dot_general(a, b, (((1,), (1,)), ((), ())), preferred_element_type=F32)


def mm_cols(a, b):
    return lax.dot_general(a, b, (((0,), (0,)), ((), ())), preferred_element_type=F32)


def ring_chip(pos):
    half = RING_CHIPS // 2
    return jnp.where(pos < half, 2 * pos, 2 * (RING_CHIPS - 1 - pos) + 1)


def ring_pos(chip):
    row, side = chip // 2, chip % 2
    return jnp.where(side == 0, row, RING_CHIPS - 1 - row)


def hop(value):
    half = RING_CHIPS // 2
    place = [2 * q if q < half else 2 * (RING_CHIPS - 1 - q) + 1 for q in range(RING_CHIPS)]
    pairs = []
    for q in range(RING_CHIPS):
        pairs.append((2 * place[q], 2 * place[(q + 1) % RING_CHIPS]))
        pairs.append((2 * place[q] + 1, 2 * place[(q - 1) % RING_CHIPS] + 1))
    return lax.ppermute(value, "dp", pairs)


def other_core(value):
    return lax.ppermute(value, "dp", [(d, d ^ 1) for d in range(2 * RING_CHIPS)])


def half_lanes(shape):
    return lax.broadcasted_iota(jnp.int32, shape, 1) < LANES // 2


def diagonal_column(row, first, count):
    shape = (count, row.shape[1])
    lane = lax.broadcasted_iota(jnp.int32, shape, 1)
    at = lax.broadcasted_iota(jnp.int32, shape, 0)
    return jnp.sum(jnp.where(lane == at + first, row, 0.0), axis=1, keepdims=True)


def load(pairs, sems):
    copies = [pltpu.make_async_copy(src, dst, sems.at[i]) for i, (src, dst) in enumerate(pairs)]
    for copy in copies:
        copy.start()
    return copies


def pack_kernel(me_ref, *refs):
    hbm, out_ref, held, sems = refs[:9], refs[9], refs[10:19], refs[19]
    gain_ref, down_up_ref, up_low_ref, sketch_ref, up_up_ref, down_low_ref, expand_ref, val_ref, label_ref = held
    copies = load(zip(hbm, held), sems)
    rows = down_up_ref.shape[0]
    half = LANES // 2
    for copy in copies:
        copy.wait()
    for b in range(rows // half):
        place = me_ref[0] * (rows // half) + b
        row = gain_ref[pl.ds(place // 2, 1), :]
        column = diagonal_column(row, (place % 2) * half, half)
        part = down_up_ref[pl.ds(b * half, half), :].astype(F32)
        out_ref[pl.ds(b * half, half), :] = (column * part).astype(BF16)
    at = rows
    out_ref[pl.ds(at, rows), :] = mm(up_low_ref[...], sketch_ref[...]).astype(BF16)
    at += rows
    out_ref[pl.ds(at, rows // 2), :] = up_up_ref[...]
    at += rows // 2
    expand = expand_ref[...]
    low = mm_rows(down_low_ref[...], jnp.concatenate([expand, expand], axis=0))
    first, second = low[: rows // 2], low[rows // 2 :]
    out_ref[pl.ds(at, rows // 2), :] = jnp.where(half_lanes(first.shape), first, second).astype(BF16)
    at += rows // 2
    wide = val_ref[...].astype(F32)
    count, width = wide.shape
    scale = lax.rsqrt(jnp.sum(wide * wide, axis=1, keepdims=True) + 1e-06)
    unit = wide * scale
    blocks = [unit[:, i * LANES : (i + 1) * LANES] for i in range(width // LANES)]
    row = label_ref[...].astype(F32)
    labels = jnp.broadcast_to(diagonal_column(row, 0, count), (count, LANES))
    blocks += [labels, labels]
    for i in range(0, len(blocks), 2):
        pair = jnp.concatenate(blocks[i : i + 2], axis=0)
        out_ref[pl.ds(at + i * count, 2 * count), :] = pair.astype(BF16)


def local_kernel(*refs):
    x_hbm, mixed_hbm, adjoint_hbm, values_hbm, target_hbm, top_target_hbm, gain_hbm, source_hbm = refs[:8]
    x_ref, mixed_ref, adjoint_ref, values_ref, target_ref, top_target_ref, turned_ref, sums_ref = refs[8:16]
    gain_ref, source_ref, sems = refs[16:]
    tokens, width = x_ref.shape
    span = width // STEPS
    copies = []
    for j in range(STEPS):
        part = pl.ds(j * span, span)
        pairs = (
            (gain_hbm.at[:, part], gain_ref.at[:, part]),
            (source_hbm.at[:, part], source_ref.at[:, part]),
            (x_hbm.at[:, part], x_ref.at[:, part]),
            (target_hbm.at[part], target_ref.at[part]),
        )
        copies.append(load(pairs, sems.at[j]))
    pairs = (
        (adjoint_hbm, adjoint_ref),
        (mixed_hbm, mixed_ref),
        (values_hbm, values_ref),
        (top_target_hbm, top_target_ref),
    )
    later = load(pairs, sems.at[STEPS])
    products = jnp.zeros((tokens, 2 * LANES), F32)
    squares = jnp.zeros((tokens, LANES), F32)
    for j in range(STEPS):
        for copy in copies[j]:
            copy.wait()
        part = slice(j * span, (j + 1) * span)
        x, source = x_ref[:, part], source_ref[:, part].astype(F32)
        gained = source * gain_ref[:, part]
        turned_ref[part, :] = jnp.concatenate([source, source], axis=0).T.astype(BF16)
        gained = jnp.concatenate([gained, gained], axis=0).T.astype(BF16)
        products = products + mm(x, jnp.concatenate([gained, target_ref[part, :]], axis=1))
        for i in range(span // LANES):
            wide = x[:, i * LANES : (i + 1) * LANES].astype(F32)
            squares = squares + wide * wide
    mean = jnp.sum(squares, axis=1, keepdims=True) * (1.0 / width)
    inverse = jnp.broadcast_to(lax.rsqrt(mean + 1e-05), (tokens, LANES))
    for i, value in enumerate((inverse, inverse * products[:, :LANES], products[:, LANES:])):
        sums_ref[:, i * LANES : (i + 1) * LANES] = value
    for copy in later:
        copy.wait()


def stage_kernel(away, first, last, me_ref, *refs):
    refs = list(refs)
    take = lambda k: [refs.pop(0) for _ in range(k)]
    counts_ref = take(1)[0] if last else None
    pieces = take(2)
    x_ref, mixed_ref, adjoint_ref, values_ref, target_ref, top_target_ref, source_ref = take(7)
    old_sums, old_bridge = (None, None) if first else take(2)
    local_ref, expand_hbm, sketch_hbm = take(3) if last else (None, None, None)
    if last:
        (out_ref,) = take(1)
    else:
        new_sums, new_bridge = take(2)
    both, up, down, expand_ref, sketch_ref, sems = refs
    rows = both.shape[0] // 2
    half, pad = rows // 2, LANES // 2
    tokens, width = x_ref.shape
    span = 2 * rows
    if last:
        more = load(((expand_hbm, expand_ref), (sketch_hbm, sketch_ref)), sems)

    me = me_ref[0]
    pos, core = ring_pos(me // 2), me % 2
    chip = ring_chip((pos + away * (2 * core - 1) + RING_CHIPS) % RING_CHIPS)
    odd = chip % 2
    mine = pl.ds(pl.multiple_of(chip * span, LANES), span)
    values_start = (chip // 2) * span + odd * (rows - pad)
    values_part = pl.ds(pl.multiple_of(values_start, LANES), rows + pad)
    side = core if away >= 0 else 1 - core
    up[pl.ds(pl.multiple_of((1 - odd) * rows, 16), pad), :] = jnp.zeros((pad, 2 * LANES), BF16)
    up[pl.ds(pl.multiple_of(odd * pad, 16), rows), pl.ds(LANES, LANES)] = top_target_ref[
        pl.ds(pl.multiple_of(chip * rows, 16), rows), :
    ]
    for piece, c in ((pieces[0], side), (pieces[1], 1 - side)):
        one = pl.ds(pl.multiple_of(c * rows, 16), rows)
        both[one, pl.ds(0, LANES)] = piece[pl.ds(0, rows), :]
        both[one, pl.ds(LANES, LANES)] = piece[pl.ds(rows, rows), :]
        up[pl.ds(pl.multiple_of(odd * pad + c * half, 16), half), pl.ds(0, LANES)] = piece[
            pl.ds(2 * rows, half), :
        ]
        packed = piece[pl.ds(2 * rows + half, half), :].astype(F32)
        turned = pltpu.roll(packed, pad, 1)
        lower = half_lanes(packed.shape)
        down[pl.ds(pl.multiple_of(c * rows, 16), half), :] = jnp.where(lower, packed, turned).astype(BF16)
        down[pl.ds(pl.multiple_of(c * rows + half, 16), half), :] = jnp.where(lower, turned, packed).astype(BF16)

    weights = both[...]
    down_up = weights[:, :LANES]
    lows = jnp.concatenate([weights[:, LANES:], target_ref[mine, :]], axis=1)
    products = []
    for activation, factor in (
        (x_ref[:, mine], weights),
        (adjoint_ref[:, mine], lows),
        (mixed_ref[:, mine], jnp.concatenate([down[...], source_ref[mine, :]], axis=1)),
        (values_ref[:, values_part], up[...]),
    ):
        product = mm(activation, factor)
        products += [product[:, :LANES], product[:, LANES:]]
    bridge = mm_cols(down_up, lows)
    if not first:
        products = [p + old_sums[:, i * LANES : (i + 1) * LANES] for i, p in enumerate(products)]
        bridge = bridge + old_bridge[...]
    if not last:
        for i in range(SUMS):
            new_sums[:, i * LANES : (i + 1) * LANES] = products[i]
        new_bridge[...] = bridge
        return

    for copy in more:
        copy.wait()
    local = [local_ref[:, i * LANES : (i + 1) * LANES] for i in range(LOCAL_SUMS)]
    inverse = local[INVERSE]
    reduced = inverse * products[X_DOWN]
    expand = expand_ref[...]
    left_two = mm_rows(reduced.astype(BF16), jnp.concatenate([expand, expand], axis=0))
    returned = products[VALUES].astype(BF16)
    right_one = ALPHA * mm(returned, sketch_ref[...])
    along = (ALPHA / width) * jnp.sum(returned.astype(F32) * reduced, axis=1, keepdims=True)
    back = mm(returned, bridge.astype(BF16))
    along = along * inverse
    right_three = products[J_LOW] + inverse * (ALPHA * back[:, :LANES] - along * products[X_LOW])
    right_four = products[J_TARGET] + inverse * (ALPHA * back[:, LANES:] - along * local[X_TARGET])
    rights = (right_one, ALPHA * products[V_TARGET], ALPHA * right_three, ALPHA * right_four)
    lefts = (local[LEFT_ONE], left_two, products[M_SOURCE], products[M_DOWN])
    place = lax.broadcasted_iota(jnp.int32, (tokens, LANES), 0)
    one, two = counts_ref[0, 0], counts_ref[0, 1]
    lower = half_lanes((tokens, LANES))
    member = (place >= jnp.where(lower, 0, one)) & (place < jnp.where(lower, one, one + two))
    spread = jnp.concatenate([jnp.where(member, left, 0.0).astype(BF16) for left in lefts], axis=0)
    feats = mm_cols(spread, jnp.concatenate([right.astype(BF16) for right in rights], axis=0))
    for e in range(2):
        own = feats[e * pad : (e + 1) * pad]
        squares = jnp.sum(own * own, keepdims=True)
        out_ref[pl.ds(e * pad, pad), :] = (own * lax.rsqrt(squares + 1e-06)).astype(BF16)


def split_kernel(block_ref, head_ref, tail_ref):
    cut = head_ref.shape[0]
    head_ref[...] = block_ref[pl.ds(0, cut), :]
    tail_ref[...] = block_ref[pl.ds(cut, tail_ref.shape[0]), :]


def best_of(block, count, spread, best):
    half = LANES // 2
    scale = float(half * LANES) ** 0.5
    at = block.shape[0] - (half + 2) * count
    wide = block[pl.ds(at, half * count), :].astype(F32)
    labels = block[pl.ds(at + half * count, 2 * count), :].astype(F32)[:count]
    for e in range(2):
        products = wide * spread[e]
        total = jnp.sum(products.reshape(half, count, LANES), axis=0)
        similar = scale * jnp.sum(total, axis=1, keepdims=True)
        for t in range(TASKS):
            here = jnp.where(labels == float(t), similar, -2.0 * scale)
            best[e][t] = jnp.maximum(best[e][t], here)


def score_kernel(blocks, count, unit_ref, *refs):
    block_refs, (out_ref, mean_ref, spread) = refs[:blocks], refs[blocks:]
    half = LANES // 2
    scale = float(half * LANES) ** 0.5
    for e in range(2):
        for i in range(half):
            row = unit_ref[pl.ds(e * half + i, 1), :].astype(F32)
            spread[e, pl.ds(i * count, count), :] = jnp.broadcast_to(row, (count, LANES))
    best = [[jnp.full((count, LANES), -2.0 * scale, F32) for _ in range(TASKS)] for _ in range(2)]
    for block in block_refs:
        best_of(block, count, spread, best)
    for e in range(2):
        values = [jnp.max(best[e][t]) for t in range(TASKS)]
        for t in range(TASKS):
            out_ref[e, t] = values[t]
        mean_ref[e] = (values[0] + values[1] + values[2]) * (1.0 / TASKS)


VMEM = pl.BlockSpec(memory_space=pltpu.VMEM)
SMEM = pl.BlockSpec(memory_space=pltpu.SMEM)
ANY = pl.BlockSpec(memory_space=pl.ANY)
HBM = pl.BlockSpec(memory_space=pltpu.HBM)


def in_hbm(arrays):
    return [pltpu.with_memory_space_constraint(a, pltpu.HBM) for a in arrays]


def params(mib):
    return pltpu.CompilerParams(vmem_limit_bytes=mib * MIB)


def cost(flops, nbytes):
    return pl.CostEstimate(flops=flops, bytes_accessed=nbytes, transcendentals=0)


def shards(
    hidden_state_input,
    attention_mixed_state,
    hidden_state_adjoint,
    attention_values_adjoint,
    sequence_token_counts,
    heldout_sketched_signals,
    benchmark_labels,
    top_rmsnorm_weights,
    top_reducer_matrix,
    top_expander_matrix,
    bottom_reducer_matrix,
    bottom_expander_matrix,
    source_sketch,
    top_reducer_sketch,
    top_expander_sketch,
    top_target_sketch,
    bottom_reducer_sketch,
    bottom_expander_sketch,
    bottom_target_sketch,
):
    me = lax.axis_index("dp").astype(jnp.int32)
    x, mixed, adjoint, values = (
        hidden_state_input,
        attention_mixed_state,
        hidden_state_adjoint,
        attention_values_adjoint,
    )
    tokens, width = x.shape
    rows = top_reducer_matrix.shape[0]
    count = heldout_sketched_signals.shape[0]

    inputs = (
        top_rmsnorm_weights.reshape(width // LANES, LANES),
        top_reducer_matrix,
        bottom_expander_matrix.T,
        bottom_reducer_sketch,
        top_expander_matrix.T,
        bottom_reducer_matrix,
        bottom_expander_sketch.T,
        heldout_sketched_signals,
        benchmark_labels.T,
    )
    own = pl.pallas_call(
        pack_kernel,
        out_shape=jax.ShapeDtypeStruct((3 * rows + (LANES // 2 + 2) * count, LANES), BF16),
        in_specs=[SMEM] + [HBM] * len(inputs),
        out_specs=VMEM,
        scratch_shapes=[pltpu.VMEM(a.shape, a.dtype) for a in inputs]
        + [pltpu.SemaphoreType.DMA((len(inputs),))],
        compiler_params=params(8),
        name="pack",
    )(me.reshape(1), *in_hbm(inputs))

    inputs = (
        x,
        mixed,
        adjoint,
        values,
        bottom_target_sketch,
        top_target_sketch,
        top_rmsnorm_weights.reshape(1, width),
        source_sketch.T,
    )
    *activations, local = pl.pallas_call(
        local_kernel,
        out_shape=[jax.ShapeDtypeStruct(a.shape, a.dtype) for a in inputs[:6]]
        + [
            jax.ShapeDtypeStruct((width, LANES), BF16),
            jax.ShapeDtypeStruct((tokens, LOCAL_SUMS * LANES), F32),
        ],
        in_specs=[HBM] * len(inputs),
        out_specs=[VMEM] * 8,
        scratch_shapes=[pltpu.VMEM(a.shape, a.dtype) for a in inputs[6:]]
        + [pltpu.SemaphoreType.DMA((STEPS + 1, 4))],
        compiler_params=params(24),
        cost_estimate=cost(tokens * width * LANES * 6, 14 * MIB),
        name="local_products",
    )(*in_hbm(inputs))

    def stage(away, pieces, sums, local=None):
        first, last = not sums, local is not None
        sums_shape, bridge_shape = (tokens, SUMS * LANES), (LANES, 2 * LANES)
        small = (top_expander_sketch.T, top_reducer_sketch)
        head = [me.reshape(1)] + ([sequence_token_counts] if last else [])
        start = len(head) + len(pieces) + len(activations)
        return pl.pallas_call(
            functools.partial(stage_kernel, away, first, last),
            out_shape=jax.ShapeDtypeStruct((LANES, LANES), BF16)
            if last
            else [jax.ShapeDtypeStruct(sums_shape, F32), jax.ShapeDtypeStruct(bridge_shape, F32)],
            in_specs=[SMEM] * len(head)
            + [VMEM] * (len(pieces) + len(activations) + len(sums))
            + ([VMEM, HBM, HBM] if last else []),
            out_specs=VMEM if last else [VMEM, VMEM],
            scratch_shapes=[
                pltpu.VMEM((2 * rows, 2 * LANES), BF16),
                pltpu.VMEM((rows + LANES // 2, 2 * LANES), BF16),
                pltpu.VMEM((2 * rows, LANES), BF16),
                pltpu.VMEM(small[0].shape, BF16),
                pltpu.VMEM(small[1].shape, BF16),
                pltpu.SemaphoreType.DMA((2,)),
            ],
            input_output_aliases={} if first or last else {start: 0, start + 1: 1},
            compiler_params=params(16),
            cost_estimate=cost(tokens * rows * LANES * 16, 2 * MIB),
            name="features" if last else "stage",
        )(*head, *pieces, *activations, *sums, *((local, *in_hbm(small)) if last else ()))

    def split(block):
        shapes = (3 * rows, LANES), (block.shape[0] - 3 * rows, LANES)
        return pl.pallas_call(
            split_kernel,
            out_shape=[jax.ShapeDtypeStruct(shape, BF16) for shape in shapes],
            in_specs=[VMEM],
            out_specs=[VMEM, VMEM],
            compiler_params=params(8),
            name="split",
        )(block)

    tie = lax.optimization_barrier
    half = RING_CHIPS // 2
    first, second = own, other_core(own)
    blocks = [first, second]
    held = [first, second]
    first, second = hop(first), hop(second)
    first, activations = tie((first, activations))
    sums = stage(0, held, [])
    second, sums = tie((second, sums))
    for k in range(1, half):
        held = [first, second]
        crossed = [other_core(first), other_core(second)]
        blocks += held + crossed
        if k == half - 1:
            first, panel = split(first)
            panel = hop(panel)
        first = hop(first)
        sums = stage(k, held, sums)
        first, sums = tie((first, sums))
        if k < half - 1:
            second = hop(second)
        sums = stage(-k, crossed, sums)
        if k < half - 1:
            second, sums = tie((second, sums))
    unit = stage(half, [first, other_core(first)], sums, local)
    blocks += [panel, other_core(panel)]

    task_best, scores = pl.pallas_call(
        functools.partial(score_kernel, len(blocks), count),
        out_shape=(jax.ShapeDtypeStruct((2, TASKS), F32), jax.ShapeDtypeStruct((2,), F32)),
        in_specs=[VMEM] * (1 + len(blocks)),
        out_specs=(SMEM, SMEM),
        scratch_shapes=[pltpu.VMEM((2, LANES // 2 * count, LANES), F32)],
        compiler_params=params(16),
        cost_estimate=cost(4 * MIB, 2 * MIB),
        name="scores",
    )(unit, *blocks)
    return (scores, task_best)


def shards_of_any_slice(
    hidden_state_input,
    attention_mixed_state,
    hidden_state_adjoint,
    attention_values_adjoint,
    sequence_token_counts,
    heldout_sketched_signals,
    benchmark_labels,
    top_rmsnorm_weights,
    top_reducer_matrix,
    top_expander_matrix,
    bottom_reducer_matrix,
    bottom_expander_matrix,
    source_sketch,
    top_reducer_sketch,
    top_expander_sketch,
    top_target_sketch,
    bottom_reducer_sketch,
    bottom_expander_sketch,
    bottom_target_sketch,
    n,
):
    me = lax.axis_index("dp")
    x, mixed, adjoint, values = (
        hidden_state_input,
        attention_mixed_state,
        hidden_state_adjoint,
        attention_values_adjoint,
    )
    tokens, width = x.shape
    rows = top_reducer_matrix.shape[0]
    up_rows = top_expander_matrix.shape[1]
    rank = top_reducer_matrix.shape[1]
    k1 = source_sketch.shape[1]
    gain = top_rmsnorm_weights
    own_gain = lax.dynamic_slice_in_dim(gain, me * rows, rows)

    down_upper = (own_gain[:, None] * top_reducer_matrix.astype(F32)).astype(BF16)
    up_lower = mm(bottom_expander_matrix.T, bottom_reducer_sketch).astype(BF16)
    down_lower = mm(bottom_reducer_matrix, bottom_expander_sketch).astype(BF16)
    packed_lower = jnp.concatenate([down_lower[: rows // 2], down_lower[rows // 2 :]], axis=1)
    factors = jnp.concatenate([down_upper, up_lower, top_expander_matrix.T, packed_lower], axis=0)
    factors = lax.all_gather(factors, "dp")

    val_wide = heldout_sketched_signals.astype(F32)
    val_unit = (
        val_wide * lax.rsqrt(jnp.sum(val_wide * val_wide, axis=1, keepdims=True) + 1e-06)
    ).astype(BF16)
    labels = jnp.broadcast_to(benchmark_labels.astype(BF16), (val_unit.shape[0], 128))
    panel = jnp.concatenate([val_unit.reshape(-1, 128), labels], axis=0)
    panel = lax.all_gather(panel, "dp")
    val_rows = val_unit.shape[0]
    cut = panel.shape[1] - val_rows
    panel_tasks = panel[:, cut:, 0].reshape(n * val_rows, 1).astype(jnp.int32)
    panel = panel[:, :cut].reshape(n * val_rows, val_unit.shape[1])

    wide = x.astype(F32)
    inverse = lax.rsqrt(jnp.mean(wide * wide, axis=1, keepdims=True) + 1e-05)
    gained_sketch = (gain[:, None] * source_sketch.astype(F32)).astype(BF16)
    left_one = inverse * mm(x, gained_sketch)
    left_three = mm(mixed, source_sketch)
    right_two = ALPHA * mm(values, top_target_sketch)

    at = 0
    down_upper = factors[:, at : at + rows].reshape(width, rank)
    at += rows
    up_lower = factors[:, at : at + rows].reshape(width, -1)
    at += rows
    up_upper = factors[:, at : at + up_rows].reshape(-1, rank)
    at += up_rows
    down_lower = factors[:, at:]
    down_lower = jnp.concatenate([down_lower[:, :, :k1], down_lower[:, :, k1:]], axis=1)
    down_lower = down_lower.reshape(width, k1)

    reduced = inverse * mm(x, down_upper)
    left_two = mm(reduced.astype(BF16), top_expander_sketch)
    left_four = mm(mixed, down_lower)
    returned = mm(values, up_upper).astype(BF16)
    right_one = ALPHA * mm(returned, top_reducer_sketch)
    along = (ALPHA / width) * jnp.sum(returned.astype(F32) * reduced, axis=1, keepdims=True)
    targets = jnp.concatenate([up_lower, bottom_target_sketch], axis=1)
    bridge = mm_cols(down_upper, targets).astype(BF16)
    rights_low = mm(adjoint, targets) + inverse * (
        ALPHA * mm(returned, bridge) - (along * inverse) * mm(x, targets)
    )
    rights_low = ALPHA * rights_low
    k2 = up_lower.shape[1]
    lefts = (left_one, left_two, left_three, left_four)
    rights = (right_one, right_two, rights_low[:, :k2], rights_low[:, k2:])

    counts = sequence_token_counts[0]
    ends = jnp.cumsum(counts)
    starts = ends - counts
    places = jnp.arange(tokens, dtype=jnp.int32)[:, None]
    member = (places >= starts[None, :]) & (places < ends[None, :])
    count_ex = counts.shape[0]
    spread = jnp.concatenate(lefts, axis=0).astype(BF16)
    member = jnp.tile(member, (4, 1))
    spread = jnp.concatenate(
        [jnp.where(member[:, e : e + 1], spread, 0) for e in range(count_ex)], axis=1
    )
    feats = mm_cols(spread, jnp.concatenate(rights, axis=0).astype(BF16))
    feats = feats.reshape(count_ex, -1)
    squares = jnp.sum(feats * feats, axis=1, keepdims=True)
    unit_rows = (feats * lax.rsqrt(squares + 1e-06)).astype(BF16)

    score_scale = float(unit_rows.shape[1]) ** 0.5
    similar = score_scale * mm_rows(unit_rows, panel)
    task_mask = panel_tasks == jnp.arange(TASKS, dtype=jnp.int32)[None, :]
    task_best = jnp.max(
        jnp.where(task_mask[None, :, :], similar[:, :, None], -2.0 * score_scale), axis=1
    )
    return (jnp.mean(task_best, axis=1), task_best)


def solution(mesh):
    n = mesh.shape["dp"]
    split = P(("parts", "dp"), None)
    by_row, by_column, whole = P("dp", None), P(None, "dp"), P()
    placed = (
        (split,) * 5
        + (by_row, by_row, whole)
        + (by_row, by_column, by_row, by_column)
        + (whole,) * 7
    )
    ours = shards if n == 2 * RING_CHIPS else functools.partial(shards_of_any_slice, n=n)
    return jax.shard_map(
        ours,
        mesh=mesh,
        in_specs=placed,
        out_specs=(P(("parts", "dp")), split),
        check_vma=False,
    )
```

```python
import functools

import jax
import jax.numpy as jnp
from jax import lax
from jax.experimental import pallas as pl
from jax.experimental.pallas import tpu as pltpu
from jax.sharding import PartitionSpec as P

TASKS = 3
ALPHA = 4.0
F32 = jnp.float32
BF16 = jnp.bfloat16
RING_CHIPS = 8
LANES = 128
STEPS = 4
X_DOWN, X_LOW, J_LOW, J_TARGET, M_DOWN, M_SOURCE, VALUES, V_TARGET, SUMS = range(9)
INVERSE, LEFT_ONE, X_TARGET, LOCAL_SUMS = range(4)
MIB = 1 << 20


def mm(a, b):
    return jnp.dot(a, b, preferred_element_type=F32)


def mm_rows(a, b):
    return lax.dot_general(a, b, (((1,), (1,)), ((), ())), preferred_element_type=F32)


def mm_cols(a, b):
    return lax.dot_general(a, b, (((0,), (0,)), ((), ())), preferred_element_type=F32)


def ring_chip(pos):
    half = RING_CHIPS // 2
    return jnp.where(pos < half, 2 * pos, 2 * (RING_CHIPS - 1 - pos) + 1)


def ring_pos(chip):
    row, side = chip // 2, chip % 2
    return jnp.where(side == 0, row, RING_CHIPS - 1 - row)


def hop(value, from_other=False):
    half = RING_CHIPS // 2
    place = [2 * q if q < half else 2 * (RING_CHIPS - 1 - q) + 1 for q in range(RING_CHIPS)]
    turn = int(from_other)
    pairs = []
    for q in range(RING_CHIPS):
        pairs.append((2 * place[q] + turn, 2 * place[(q + 1) % RING_CHIPS]))
        pairs.append((2 * place[q] + 1 - turn, 2 * place[(q - 1) % RING_CHIPS] + 1))
    return lax.ppermute(value, "dp", pairs)


def other_core(value):
    return lax.ppermute(value, "dp", [(d, d ^ 1) for d in range(2 * RING_CHIPS)])


def half_lanes(shape):
    return lax.broadcasted_iota(jnp.int32, shape, 1) < LANES // 2


def diagonal_column(row, first, count):
    shape = (count, row.shape[1])
    lane = lax.broadcasted_iota(jnp.int32, shape, 1)
    at = lax.broadcasted_iota(jnp.int32, shape, 0)
    return jnp.sum(jnp.where(lane == at + first, row, 0.0), axis=1, keepdims=True)


def load(pairs, sems):
    copies = [pltpu.make_async_copy(src, dst, sems.at[i]) for i, (src, dst) in enumerate(pairs)]
    for copy in copies:
        copy.start()
    return copies


def pack_kernel(me_ref, *refs):
    hbm, out_ref, held, sems = refs[:9], refs[9], refs[10:19], refs[19]
    gain_ref, down_up_ref, up_low_ref, sketch_ref, up_up_ref, down_low_ref, expand_ref, val_ref, label_ref = held
    copies = load(zip(hbm, held), sems)
    rows = down_up_ref.shape[0]
    half = LANES // 2
    for copy in copies:
        copy.wait()
    for b in range(rows // half):
        place = me_ref[0] * (rows // half) + b
        row = gain_ref[pl.ds(place // 2, 1), :]
        column = diagonal_column(row, (place % 2) * half, half)
        part = down_up_ref[pl.ds(b * half, half), :].astype(F32)
        out_ref[pl.ds(b * half, half), :] = (column * part).astype(BF16)
    at = rows
    out_ref[pl.ds(at, rows), :] = mm(up_low_ref[...], sketch_ref[...]).astype(BF16)
    at += rows
    out_ref[pl.ds(at, rows // 2), :] = up_up_ref[...]
    at += rows // 2
    expand = expand_ref[...]
    low = mm_rows(down_low_ref[...], jnp.concatenate([expand, expand], axis=0))
    first, second = low[: rows // 2], low[rows // 2 :]
    out_ref[pl.ds(at, rows // 2), :] = jnp.where(half_lanes(first.shape), first, second).astype(BF16)
    at += rows // 2
    wide = val_ref[...].astype(F32)
    count, width = wide.shape
    scale = lax.rsqrt(jnp.sum(wide * wide, axis=1, keepdims=True) + 1e-06)
    unit = wide * scale
    blocks = [unit[:, i * LANES : (i + 1) * LANES] for i in range(width // LANES)]
    row = label_ref[...].astype(F32)
    labels = jnp.broadcast_to(diagonal_column(row, 0, count), (count, LANES))
    blocks += [labels, labels]
    for i in range(0, len(blocks), 2):
        pair = jnp.concatenate(blocks[i : i + 2], axis=0)
        out_ref[pl.ds(at + i * count, 2 * count), :] = pair.astype(BF16)


def local_kernel(*refs):
    x_hbm, mixed_hbm, adjoint_hbm, values_hbm, target_hbm, top_target_hbm, gain_hbm, source_hbm = refs[:8]
    x_ref, mixed_ref, adjoint_ref, values_ref, target_ref, top_target_ref, turned_ref, sums_ref = refs[8:16]
    gain_ref, source_ref, sems = refs[16:]
    tokens, width = x_ref.shape
    span = width // STEPS
    copies = []
    for j in range(STEPS):
        part = pl.ds(j * span, span)
        pairs = (
            (gain_hbm.at[:, part], gain_ref.at[:, part]),
            (source_hbm.at[:, part], source_ref.at[:, part]),
            (x_hbm.at[:, part], x_ref.at[:, part]),
            (target_hbm.at[part], target_ref.at[part]),
        )
        copies.append(load(pairs, sems.at[j]))
    pairs = (
        (adjoint_hbm, adjoint_ref),
        (mixed_hbm, mixed_ref),
        (values_hbm, values_ref),
        (top_target_hbm, top_target_ref),
    )
    later = load(pairs, sems.at[STEPS])
    products = jnp.zeros((tokens, 2 * LANES), F32)
    squares = jnp.zeros((tokens, LANES), F32)
    for j in range(STEPS):
        for copy in copies[j]:
            copy.wait()
        part = slice(j * span, (j + 1) * span)
        x, source = x_ref[:, part], source_ref[:, part].astype(F32)
        gained = source * gain_ref[:, part]
        turned_ref[part, :] = jnp.concatenate([source, source], axis=0).T.astype(BF16)
        gained = jnp.concatenate([gained, gained], axis=0).T.astype(BF16)
        products = products + mm(x, jnp.concatenate([gained, target_ref[part, :]], axis=1))
        for i in range(span // LANES):
            wide = x[:, i * LANES : (i + 1) * LANES].astype(F32)
            squares = squares + wide * wide
    mean = jnp.sum(squares, axis=1, keepdims=True) * (1.0 / width)
    inverse = jnp.broadcast_to(lax.rsqrt(mean + 1e-05), (tokens, LANES))
    for i, value in enumerate((inverse, inverse * products[:, :LANES], products[:, LANES:])):
        sums_ref[:, i * LANES : (i + 1) * LANES] = value
    for copy in later:
        copy.wait()


def stage_kernel(away, first, me_ref, *refs):
    refs = list(refs)
    take = lambda k: [refs.pop(0) for _ in range(k)]
    pieces = take(2)
    x_ref, mixed_ref, adjoint_ref, values_ref, target_ref, top_target_ref, source_ref = take(7)
    old_sums, old_bridge = (None, None) if first else take(2)
    new_sums, new_bridge, both, up, down = refs
    rows = both.shape[0] // 2
    half, pad = rows // 2, LANES // 2
    span = 2 * rows
    me = me_ref[0]
    pos, core = ring_pos(me // 2), me % 2
    chip = ring_chip((pos + away * (2 * core - 1) + RING_CHIPS) % RING_CHIPS)
    odd = chip % 2
    mine = pl.ds(pl.multiple_of(chip * span, LANES), span)
    values_start = (chip // 2) * span + odd * (rows - pad)
    values_part = pl.ds(pl.multiple_of(values_start, LANES), rows + pad)
    side = core if away >= 0 else 1 - core
    up[pl.ds(pl.multiple_of((1 - odd) * rows, 16), pad), :] = jnp.zeros((pad, 2 * LANES), BF16)
    up[pl.ds(pl.multiple_of(odd * pad, 16), rows), pl.ds(LANES, LANES)] = top_target_ref[
        pl.ds(pl.multiple_of(chip * rows, 16), rows), :
    ]
    for piece, c in ((pieces[0], side), (pieces[1], 1 - side)):
        one = pl.ds(pl.multiple_of(c * rows, 16), rows)
        both[one, pl.ds(0, LANES)] = piece[pl.ds(0, rows), :]
        both[one, pl.ds(LANES, LANES)] = piece[pl.ds(rows, rows), :]
        up[pl.ds(pl.multiple_of(odd * pad + c * half, 16), half), pl.ds(0, LANES)] = piece[
            pl.ds(2 * rows, half), :
        ]
        packed = piece[pl.ds(2 * rows + half, half), :].astype(F32)
        turned = pltpu.roll(packed, pad, 1)
        lower = half_lanes(packed.shape)
        down[pl.ds(pl.multiple_of(c * rows, 16), half), :] = jnp.where(lower, packed, turned).astype(BF16)
        down[pl.ds(pl.multiple_of(c * rows + half, 16), half), :] = jnp.where(lower, turned, packed).astype(BF16)

    weights = both[...]
    down_up = weights[:, :LANES]
    lows = jnp.concatenate([weights[:, LANES:], target_ref[mine, :]], axis=1)
    products = []
    for activation, factor in (
        (x_ref[:, mine], weights),
        (adjoint_ref[:, mine], lows),
        (mixed_ref[:, mine], jnp.concatenate([down[...], source_ref[mine, :]], axis=1)),
        (values_ref[:, values_part], up[...]),
    ):
        product = mm(activation, factor)
        products += [product[:, :LANES], product[:, LANES:]]
    bridge = mm_cols(down_up, lows)
    if not first:
        products = [p + old_sums[:, i * LANES : (i + 1) * LANES] for i, p in enumerate(products)]
        bridge = bridge + old_bridge[...]
    for i in range(SUMS):
        new_sums[:, i * LANES : (i + 1) * LANES] = products[i]
    new_bridge[...] = bridge


def feature_kernel(width, counts_ref, sums_ref, bridge_ref, local_ref, expand_hbm, sketch_hbm, out_ref, *scratch):
    expand_ref, sketch_ref, sems = scratch
    more = load(((expand_hbm, expand_ref), (sketch_hbm, sketch_ref)), sems)
    tokens = sums_ref.shape[0]
    pad = LANES // 2
    products = [sums_ref[:, i * LANES : (i + 1) * LANES] for i in range(SUMS)]
    local = [local_ref[:, i * LANES : (i + 1) * LANES] for i in range(LOCAL_SUMS)]
    bridge = bridge_ref[...]
    for copy in more:
        copy.wait()
    inverse = local[INVERSE]
    reduced = inverse * products[X_DOWN]
    expand = expand_ref[...]
    left_two = mm_rows(reduced.astype(BF16), jnp.concatenate([expand, expand], axis=0))
    returned = products[VALUES].astype(BF16)
    right_one = ALPHA * mm(returned, sketch_ref[...])
    along = (ALPHA / width) * jnp.sum(returned.astype(F32) * reduced, axis=1, keepdims=True)
    back = mm(returned, bridge.astype(BF16))
    along = along * inverse
    right_three = products[J_LOW] + inverse * (ALPHA * back[:, :LANES] - along * products[X_LOW])
    right_four = products[J_TARGET] + inverse * (ALPHA * back[:, LANES:] - along * local[X_TARGET])
    rights = (right_one, ALPHA * products[V_TARGET], ALPHA * right_three, ALPHA * right_four)
    lefts = (local[LEFT_ONE], left_two, products[M_SOURCE], products[M_DOWN])
    place = lax.broadcasted_iota(jnp.int32, (tokens, LANES), 0)
    one, two = counts_ref[0, 0], counts_ref[0, 1]
    lower = half_lanes((tokens, LANES))
    member = (place >= jnp.where(lower, 0, one)) & (place < jnp.where(lower, one, one + two))
    spread = jnp.concatenate([jnp.where(member, left, 0.0).astype(BF16) for left in lefts], axis=0)
    feats = mm_cols(spread, jnp.concatenate([right.astype(BF16) for right in rights], axis=0))
    for e in range(2):
        own = feats[e * pad : (e + 1) * pad]
        squares = jnp.sum(own * own, keepdims=True)
        out_ref[pl.ds(e * pad, pad), :] = (own * lax.rsqrt(squares + 1e-06)).astype(BF16).astype(F32)


def score_kernel(blocks, count, unit_ref, *refs):
    block_refs, (out_ref, mean_ref) = refs[:blocks], refs[blocks:]
    half = LANES // 2
    scale = float(half * LANES) ** 0.5
    starts = [block.shape[0] - (half + 2) * count for block in block_refs]
    shape = (count, LANES)
    totals = [[jnp.zeros(shape, F32) for _ in range(2)] for _ in block_refs]
    for i in range(0, half, 2):
        units = [
            [jnp.broadcast_to(unit_ref[pl.ds(e * half + i + k, 1), :], shape) for k in range(2)]
            for e in range(2)
        ]
        for b, block in enumerate(block_refs):
            wide = block[pl.ds(starts[b] + i * count, 2 * count), :].astype(F32)
            for e in range(2):
                totals[b][e] = totals[b][e] + (wide[:count] * units[e][0] + wide[count:] * units[e][1])
    best = [[jnp.full(shape, -2.0 * scale, F32) for _ in range(TASKS)] for _ in range(2)]
    for b, block in enumerate(block_refs):
        labels = block[pl.ds(starts[b] + half * count, 2 * count), :].astype(F32)[:count]
        for e in range(2):
            similar = scale * jnp.sum(totals[b][e], axis=1, keepdims=True)
            for t in range(TASKS):
                best[e][t] = jnp.maximum(best[e][t], jnp.where(labels == float(t), similar, -2.0 * scale))
    for e in range(2):
        values = [jnp.max(best[e][t]) for t in range(TASKS)]
        for t in range(TASKS):
            out_ref[e, t] = values[t]
        mean_ref[e] = (values[0] + values[1] + values[2]) * (1.0 / TASKS)


VMEM = pl.BlockSpec(memory_space=pltpu.VMEM)
SMEM = pl.BlockSpec(memory_space=pltpu.SMEM)
ANY = pl.BlockSpec(memory_space=pl.ANY)
HBM = pl.BlockSpec(memory_space=pltpu.HBM)


def in_hbm(arrays):
    return [pltpu.with_memory_space_constraint(a, pltpu.HBM) for a in arrays]


def params(mib):
    return pltpu.CompilerParams(vmem_limit_bytes=mib * MIB)


def cost(flops, nbytes):
    return pl.CostEstimate(flops=flops, bytes_accessed=nbytes, transcendentals=0)


def shards(
    hidden_state_input,
    attention_mixed_state,
    hidden_state_adjoint,
    attention_values_adjoint,
    sequence_token_counts,
    heldout_sketched_signals,
    benchmark_labels,
    top_rmsnorm_weights,
    top_reducer_matrix,
    top_expander_matrix,
    bottom_reducer_matrix,
    bottom_expander_matrix,
    source_sketch,
    top_reducer_sketch,
    top_expander_sketch,
    top_target_sketch,
    bottom_reducer_sketch,
    bottom_expander_sketch,
    bottom_target_sketch,
):
    me = lax.axis_index("dp").astype(jnp.int32)
    x, mixed, adjoint, values = (
        hidden_state_input,
        attention_mixed_state,
        hidden_state_adjoint,
        attention_values_adjoint,
    )
    tokens, width = x.shape
    rows = top_reducer_matrix.shape[0]
    count = heldout_sketched_signals.shape[0]

    inputs = (
        top_rmsnorm_weights.reshape(width // LANES, LANES),
        top_reducer_matrix,
        bottom_expander_matrix.T,
        bottom_reducer_sketch,
        top_expander_matrix.T,
        bottom_reducer_matrix,
        bottom_expander_sketch.T,
        heldout_sketched_signals,
        benchmark_labels.T,
    )
    own = pl.pallas_call(
        pack_kernel,
        out_shape=jax.ShapeDtypeStruct((3 * rows + (LANES // 2 + 2) * count, LANES), BF16),
        in_specs=[SMEM] + [HBM] * len(inputs),
        out_specs=VMEM,
        scratch_shapes=[pltpu.VMEM(a.shape, a.dtype) for a in inputs]
        + [pltpu.SemaphoreType.DMA((len(inputs),))],
        compiler_params=params(8),
        name="pack",
    )(me.reshape(1), *in_hbm(inputs))

    inputs = (
        x,
        mixed,
        adjoint,
        values,
        bottom_target_sketch,
        top_target_sketch,
        top_rmsnorm_weights.reshape(1, width),
        source_sketch.T,
    )
    *activations, local = pl.pallas_call(
        local_kernel,
        out_shape=[jax.ShapeDtypeStruct(a.shape, a.dtype) for a in inputs[:6]]
        + [
            jax.ShapeDtypeStruct((width, LANES), BF16),
            jax.ShapeDtypeStruct((tokens, LOCAL_SUMS * LANES), F32),
        ],
        in_specs=[HBM] * len(inputs),
        out_specs=[VMEM] * 8,
        scratch_shapes=[pltpu.VMEM(a.shape, a.dtype) for a in inputs[6:]]
        + [pltpu.SemaphoreType.DMA((STEPS + 1, 4))],
        compiler_params=params(24),
        cost_estimate=cost(tokens * width * LANES * 6, 14 * MIB),
        name="local_products",
    )(*in_hbm(inputs))

    def stage(away, pieces, sums):
        first = not sums
        start = 1 + len(pieces) + len(activations)
        return pl.pallas_call(
            functools.partial(stage_kernel, away, first),
            out_shape=[
                jax.ShapeDtypeStruct((tokens, SUMS * LANES), F32),
                jax.ShapeDtypeStruct((LANES, 2 * LANES), F32),
            ],
            in_specs=[SMEM] + [VMEM] * (len(pieces) + len(activations) + len(sums)),
            out_specs=[VMEM, VMEM],
            scratch_shapes=[
                pltpu.VMEM((2 * rows, 2 * LANES), BF16),
                pltpu.VMEM((rows + LANES // 2, 2 * LANES), BF16),
                pltpu.VMEM((2 * rows, LANES), BF16),
            ],
            input_output_aliases={} if first else {start: 0, start + 1: 1},
            compiler_params=params(16),
            cost_estimate=cost(tokens * rows * LANES * 16, 2 * MIB),
            name="stage",
        )(me.reshape(1), *pieces, *activations, *sums)

    tie = lax.optimization_barrier
    half = RING_CHIPS // 2
    held = [own, other_core(own)]
    blocks = list(held)
    first, second = hop(own), hop(own, from_other=True)
    first, activations = tie((first, activations))
    sums = stage(0, held, [])
    second, sums = tie((second, sums))
    for k in range(1, half):
        held = [first, second]
        crossed = [other_core(first), other_core(second)]
        blocks += held + crossed
        first = hop(first)
        sums = stage(k, held, sums)
        first, sums = tie((first, sums))
        if k < half - 1:
            second = hop(second)
        sums = stage(-k, crossed, sums)
        if k < half - 1:
            second, sums = tie((second, sums))
    held = [first, other_core(first)]
    blocks += held
    sums = stage(half, held, sums)
    small = (top_expander_sketch.T, top_reducer_sketch)
    unit = pl.pallas_call(
        functools.partial(feature_kernel, width),
        out_shape=jax.ShapeDtypeStruct((LANES, LANES), F32),
        in_specs=[SMEM] + [VMEM] * 3 + [HBM] * 2,
        out_specs=VMEM,
        scratch_shapes=[pltpu.VMEM(a.shape, a.dtype) for a in small] + [pltpu.SemaphoreType.DMA((2,))],
        compiler_params=params(16),
        cost_estimate=cost(tokens * LANES * LANES * 20, 4 * MIB),
        name="features",
    )(sequence_token_counts, *sums, local, *in_hbm(small))

    task_best, scores = pl.pallas_call(
        functools.partial(score_kernel, len(blocks), count),
        out_shape=(jax.ShapeDtypeStruct((2, TASKS), F32), jax.ShapeDtypeStruct((2,), F32)),
        in_specs=[VMEM] * (1 + len(blocks)),
        out_specs=(SMEM, SMEM),
        compiler_params=params(16),
        cost_estimate=cost(4 * MIB, 2 * MIB),
        name="scores",
    )(unit, *blocks)
    return (scores, task_best)


def shards_of_any_slice(
    hidden_state_input,
    attention_mixed_state,
    hidden_state_adjoint,
    attention_values_adjoint,
    sequence_token_counts,
    heldout_sketched_signals,
    benchmark_labels,
    top_rmsnorm_weights,
    top_reducer_matrix,
    top_expander_matrix,
    bottom_reducer_matrix,
    bottom_expander_matrix,
    source_sketch,
    top_reducer_sketch,
    top_expander_sketch,
    top_target_sketch,
    bottom_reducer_sketch,
    bottom_expander_sketch,
    bottom_target_sketch,
    n,
):
    me = lax.axis_index("dp")
    x, mixed, adjoint, values = (
        hidden_state_input,
        attention_mixed_state,
        hidden_state_adjoint,
        attention_values_adjoint,
    )
    tokens, width = x.shape
    rows = top_reducer_matrix.shape[0]
    up_rows = top_expander_matrix.shape[1]
    rank = top_reducer_matrix.shape[1]
    k1 = source_sketch.shape[1]
    gain = top_rmsnorm_weights
    own_gain = lax.dynamic_slice_in_dim(gain, me * rows, rows)

    down_upper = (own_gain[:, None] * top_reducer_matrix.astype(F32)).astype(BF16)
    up_lower = mm(bottom_expander_matrix.T, bottom_reducer_sketch).astype(BF16)
    down_lower = mm(bottom_reducer_matrix, bottom_expander_sketch).astype(BF16)
    packed_lower = jnp.concatenate([down_lower[: rows // 2], down_lower[rows // 2 :]], axis=1)
    factors = jnp.concatenate([down_upper, up_lower, top_expander_matrix.T, packed_lower], axis=0)
    factors = lax.all_gather(factors, "dp")

    val_wide = heldout_sketched_signals.astype(F32)
    val_unit = (
        val_wide * lax.rsqrt(jnp.sum(val_wide * val_wide, axis=1, keepdims=True) + 1e-06)
    ).astype(BF16)
    labels = jnp.broadcast_to(benchmark_labels.astype(BF16), (val_unit.shape[0], 128))
    panel = jnp.concatenate([val_unit.reshape(-1, 128), labels], axis=0)
    panel = lax.all_gather(panel, "dp")
    val_rows = val_unit.shape[0]
    cut = panel.shape[1] - val_rows
    panel_tasks = panel[:, cut:, 0].reshape(n * val_rows, 1).astype(jnp.int32)
    panel = panel[:, :cut].reshape(n * val_rows, val_unit.shape[1])

    wide = x.astype(F32)
    inverse = lax.rsqrt(jnp.mean(wide * wide, axis=1, keepdims=True) + 1e-05)
    gained_sketch = (gain[:, None] * source_sketch.astype(F32)).astype(BF16)
    left_one = inverse * mm(x, gained_sketch)
    left_three = mm(mixed, source_sketch)
    right_two = ALPHA * mm(values, top_target_sketch)

    at = 0
    down_upper = factors[:, at : at + rows].reshape(width, rank)
    at += rows
    up_lower = factors[:, at : at + rows].reshape(width, -1)
    at += rows
    up_upper = factors[:, at : at + up_rows].reshape(-1, rank)
    at += up_rows
    down_lower = factors[:, at:]
    down_lower = jnp.concatenate([down_lower[:, :, :k1], down_lower[:, :, k1:]], axis=1)
    down_lower = down_lower.reshape(width, k1)

    reduced = inverse * mm(x, down_upper)
    left_two = mm(reduced.astype(BF16), top_expander_sketch)
    left_four = mm(mixed, down_lower)
    returned = mm(values, up_upper).astype(BF16)
    right_one = ALPHA * mm(returned, top_reducer_sketch)
    along = (ALPHA / width) * jnp.sum(returned.astype(F32) * reduced, axis=1, keepdims=True)
    targets = jnp.concatenate([up_lower, bottom_target_sketch], axis=1)
    bridge = mm_cols(down_upper, targets).astype(BF16)
    rights_low = mm(adjoint, targets) + inverse * (
        ALPHA * mm(returned, bridge) - (along * inverse) * mm(x, targets)
    )
    rights_low = ALPHA * rights_low
    k2 = up_lower.shape[1]
    lefts = (left_one, left_two, left_three, left_four)
    rights = (right_one, right_two, rights_low[:, :k2], rights_low[:, k2:])

    counts = sequence_token_counts[0]
    ends = jnp.cumsum(counts)
    starts = ends - counts
    places = jnp.arange(tokens, dtype=jnp.int32)[:, None]
    member = (places >= starts[None, :]) & (places < ends[None, :])
    count_ex = counts.shape[0]
    spread = jnp.concatenate(lefts, axis=0).astype(BF16)
    member = jnp.tile(member, (4, 1))
    spread = jnp.concatenate(
        [jnp.where(member[:, e : e + 1], spread, 0) for e in range(count_ex)], axis=1
    )
    feats = mm_cols(spread, jnp.concatenate(rights, axis=0).astype(BF16))
    feats = feats.reshape(count_ex, -1)
    squares = jnp.sum(feats * feats, axis=1, keepdims=True)
    unit_rows = (feats * lax.rsqrt(squares + 1e-06)).astype(BF16)

    score_scale = float(unit_rows.shape[1]) ** 0.5
    similar = score_scale * mm_rows(unit_rows, panel)
    task_mask = panel_tasks == jnp.arange(TASKS, dtype=jnp.int32)[None, :]
    task_best = jnp.max(
        jnp.where(task_mask[None, :, :], similar[:, :, None], -2.0 * score_scale), axis=1
    )
    return (jnp.mean(task_best, axis=1), task_best)


def solution(mesh):
    n = mesh.shape["dp"]
    split = P(("parts", "dp"), None)
    by_row, by_column, whole = P("dp", None), P(None, "dp"), P()
    placed = (
        (split,) * 5
        + (by_row, by_row, whole)
        + (by_row, by_column, by_row, by_column)
        + (whole,) * 7
    )
    ours = shards if n == 2 * RING_CHIPS else functools.partial(shards_of_any_slice, n=n)
    return jax.shard_map(
        ours,
        mesh=mesh,
        in_specs=placed,
        out_specs=(P(("parts", "dp")), split),
        check_vma=False,
    )
```

```python
import functools

import jax
import jax.numpy as jnp
from jax import lax
from jax.experimental import pallas as pl
from jax.experimental.pallas import tpu as pltpu
from jax.sharding import PartitionSpec as P

TASKS = 3
ALPHA = 4.0
F32 = jnp.float32
BF16 = jnp.bfloat16
RING_CHIPS = 8
LANES = 128
STEPS = 4
X_DOWN, X_LOW, J_LOW, J_TARGET, M_DOWN, M_SOURCE, VALUES, V_TARGET, SUMS = range(9)
INVERSE, LEFT_ONE, X_TARGET, LOCAL_SUMS = range(4)
MIB = 1 << 20


def mm(a, b):
    return jnp.dot(a, b, preferred_element_type=F32)


def mm_rows(a, b):
    return lax.dot_general(a, b, (((1,), (1,)), ((), ())), preferred_element_type=F32)


def mm_cols(a, b):
    return lax.dot_general(a, b, (((0,), (0,)), ((), ())), preferred_element_type=F32)


def ring_chip(pos):
    half = RING_CHIPS // 2
    return jnp.where(pos < half, 2 * pos, 2 * (RING_CHIPS - 1 - pos) + 1)


def ring_pos(chip):
    row, side = chip // 2, chip % 2
    return jnp.where(side == 0, row, RING_CHIPS - 1 - row)


def hop(value):
    half = RING_CHIPS // 2
    place = [2 * q if q < half else 2 * (RING_CHIPS - 1 - q) + 1 for q in range(RING_CHIPS)]
    pairs = []
    for q in range(RING_CHIPS):
        pairs.append((2 * place[q], 2 * place[(q + 1) % RING_CHIPS]))
        pairs.append((2 * place[q] + 1, 2 * place[(q - 1) % RING_CHIPS] + 1))
    return lax.ppermute(value, "dp", pairs)


def other_core(value):
    return lax.ppermute(value, "dp", [(d, d ^ 1) for d in range(2 * RING_CHIPS)])


def half_lanes(shape):
    return lax.broadcasted_iota(jnp.int32, shape, 1) < LANES // 2


def diagonal_column(row, first, count):
    shape = (count, row.shape[1])
    lane = lax.broadcasted_iota(jnp.int32, shape, 1)
    at = lax.broadcasted_iota(jnp.int32, shape, 0)
    return jnp.sum(jnp.where(lane == at + first, row, 0.0), axis=1, keepdims=True)


def load(pairs, sems):
    copies = [pltpu.make_async_copy(src, dst, sems.at[i]) for i, (src, dst) in enumerate(pairs)]
    for copy in copies:
        copy.start()
    return copies


def pack_kernel(me_ref, *refs):
    hbm, out_ref, held, sems = refs[:9], refs[9], refs[10:19], refs[19]
    gain_ref, down_up_ref, up_low_ref, sketch_ref, up_up_ref, down_low_ref, expand_ref, val_ref, label_ref = held
    copies = load(zip(hbm, held), sems)
    rows = down_up_ref.shape[0]
    half = LANES // 2
    for copy in copies:
        copy.wait()
    for b in range(rows // half):
        place = me_ref[0] * (rows // half) + b
        row = gain_ref[pl.ds(place // 2, 1), :]
        column = diagonal_column(row, (place % 2) * half, half)
        part = down_up_ref[pl.ds(b * half, half), :].astype(F32)
        out_ref[pl.ds(b * half, half), :] = (column * part).astype(BF16)
    at = rows
    out_ref[pl.ds(at, rows), :] = mm(up_low_ref[...], sketch_ref[...]).astype(BF16)
    at += rows
    out_ref[pl.ds(at, rows // 2), :] = up_up_ref[...]
    at += rows // 2
    expand = expand_ref[...]
    low = mm_rows(down_low_ref[...], jnp.concatenate([expand, expand], axis=0))
    first, second = low[: rows // 2], low[rows // 2 :]
    out_ref[pl.ds(at, rows // 2), :] = jnp.where(half_lanes(first.shape), first, second).astype(BF16)
    at += rows // 2
    wide = val_ref[...].astype(F32)
    count, width = wide.shape
    scale = lax.rsqrt(jnp.sum(wide * wide, axis=1, keepdims=True) + 1e-06)
    unit = wide * scale
    blocks = [unit[:, i * LANES : (i + 1) * LANES] for i in range(width // LANES)]
    row = label_ref[...].astype(F32)
    labels = jnp.broadcast_to(diagonal_column(row, 0, count), (count, LANES))
    blocks += [labels, labels]
    for i in range(0, len(blocks), 2):
        pair = jnp.concatenate(blocks[i : i + 2], axis=0)
        out_ref[pl.ds(at + i * count, 2 * count), :] = pair.astype(BF16)


def local_kernel(*refs):
    x_hbm, mixed_hbm, adjoint_hbm, values_hbm, target_hbm, top_target_hbm, gain_hbm, source_hbm = refs[:8]
    x_ref, mixed_ref, adjoint_ref, values_ref, target_ref, top_target_ref, turned_ref, sums_ref = refs[8:16]
    gain_ref, source_ref, sems = refs[16:]
    tokens, width = x_ref.shape
    span = width // STEPS
    copies = []
    for j in range(STEPS):
        part = pl.ds(j * span, span)
        pairs = (
            (gain_hbm.at[:, part], gain_ref.at[:, part]),
            (source_hbm.at[:, part], source_ref.at[:, part]),
            (x_hbm.at[:, part], x_ref.at[:, part]),
            (target_hbm.at[part], target_ref.at[part]),
        )
        copies.append(load(pairs, sems.at[j]))
    pairs = (
        (adjoint_hbm, adjoint_ref),
        (mixed_hbm, mixed_ref),
        (values_hbm, values_ref),
        (top_target_hbm, top_target_ref),
    )
    later = load(pairs, sems.at[STEPS])
    products = jnp.zeros((tokens, 2 * LANES), F32)
    squares = jnp.zeros((tokens, LANES), F32)
    for j in range(STEPS):
        for copy in copies[j]:
            copy.wait()
        part = slice(j * span, (j + 1) * span)
        x, source = x_ref[:, part], source_ref[:, part].astype(F32)
        gained = source * gain_ref[:, part]
        turned_ref[part, :] = jnp.concatenate([source, source], axis=0).T.astype(BF16)
        gained = jnp.concatenate([gained, gained], axis=0).T.astype(BF16)
        products = products + mm(x, jnp.concatenate([gained, target_ref[part, :]], axis=1))
        for i in range(span // LANES):
            wide = x[:, i * LANES : (i + 1) * LANES].astype(F32)
            squares = squares + wide * wide
    mean = jnp.sum(squares, axis=1, keepdims=True) * (1.0 / width)
    inverse = jnp.broadcast_to(lax.rsqrt(mean + 1e-05), (tokens, LANES))
    for i, value in enumerate((inverse, inverse * products[:, :LANES], products[:, LANES:])):
        sums_ref[:, i * LANES : (i + 1) * LANES] = value
    for copy in later:
        copy.wait()


def add_stage(away, me_ref, pieces, held, old, scratch):
    x_ref, mixed_ref, adjoint_ref, values_ref, target_ref, top_target_ref, source_ref = held
    both, up, down = scratch
    rows = both.shape[0] // 2
    half, pad = rows // 2, LANES // 2
    span = 2 * rows
    me = me_ref[0]
    pos, core = ring_pos(me // 2), me % 2
    chip = ring_chip((pos + away * (2 * core - 1) + RING_CHIPS) % RING_CHIPS)
    odd = chip % 2
    mine = pl.ds(pl.multiple_of(chip * span, LANES), span)
    values_start = (chip // 2) * span + odd * (rows - pad)
    values_part = pl.ds(pl.multiple_of(values_start, LANES), rows + pad)
    side = core if away >= 0 else 1 - core
    up[pl.ds(pl.multiple_of((1 - odd) * rows, 16), pad), :] = jnp.zeros((pad, 2 * LANES), BF16)
    up[pl.ds(pl.multiple_of(odd * pad, 16), rows), pl.ds(LANES, LANES)] = top_target_ref[
        pl.ds(pl.multiple_of(chip * rows, 16), rows), :
    ]
    for piece, c in ((pieces[0], side), (pieces[1], 1 - side)):
        one = pl.ds(pl.multiple_of(c * rows, 16), rows)
        both[one, pl.ds(0, LANES)] = piece[pl.ds(0, rows), :]
        both[one, pl.ds(LANES, LANES)] = piece[pl.ds(rows, rows), :]
        up[pl.ds(pl.multiple_of(odd * pad + c * half, 16), half), pl.ds(0, LANES)] = piece[
            pl.ds(2 * rows, half), :
        ]
        packed = piece[pl.ds(2 * rows + half, half), :].astype(F32)
        turned = pltpu.roll(packed, pad, 1)
        lower = half_lanes(packed.shape)
        down[pl.ds(pl.multiple_of(c * rows, 16), half), :] = jnp.where(lower, packed, turned).astype(BF16)
        down[pl.ds(pl.multiple_of(c * rows + half, 16), half), :] = jnp.where(lower, turned, packed).astype(BF16)

    weights = both[...]
    down_up = weights[:, :LANES]
    lows = jnp.concatenate([weights[:, LANES:], target_ref[mine, :]], axis=1)
    products = []
    for activation, factor in (
        (x_ref[:, mine], weights),
        (adjoint_ref[:, mine], lows),
        (mixed_ref[:, mine], jnp.concatenate([down[...], source_ref[mine, :]], axis=1)),
        (values_ref[:, values_part], up[...]),
    ):
        product = mm(activation, factor)
        products += [product[:, :LANES], product[:, LANES:]]
    bridge = mm_cols(down_up, lows)
    if old:
        old_sums, old_bridge = old
        products = [p + old_sums[:, i * LANES : (i + 1) * LANES] for i, p in enumerate(products)]
        bridge = bridge + old_bridge[...]
    return products, bridge


def stage_kernel(away, first, me_ref, *refs):
    pieces, held, old = refs[:2], refs[2:9], refs[9:-5]
    (new_sums, new_bridge), scratch = refs[-5:-3], refs[-3:]
    products, bridge = add_stage(away, me_ref, pieces, held, old, scratch)
    for i in range(SUMS):
        new_sums[:, i * LANES : (i + 1) * LANES] = products[i]
    new_bridge[...] = bridge


def finish_kernel(away, blocks, count, me_ref, counts_ref, *refs):
    block_refs, refs = refs[:blocks], refs[blocks:]
    held, old, local_ref, small_hbm, refs = refs[:7], refs[7:9], refs[9], refs[10:12], refs[12:]
    (out_ref, mean_ref), scratch, (expand_ref, sketch_ref, panel, sems) = refs[:2], refs[2:5], refs[5:]
    more = load(zip(small_hbm, (expand_ref, sketch_ref)), sems)
    products, bridge = add_stage(away, me_ref, block_refs[-2:], held, old, scratch)
    local = [local_ref[:, i * LANES : (i + 1) * LANES] for i in range(LOCAL_SUMS)]
    tokens, width = held[0].shape
    half = LANES // 2

    starts = [block.shape[0] - (half + 2) * count for block in block_refs]
    for i in range(0, half, 2):
        wide = [block[pl.ds(at + i * count, 2 * count), :].astype(F32) for block, at in zip(block_refs, starts)]
        for k in range(2):
            rows = jnp.concatenate([w[k * count : (k + 1) * count] for w in wide], axis=0)
            panel[:, pl.ds((i + k) * LANES, LANES)] = rows.astype(BF16)
    labels = jnp.concatenate(
        [
            block[pl.ds(at + half * count, 2 * count), :].astype(F32)[:count]
            for block, at in zip(block_refs, starts)
        ],
        axis=0,
    )

    for copy in more:
        copy.wait()
    inverse = local[INVERSE]
    reduced = inverse * products[X_DOWN]
    expand = expand_ref[...]
    left_two = mm_rows(reduced.astype(BF16), jnp.concatenate([expand, expand], axis=0))
    returned = products[VALUES].astype(BF16)
    right_one = ALPHA * mm(returned, sketch_ref[...])
    along = (ALPHA / width) * jnp.sum(returned.astype(F32) * reduced, axis=1, keepdims=True)
    back = mm(returned, bridge.astype(BF16))
    along = along * inverse
    right_three = products[J_LOW] + inverse * (ALPHA * back[:, :LANES] - along * products[X_LOW])
    right_four = products[J_TARGET] + inverse * (ALPHA * back[:, LANES:] - along * local[X_TARGET])
    rights = (right_one, ALPHA * products[V_TARGET], ALPHA * right_three, ALPHA * right_four)
    lefts = (local[LEFT_ONE], left_two, products[M_SOURCE], products[M_DOWN])
    place = lax.broadcasted_iota(jnp.int32, (tokens, LANES), 0)
    one, two = counts_ref[0, 0], counts_ref[0, 1]
    lower = half_lanes((tokens, LANES))
    member = (place >= jnp.where(lower, 0, one)) & (place < jnp.where(lower, one, one + two))
    spread = jnp.concatenate([jnp.where(member, left, 0.0).astype(BF16) for left in lefts], axis=0)
    feats = mm_cols(spread, jnp.concatenate([right.astype(BF16) for right in rights], axis=0))
    lower = lax.broadcasted_iota(jnp.int32, (8, LANES), 0) < 4
    unit = []
    for e in range(2):
        own = feats[e * half : (e + 1) * half]
        squares = jnp.sum(own * own, keepdims=True)
        unit.append(own * lax.rsqrt(squares + 1e-06))
    tiles = [
        jnp.where(lower, unit[0][i : i + 1], unit[1][i : i + 1]).astype(BF16) for i in range(half)
    ]
    scale = float(half * LANES) ** 0.5
    similar = scale * mm_rows(panel[...], jnp.concatenate(tiles, axis=1))
    labels = labels[:, : similar.shape[1]]
    values = []
    for t in range(TASKS):
        best = jnp.max(jnp.where(labels == float(t), similar, -2.0 * scale), axis=0, keepdims=True)
        values.append([jnp.max(best[:, 4 * e : 4 * e + 4]) for e in range(2)])
    for e in range(2):
        for t in range(TASKS):
            out_ref[e, t] = values[t][e]
        mean_ref[e] = (values[0][e] + values[1][e] + values[2][e]) * (1.0 / TASKS)


VMEM = pl.BlockSpec(memory_space=pltpu.VMEM)
SMEM = pl.BlockSpec(memory_space=pltpu.SMEM)
ANY = pl.BlockSpec(memory_space=pl.ANY)
HBM = pl.BlockSpec(memory_space=pltpu.HBM)


def in_hbm(arrays):
    return [pltpu.with_memory_space_constraint(a, pltpu.HBM) for a in arrays]


def params(mib):
    return pltpu.CompilerParams(vmem_limit_bytes=mib * MIB)


def cost(flops, nbytes):
    return pl.CostEstimate(flops=flops, bytes_accessed=nbytes, transcendentals=0)


def shards(
    hidden_state_input,
    attention_mixed_state,
    hidden_state_adjoint,
    attention_values_adjoint,
    sequence_token_counts,
    heldout_sketched_signals,
    benchmark_labels,
    top_rmsnorm_weights,
    top_reducer_matrix,
    top_expander_matrix,
    bottom_reducer_matrix,
    bottom_expander_matrix,
    source_sketch,
    top_reducer_sketch,
    top_expander_sketch,
    top_target_sketch,
    bottom_reducer_sketch,
    bottom_expander_sketch,
    bottom_target_sketch,
):
    me = lax.axis_index("dp").astype(jnp.int32)
    x, mixed, adjoint, values = (
        hidden_state_input,
        attention_mixed_state,
        hidden_state_adjoint,
        attention_values_adjoint,
    )
    tokens, width = x.shape
    rows = top_reducer_matrix.shape[0]
    count = heldout_sketched_signals.shape[0]

    inputs = (
        top_rmsnorm_weights.reshape(width // LANES, LANES),
        top_reducer_matrix,
        bottom_expander_matrix.T,
        bottom_reducer_sketch,
        top_expander_matrix.T,
        bottom_reducer_matrix,
        bottom_expander_sketch.T,
        heldout_sketched_signals,
        benchmark_labels.T,
    )
    own = pl.pallas_call(
        pack_kernel,
        out_shape=jax.ShapeDtypeStruct((3 * rows + (LANES // 2 + 2) * count, LANES), BF16),
        in_specs=[SMEM] + [HBM] * len(inputs),
        out_specs=VMEM,
        scratch_shapes=[pltpu.VMEM(a.shape, a.dtype) for a in inputs]
        + [pltpu.SemaphoreType.DMA((len(inputs),))],
        compiler_params=params(8),
        name="pack",
    )(me.reshape(1), *in_hbm(inputs))

    inputs = (
        x,
        mixed,
        adjoint,
        values,
        bottom_target_sketch,
        top_target_sketch,
        top_rmsnorm_weights.reshape(1, width),
        source_sketch.T,
    )
    *activations, local = pl.pallas_call(
        local_kernel,
        out_shape=[jax.ShapeDtypeStruct(a.shape, a.dtype) for a in inputs[:6]]
        + [
            jax.ShapeDtypeStruct((width, LANES), BF16),
            jax.ShapeDtypeStruct((tokens, LOCAL_SUMS * LANES), F32),
        ],
        in_specs=[HBM] * len(inputs),
        out_specs=[VMEM] * 8,
        scratch_shapes=[pltpu.VMEM(a.shape, a.dtype) for a in inputs[6:]]
        + [pltpu.SemaphoreType.DMA((STEPS + 1, 4))],
        compiler_params=params(24),
        cost_estimate=cost(tokens * width * LANES * 6, 14 * MIB),
        name="local_products",
    )(*in_hbm(inputs))

    stage_scratch = [
        pltpu.VMEM((2 * rows, 2 * LANES), BF16),
        pltpu.VMEM((rows + LANES // 2, 2 * LANES), BF16),
        pltpu.VMEM((2 * rows, LANES), BF16),
    ]

    def stage(away, pieces, sums):
        first = not sums
        start = 1 + len(pieces) + len(activations)
        return pl.pallas_call(
            functools.partial(stage_kernel, away, first),
            out_shape=[
                jax.ShapeDtypeStruct((tokens, SUMS * LANES), F32),
                jax.ShapeDtypeStruct((LANES, 2 * LANES), F32),
            ],
            in_specs=[SMEM] + [VMEM] * (len(pieces) + len(activations) + len(sums)),
            out_specs=[VMEM, VMEM],
            scratch_shapes=stage_scratch,
            input_output_aliases={} if first else {start: 0, start + 1: 1},
            compiler_params=params(16),
            cost_estimate=cost(tokens * rows * LANES * 16, 2 * MIB),
            name="stage",
        )(me.reshape(1), *pieces, *activations, *sums)

    tie = lax.optimization_barrier
    half = RING_CHIPS // 2
    held = [own, other_core(own)]
    blocks = list(held)
    first, second = hop(held[0]), hop(held[1])
    first, activations = tie((first, activations))
    sums = stage(0, held, [])
    second, sums = tie((second, sums))
    for k in range(1, half):
        held = [first, second]
        crossed = [other_core(first), other_core(second)]
        blocks += held + crossed
        first = hop(first)
        sums = stage(k, held, sums)
        first, sums = tie((first, sums))
        if k < half - 1:
            second = hop(second)
        sums = stage(-k, crossed, sums)
        if k < half - 1:
            second, sums = tie((second, sums))
    held = [first, other_core(first)]
    blocks += held
    small = (top_expander_sketch.T, top_reducer_sketch)
    task_best, scores = pl.pallas_call(
        functools.partial(finish_kernel, half, len(blocks), count),
        out_shape=(jax.ShapeDtypeStruct((2, TASKS), F32), jax.ShapeDtypeStruct((2,), F32)),
        in_specs=[SMEM] * 2 + [VMEM] * (len(blocks) + len(activations) + 3) + [HBM] * 2,
        out_specs=(SMEM, SMEM),
        scratch_shapes=stage_scratch
        + [pltpu.VMEM(a.shape, a.dtype) for a in small]
        + [
            pltpu.VMEM((len(blocks) * count, LANES // 2 * LANES), BF16),
            pltpu.SemaphoreType.DMA((2,)),
        ],
        compiler_params=params(24),
        cost_estimate=cost(tokens * rows * LANES * 40, 8 * MIB),
        name="finish",
    )(me.reshape(1), sequence_token_counts, *blocks, *activations, *sums, local, *in_hbm(small))
    return (scores, task_best)


def shards_of_any_slice(
    hidden_state_input,
    attention_mixed_state,
    hidden_state_adjoint,
    attention_values_adjoint,
    sequence_token_counts,
    heldout_sketched_signals,
    benchmark_labels,
    top_rmsnorm_weights,
    top_reducer_matrix,
    top_expander_matrix,
    bottom_reducer_matrix,
    bottom_expander_matrix,
    source_sketch,
    top_reducer_sketch,
    top_expander_sketch,
    top_target_sketch,
    bottom_reducer_sketch,
    bottom_expander_sketch,
    bottom_target_sketch,
    n,
):
    me = lax.axis_index("dp")
    x, mixed, adjoint, values = (
        hidden_state_input,
        attention_mixed_state,
        hidden_state_adjoint,
        attention_values_adjoint,
    )
    tokens, width = x.shape
    rows = top_reducer_matrix.shape[0]
    up_rows = top_expander_matrix.shape[1]
    rank = top_reducer_matrix.shape[1]
    k1 = source_sketch.shape[1]
    gain = top_rmsnorm_weights
    own_gain = lax.dynamic_slice_in_dim(gain, me * rows, rows)

    down_upper = (own_gain[:, None] * top_reducer_matrix.astype(F32)).astype(BF16)
    up_lower = mm(bottom_expander_matrix.T, bottom_reducer_sketch).astype(BF16)
    down_lower = mm(bottom_reducer_matrix, bottom_expander_sketch).astype(BF16)
    packed_lower = jnp.concatenate([down_lower[: rows // 2], down_lower[rows // 2 :]], axis=1)
    factors = jnp.concatenate([down_upper, up_lower, top_expander_matrix.T, packed_lower], axis=0)
    factors = lax.all_gather(factors, "dp")

    val_wide = heldout_sketched_signals.astype(F32)
    val_unit = (
        val_wide * lax.rsqrt(jnp.sum(val_wide * val_wide, axis=1, keepdims=True) + 1e-06)
    ).astype(BF16)
    labels = jnp.broadcast_to(benchmark_labels.astype(BF16), (val_unit.shape[0], 128))
    panel = jnp.concatenate([val_unit.reshape(-1, 128), labels], axis=0)
    panel = lax.all_gather(panel, "dp")
    val_rows = val_unit.shape[0]
    cut = panel.shape[1] - val_rows
    panel_tasks = panel[:, cut:, 0].reshape(n * val_rows, 1).astype(jnp.int32)
    panel = panel[:, :cut].reshape(n * val_rows, val_unit.shape[1])

    wide = x.astype(F32)
    inverse = lax.rsqrt(jnp.mean(wide * wide, axis=1, keepdims=True) + 1e-05)
    gained_sketch = (gain[:, None] * source_sketch.astype(F32)).astype(BF16)
    left_one = inverse * mm(x, gained_sketch)
    left_three = mm(mixed, source_sketch)
    right_two = ALPHA * mm(values, top_target_sketch)

    at = 0
    down_upper = factors[:, at : at + rows].reshape(width, rank)
    at += rows
    up_lower = factors[:, at : at + rows].reshape(width, -1)
    at += rows
    up_upper = factors[:, at : at + up_rows].reshape(-1, rank)
    at += up_rows
    down_lower = factors[:, at:]
    down_lower = jnp.concatenate([down_lower[:, :, :k1], down_lower[:, :, k1:]], axis=1)
    down_lower = down_lower.reshape(width, k1)

    reduced = inverse * mm(x, down_upper)
    left_two = mm(reduced.astype(BF16), top_expander_sketch)
    left_four = mm(mixed, down_lower)
    returned = mm(values, up_upper).astype(BF16)
    right_one = ALPHA * mm(returned, top_reducer_sketch)
    along = (ALPHA / width) * jnp.sum(returned.astype(F32) * reduced, axis=1, keepdims=True)
    targets = jnp.concatenate([up_lower, bottom_target_sketch], axis=1)
    bridge = mm_cols(down_upper, targets).astype(BF16)
    rights_low = mm(adjoint, targets) + inverse * (
        ALPHA * mm(returned, bridge) - (along * inverse) * mm(x, targets)
    )
    rights_low = ALPHA * rights_low
    k2 = up_lower.shape[1]
    lefts = (left_one, left_two, left_three, left_four)
    rights = (right_one, right_two, rights_low[:, :k2], rights_low[:, k2:])

    counts = sequence_token_counts[0]
    ends = jnp.cumsum(counts)
    starts = ends - counts
    places = jnp.arange(tokens, dtype=jnp.int32)[:, None]
    member = (places >= starts[None, :]) & (places < ends[None, :])
    count_ex = counts.shape[0]
    spread = jnp.concatenate(lefts, axis=0).astype(BF16)
    member = jnp.tile(member, (4, 1))
    spread = jnp.concatenate(
        [jnp.where(member[:, e : e + 1], spread, 0) for e in range(count_ex)], axis=1
    )
    feats = mm_cols(spread, jnp.concatenate(rights, axis=0).astype(BF16))
    feats = feats.reshape(count_ex, -1)
    squares = jnp.sum(feats * feats, axis=1, keepdims=True)
    unit_rows = (feats * lax.rsqrt(squares + 1e-06)).astype(BF16)

    score_scale = float(unit_rows.shape[1]) ** 0.5
    similar = score_scale * mm_rows(unit_rows, panel)
    task_mask = panel_tasks == jnp.arange(TASKS, dtype=jnp.int32)[None, :]
    task_best = jnp.max(
        jnp.where(task_mask[None, :, :], similar[:, :, None], -2.0 * score_scale), axis=1
    )
    return (jnp.mean(task_best, axis=1), task_best)


def solution(mesh):
    n = mesh.shape["dp"]
    split = P(("parts", "dp"), None)
    by_row, by_column, whole = P("dp", None), P(None, "dp"), P()
    placed = (
        (split,) * 5
        + (by_row, by_row, whole)
        + (by_row, by_column, by_row, by_column)
        + (whole,) * 7
    )
    ours = shards if n == 2 * RING_CHIPS else functools.partial(shards_of_any_slice, n=n)
    return jax.shard_map(
        ours,
        mesh=mesh,
        in_specs=placed,
        out_specs=(P(("parts", "dp")), split),
        check_vma=False,
    )
```

```python
import functools

import jax
import jax.numpy as jnp
from jax import lax
from jax.experimental import pallas as pl
from jax.experimental.pallas import tpu as pltpu
from jax.sharding import PartitionSpec as P

TASKS = 3
ALPHA = 4.0
F32 = jnp.float32
BF16 = jnp.bfloat16
RING_CHIPS = 8
LANES = 128
STEPS = 4
X_DOWN, X_LOW, J_LOW, J_TARGET, M_DOWN, M_SOURCE, VALUES, V_TARGET, SUMS = range(9)
INVERSE, LEFT_ONE, X_TARGET, LOCAL_SUMS = range(4)
MIB = 1 << 20


def mm(a, b):
    return jnp.dot(a, b, preferred_element_type=F32)


def mm_rows(a, b):
    return lax.dot_general(a, b, (((1,), (1,)), ((), ())), preferred_element_type=F32)


def mm_cols(a, b):
    return lax.dot_general(a, b, (((0,), (0,)), ((), ())), preferred_element_type=F32)


def ring_chip(pos):
    half = RING_CHIPS // 2
    return jnp.where(pos < half, 2 * pos, 2 * (RING_CHIPS - 1 - pos) + 1)


def ring_pos(chip):
    row, side = chip // 2, chip % 2
    return jnp.where(side == 0, row, RING_CHIPS - 1 - row)


def hop(value):
    half = RING_CHIPS // 2
    place = [2 * q if q < half else 2 * (RING_CHIPS - 1 - q) + 1 for q in range(RING_CHIPS)]
    pairs = []
    for q in range(RING_CHIPS):
        pairs.append((2 * place[q], 2 * place[(q + 1) % RING_CHIPS]))
        pairs.append((2 * place[q] + 1, 2 * place[(q - 1) % RING_CHIPS] + 1))
    return lax.ppermute(value, "dp", pairs)


def other_core(value):
    return lax.ppermute(value, "dp", [(d, d ^ 1) for d in range(2 * RING_CHIPS)])


def half_lanes(shape):
    return lax.broadcasted_iota(jnp.int32, shape, 1) < LANES // 2


def diagonal_column(row, first, count):
    shape = (count, row.shape[1])
    lane = lax.broadcasted_iota(jnp.int32, shape, 1)
    at = lax.broadcasted_iota(jnp.int32, shape, 0)
    return jnp.sum(jnp.where(lane == at + first, row, 0.0), axis=1, keepdims=True)


def load(pairs, sems):
    copies = [pltpu.make_async_copy(src, dst, sems.at[i]) for i, (src, dst) in enumerate(pairs)]
    for copy in copies:
        copy.start()
    return copies


def pack_kernel(me_ref, *refs):
    hbm, out_ref, held, sems = refs[:9], refs[9], refs[10:19], refs[19]
    gain_ref, down_up_ref, up_low_ref, sketch_ref, up_up_ref, down_low_ref, expand_ref, val_ref, label_ref = held
    copies = load(zip(hbm, held), sems)
    rows = down_up_ref.shape[0]
    half = LANES // 2
    for copy in copies:
        copy.wait()
    for b in range(rows // half):
        place = me_ref[0] * (rows // half) + b
        row = gain_ref[pl.ds(place // 2, 1), :]
        column = diagonal_column(row, (place % 2) * half, half)
        part = down_up_ref[pl.ds(b * half, half), :].astype(F32)
        out_ref[pl.ds(b * half, half), :] = (column * part).astype(BF16)
    at = rows
    out_ref[pl.ds(at, rows), :] = mm(up_low_ref[...], sketch_ref[...]).astype(BF16)
    at += rows
    out_ref[pl.ds(at, rows // 2), :] = up_up_ref[...]
    at += rows // 2
    expand = expand_ref[...]
    low = mm_rows(down_low_ref[...], jnp.concatenate([expand, expand], axis=0))
    first, second = low[: rows // 2], low[rows // 2 :]
    out_ref[pl.ds(at, rows // 2), :] = jnp.where(half_lanes(first.shape), first, second).astype(BF16)
    at += rows // 2
    wide = val_ref[...].astype(F32)
    count, width = wide.shape
    scale = lax.rsqrt(jnp.sum(wide * wide, axis=1, keepdims=True) + 1e-06)
    unit = wide * scale
    blocks = [unit[:, i * LANES : (i + 1) * LANES] for i in range(width // LANES)]
    row = label_ref[...].astype(F32)
    labels = jnp.broadcast_to(diagonal_column(row, 0, count), (count, LANES))
    blocks += [labels, labels]
    for i in range(0, len(blocks), 2):
        pair = jnp.concatenate(blocks[i : i + 2], axis=0)
        out_ref[pl.ds(at + i * count, 2 * count), :] = pair.astype(BF16)


def local_kernel(*refs):
    x_hbm, mixed_hbm, adjoint_hbm, values_hbm, target_hbm, top_target_hbm, gain_hbm, source_hbm = refs[:8]
    x_ref, mixed_ref, adjoint_ref, values_ref, target_ref, top_target_ref, turned_ref, sums_ref = refs[8:16]
    gain_ref, source_ref, sems = refs[16:]
    tokens, width = x_ref.shape
    span = width // STEPS
    copies = []
    for j in range(STEPS):
        part = pl.ds(j * span, span)
        pairs = (
            (gain_hbm.at[:, part], gain_ref.at[:, part]),
            (source_hbm.at[:, part], source_ref.at[:, part]),
            (x_hbm.at[:, part], x_ref.at[:, part]),
            (target_hbm.at[part], target_ref.at[part]),
        )
        copies.append(load(pairs, sems.at[j]))
    pairs = (
        (adjoint_hbm, adjoint_ref),
        (mixed_hbm, mixed_ref),
        (values_hbm, values_ref),
        (top_target_hbm, top_target_ref),
    )
    later = load(pairs, sems.at[STEPS])
    products = jnp.zeros((tokens, 2 * LANES), F32)
    squares = jnp.zeros((tokens, LANES), F32)
    for j in range(STEPS):
        for copy in copies[j]:
            copy.wait()
        part = slice(j * span, (j + 1) * span)
        x, source = x_ref[:, part], source_ref[:, part].astype(F32)
        gained = source * gain_ref[:, part]
        turned_ref[part, :] = jnp.concatenate([source, source], axis=0).T.astype(BF16)
        gained = jnp.concatenate([gained, gained], axis=0).T.astype(BF16)
        products = products + mm(x, jnp.concatenate([gained, target_ref[part, :]], axis=1))
        for i in range(span // LANES):
            wide = x[:, i * LANES : (i + 1) * LANES].astype(F32)
            squares = squares + wide * wide
    mean = jnp.sum(squares, axis=1, keepdims=True) * (1.0 / width)
    inverse = jnp.broadcast_to(lax.rsqrt(mean + 1e-05), (tokens, LANES))
    for i, value in enumerate((inverse, inverse * products[:, :LANES], products[:, LANES:])):
        sums_ref[:, i * LANES : (i + 1) * LANES] = value
    for copy in later:
        copy.wait()


def add_stage(away, me_ref, pieces, held, old, scratch):
    x_ref, mixed_ref, adjoint_ref, values_ref, target_ref, top_target_ref, source_ref = held
    both, up, down = scratch
    rows = both.shape[0] // 2
    half, pad = rows // 2, LANES // 2
    span = 2 * rows
    me = me_ref[0]
    pos, core = ring_pos(me // 2), me % 2
    chip = ring_chip((pos + away * (2 * core - 1) + RING_CHIPS) % RING_CHIPS)
    odd = chip % 2
    mine = pl.ds(pl.multiple_of(chip * span, LANES), span)
    values_start = (chip // 2) * span + odd * (rows - pad)
    values_part = pl.ds(pl.multiple_of(values_start, LANES), rows + pad)
    side = core if away >= 0 else 1 - core
    up[pl.ds(pl.multiple_of((1 - odd) * rows, 16), pad), :] = jnp.zeros((pad, 2 * LANES), BF16)
    up[pl.ds(pl.multiple_of(odd * pad, 16), rows), pl.ds(LANES, LANES)] = top_target_ref[
        pl.ds(pl.multiple_of(chip * rows, 16), rows), :
    ]
    for piece, c in ((pieces[0], side), (pieces[1], 1 - side)):
        one = pl.ds(pl.multiple_of(c * rows, 16), rows)
        both[one, pl.ds(0, LANES)] = piece[pl.ds(0, rows), :]
        both[one, pl.ds(LANES, LANES)] = piece[pl.ds(rows, rows), :]
        up[pl.ds(pl.multiple_of(odd * pad + c * half, 16), half), pl.ds(0, LANES)] = piece[
            pl.ds(2 * rows, half), :
        ]
        packed = piece[pl.ds(2 * rows + half, half), :].astype(F32)
        turned = pltpu.roll(packed, pad, 1)
        lower = half_lanes(packed.shape)
        down[pl.ds(pl.multiple_of(c * rows, 16), half), :] = jnp.where(lower, packed, turned).astype(BF16)
        down[pl.ds(pl.multiple_of(c * rows + half, 16), half), :] = jnp.where(lower, turned, packed).astype(BF16)

    weights = both[...]
    down_up = weights[:, :LANES]
    lows = jnp.concatenate([weights[:, LANES:], target_ref[mine, :]], axis=1)
    products = []
    for activation, factor in (
        (x_ref[:, mine], weights),
        (adjoint_ref[:, mine], lows),
        (mixed_ref[:, mine], jnp.concatenate([down[...], source_ref[mine, :]], axis=1)),
        (values_ref[:, values_part], up[...]),
    ):
        product = mm(activation, factor)
        products += [product[:, :LANES], product[:, LANES:]]
    bridge = mm_cols(down_up, lows)
    if old:
        old_sums, old_bridge = old
        products = [p + old_sums[:, i * LANES : (i + 1) * LANES] for i, p in enumerate(products)]
        bridge = bridge + old_bridge[...]
    return products, bridge


def stage_kernel(away, first, me_ref, *refs):
    pieces, held, old = refs[:2], refs[2:9], refs[9:-5]
    (new_sums, new_bridge), scratch = refs[-5:-3], refs[-3:]
    products, bridge = add_stage(away, me_ref, pieces, held, old, scratch)
    for i in range(SUMS):
        new_sums[:, i * LANES : (i + 1) * LANES] = products[i]
    new_bridge[...] = bridge


def feature_kernel(away, me_ref, counts_ref, *refs):
    pieces, held, old, local_ref, small_hbm, refs = refs[:2], refs[2:9], refs[9:11], refs[11], refs[12:14], refs[14:]
    out_ref, scratch, (expand_ref, sketch_ref, sems) = refs[0], refs[1:4], refs[4:]
    more = load(zip(small_hbm, (expand_ref, sketch_ref)), sems)
    products, bridge = add_stage(away, me_ref, pieces, held, old, scratch)
    local = [local_ref[:, i * LANES : (i + 1) * LANES] for i in range(LOCAL_SUMS)]
    tokens, width = held[0].shape
    half = LANES // 2
    for copy in more:
        copy.wait()
    inverse = local[INVERSE]
    reduced = inverse * products[X_DOWN]
    expand = expand_ref[...]
    left_two = mm_rows(reduced.astype(BF16), jnp.concatenate([expand, expand], axis=0))
    returned = products[VALUES].astype(BF16)
    right_one = ALPHA * mm(returned, sketch_ref[...])
    along = (ALPHA / width) * jnp.sum(returned.astype(F32) * reduced, axis=1, keepdims=True)
    back = mm(returned, bridge.astype(BF16))
    along = along * inverse
    right_three = products[J_LOW] + inverse * (ALPHA * back[:, :LANES] - along * products[X_LOW])
    right_four = products[J_TARGET] + inverse * (ALPHA * back[:, LANES:] - along * local[X_TARGET])
    rights = (right_one, ALPHA * products[V_TARGET], ALPHA * right_three, ALPHA * right_four)
    lefts = (local[LEFT_ONE], left_two, products[M_SOURCE], products[M_DOWN])
    place = lax.broadcasted_iota(jnp.int32, (tokens, LANES), 0)
    one, two = counts_ref[0, 0], counts_ref[0, 1]
    lower = half_lanes((tokens, LANES))
    member = (place >= jnp.where(lower, 0, one)) & (place < jnp.where(lower, one, one + two))
    spread = jnp.concatenate([jnp.where(member, left, 0.0).astype(BF16) for left in lefts], axis=0)
    feats = mm_cols(spread, jnp.concatenate([right.astype(BF16) for right in rights], axis=0))
    for e in range(2):
        own = feats[e * half : (e + 1) * half]
        squares = jnp.sum(own * own, keepdims=True)
        out_ref[pl.ds(e * half, half), :] = (own * lax.rsqrt(squares + 1e-06)).astype(BF16).astype(F32)


def split_kernel(block_ref, *refs):
    head_ref, tail_ref = refs[-2:]
    cut, tail = head_ref.shape[0], block_ref.shape[0] - head_ref.shape[0]
    head_ref[...] = block_ref[pl.ds(0, cut), :]
    if len(refs) == 3:
        tail_ref[pl.ds(0, tail), :] = refs[0][...]
    tail_ref[pl.ds(tail_ref.shape[0] - tail, tail), :] = block_ref[pl.ds(cut, tail), :]


def best_of(places, count, unit_ref, best):
    half = LANES // 2
    scale = float(half * LANES) ** 0.5
    shape = (count, LANES)
    totals = [[jnp.zeros(shape, F32) for _ in range(2)] for _ in places]
    for i in range(0, half, 2):
        units = [
            [jnp.broadcast_to(unit_ref[pl.ds(e * half + i + k, 1), :], shape) for k in range(2)]
            for e in range(2)
        ]
        for b, (block, start) in enumerate(places):
            wide = block[pl.ds(start + i * count, 2 * count), :].astype(F32)
            for e in range(2):
                totals[b][e] = totals[b][e] + (wide[:count] * units[e][0] + wide[count:] * units[e][1])
    for b, (block, start) in enumerate(places):
        labels = block[pl.ds(start + half * count, 2 * count), :].astype(F32)[:count]
        for e in range(2):
            similar = scale * jnp.sum(totals[b][e], axis=1, keepdims=True)
            for t in range(TASKS):
                best[e][t] = jnp.maximum(best[e][t], jnp.where(labels == float(t), similar, -2.0 * scale))


def places_of(blocks, count):
    size = (LANES // 2 + 2) * count
    places = []
    for block in blocks:
        total = block.shape[0]
        firsts = range(0, total, size) if total % size == 0 else [total - size]
        places += [(block, first) for first in firsts]
    return places


def score_kernel(blocks, count, unit_ref, *refs):
    block_refs, best_ref = refs[:blocks], refs[blocks]
    lowest = -2.0 * float(LANES // 2 * LANES) ** 0.5
    best = [[jnp.full((count, LANES), lowest, F32) for _ in range(TASKS)] for _ in range(2)]
    best_of(places_of(block_refs, count), count, unit_ref, best)
    for e in range(2):
        for t in range(TASKS):
            best_ref[e, t] = best[e][t]


def last_score_kernel(count, unit_ref, block_ref, best_ref, out_ref, mean_ref):
    best = [[best_ref[e, t] for t in range(TASKS)] for e in range(2)]
    best_of(places_of([block_ref], count), count, unit_ref, best)
    for e in range(2):
        values = [jnp.max(best[e][t]) for t in range(TASKS)]
        for t in range(TASKS):
            out_ref[e, t] = values[t]
        mean_ref[e] = (values[0] + values[1] + values[2]) * (1.0 / TASKS)


VMEM = pl.BlockSpec(memory_space=pltpu.VMEM)
SMEM = pl.BlockSpec(memory_space=pltpu.SMEM)
ANY = pl.BlockSpec(memory_space=pl.ANY)
HBM = pl.BlockSpec(memory_space=pltpu.HBM)


def in_hbm(arrays):
    return [pltpu.with_memory_space_constraint(a, pltpu.HBM) for a in arrays]


def params(mib):
    return pltpu.CompilerParams(vmem_limit_bytes=mib * MIB)


def cost(flops, nbytes):
    return pl.CostEstimate(flops=flops, bytes_accessed=nbytes, transcendentals=0)


def shards(
    hidden_state_input,
    attention_mixed_state,
    hidden_state_adjoint,
    attention_values_adjoint,
    sequence_token_counts,
    heldout_sketched_signals,
    benchmark_labels,
    top_rmsnorm_weights,
    top_reducer_matrix,
    top_expander_matrix,
    bottom_reducer_matrix,
    bottom_expander_matrix,
    source_sketch,
    top_reducer_sketch,
    top_expander_sketch,
    top_target_sketch,
    bottom_reducer_sketch,
    bottom_expander_sketch,
    bottom_target_sketch,
):
    me = lax.axis_index("dp").astype(jnp.int32)
    x, mixed, adjoint, values = (
        hidden_state_input,
        attention_mixed_state,
        hidden_state_adjoint,
        attention_values_adjoint,
    )
    tokens, width = x.shape
    rows = top_reducer_matrix.shape[0]
    count = heldout_sketched_signals.shape[0]

    inputs = (
        top_rmsnorm_weights.reshape(width // LANES, LANES),
        top_reducer_matrix,
        bottom_expander_matrix.T,
        bottom_reducer_sketch,
        top_expander_matrix.T,
        bottom_reducer_matrix,
        bottom_expander_sketch.T,
        heldout_sketched_signals,
        benchmark_labels.T,
    )
    own = pl.pallas_call(
        pack_kernel,
        out_shape=jax.ShapeDtypeStruct((3 * rows + (LANES // 2 + 2) * count, LANES), BF16),
        in_specs=[SMEM] + [HBM] * len(inputs),
        out_specs=VMEM,
        scratch_shapes=[pltpu.VMEM(a.shape, a.dtype) for a in inputs]
        + [pltpu.SemaphoreType.DMA((len(inputs),))],
        compiler_params=params(8),
        name="pack",
    )(me.reshape(1), *in_hbm(inputs))

    inputs = (
        x,
        mixed,
        adjoint,
        values,
        bottom_target_sketch,
        top_target_sketch,
        top_rmsnorm_weights.reshape(1, width),
        source_sketch.T,
    )
    *activations, local = pl.pallas_call(
        local_kernel,
        out_shape=[jax.ShapeDtypeStruct(a.shape, a.dtype) for a in inputs[:6]]
        + [
            jax.ShapeDtypeStruct((width, LANES), BF16),
            jax.ShapeDtypeStruct((tokens, LOCAL_SUMS * LANES), F32),
        ],
        in_specs=[HBM] * len(inputs),
        out_specs=[VMEM] * 8,
        scratch_shapes=[pltpu.VMEM(a.shape, a.dtype) for a in inputs[6:]]
        + [pltpu.SemaphoreType.DMA((STEPS + 1, 4))],
        compiler_params=params(24),
        cost_estimate=cost(tokens * width * LANES * 6, 14 * MIB),
        name="local_products",
    )(*in_hbm(inputs))

    stage_scratch = [
        pltpu.VMEM((2 * rows, 2 * LANES), BF16),
        pltpu.VMEM((rows + LANES // 2, 2 * LANES), BF16),
        pltpu.VMEM((2 * rows, LANES), BF16),
    ]

    def stage(away, pieces, sums):
        first = not sums
        start = 1 + len(pieces) + len(activations)
        return pl.pallas_call(
            functools.partial(stage_kernel, away, first),
            out_shape=[
                jax.ShapeDtypeStruct((tokens, SUMS * LANES), F32),
                jax.ShapeDtypeStruct((LANES, 2 * LANES), F32),
            ],
            in_specs=[SMEM] + [VMEM] * (len(pieces) + len(activations) + len(sums)),
            out_specs=[VMEM, VMEM],
            scratch_shapes=stage_scratch,
            input_output_aliases={} if first else {start: 0, start + 1: 1},
            compiler_params=params(16),
            cost_estimate=cost(tokens * rows * LANES * 16, 2 * MIB),
            name="stage",
        )(me.reshape(1), *pieces, *activations, *sums)

    def split(block, *tails):
        tail = block.shape[0] - 3 * rows
        shapes = (3 * rows, LANES), ((1 + len(tails)) * tail, LANES)
        return pl.pallas_call(
            split_kernel,
            out_shape=[jax.ShapeDtypeStruct(shape, BF16) for shape in shapes],
            in_specs=[VMEM] * (1 + len(tails)),
            out_specs=[VMEM, VMEM],
            compiler_params=params(8),
            name="split",
        )(block, *tails)

    tie = lax.optimization_barrier
    half = RING_CHIPS // 2
    held = [own, other_core(own)]
    blocks = list(held)
    first, second = hop(held[0]), hop(held[1])
    first, activations = tie((first, activations))
    sums = stage(0, held, [])
    second, sums = tie((second, sums))
    for k in range(1, half):
        held = [first, second]
        crossed = [other_core(first), other_core(second)]
        blocks += [first, crossed[0]]
        if k < half - 1:
            blocks += [second, crossed[1]]
        else:
            first, tails = split(first, tail)
        first = hop(first)
        sums = stage(k, held, sums)
        first, sums = tie((first, sums))
        if k == half - 2:
            second, tail = split(second)
        if k < half - 1:
            second = hop(second)
        sums = stage(-k, crossed, sums)
        if k < half - 1:
            second, sums = tie((second, sums))
    tails = hop(tails)
    small = (top_expander_sketch.T, top_reducer_sketch)
    unit = pl.pallas_call(
        functools.partial(feature_kernel, half),
        out_shape=jax.ShapeDtypeStruct((LANES, LANES), F32),
        in_specs=[SMEM] * 2 + [VMEM] * (2 + len(activations) + 3) + [HBM] * 2,
        out_specs=VMEM,
        scratch_shapes=stage_scratch
        + [pltpu.VMEM(a.shape, a.dtype) for a in small]
        + [pltpu.SemaphoreType.DMA((2,))],
        compiler_params=params(16),
        cost_estimate=cost(1, 1),
        name="features",
    )(
        me.reshape(1),
        sequence_token_counts,
        first,
        other_core(first),
        *activations,
        *sums,
        local,
        *in_hbm(small),
    )
    tails, unit = tie((tails, unit))
    blocks.append(tails)
    best = pl.pallas_call(
        functools.partial(score_kernel, len(blocks), count),
        out_shape=jax.ShapeDtypeStruct((2, TASKS, count, LANES), F32),
        in_specs=[VMEM] * (1 + len(blocks)),
        out_specs=VMEM,
        compiler_params=params(16),
        cost_estimate=cost(4 * MIB, 2 * MIB),
        name="scores",
    )(unit, *blocks)
    task_best, scores = pl.pallas_call(
        functools.partial(last_score_kernel, count),
        out_shape=(jax.ShapeDtypeStruct((2, TASKS), F32), jax.ShapeDtypeStruct((2,), F32)),
        in_specs=[VMEM] * 3,
        out_specs=(SMEM, SMEM),
        compiler_params=params(8),
        name="last_scores",
    )(unit, other_core(tails), best)
    return (scores, task_best)


def shards_of_any_slice(
    hidden_state_input,
    attention_mixed_state,
    hidden_state_adjoint,
    attention_values_adjoint,
    sequence_token_counts,
    heldout_sketched_signals,
    benchmark_labels,
    top_rmsnorm_weights,
    top_reducer_matrix,
    top_expander_matrix,
    bottom_reducer_matrix,
    bottom_expander_matrix,
    source_sketch,
    top_reducer_sketch,
    top_expander_sketch,
    top_target_sketch,
    bottom_reducer_sketch,
    bottom_expander_sketch,
    bottom_target_sketch,
    n,
):
    me = lax.axis_index("dp")
    x, mixed, adjoint, values = (
        hidden_state_input,
        attention_mixed_state,
        hidden_state_adjoint,
        attention_values_adjoint,
    )
    tokens, width = x.shape
    rows = top_reducer_matrix.shape[0]
    up_rows = top_expander_matrix.shape[1]
    rank = top_reducer_matrix.shape[1]
    k1 = source_sketch.shape[1]
    gain = top_rmsnorm_weights
    own_gain = lax.dynamic_slice_in_dim(gain, me * rows, rows)

    down_upper = (own_gain[:, None] * top_reducer_matrix.astype(F32)).astype(BF16)
    up_lower = mm(bottom_expander_matrix.T, bottom_reducer_sketch).astype(BF16)
    down_lower = mm(bottom_reducer_matrix, bottom_expander_sketch).astype(BF16)
    packed_lower = jnp.concatenate([down_lower[: rows // 2], down_lower[rows // 2 :]], axis=1)
    factors = jnp.concatenate([down_upper, up_lower, top_expander_matrix.T, packed_lower], axis=0)
    factors = lax.all_gather(factors, "dp")

    val_wide = heldout_sketched_signals.astype(F32)
    val_unit = (
        val_wide * lax.rsqrt(jnp.sum(val_wide * val_wide, axis=1, keepdims=True) + 1e-06)
    ).astype(BF16)
    labels = jnp.broadcast_to(benchmark_labels.astype(BF16), (val_unit.shape[0], 128))
    panel = jnp.concatenate([val_unit.reshape(-1, 128), labels], axis=0)
    panel = lax.all_gather(panel, "dp")
    val_rows = val_unit.shape[0]
    cut = panel.shape[1] - val_rows
    panel_tasks = panel[:, cut:, 0].reshape(n * val_rows, 1).astype(jnp.int32)
    panel = panel[:, :cut].reshape(n * val_rows, val_unit.shape[1])

    wide = x.astype(F32)
    inverse = lax.rsqrt(jnp.mean(wide * wide, axis=1, keepdims=True) + 1e-05)
    gained_sketch = (gain[:, None] * source_sketch.astype(F32)).astype(BF16)
    left_one = inverse * mm(x, gained_sketch)
    left_three = mm(mixed, source_sketch)
    right_two = ALPHA * mm(values, top_target_sketch)

    at = 0
    down_upper = factors[:, at : at + rows].reshape(width, rank)
    at += rows
    up_lower = factors[:, at : at + rows].reshape(width, -1)
    at += rows
    up_upper = factors[:, at : at + up_rows].reshape(-1, rank)
    at += up_rows
    down_lower = factors[:, at:]
    down_lower = jnp.concatenate([down_lower[:, :, :k1], down_lower[:, :, k1:]], axis=1)
    down_lower = down_lower.reshape(width, k1)

    reduced = inverse * mm(x, down_upper)
    left_two = mm(reduced.astype(BF16), top_expander_sketch)
    left_four = mm(mixed, down_lower)
    returned = mm(values, up_upper).astype(BF16)
    right_one = ALPHA * mm(returned, top_reducer_sketch)
    along = (ALPHA / width) * jnp.sum(returned.astype(F32) * reduced, axis=1, keepdims=True)
    targets = jnp.concatenate([up_lower, bottom_target_sketch], axis=1)
    bridge = mm_cols(down_upper, targets).astype(BF16)
    rights_low = mm(adjoint, targets) + inverse * (
        ALPHA * mm(returned, bridge) - (along * inverse) * mm(x, targets)
    )
    rights_low = ALPHA * rights_low
    k2 = up_lower.shape[1]
    lefts = (left_one, left_two, left_three, left_four)
    rights = (right_one, right_two, rights_low[:, :k2], rights_low[:, k2:])

    counts = sequence_token_counts[0]
    ends = jnp.cumsum(counts)
    starts = ends - counts
    places = jnp.arange(tokens, dtype=jnp.int32)[:, None]
    member = (places >= starts[None, :]) & (places < ends[None, :])
    count_ex = counts.shape[0]
    spread = jnp.concatenate(lefts, axis=0).astype(BF16)
    member = jnp.tile(member, (4, 1))
    spread = jnp.concatenate(
        [jnp.where(member[:, e : e + 1], spread, 0) for e in range(count_ex)], axis=1
    )
    feats = mm_cols(spread, jnp.concatenate(rights, axis=0).astype(BF16))
    feats = feats.reshape(count_ex, -1)
    squares = jnp.sum(feats * feats, axis=1, keepdims=True)
    unit_rows = (feats * lax.rsqrt(squares + 1e-06)).astype(BF16)

    score_scale = float(unit_rows.shape[1]) ** 0.5
    similar = score_scale * mm_rows(unit_rows, panel)
    task_mask = panel_tasks == jnp.arange(TASKS, dtype=jnp.int32)[None, :]
    task_best = jnp.max(
        jnp.where(task_mask[None, :, :], similar[:, :, None], -2.0 * score_scale), axis=1
    )
    return (jnp.mean(task_best, axis=1), task_best)


def solution(mesh):
    n = mesh.shape["dp"]
    split = P(("parts", "dp"), None)
    by_row, by_column, whole = P("dp", None), P(None, "dp"), P()
    placed = (
        (split,) * 5
        + (by_row, by_row, whole)
        + (by_row, by_column, by_row, by_column)
        + (whole,) * 7
    )
    ours = shards if n == 2 * RING_CHIPS else functools.partial(shards_of_any_slice, n=n)
    return jax.shard_map(
        ours,
        mesh=mesh,
        in_specs=placed,
        out_specs=(P(("parts", "dp")), split),
        check_vma=False,
    )
```

```python
import functools

import jax
import jax.numpy as jnp
from jax import lax
from jax.experimental import pallas as pl
from jax.experimental.pallas import tpu as pltpu
from jax.sharding import PartitionSpec as P

TASKS = 3
ALPHA = 4.0
F32 = jnp.float32
BF16 = jnp.bfloat16
RING_CHIPS = 8
LANES = 128
STEPS = 4
X_DOWN, X_LOW, J_LOW, J_TARGET, M_DOWN, M_SOURCE, VALUES, V_TARGET, SUMS = range(9)
INVERSE, LEFT_ONE, X_TARGET, LOCAL_SUMS = range(4)
MIB = 1 << 20


def mm(a, b):
    return jnp.dot(a, b, preferred_element_type=F32)


def mm_rows(a, b):
    return lax.dot_general(a, b, (((1,), (1,)), ((), ())), preferred_element_type=F32)


def mm_cols(a, b):
    return lax.dot_general(a, b, (((0,), (0,)), ((), ())), preferred_element_type=F32)


def ring_chip(pos):
    half = RING_CHIPS // 2
    return jnp.where(pos < half, 2 * pos, 2 * (RING_CHIPS - 1 - pos) + 1)


def ring_pos(chip):
    row, side = chip // 2, chip % 2
    return jnp.where(side == 0, row, RING_CHIPS - 1 - row)


def hop(value, from_other=False):
    half = RING_CHIPS // 2
    place = [2 * q if q < half else 2 * (RING_CHIPS - 1 - q) + 1 for q in range(RING_CHIPS)]
    turn = int(from_other)
    pairs = []
    for q in range(RING_CHIPS):
        pairs.append((2 * place[q] + turn, 2 * place[(q + 1) % RING_CHIPS]))
        pairs.append((2 * place[q] + 1 - turn, 2 * place[(q - 1) % RING_CHIPS] + 1))
    return lax.ppermute(value, "dp", pairs)


def other_core(value):
    return lax.ppermute(value, "dp", [(d, d ^ 1) for d in range(2 * RING_CHIPS)])


def half_lanes(shape):
    return lax.broadcasted_iota(jnp.int32, shape, 1) < LANES // 2


def diagonal_column(row, first, count):
    shape = (count, row.shape[1])
    lane = lax.broadcasted_iota(jnp.int32, shape, 1)
    at = lax.broadcasted_iota(jnp.int32, shape, 0)
    return jnp.sum(jnp.where(lane == at + first, row, 0.0), axis=1, keepdims=True)


def load(pairs, sems):
    copies = [pltpu.make_async_copy(src, dst, sems.at[i]) for i, (src, dst) in enumerate(pairs)]
    for copy in copies:
        copy.start()
    return copies


def pack_kernel(me_ref, *refs):
    hbm, out_ref, held, sems = refs[:9], refs[9], refs[10:19], refs[19]
    gain_ref, down_up_ref, up_low_ref, sketch_ref, up_up_ref, down_low_ref, expand_ref, val_ref, label_ref = held
    copies = load(zip(hbm, held), sems)
    rows = down_up_ref.shape[0]
    half = LANES // 2
    for copy in copies:
        copy.wait()
    for b in range(rows // half):
        place = me_ref[0] * (rows // half) + b
        row = gain_ref[pl.ds(place // 2, 1), :]
        column = diagonal_column(row, (place % 2) * half, half)
        part = down_up_ref[pl.ds(b * half, half), :].astype(F32)
        out_ref[pl.ds(b * half, half), :] = (column * part).astype(BF16)
    at = rows
    out_ref[pl.ds(at, rows), :] = mm(up_low_ref[...], sketch_ref[...]).astype(BF16)
    at += rows
    out_ref[pl.ds(at, rows // 2), :] = up_up_ref[...]
    at += rows // 2
    expand = expand_ref[...]
    low = mm_rows(down_low_ref[...], jnp.concatenate([expand, expand], axis=0))
    first, second = low[: rows // 2], low[rows // 2 :]
    out_ref[pl.ds(at, rows // 2), :] = jnp.where(half_lanes(first.shape), first, second).astype(BF16)
    at += rows // 2
    wide = val_ref[...].astype(F32)
    count, width = wide.shape
    scale = lax.rsqrt(jnp.sum(wide * wide, axis=1, keepdims=True) + 1e-06)
    unit = wide * scale
    blocks = [unit[:, i * LANES : (i + 1) * LANES] for i in range(width // LANES)]
    row = label_ref[...].astype(F32)
    labels = jnp.broadcast_to(diagonal_column(row, 0, count), (count, LANES))
    blocks += [labels, labels]
    for i in range(0, len(blocks), 2):
        pair = jnp.concatenate(blocks[i : i + 2], axis=0)
        out_ref[pl.ds(at + i * count, 2 * count), :] = pair.astype(BF16)


def local_kernel(*refs):
    x_hbm, target_hbm, gain_hbm, source_hbm, x_ref, target_ref, turned_ref, sums_ref = refs[:8]
    gain_ref, source_ref, sems = refs[8:]
    tokens, width = x_ref.shape
    span = width // STEPS
    copies = []
    for j in range(STEPS):
        part = pl.ds(j * span, span)
        pairs = (
            (gain_hbm.at[:, part], gain_ref.at[:, part]),
            (source_hbm.at[:, part], source_ref.at[:, part]),
            (x_hbm.at[:, part], x_ref.at[:, part]),
            (target_hbm.at[part], target_ref.at[part]),
        )
        copies.append(load(pairs, sems.at[j]))
    products = jnp.zeros((tokens, 2 * LANES), F32)
    squares = jnp.zeros((tokens, LANES), F32)
    for j in range(STEPS):
        for copy in copies[j]:
            copy.wait()
        part = slice(j * span, (j + 1) * span)
        x, source = x_ref[:, part], source_ref[:, part].astype(F32)
        gained = source * gain_ref[:, part]
        turned_ref[part, :] = jnp.concatenate([source, source], axis=0).T.astype(BF16)
        gained = jnp.concatenate([gained, gained], axis=0).T.astype(BF16)
        products = products + mm(x, jnp.concatenate([gained, target_ref[part, :]], axis=1))
        for i in range(span // LANES):
            wide = x[:, i * LANES : (i + 1) * LANES].astype(F32)
            squares = squares + wide * wide
    mean = jnp.sum(squares, axis=1, keepdims=True) * (1.0 / width)
    inverse = jnp.broadcast_to(lax.rsqrt(mean + 1e-05), (tokens, LANES))
    for i, value in enumerate((inverse, inverse * products[:, :LANES], products[:, LANES:])):
        sums_ref[:, i * LANES : (i + 1) * LANES] = value


def fetch_kernel(after_ref, *refs):
    count = (len(refs) - 1) // 2
    for copy in load(zip(refs[:count], refs[count:-1]), refs[-1]):
        copy.wait()


def add_stage(away, me_ref, pieces, held, old, scratch):
    x_ref, mixed_ref, adjoint_ref, values_ref, target_ref, top_target_ref, source_ref = held
    both, up, down = scratch
    rows = both.shape[0] // 2
    half, pad = rows // 2, LANES // 2
    span = 2 * rows
    me = me_ref[0]
    pos, core = ring_pos(me // 2), me % 2
    chip = ring_chip((pos + away * (2 * core - 1) + RING_CHIPS) % RING_CHIPS)
    odd = chip % 2
    mine = pl.ds(pl.multiple_of(chip * span, LANES), span)
    values_start = (chip // 2) * span + odd * (rows - pad)
    values_part = pl.ds(pl.multiple_of(values_start, LANES), rows + pad)
    side = core if away >= 0 else 1 - core
    up[pl.ds(pl.multiple_of((1 - odd) * rows, 16), pad), :] = jnp.zeros((pad, 2 * LANES), BF16)
    up[pl.ds(pl.multiple_of(odd * pad, 16), rows), pl.ds(LANES, LANES)] = top_target_ref[
        pl.ds(pl.multiple_of(chip * rows, 16), rows), :
    ]
    for piece, c in ((pieces[0], side), (pieces[1], 1 - side)):
        one = pl.ds(pl.multiple_of(c * rows, 16), rows)
        both[one, pl.ds(0, LANES)] = piece[pl.ds(0, rows), :]
        both[one, pl.ds(LANES, LANES)] = piece[pl.ds(rows, rows), :]
        up[pl.ds(pl.multiple_of(odd * pad + c * half, 16), half), pl.ds(0, LANES)] = piece[
            pl.ds(2 * rows, half), :
        ]
        packed = piece[pl.ds(2 * rows + half, half), :].astype(F32)
        turned = pltpu.roll(packed, pad, 1)
        lower = half_lanes(packed.shape)
        down[pl.ds(pl.multiple_of(c * rows, 16), half), :] = jnp.where(lower, packed, turned).astype(BF16)
        down[pl.ds(pl.multiple_of(c * rows + half, 16), half), :] = jnp.where(lower, turned, packed).astype(BF16)

    weights = both[...]
    down_up = weights[:, :LANES]
    lows = jnp.concatenate([weights[:, LANES:], target_ref[mine, :]], axis=1)
    products = []
    for activation, factor in (
        (x_ref[:, mine], weights),
        (adjoint_ref[:, mine], lows),
        (mixed_ref[:, mine], jnp.concatenate([down[...], source_ref[mine, :]], axis=1)),
        (values_ref[:, values_part], up[...]),
    ):
        product = mm(activation, factor)
        products += [product[:, :LANES], product[:, LANES:]]
    bridge = mm_cols(down_up, lows)
    if old:
        old_sums, old_bridge = old
        products = [p + old_sums[:, i * LANES : (i + 1) * LANES] for i, p in enumerate(products)]
        bridge = bridge + old_bridge[...]
    return products, bridge


def stage_kernel(away, first, me_ref, *refs):
    pieces, held, old = refs[:2], refs[2:9], refs[9:-5]
    (new_sums, new_bridge), scratch = refs[-5:-3], refs[-3:]
    products, bridge = add_stage(away, me_ref, pieces, held, old, scratch)
    for i in range(SUMS):
        new_sums[:, i * LANES : (i + 1) * LANES] = products[i]
    new_bridge[...] = bridge


def feature_kernel(away, me_ref, counts_ref, *refs):
    pieces, held, old, local_ref, small_hbm, refs = refs[:2], refs[2:9], refs[9:11], refs[11], refs[12:14], refs[14:]
    out_ref, scratch, (expand_ref, sketch_ref, sems) = refs[0], refs[1:4], refs[4:]
    more = load(zip(small_hbm, (expand_ref, sketch_ref)), sems)
    products, bridge = add_stage(away, me_ref, pieces, held, old, scratch)
    local = [local_ref[:, i * LANES : (i + 1) * LANES] for i in range(LOCAL_SUMS)]
    tokens, width = held[0].shape
    half = LANES // 2
    for copy in more:
        copy.wait()
    inverse = local[INVERSE]
    reduced = inverse * products[X_DOWN]
    expand = expand_ref[...]
    left_two = mm_rows(reduced.astype(BF16), jnp.concatenate([expand, expand], axis=0))
    returned = products[VALUES].astype(BF16)
    right_one = ALPHA * mm(returned, sketch_ref[...])
    along = (ALPHA / width) * jnp.sum(returned.astype(F32) * reduced, axis=1, keepdims=True)
    back = mm(returned, bridge.astype(BF16))
    along = along * inverse
    right_three = products[J_LOW] + inverse * (ALPHA * back[:, :LANES] - along * products[X_LOW])
    right_four = products[J_TARGET] + inverse * (ALPHA * back[:, LANES:] - along * local[X_TARGET])
    rights = (right_one, ALPHA * products[V_TARGET], ALPHA * right_three, ALPHA * right_four)
    lefts = (local[LEFT_ONE], left_two, products[M_SOURCE], products[M_DOWN])
    place = lax.broadcasted_iota(jnp.int32, (tokens, LANES), 0)
    one, two = counts_ref[0, 0], counts_ref[0, 1]
    lower = half_lanes((tokens, LANES))
    member = (place >= jnp.where(lower, 0, one)) & (place < jnp.where(lower, one, one + two))
    spread = jnp.concatenate([jnp.where(member, left, 0.0).astype(BF16) for left in lefts], axis=0)
    feats = mm_cols(spread, jnp.concatenate([right.astype(BF16) for right in rights], axis=0))
    for e in range(2):
        own = feats[e * half : (e + 1) * half]
        squares = jnp.sum(own * own, keepdims=True)
        out_ref[pl.ds(e * half, half), :] = (own * lax.rsqrt(squares + 1e-06)).astype(BF16).astype(F32)


def split_kernel(block_ref, *refs):
    head_ref, tail_ref = refs[-2:]
    cut, tail = head_ref.shape[0], block_ref.shape[0] - head_ref.shape[0]
    head_ref[...] = block_ref[pl.ds(0, cut), :]
    if len(refs) == 3:
        tail_ref[pl.ds(0, tail), :] = refs[0][...]
    tail_ref[pl.ds(tail_ref.shape[0] - tail, tail), :] = block_ref[pl.ds(cut, tail), :]


def best_of(places, count, unit_ref, best):
    half = LANES // 2
    scale = float(half * LANES) ** 0.5
    shape = (count, LANES)
    totals = [[jnp.zeros(shape, F32) for _ in range(2)] for _ in places]
    for i in range(0, half, 2):
        units = [
            [jnp.broadcast_to(unit_ref[pl.ds(e * half + i + k, 1), :], shape) for k in range(2)]
            for e in range(2)
        ]
        for b, (block, start) in enumerate(places):
            wide = block[pl.ds(start + i * count, 2 * count), :].astype(F32)
            for e in range(2):
                totals[b][e] = totals[b][e] + (wide[:count] * units[e][0] + wide[count:] * units[e][1])
    for b, (block, start) in enumerate(places):
        labels = block[pl.ds(start + half * count, 2 * count), :].astype(F32)[:count]
        for e in range(2):
            similar = scale * jnp.sum(totals[b][e], axis=1, keepdims=True)
            for t in range(TASKS):
                best[e][t] = jnp.maximum(best[e][t], jnp.where(labels == float(t), similar, -2.0 * scale))


def places_of(blocks, count):
    size = (LANES // 2 + 2) * count
    places = []
    for block in blocks:
        total = block.shape[0]
        firsts = range(0, total, size) if total % size == 0 else [total - size]
        places += [(block, first) for first in firsts]
    return places


def score_kernel(blocks, count, unit_ref, *refs):
    block_refs, best_ref = refs[:blocks], refs[blocks]
    lowest = -2.0 * float(LANES // 2 * LANES) ** 0.5
    best = [[jnp.full((count, LANES), lowest, F32) for _ in range(TASKS)] for _ in range(2)]
    best_of(places_of(block_refs, count), count, unit_ref, best)
    for e in range(2):
        for t in range(TASKS):
            best_ref[e, t] = best[e][t]


def last_score_kernel(count, unit_ref, block_ref, best_ref, out_ref, mean_ref):
    best = [[best_ref[e, t] for t in range(TASKS)] for e in range(2)]
    best_of(places_of([block_ref], count), count, unit_ref, best)
    lane = lax.broadcasted_iota(jnp.int32, (1, LANES), 1)
    means = []
    for e in range(2):
        values = [jnp.max(best[e][t], axis=0, keepdims=True) for t in range(TASKS)]
        row = jnp.where(lane == 0, values[0], jnp.where(lane == 1, values[1], values[2]))
        out_ref[pl.ds(e, 1), :] = row[:, :TASKS]
        means.append((values[0] + values[1] + values[2]) * (1.0 / TASKS))
    mean_ref[...] = jnp.where(lane == 0, means[0], means[1])[:, :2]


VMEM = pl.BlockSpec(memory_space=pltpu.VMEM)
SMEM = pl.BlockSpec(memory_space=pltpu.SMEM)
ANY = pl.BlockSpec(memory_space=pl.ANY)
HBM = pl.BlockSpec(memory_space=pltpu.HBM)


def in_hbm(arrays):
    return [pltpu.with_memory_space_constraint(a, pltpu.HBM) for a in arrays]


def params(mib):
    return pltpu.CompilerParams(vmem_limit_bytes=mib * MIB)


def cost(flops, nbytes):
    return pl.CostEstimate(flops=flops, bytes_accessed=nbytes, transcendentals=0)


def shards(
    hidden_state_input,
    attention_mixed_state,
    hidden_state_adjoint,
    attention_values_adjoint,
    sequence_token_counts,
    heldout_sketched_signals,
    benchmark_labels,
    top_rmsnorm_weights,
    top_reducer_matrix,
    top_expander_matrix,
    bottom_reducer_matrix,
    bottom_expander_matrix,
    source_sketch,
    top_reducer_sketch,
    top_expander_sketch,
    top_target_sketch,
    bottom_reducer_sketch,
    bottom_expander_sketch,
    bottom_target_sketch,
):
    me = lax.axis_index("dp").astype(jnp.int32)
    x, mixed, adjoint, values = (
        hidden_state_input,
        attention_mixed_state,
        hidden_state_adjoint,
        attention_values_adjoint,
    )
    tokens, width = x.shape
    rows = top_reducer_matrix.shape[0]
    count = heldout_sketched_signals.shape[0]

    inputs = (
        top_rmsnorm_weights.reshape(width // LANES, LANES),
        top_reducer_matrix,
        bottom_expander_matrix.T,
        bottom_reducer_sketch,
        top_expander_matrix.T,
        bottom_reducer_matrix,
        bottom_expander_sketch.T,
        heldout_sketched_signals,
        benchmark_labels.T,
    )
    own = pl.pallas_call(
        pack_kernel,
        out_shape=jax.ShapeDtypeStruct((3 * rows + (LANES // 2 + 2) * count, LANES), BF16),
        in_specs=[SMEM] + [HBM] * len(inputs),
        out_specs=VMEM,
        scratch_shapes=[pltpu.VMEM(a.shape, a.dtype) for a in inputs]
        + [pltpu.SemaphoreType.DMA((len(inputs),))],
        compiler_params=params(8),
        name="pack",
    )(me.reshape(1), *in_hbm(inputs))

    tie = lax.optimization_barrier
    inputs = (x, bottom_target_sketch, top_rmsnorm_weights.reshape(1, width), source_sketch.T)
    upper, low_target, source, local = pl.pallas_call(
        local_kernel,
        out_shape=[jax.ShapeDtypeStruct(a.shape, a.dtype) for a in inputs[:2]]
        + [
            jax.ShapeDtypeStruct((width, LANES), BF16),
            jax.ShapeDtypeStruct((tokens, LOCAL_SUMS * LANES), F32),
        ],
        in_specs=[HBM] * len(inputs),
        out_specs=[VMEM] * 4,
        scratch_shapes=[pltpu.VMEM(a.shape, a.dtype) for a in inputs[2:]]
        + [pltpu.SemaphoreType.DMA((STEPS, len(inputs)))],
        compiler_params=params(16),
        cost_estimate=cost(tokens * width * LANES * 4, 6 * MIB),
        name="local_products",
    )(*in_hbm(inputs))
    own_late, local = tie((own, local))
    inputs = (mixed, adjoint, values, top_target_sketch)
    fetched = pl.pallas_call(
        fetch_kernel,
        out_shape=[jax.ShapeDtypeStruct(a.shape, a.dtype) for a in inputs],
        in_specs=[VMEM] + [HBM] * len(inputs),
        out_specs=[VMEM] * len(inputs),
        scratch_shapes=[pltpu.SemaphoreType.DMA((len(inputs),))],
        compiler_params=params(16),
        cost_estimate=cost(1, 8 * MIB),
        name="fetch",
    )(local, *in_hbm(inputs))
    activations = [upper, *fetched[:3], low_target, fetched[3], source]

    stage_scratch = [
        pltpu.VMEM((2 * rows, 2 * LANES), BF16),
        pltpu.VMEM((rows + LANES // 2, 2 * LANES), BF16),
        pltpu.VMEM((2 * rows, LANES), BF16),
    ]

    def stage(away, pieces, sums):
        first = not sums
        start = 1 + len(pieces) + len(activations)
        return pl.pallas_call(
            functools.partial(stage_kernel, away, first),
            out_shape=[
                jax.ShapeDtypeStruct((tokens, SUMS * LANES), F32),
                jax.ShapeDtypeStruct((LANES, 2 * LANES), F32),
            ],
            in_specs=[SMEM] + [VMEM] * (len(pieces) + len(activations) + len(sums)),
            out_specs=[VMEM, VMEM],
            scratch_shapes=stage_scratch,
            input_output_aliases={} if first else {start: 0, start + 1: 1},
            compiler_params=params(16),
            cost_estimate=cost(tokens * rows * LANES * 16, 2 * MIB),
            name="stage",
        )(me.reshape(1), *pieces, *activations, *sums)

    def split(block, *tails):
        tail = block.shape[0] - 3 * rows
        shapes = (3 * rows, LANES), ((1 + len(tails)) * tail, LANES)
        return pl.pallas_call(
            split_kernel,
            out_shape=[jax.ShapeDtypeStruct(shape, BF16) for shape in shapes],
            in_specs=[VMEM] * (1 + len(tails)),
            out_specs=[VMEM, VMEM],
            compiler_params=params(8),
            name="split",
        )(block, *tails)

    half = RING_CHIPS // 2
    held = [own, other_core(own_late)]
    blocks = list(held)
    first, second = hop(own), hop(own_late, from_other=True)
    first, activations = tie((first, activations))
    sums = stage(0, held, [])
    second, sums = tie((second, sums))
    for k in range(1, half):
        held = [first, second]
        crossed = [other_core(first), other_core(second)]
        blocks += [first, crossed[0]]
        if k < half - 1:
            blocks += [second, crossed[1]]
        else:
            first, tails = split(first, tail)
        first = hop(first)
        sums = stage(k, held, sums)
        first, sums = tie((first, sums))
        if k == half - 2:
            second, tail = split(second)
        if k < half - 1:
            second = hop(second)
        sums = stage(-k, crossed, sums)
        if k < half - 1:
            second, sums = tie((second, sums))
    tails = hop(tails)
    small = (top_expander_sketch.T, top_reducer_sketch)
    unit = pl.pallas_call(
        functools.partial(feature_kernel, half),
        out_shape=jax.ShapeDtypeStruct((LANES, LANES), F32),
        in_specs=[SMEM] * 2 + [VMEM] * (2 + len(activations) + 3) + [HBM] * 2,
        out_specs=VMEM,
        scratch_shapes=stage_scratch
        + [pltpu.VMEM(a.shape, a.dtype) for a in small]
        + [pltpu.SemaphoreType.DMA((2,))],
        compiler_params=params(16),
        cost_estimate=cost(1, 1),
        name="features",
    )(
        me.reshape(1),
        sequence_token_counts,
        first,
        other_core(first),
        *activations,
        *sums,
        local,
        *in_hbm(small),
    )
    tails, unit = tie((tails, unit))
    blocks.append(tails)
    best = pl.pallas_call(
        functools.partial(score_kernel, len(blocks), count),
        out_shape=jax.ShapeDtypeStruct((2, TASKS, count, LANES), F32),
        in_specs=[VMEM] * (1 + len(blocks)),
        out_specs=VMEM,
        compiler_params=params(16),
        cost_estimate=cost(4 * MIB, 2 * MIB),
        name="scores",
    )(unit, *blocks)
    task_best, scores = pl.pallas_call(
        functools.partial(last_score_kernel, count),
        out_shape=(jax.ShapeDtypeStruct((2, TASKS), F32), jax.ShapeDtypeStruct((1, 2), F32)),
        in_specs=[VMEM] * 3,
        out_specs=(VMEM, VMEM),
        compiler_params=params(8),
        name="last_scores",
    )(unit, other_core(tails), best)
    return (scores.reshape(2), task_best)


def shards_of_any_slice(
    hidden_state_input,
    attention_mixed_state,
    hidden_state_adjoint,
    attention_values_adjoint,
    sequence_token_counts,
    heldout_sketched_signals,
    benchmark_labels,
    top_rmsnorm_weights,
    top_reducer_matrix,
    top_expander_matrix,
    bottom_reducer_matrix,
    bottom_expander_matrix,
    source_sketch,
    top_reducer_sketch,
    top_expander_sketch,
    top_target_sketch,
    bottom_reducer_sketch,
    bottom_expander_sketch,
    bottom_target_sketch,
    n,
):
    me = lax.axis_index("dp")
    x, mixed, adjoint, values = (
        hidden_state_input,
        attention_mixed_state,
        hidden_state_adjoint,
        attention_values_adjoint,
    )
    tokens, width = x.shape
    rows = top_reducer_matrix.shape[0]
    up_rows = top_expander_matrix.shape[1]
    rank = top_reducer_matrix.shape[1]
    k1 = source_sketch.shape[1]
    gain = top_rmsnorm_weights
    own_gain = lax.dynamic_slice_in_dim(gain, me * rows, rows)

    down_upper = (own_gain[:, None] * top_reducer_matrix.astype(F32)).astype(BF16)
    up_lower = mm(bottom_expander_matrix.T, bottom_reducer_sketch).astype(BF16)
    down_lower = mm(bottom_reducer_matrix, bottom_expander_sketch).astype(BF16)
    packed_lower = jnp.concatenate([down_lower[: rows // 2], down_lower[rows // 2 :]], axis=1)
    factors = jnp.concatenate([down_upper, up_lower, top_expander_matrix.T, packed_lower], axis=0)
    factors = lax.all_gather(factors, "dp")

    val_wide = heldout_sketched_signals.astype(F32)
    val_unit = (
        val_wide * lax.rsqrt(jnp.sum(val_wide * val_wide, axis=1, keepdims=True) + 1e-06)
    ).astype(BF16)
    labels = jnp.broadcast_to(benchmark_labels.astype(BF16), (val_unit.shape[0], 128))
    panel = jnp.concatenate([val_unit.reshape(-1, 128), labels], axis=0)
    panel = lax.all_gather(panel, "dp")
    val_rows = val_unit.shape[0]
    cut = panel.shape[1] - val_rows
    panel_tasks = panel[:, cut:, 0].reshape(n * val_rows, 1).astype(jnp.int32)
    panel = panel[:, :cut].reshape(n * val_rows, val_unit.shape[1])

    wide = x.astype(F32)
    inverse = lax.rsqrt(jnp.mean(wide * wide, axis=1, keepdims=True) + 1e-05)
    gained_sketch = (gain[:, None] * source_sketch.astype(F32)).astype(BF16)
    left_one = inverse * mm(x, gained_sketch)
    left_three = mm(mixed, source_sketch)
    right_two = ALPHA * mm(values, top_target_sketch)

    at = 0
    down_upper = factors[:, at : at + rows].reshape(width, rank)
    at += rows
    up_lower = factors[:, at : at + rows].reshape(width, -1)
    at += rows
    up_upper = factors[:, at : at + up_rows].reshape(-1, rank)
    at += up_rows
    down_lower = factors[:, at:]
    down_lower = jnp.concatenate([down_lower[:, :, :k1], down_lower[:, :, k1:]], axis=1)
    down_lower = down_lower.reshape(width, k1)

    reduced = inverse * mm(x, down_upper)
    left_two = mm(reduced.astype(BF16), top_expander_sketch)
    left_four = mm(mixed, down_lower)
    returned = mm(values, up_upper).astype(BF16)
    right_one = ALPHA * mm(returned, top_reducer_sketch)
    along = (ALPHA / width) * jnp.sum(returned.astype(F32) * reduced, axis=1, keepdims=True)
    targets = jnp.concatenate([up_lower, bottom_target_sketch], axis=1)
    bridge = mm_cols(down_upper, targets).astype(BF16)
    rights_low = mm(adjoint, targets) + inverse * (
        ALPHA * mm(returned, bridge) - (along * inverse) * mm(x, targets)
    )
    rights_low = ALPHA * rights_low
    k2 = up_lower.shape[1]
    lefts = (left_one, left_two, left_three, left_four)
    rights = (right_one, right_two, rights_low[:, :k2], rights_low[:, k2:])

    counts = sequence_token_counts[0]
    ends = jnp.cumsum(counts)
    starts = ends - counts
    places = jnp.arange(tokens, dtype=jnp.int32)[:, None]
    member = (places >= starts[None, :]) & (places < ends[None, :])
    count_ex = counts.shape[0]
    spread = jnp.concatenate(lefts, axis=0).astype(BF16)
    member = jnp.tile(member, (4, 1))
    spread = jnp.concatenate(
        [jnp.where(member[:, e : e + 1], spread, 0) for e in range(count_ex)], axis=1
    )
    feats = mm_cols(spread, jnp.concatenate(rights, axis=0).astype(BF16))
    feats = feats.reshape(count_ex, -1)
    squares = jnp.sum(feats * feats, axis=1, keepdims=True)
    unit_rows = (feats * lax.rsqrt(squares + 1e-06)).astype(BF16)

    score_scale = float(unit_rows.shape[1]) ** 0.5
    similar = score_scale * mm_rows(unit_rows, panel)
    task_mask = panel_tasks == jnp.arange(TASKS, dtype=jnp.int32)[None, :]
    task_best = jnp.max(
        jnp.where(task_mask[None, :, :], similar[:, :, None], -2.0 * score_scale), axis=1
    )
    return (jnp.mean(task_best, axis=1), task_best)


def solution(mesh):
    n = mesh.shape["dp"]
    split = P(("parts", "dp"), None)
    by_row, by_column, whole = P("dp", None), P(None, "dp"), P()
    placed = (
        (split,) * 5
        + (by_row, by_row, whole)
        + (by_row, by_column, by_row, by_column)
        + (whole,) * 7
    )
    ours = shards if n == 2 * RING_CHIPS else functools.partial(shards_of_any_slice, n=n)
    return jax.shard_map(
        ours,
        mesh=mesh,
        in_specs=placed,
        out_specs=(P(("parts", "dp")), split),
        check_vma=False,
    )
```

```python
import functools

import jax
import jax.numpy as jnp
from jax import lax
from jax.experimental import pallas as pl
from jax.experimental.pallas import tpu as pltpu
from jax.sharding import PartitionSpec as P

TASKS = 3
ALPHA = 4.0
F32 = jnp.float32
BF16 = jnp.bfloat16
RING_CHIPS = 8
LANES = 128
STEPS = 4
X_DOWN, X_LOW, J_LOW, J_TARGET, M_DOWN, M_SOURCE, VALUES, V_TARGET, SUMS = range(9)
INVERSE, LEFT_ONE, X_TARGET, LOCAL_SUMS = range(4)
MIB = 1 << 20


def mm(a, b):
    return jnp.dot(a, b, preferred_element_type=F32)


def mm_rows(a, b):
    return lax.dot_general(a, b, (((1,), (1,)), ((), ())), preferred_element_type=F32)


def mm_cols(a, b):
    return lax.dot_general(a, b, (((0,), (0,)), ((), ())), preferred_element_type=F32)


def ring_chip(pos):
    half = RING_CHIPS // 2
    return jnp.where(pos < half, 2 * pos, 2 * (RING_CHIPS - 1 - pos) + 1)


def ring_pos(chip):
    row, side = chip // 2, chip % 2
    return jnp.where(side == 0, row, RING_CHIPS - 1 - row)


def hop(value, from_other=False):
    half = RING_CHIPS // 2
    place = [2 * q if q < half else 2 * (RING_CHIPS - 1 - q) + 1 for q in range(RING_CHIPS)]
    turn = int(from_other)
    pairs = []
    for q in range(RING_CHIPS):
        pairs.append((2 * place[q] + turn, 2 * place[(q + 1) % RING_CHIPS]))
        pairs.append((2 * place[q] + 1 - turn, 2 * place[(q - 1) % RING_CHIPS] + 1))
    return lax.ppermute(value, "dp", pairs)


def other_core(value):
    return lax.ppermute(value, "dp", [(d, d ^ 1) for d in range(2 * RING_CHIPS)])


def half_lanes(shape):
    return lax.broadcasted_iota(jnp.int32, shape, 1) < LANES // 2


def diagonal_column(row, first, count):
    shape = (count, row.shape[1])
    lane = lax.broadcasted_iota(jnp.int32, shape, 1)
    at = lax.broadcasted_iota(jnp.int32, shape, 0)
    return jnp.sum(jnp.where(lane == at + first, row, 0.0), axis=1, keepdims=True)


def load(pairs, sems):
    copies = [pltpu.make_async_copy(src, dst, sems.at[i]) for i, (src, dst) in enumerate(pairs)]
    for copy in copies:
        copy.start()
    return copies


def pack_kernel(me_ref, *refs):
    hbm, out_ref, held, sems = refs[:9], refs[9], refs[10:19], refs[19]
    gain_ref, down_up_ref, up_low_ref, sketch_ref, up_up_ref, down_low_ref, expand_ref, val_ref, label_ref = held
    copies = load(zip(hbm, held), sems)
    rows = down_up_ref.shape[0]
    half = LANES // 2
    for copy in copies:
        copy.wait()
    for b in range(rows // half):
        place = me_ref[0] * (rows // half) + b
        row = gain_ref[pl.ds(place // 2, 1), :]
        column = diagonal_column(row, (place % 2) * half, half)
        part = down_up_ref[pl.ds(b * half, half), :].astype(F32)
        out_ref[pl.ds(b * half, half), :] = (column * part).astype(BF16)
    at = rows
    out_ref[pl.ds(at, rows), :] = mm(up_low_ref[...], sketch_ref[...]).astype(BF16)
    at += rows
    out_ref[pl.ds(at, rows // 2), :] = up_up_ref[...]
    at += rows // 2
    expand = expand_ref[...]
    low = mm_rows(down_low_ref[...], jnp.concatenate([expand, expand], axis=0))
    first, second = low[: rows // 2], low[rows // 2 :]
    out_ref[pl.ds(at, rows // 2), :] = jnp.where(half_lanes(first.shape), first, second).astype(BF16)
    at += rows // 2
    wide = val_ref[...].astype(F32)
    count, width = wide.shape
    scale = lax.rsqrt(jnp.sum(wide * wide, axis=1, keepdims=True) + 1e-06)
    unit = wide * scale
    blocks = [unit[:, i * LANES : (i + 1) * LANES] for i in range(width // LANES)]
    row = label_ref[...].astype(F32)
    labels = jnp.broadcast_to(diagonal_column(row, 0, count), (count, LANES))
    blocks += [labels, labels]
    for i in range(0, len(blocks), 2):
        pair = jnp.concatenate(blocks[i : i + 2], axis=0)
        out_ref[pl.ds(at + i * count, 2 * count), :] = pair.astype(BF16)


def doubled(value, which):
    turned = pltpu.roll(value, LANES // 2, 1)
    lower = half_lanes(value.shape)
    return jnp.where(lower, turned, value) if which else jnp.where(lower, value, turned)


def local_kernel(*refs):
    x_hbm, target_hbm, gain_hbm, source_hbm, x_ref, target_ref, turned_ref, sums_ref = refs[:8]
    gain_ref, source_ref, sems = refs[8:]
    tokens, width = x_ref.shape
    span = width // STEPS
    copies = []
    for j in range(STEPS):
        part = pl.ds(j * span, span)
        pairs = (
            (gain_hbm.at[:, part], gain_ref.at[:, part]),
            (source_hbm.at[:, part], source_ref.at[:, part]),
            (x_hbm.at[:, part], x_ref.at[:, part]),
            (target_hbm.at[part], target_ref.at[part]),
        )
        copies.append(load(pairs, sems.at[j]))
    products = jnp.zeros((tokens, 2 * LANES), F32)
    squares = jnp.zeros((tokens, LANES), F32)
    for j in range(STEPS):
        for copy in copies[j]:
            copy.wait()
        part = slice(j * span, (j + 1) * span)
        x, source = x_ref[:, part], source_ref[:, part]
        gained = (source.astype(F32) * gain_ref[:, part]).astype(BF16)
        turned = jnp.concatenate([source, gained], axis=0).T
        turned_ref[part, :] = turned
        products = products + mm(x, jnp.concatenate([turned, target_ref[part, :]], axis=1))
        for i in range(span // LANES):
            wide = x[:, i * LANES : (i + 1) * LANES].astype(F32)
            squares = squares + wide * wide
    mean = jnp.sum(squares, axis=1, keepdims=True) * (1.0 / width)
    inverse = jnp.broadcast_to(lax.rsqrt(mean + 1e-05), (tokens, LANES))
    left_one = inverse * doubled(products[:, :LANES], 1)
    for i, value in enumerate((inverse, left_one, products[:, LANES:])):
        sums_ref[:, i * LANES : (i + 1) * LANES] = value


def fetch_kernel(after_ref, *refs):
    count = (len(refs) - 1) // 2
    pairs = []
    for src, dst in zip(refs[:count], refs[count:-1]):
        rows = src.shape[0] // STEPS
        pairs += [(src.at[pl.ds(j * rows, rows)], dst.at[pl.ds(j * rows, rows)]) for j in range(STEPS)]
    for copy in load(pairs, refs[-1]):
        copy.wait()


def add_stage(away, me_ref, pieces, held, old, scratch):
    x_ref, mixed_ref, adjoint_ref, values_ref, target_ref, top_target_ref, source_ref = held
    both, up, down = scratch
    rows = both.shape[0] // 2
    half, pad = rows // 2, LANES // 2
    span = 2 * rows
    me = me_ref[0]
    pos, core = ring_pos(me // 2), me % 2
    chip = ring_chip((pos + away * (2 * core - 1) + RING_CHIPS) % RING_CHIPS)
    odd = chip % 2
    mine = pl.ds(pl.multiple_of(chip * span, LANES), span)
    values_start = (chip // 2) * span + odd * (rows - pad)
    values_part = pl.ds(pl.multiple_of(values_start, LANES), rows + pad)
    side = core if away >= 0 else 1 - core
    up[pl.ds(pl.multiple_of((1 - odd) * rows, 16), pad), :] = jnp.zeros((pad, 2 * LANES), BF16)
    up[pl.ds(pl.multiple_of(odd * pad, 16), rows), pl.ds(LANES, LANES)] = top_target_ref[
        pl.ds(pl.multiple_of(chip * rows, 16), rows), :
    ]
    for piece, c in ((pieces[0], side), (pieces[1], 1 - side)):
        one = pl.ds(pl.multiple_of(c * rows, 16), rows)
        both[one, pl.ds(0, LANES)] = piece[pl.ds(0, rows), :]
        both[one, pl.ds(LANES, LANES)] = piece[pl.ds(rows, rows), :]
        up[pl.ds(pl.multiple_of(odd * pad + c * half, 16), half), pl.ds(0, LANES)] = piece[
            pl.ds(2 * rows, half), :
        ]
        packed = piece[pl.ds(2 * rows + half, half), :].astype(F32)
        turned = pltpu.roll(packed, pad, 1)
        lower = half_lanes(packed.shape)
        down[pl.ds(pl.multiple_of(c * rows, 16), half), :] = jnp.where(lower, packed, turned).astype(BF16)
        down[pl.ds(pl.multiple_of(c * rows + half, 16), half), :] = jnp.where(lower, turned, packed).astype(BF16)

    weights = both[...]
    down_up = weights[:, :LANES]
    lows = jnp.concatenate([weights[:, LANES:], target_ref[mine, :]], axis=1)
    products = []
    for activation, factor in (
        (x_ref[:, mine], weights),
        (adjoint_ref[:, mine], lows),
        (mixed_ref[:, mine], jnp.concatenate([down[...], source_ref[mine, :]], axis=1)),
        (values_ref[:, values_part], up[...]),
    ):
        product = mm(activation, factor)
        products += [product[:, :LANES], product[:, LANES:]]
    bridge = mm_cols(down_up, lows)
    if old:
        old_sums, old_bridge = old
        products = [p + old_sums[:, i * LANES : (i + 1) * LANES] for i, p in enumerate(products)]
        bridge = bridge + old_bridge[...]
    return products, bridge


def stage_kernel(away, first, me_ref, *refs):
    pieces, held, old = refs[:2], refs[2:9], refs[9:-5]
    (new_sums, new_bridge), scratch = refs[-5:-3], refs[-3:]
    products, bridge = add_stage(away, me_ref, pieces, held, old, scratch)
    for i in range(SUMS):
        new_sums[:, i * LANES : (i + 1) * LANES] = products[i]
    new_bridge[...] = bridge


def feature_kernel(away, me_ref, counts_ref, *refs):
    pieces, held, old, local_ref, small_hbm, refs = refs[:2], refs[2:9], refs[9:11], refs[11], refs[12:14], refs[14:]
    out_ref, scratch, (expand_ref, sketch_ref, sems) = refs[0], refs[1:4], refs[4:]
    more = load(zip(small_hbm, (expand_ref, sketch_ref)), sems)
    products, bridge = add_stage(away, me_ref, pieces, held, old, scratch)
    local = [local_ref[:, i * LANES : (i + 1) * LANES] for i in range(LOCAL_SUMS)]
    tokens, width = held[0].shape
    half = LANES // 2
    for copy in more:
        copy.wait()
    inverse = local[INVERSE]
    reduced = inverse * products[X_DOWN]
    expand = expand_ref[...]
    left_two = mm_rows(reduced.astype(BF16), jnp.concatenate([expand, expand], axis=0))
    returned = products[VALUES].astype(BF16)
    right_one = ALPHA * mm(returned, sketch_ref[...])
    along = (ALPHA / width) * jnp.sum(returned.astype(F32) * reduced, axis=1, keepdims=True)
    back = mm(returned, bridge.astype(BF16))
    along = along * inverse
    right_three = products[J_LOW] + inverse * (ALPHA * back[:, :LANES] - along * products[X_LOW])
    right_four = products[J_TARGET] + inverse * (ALPHA * back[:, LANES:] - along * local[X_TARGET])
    rights = (right_one, ALPHA * products[V_TARGET], ALPHA * right_three, ALPHA * right_four)
    lefts = (local[LEFT_ONE], left_two, doubled(products[M_SOURCE], 0), products[M_DOWN])
    place = lax.broadcasted_iota(jnp.int32, (tokens, LANES), 0)
    one, two = counts_ref[0, 0], counts_ref[0, 1]
    lower = half_lanes((tokens, LANES))
    member = (place >= jnp.where(lower, 0, one)) & (place < jnp.where(lower, one, one + two))
    spread = jnp.concatenate([jnp.where(member, left, 0.0).astype(BF16) for left in lefts], axis=0)
    feats = mm_cols(spread, jnp.concatenate([right.astype(BF16) for right in rights], axis=0))
    for e in range(2):
        own = feats[e * half : (e + 1) * half]
        squares = jnp.sum(own * own, keepdims=True)
        out_ref[pl.ds(e * half, half), :] = (own * lax.rsqrt(squares + 1e-06)).astype(BF16).astype(F32)


def split_kernel(block_ref, *refs):
    head_ref, tail_ref = refs[-2:]
    cut, tail = head_ref.shape[0], block_ref.shape[0] - head_ref.shape[0]
    head_ref[...] = block_ref[pl.ds(0, cut), :]
    if len(refs) == 3:
        tail_ref[pl.ds(0, tail), :] = refs[0][...]
    tail_ref[pl.ds(tail_ref.shape[0] - tail, tail), :] = block_ref[pl.ds(cut, tail), :]


def best_of(places, count, unit_ref, best):
    half = LANES // 2
    scale = float(half * LANES) ** 0.5
    shape = (count, LANES)
    totals = [[jnp.zeros(shape, F32) for _ in range(2)] for _ in places]
    for i in range(0, half, 2):
        units = [
            [jnp.broadcast_to(unit_ref[pl.ds(e * half + i + k, 1), :], shape) for k in range(2)]
            for e in range(2)
        ]
        for b, (block, start) in enumerate(places):
            wide = block[pl.ds(start + i * count, 2 * count), :].astype(F32)
            for e in range(2):
                totals[b][e] = totals[b][e] + (wide[:count] * units[e][0] + wide[count:] * units[e][1])
    for b, (block, start) in enumerate(places):
        labels = block[pl.ds(start + half * count, 2 * count), :].astype(F32)[:count]
        for e in range(2):
            similar = scale * jnp.sum(totals[b][e], axis=1, keepdims=True)
            for t in range(TASKS):
                best[e][t] = jnp.maximum(best[e][t], jnp.where(labels == float(t), similar, -2.0 * scale))


def places_of(blocks, count):
    size = (LANES // 2 + 2) * count
    places = []
    for block in blocks:
        total = block.shape[0]
        firsts = range(0, total, size) if total % size == 0 else [total - size]
        places += [(block, first) for first in firsts]
    return places


def score_kernel(blocks, count, unit_ref, *refs):
    block_refs, best_ref = refs[:blocks], refs[blocks]
    lowest = -2.0 * float(LANES // 2 * LANES) ** 0.5
    best = [[jnp.full((count, LANES), lowest, F32) for _ in range(TASKS)] for _ in range(2)]
    best_of(places_of(block_refs, count), count, unit_ref, best)
    for e in range(2):
        for t in range(TASKS):
            best_ref[e, t] = best[e][t]


def last_score_kernel(count, unit_ref, block_ref, best_ref, out_ref, mean_ref):
    best = [[best_ref[e, t] for t in range(TASKS)] for e in range(2)]
    best_of(places_of([block_ref], count), count, unit_ref, best)
    lane = lax.broadcasted_iota(jnp.int32, (1, LANES), 1)
    means = []
    for e in range(2):
        values = [jnp.max(best[e][t], axis=0, keepdims=True) for t in range(TASKS)]
        row = jnp.where(lane == 0, values[0], jnp.where(lane == 1, values[1], values[2]))
        out_ref[pl.ds(e, 1), :] = row[:, :TASKS]
        means.append((values[0] + values[1] + values[2]) * (1.0 / TASKS))
    mean_ref[...] = jnp.where(lane == 0, means[0], means[1])[:, :2]


VMEM = pl.BlockSpec(memory_space=pltpu.VMEM)
SMEM = pl.BlockSpec(memory_space=pltpu.SMEM)
ANY = pl.BlockSpec(memory_space=pl.ANY)
HBM = pl.BlockSpec(memory_space=pltpu.HBM)


def in_hbm(arrays):
    return [pltpu.with_memory_space_constraint(a, pltpu.HBM) for a in arrays]


def params(mib):
    return pltpu.CompilerParams(vmem_limit_bytes=mib * MIB)


def cost(flops, nbytes):
    return pl.CostEstimate(flops=flops, bytes_accessed=nbytes, transcendentals=0)


def shards(
    hidden_state_input,
    attention_mixed_state,
    hidden_state_adjoint,
    attention_values_adjoint,
    sequence_token_counts,
    heldout_sketched_signals,
    benchmark_labels,
    top_rmsnorm_weights,
    top_reducer_matrix,
    top_expander_matrix,
    bottom_reducer_matrix,
    bottom_expander_matrix,
    source_sketch,
    top_reducer_sketch,
    top_expander_sketch,
    top_target_sketch,
    bottom_reducer_sketch,
    bottom_expander_sketch,
    bottom_target_sketch,
):
    me = lax.axis_index("dp").astype(jnp.int32)
    x, mixed, adjoint, values = (
        hidden_state_input,
        attention_mixed_state,
        hidden_state_adjoint,
        attention_values_adjoint,
    )
    tokens, width = x.shape
    rows = top_reducer_matrix.shape[0]
    count = heldout_sketched_signals.shape[0]

    inputs = (
        top_rmsnorm_weights.reshape(width // LANES, LANES),
        top_reducer_matrix,
        bottom_expander_matrix.T,
        bottom_reducer_sketch,
        top_expander_matrix.T,
        bottom_reducer_matrix,
        bottom_expander_sketch.T,
        heldout_sketched_signals,
        benchmark_labels.T,
    )
    own = pl.pallas_call(
        pack_kernel,
        out_shape=jax.ShapeDtypeStruct((3 * rows + (LANES // 2 + 2) * count, LANES), BF16),
        in_specs=[SMEM] + [HBM] * len(inputs),
        out_specs=VMEM,
        scratch_shapes=[pltpu.VMEM(a.shape, a.dtype) for a in inputs]
        + [pltpu.SemaphoreType.DMA((len(inputs),))],
        compiler_params=params(8),
        name="pack",
    )(me.reshape(1), *in_hbm(inputs))

    tie = lax.optimization_barrier
    inputs = (x, bottom_target_sketch, top_rmsnorm_weights.reshape(1, width), source_sketch.T)
    upper, low_target, source, local = pl.pallas_call(
        local_kernel,
        out_shape=[jax.ShapeDtypeStruct(a.shape, a.dtype) for a in inputs[:2]]
        + [
            jax.ShapeDtypeStruct((width, LANES), BF16),
            jax.ShapeDtypeStruct((tokens, LOCAL_SUMS * LANES), F32),
        ],
        in_specs=[HBM] * len(inputs),
        out_specs=[VMEM] * 4,
        scratch_shapes=[pltpu.VMEM(a.shape, a.dtype) for a in inputs[2:]]
        + [pltpu.SemaphoreType.DMA((STEPS, len(inputs)))],
        compiler_params=params(16),
        cost_estimate=cost(tokens * width * LANES * 4, 6 * MIB),
        name="local_products",
    )(*in_hbm(inputs))
    own_late, local = tie((own, local))
    inputs = (mixed, adjoint, values, top_target_sketch)
    fetched = pl.pallas_call(
        fetch_kernel,
        out_shape=[jax.ShapeDtypeStruct(a.shape, a.dtype) for a in inputs],
        in_specs=[VMEM] + [HBM] * len(inputs),
        out_specs=[VMEM] * len(inputs),
        scratch_shapes=[pltpu.SemaphoreType.DMA((STEPS * len(inputs),))],
        compiler_params=params(16),
        cost_estimate=cost(1, 8 * MIB),
        name="fetch",
    )(local, *in_hbm(inputs))
    activations = [upper, *fetched[:3], low_target, fetched[3], source]

    stage_scratch = [
        pltpu.VMEM((2 * rows, 2 * LANES), BF16),
        pltpu.VMEM((rows + LANES // 2, 2 * LANES), BF16),
        pltpu.VMEM((2 * rows, LANES), BF16),
    ]

    def stage(away, pieces, sums):
        first = not sums
        start = 1 + len(pieces) + len(activations)
        return pl.pallas_call(
            functools.partial(stage_kernel, away, first),
            out_shape=[
                jax.ShapeDtypeStruct((tokens, SUMS * LANES), F32),
                jax.ShapeDtypeStruct((LANES, 2 * LANES), F32),
            ],
            in_specs=[SMEM] + [VMEM] * (len(pieces) + len(activations) + len(sums)),
            out_specs=[VMEM, VMEM],
            scratch_shapes=stage_scratch,
            input_output_aliases={} if first else {start: 0, start + 1: 1},
            compiler_params=params(16),
            cost_estimate=cost(tokens * rows * LANES * 16, 2 * MIB),
            name="stage",
        )(me.reshape(1), *pieces, *activations, *sums)

    def split(block, *tails):
        tail = block.shape[0] - 3 * rows
        shapes = (3 * rows, LANES), ((1 + len(tails)) * tail, LANES)
        return pl.pallas_call(
            split_kernel,
            out_shape=[jax.ShapeDtypeStruct(shape, BF16) for shape in shapes],
            in_specs=[VMEM] * (1 + len(tails)),
            out_specs=[VMEM, VMEM],
            compiler_params=params(8),
            name="split",
        )(block, *tails)

    half = RING_CHIPS // 2
    held = [own, other_core(own_late)]
    blocks = list(held)
    first, second = hop(own), hop(own_late, from_other=True)
    first, activations = tie((first, activations))
    sums = stage(0, held, [])
    second, sums = tie((second, sums))
    for k in range(1, half):
        held = [first, second]
        crossed = [other_core(first), other_core(second)]
        blocks += [first, crossed[0]]
        if k < half - 1:
            blocks += [second, crossed[1]]
        else:
            first, tails = split(first, tail)
        first = hop(first)
        sums = stage(k, held, sums)
        first, sums = tie((first, sums))
        if k == half - 2:
            second, tail = split(second)
        if k < half - 1:
            second = hop(second)
        sums = stage(-k, crossed, sums)
        if k < half - 1:
            second, sums = tie((second, sums))
    tails = hop(tails)
    small = (top_expander_sketch.T, top_reducer_sketch)
    unit = pl.pallas_call(
        functools.partial(feature_kernel, half),
        out_shape=jax.ShapeDtypeStruct((LANES, LANES), F32),
        in_specs=[SMEM] * 2 + [VMEM] * (2 + len(activations) + 3) + [HBM] * 2,
        out_specs=VMEM,
        scratch_shapes=stage_scratch
        + [pltpu.VMEM(a.shape, a.dtype) for a in small]
        + [pltpu.SemaphoreType.DMA((2,))],
        compiler_params=params(16),
        cost_estimate=cost(1, 1),
        name="features",
    )(
        me.reshape(1),
        sequence_token_counts,
        first,
        other_core(first),
        *activations,
        *sums,
        local,
        *in_hbm(small),
    )
    tails, unit = tie((tails, unit))
    blocks.append(tails)
    best = pl.pallas_call(
        functools.partial(score_kernel, len(blocks), count),
        out_shape=jax.ShapeDtypeStruct((2, TASKS, count, LANES), F32),
        in_specs=[VMEM] * (1 + len(blocks)),
        out_specs=VMEM,
        compiler_params=params(16),
        cost_estimate=cost(4 * MIB, 2 * MIB),
        name="scores",
    )(unit, *blocks)
    task_best, scores = pl.pallas_call(
        functools.partial(last_score_kernel, count),
        out_shape=(jax.ShapeDtypeStruct((2, TASKS), F32), jax.ShapeDtypeStruct((1, 2), F32)),
        in_specs=[VMEM] * 3,
        out_specs=(VMEM, VMEM),
        compiler_params=params(8),
        name="last_scores",
    )(unit, other_core(tails), best)
    return (scores.reshape(2), task_best)


def shards_of_any_slice(
    hidden_state_input,
    attention_mixed_state,
    hidden_state_adjoint,
    attention_values_adjoint,
    sequence_token_counts,
    heldout_sketched_signals,
    benchmark_labels,
    top_rmsnorm_weights,
    top_reducer_matrix,
    top_expander_matrix,
    bottom_reducer_matrix,
    bottom_expander_matrix,
    source_sketch,
    top_reducer_sketch,
    top_expander_sketch,
    top_target_sketch,
    bottom_reducer_sketch,
    bottom_expander_sketch,
    bottom_target_sketch,
    n,
):
    me = lax.axis_index("dp")
    x, mixed, adjoint, values = (
        hidden_state_input,
        attention_mixed_state,
        hidden_state_adjoint,
        attention_values_adjoint,
    )
    tokens, width = x.shape
    rows = top_reducer_matrix.shape[0]
    up_rows = top_expander_matrix.shape[1]
    rank = top_reducer_matrix.shape[1]
    k1 = source_sketch.shape[1]
    gain = top_rmsnorm_weights
    own_gain = lax.dynamic_slice_in_dim(gain, me * rows, rows)

    down_upper = (own_gain[:, None] * top_reducer_matrix.astype(F32)).astype(BF16)
    up_lower = mm(bottom_expander_matrix.T, bottom_reducer_sketch).astype(BF16)
    down_lower = mm(bottom_reducer_matrix, bottom_expander_sketch).astype(BF16)
    packed_lower = jnp.concatenate([down_lower[: rows // 2], down_lower[rows // 2 :]], axis=1)
    factors = jnp.concatenate([down_upper, up_lower, top_expander_matrix.T, packed_lower], axis=0)
    factors = lax.all_gather(factors, "dp")

    val_wide = heldout_sketched_signals.astype(F32)
    val_unit = (
        val_wide * lax.rsqrt(jnp.sum(val_wide * val_wide, axis=1, keepdims=True) + 1e-06)
    ).astype(BF16)
    labels = jnp.broadcast_to(benchmark_labels.astype(BF16), (val_unit.shape[0], 128))
    panel = jnp.concatenate([val_unit.reshape(-1, 128), labels], axis=0)
    panel = lax.all_gather(panel, "dp")
    val_rows = val_unit.shape[0]
    cut = panel.shape[1] - val_rows
    panel_tasks = panel[:, cut:, 0].reshape(n * val_rows, 1).astype(jnp.int32)
    panel = panel[:, :cut].reshape(n * val_rows, val_unit.shape[1])

    wide = x.astype(F32)
    inverse = lax.rsqrt(jnp.mean(wide * wide, axis=1, keepdims=True) + 1e-05)
    gained_sketch = (gain[:, None] * source_sketch.astype(F32)).astype(BF16)
    left_one = inverse * mm(x, gained_sketch)
    left_three = mm(mixed, source_sketch)
    right_two = ALPHA * mm(values, top_target_sketch)

    at = 0
    down_upper = factors[:, at : at + rows].reshape(width, rank)
    at += rows
    up_lower = factors[:, at : at + rows].reshape(width, -1)
    at += rows
    up_upper = factors[:, at : at + up_rows].reshape(-1, rank)
    at += up_rows
    down_lower = factors[:, at:]
    down_lower = jnp.concatenate([down_lower[:, :, :k1], down_lower[:, :, k1:]], axis=1)
    down_lower = down_lower.reshape(width, k1)

    reduced = inverse * mm(x, down_upper)
    left_two = mm(reduced.astype(BF16), top_expander_sketch)
    left_four = mm(mixed, down_lower)
    returned = mm(values, up_upper).astype(BF16)
    right_one = ALPHA * mm(returned, top_reducer_sketch)
    along = (ALPHA / width) * jnp.sum(returned.astype(F32) * reduced, axis=1, keepdims=True)
    targets = jnp.concatenate([up_lower, bottom_target_sketch], axis=1)
    bridge = mm_cols(down_upper, targets).astype(BF16)
    rights_low = mm(adjoint, targets) + inverse * (
        ALPHA * mm(returned, bridge) - (along * inverse) * mm(x, targets)
    )
    rights_low = ALPHA * rights_low
    k2 = up_lower.shape[1]
    lefts = (left_one, left_two, left_three, left_four)
    rights = (right_one, right_two, rights_low[:, :k2], rights_low[:, k2:])

    counts = sequence_token_counts[0]
    ends = jnp.cumsum(counts)
    starts = ends - counts
    places = jnp.arange(tokens, dtype=jnp.int32)[:, None]
    member = (places >= starts[None, :]) & (places < ends[None, :])
    count_ex = counts.shape[0]
    spread = jnp.concatenate(lefts, axis=0).astype(BF16)
    member = jnp.tile(member, (4, 1))
    spread = jnp.concatenate(
        [jnp.where(member[:, e : e + 1], spread, 0) for e in range(count_ex)], axis=1
    )
    feats = mm_cols(spread, jnp.concatenate(rights, axis=0).astype(BF16))
    feats = feats.reshape(count_ex, -1)
    squares = jnp.sum(feats * feats, axis=1, keepdims=True)
    unit_rows = (feats * lax.rsqrt(squares + 1e-06)).astype(BF16)

    score_scale = float(unit_rows.shape[1]) ** 0.5
    similar = score_scale * mm_rows(unit_rows, panel)
    task_mask = panel_tasks == jnp.arange(TASKS, dtype=jnp.int32)[None, :]
    task_best = jnp.max(
        jnp.where(task_mask[None, :, :], similar[:, :, None], -2.0 * score_scale), axis=1
    )
    return (jnp.mean(task_best, axis=1), task_best)


def solution(mesh):
    n = mesh.shape["dp"]
    split = P(("parts", "dp"), None)
    by_row, by_column, whole = P("dp", None), P(None, "dp"), P()
    placed = (
        (split,) * 5
        + (by_row, by_row, whole)
        + (by_row, by_column, by_row, by_column)
        + (whole,) * 7
    )
    ours = shards if n == 2 * RING_CHIPS else functools.partial(shards_of_any_slice, n=n)
    return jax.shard_map(
        ours,
        mesh=mesh,
        in_specs=placed,
        out_specs=(P(("parts", "dp")), split),
        check_vma=False,
    )
```

```python
import functools

import jax
import jax.numpy as jnp
from jax import lax
from jax.experimental import pallas as pl
from jax.experimental.pallas import tpu as pltpu
from jax.sharding import PartitionSpec as P

TASKS = 3
ALPHA = 4.0
F32 = jnp.float32
BF16 = jnp.bfloat16
RING_CHIPS = 8
LANES = 128
STEPS = 4
X_DOWN, X_LOW, J_LOW, J_TARGET, M_DOWN, M_SOURCE, VALUES, V_TARGET, SUMS = range(9)
INVERSE, LEFT_ONE, X_TARGET, LOCAL_SUMS = range(4)
MIB = 1 << 20


def mm(a, b):
    return jnp.dot(a, b, preferred_element_type=F32)


def mm_rows(a, b):
    return lax.dot_general(a, b, (((1,), (1,)), ((), ())), preferred_element_type=F32)


def mm_cols(a, b):
    return lax.dot_general(a, b, (((0,), (0,)), ((), ())), preferred_element_type=F32)


def ring_chip(pos):
    half = RING_CHIPS // 2
    return jnp.where(pos < half, 2 * pos, 2 * (RING_CHIPS - 1 - pos) + 1)


def ring_pos(chip):
    row, side = chip // 2, chip % 2
    return jnp.where(side == 0, row, RING_CHIPS - 1 - row)


def hop(value, from_other=False):
    half = RING_CHIPS // 2
    place = [2 * q if q < half else 2 * (RING_CHIPS - 1 - q) + 1 for q in range(RING_CHIPS)]
    turn = int(from_other)
    pairs = []
    for q in range(RING_CHIPS):
        pairs.append((2 * place[q] + turn, 2 * place[(q + 1) % RING_CHIPS]))
        pairs.append((2 * place[q] + 1 - turn, 2 * place[(q - 1) % RING_CHIPS] + 1))
    return lax.ppermute(value, "dp", pairs)


def other_core(value):
    return lax.ppermute(value, "dp", [(d, d ^ 1) for d in range(2 * RING_CHIPS)])


def half_lanes(shape):
    return lax.broadcasted_iota(jnp.int32, shape, 1) < LANES // 2


def diagonal_column(row, first, count):
    shape = (count, row.shape[1])
    lane = lax.broadcasted_iota(jnp.int32, shape, 1)
    at = lax.broadcasted_iota(jnp.int32, shape, 0)
    return jnp.sum(jnp.where(lane == at + first, row, 0.0), axis=1, keepdims=True)


def load(pairs, sems):
    copies = [pltpu.make_async_copy(src, dst, sems.at[i]) for i, (src, dst) in enumerate(pairs)]
    for copy in copies:
        copy.start()
    return copies


def pack_kernel(me_ref, *refs):
    hbm, out_ref, held, sems = refs[:9], refs[9], refs[10:19], refs[19]
    gain_ref, down_up_ref, up_low_ref, sketch_ref, up_up_ref, down_low_ref, expand_ref, val_ref, label_ref = held
    copies = load(zip(hbm, held), sems)
    rows = down_up_ref.shape[0]
    half = LANES // 2
    for copy in copies:
        copy.wait()
    for b in range(rows // half):
        place = me_ref[0] * (rows // half) + b
        row = gain_ref[pl.ds(place // 2, 1), :]
        column = diagonal_column(row, (place % 2) * half, half)
        part = down_up_ref[pl.ds(b * half, half), :].astype(F32)
        out_ref[pl.ds(b * half, half), :] = (column * part).astype(BF16)
    at = rows
    out_ref[pl.ds(at, rows), :] = mm(up_low_ref[...], sketch_ref[...]).astype(BF16)
    at += rows
    out_ref[pl.ds(at, rows // 2), :] = up_up_ref[...]
    at += rows // 2
    expand = expand_ref[...]
    low = mm_rows(down_low_ref[...], jnp.concatenate([expand, expand], axis=0))
    first, second = low[: rows // 2], low[rows // 2 :]
    out_ref[pl.ds(at, rows // 2), :] = jnp.where(half_lanes(first.shape), first, second).astype(BF16)
    at += rows // 2
    wide = val_ref[...].astype(F32)
    count, width = wide.shape
    scale = lax.rsqrt(jnp.sum(wide * wide, axis=1, keepdims=True) + 1e-06)
    unit = wide * scale
    blocks = [unit[:, i * LANES : (i + 1) * LANES] for i in range(width // LANES)]
    row = label_ref[...].astype(F32)
    labels = jnp.broadcast_to(diagonal_column(row, 0, count), (count, LANES))
    blocks += [labels, labels]
    for i in range(0, len(blocks), 2):
        pair = jnp.concatenate(blocks[i : i + 2], axis=0)
        out_ref[pl.ds(at + i * count, 2 * count), :] = pair.astype(BF16)


def doubled(value, which):
    turned = pltpu.roll(value, LANES // 2, 1)
    lower = half_lanes(value.shape)
    return jnp.where(lower, turned, value) if which else jnp.where(lower, value, turned)


def local_kernel(after_ref, *refs):
    x_hbm, values_hbm, target_hbm, gain_hbm, source_hbm = refs[:5]
    x_ref, values_ref, target_ref, turned_ref, sums_ref = refs[5:10]
    gain_ref, source_ref, sems = refs[10:]
    tokens, width = x_ref.shape
    span = width // STEPS
    copies = []
    for j in range(STEPS):
        part = pl.ds(j * span, span)
        pairs = (
            (gain_hbm.at[:, part], gain_ref.at[:, part]),
            (source_hbm.at[:, part], source_ref.at[:, part]),
            (x_hbm.at[:, part], x_ref.at[:, part]),
            (target_hbm.at[part], target_ref.at[part]),
        )
        copies.append(load(pairs, sems.at[j]))
    later = load(((values_hbm, values_ref),), sems.at[STEPS])
    products = jnp.zeros((tokens, 2 * LANES), F32)
    squares = jnp.zeros((tokens, LANES), F32)
    for j in range(STEPS):
        for copy in copies[j]:
            copy.wait()
        part = slice(j * span, (j + 1) * span)
        x, source = x_ref[:, part], source_ref[:, part]
        gained = (source.astype(F32) * gain_ref[:, part]).astype(BF16)
        turned = jnp.concatenate([source, gained], axis=0).T
        turned_ref[part, :] = turned
        products = products + mm(x, jnp.concatenate([turned, target_ref[part, :]], axis=1))
        for i in range(span // LANES):
            wide = x[:, i * LANES : (i + 1) * LANES].astype(F32)
            squares = squares + wide * wide
    mean = jnp.sum(squares, axis=1, keepdims=True) * (1.0 / width)
    inverse = jnp.broadcast_to(lax.rsqrt(mean + 1e-05), (tokens, LANES))
    left_one = inverse * doubled(products[:, :LANES], 1)
    for i, value in enumerate((inverse, left_one, products[:, LANES:])):
        sums_ref[:, i * LANES : (i + 1) * LANES] = value
    for copy in later:
        copy.wait()


def fetch_kernel(*refs):
    count = (len(refs) - 1) // 2
    pairs = []
    for src, dst in zip(refs[:count], refs[count:-1]):
        rows = src.shape[0] // STEPS
        pairs += [(src.at[pl.ds(j * rows, rows)], dst.at[pl.ds(j * rows, rows)]) for j in range(STEPS)]
    for copy in load(pairs, refs[-1]):
        copy.wait()


def add_stage(away, me_ref, pieces, held, old, scratch):
    x_ref, mixed_ref, adjoint_ref, values_ref, target_ref, top_target_ref, source_ref = held
    both, up, down = scratch
    rows = both.shape[0] // 2
    half, pad = rows // 2, LANES // 2
    span = 2 * rows
    me = me_ref[0]
    pos, core = ring_pos(me // 2), me % 2
    chip = ring_chip((pos + away * (2 * core - 1) + RING_CHIPS) % RING_CHIPS)
    odd = chip % 2
    mine = pl.ds(pl.multiple_of(chip * span, LANES), span)
    values_start = (chip // 2) * span + odd * (rows - pad)
    values_part = pl.ds(pl.multiple_of(values_start, LANES), rows + pad)
    side = core if away >= 0 else 1 - core
    up[pl.ds(pl.multiple_of((1 - odd) * rows, 16), pad), :] = jnp.zeros((pad, 2 * LANES), BF16)
    up[pl.ds(pl.multiple_of(odd * pad, 16), rows), pl.ds(LANES, LANES)] = top_target_ref[
        pl.ds(pl.multiple_of(chip * rows, 16), rows), :
    ]
    for piece, c in ((pieces[0], side), (pieces[1], 1 - side)):
        one = pl.ds(pl.multiple_of(c * rows, 16), rows)
        both[one, pl.ds(0, LANES)] = piece[pl.ds(0, rows), :]
        both[one, pl.ds(LANES, LANES)] = piece[pl.ds(rows, rows), :]
        up[pl.ds(pl.multiple_of(odd * pad + c * half, 16), half), pl.ds(0, LANES)] = piece[
            pl.ds(2 * rows, half), :
        ]
        packed = piece[pl.ds(2 * rows + half, half), :].astype(F32)
        turned = pltpu.roll(packed, pad, 1)
        lower = half_lanes(packed.shape)
        down[pl.ds(pl.multiple_of(c * rows, 16), half), :] = jnp.where(lower, packed, turned).astype(BF16)
        down[pl.ds(pl.multiple_of(c * rows + half, 16), half), :] = jnp.where(lower, turned, packed).astype(BF16)

    weights = both[...]
    down_up = weights[:, :LANES]
    lows = jnp.concatenate([weights[:, LANES:], target_ref[mine, :]], axis=1)
    products = []
    for activation, factor in (
        (x_ref[:, mine], weights),
        (adjoint_ref[:, mine], lows),
        (mixed_ref[:, mine], jnp.concatenate([down[...], source_ref[mine, :]], axis=1)),
        (values_ref[:, values_part], up[...]),
    ):
        product = mm(activation, factor)
        products += [product[:, :LANES], product[:, LANES:]]
    bridge = mm_cols(down_up, lows)
    if old:
        old_sums, old_bridge = old
        products = [p + old_sums[:, i * LANES : (i + 1) * LANES] for i, p in enumerate(products)]
        bridge = bridge + old_bridge[...]
    return products, bridge


def stage_kernel(away, first, me_ref, *refs):
    pieces, held, old = refs[:2], refs[2:9], refs[9:-5]
    (new_sums, new_bridge), scratch = refs[-5:-3], refs[-3:]
    products, bridge = add_stage(away, me_ref, pieces, held, old, scratch)
    for i in range(SUMS):
        new_sums[:, i * LANES : (i + 1) * LANES] = products[i]
    new_bridge[...] = bridge


def feature_kernel(away, me_ref, counts_ref, *refs):
    pieces, held, old, local_ref, small_hbm, refs = refs[:2], refs[2:9], refs[9:11], refs[11], refs[12:14], refs[14:]
    out_ref, scratch, (expand_ref, sketch_ref, sems) = refs[0], refs[1:4], refs[4:]
    more = load(zip(small_hbm, (expand_ref, sketch_ref)), sems)
    products, bridge = add_stage(away, me_ref, pieces, held, old, scratch)
    local = [local_ref[:, i * LANES : (i + 1) * LANES] for i in range(LOCAL_SUMS)]
    tokens, width = held[0].shape
    half = LANES // 2
    for copy in more:
        copy.wait()
    inverse = local[INVERSE]
    reduced = inverse * products[X_DOWN]
    expand = expand_ref[...]
    left_two = mm_rows(reduced.astype(BF16), jnp.concatenate([expand, expand], axis=0))
    returned = products[VALUES].astype(BF16)
    right_one = ALPHA * mm(returned, sketch_ref[...])
    along = (ALPHA / width) * jnp.sum(returned.astype(F32) * reduced, axis=1, keepdims=True)
    back = mm(returned, bridge.astype(BF16))
    along = along * inverse
    right_three = products[J_LOW] + inverse * (ALPHA * back[:, :LANES] - along * products[X_LOW])
    right_four = products[J_TARGET] + inverse * (ALPHA * back[:, LANES:] - along * local[X_TARGET])
    rights = (right_one, ALPHA * products[V_TARGET], ALPHA * right_three, ALPHA * right_four)
    lefts = (local[LEFT_ONE], left_two, doubled(products[M_SOURCE], 0), products[M_DOWN])
    place = lax.broadcasted_iota(jnp.int32, (tokens, LANES), 0)
    one, two = counts_ref[0, 0], counts_ref[0, 1]
    lower = half_lanes((tokens, LANES))
    member = (place >= jnp.where(lower, 0, one)) & (place < jnp.where(lower, one, one + two))
    spread = jnp.concatenate([jnp.where(member, left, 0.0).astype(BF16) for left in lefts], axis=0)
    feats = mm_cols(spread, jnp.concatenate([right.astype(BF16) for right in rights], axis=0))
    for e in range(2):
        own = feats[e * half : (e + 1) * half]
        squares = jnp.sum(own * own, keepdims=True)
        out_ref[pl.ds(e * half, half), :] = (own * lax.rsqrt(squares + 1e-06)).astype(BF16).astype(F32)


def split_kernel(block_ref, *refs):
    head_ref, tail_ref = refs[-2:]
    cut, tail = head_ref.shape[0], block_ref.shape[0] - head_ref.shape[0]
    head_ref[...] = block_ref[pl.ds(0, cut), :]
    if len(refs) == 3:
        tail_ref[pl.ds(0, tail), :] = refs[0][...]
    tail_ref[pl.ds(tail_ref.shape[0] - tail, tail), :] = block_ref[pl.ds(cut, tail), :]


def best_of(places, count, unit_ref, best):
    half = LANES // 2
    scale = float(half * LANES) ** 0.5
    shape = (count, LANES)
    totals = [[jnp.zeros(shape, F32) for _ in range(2)] for _ in places]
    for i in range(0, half, 2):
        units = [
            [jnp.broadcast_to(unit_ref[pl.ds(e * half + i + k, 1), :], shape) for k in range(2)]
            for e in range(2)
        ]
        for b, (block, start) in enumerate(places):
            wide = block[pl.ds(start + i * count, 2 * count), :].astype(F32)
            for e in range(2):
                totals[b][e] = totals[b][e] + (wide[:count] * units[e][0] + wide[count:] * units[e][1])
    for b, (block, start) in enumerate(places):
        labels = block[pl.ds(start + half * count, 2 * count), :].astype(F32)[:count]
        for e in range(2):
            similar = scale * jnp.sum(totals[b][e], axis=1, keepdims=True)
            for t in range(TASKS):
                best[e][t] = jnp.maximum(best[e][t], jnp.where(labels == float(t), similar, -2.0 * scale))


def places_of(blocks, count):
    size = (LANES // 2 + 2) * count
    places = []
    for block in blocks:
        total = block.shape[0]
        firsts = range(0, total, size) if total % size == 0 else [total - size]
        places += [(block, first) for first in firsts]
    return places


def score_kernel(blocks, count, unit_ref, *refs):
    block_refs, best_ref = refs[:blocks], refs[blocks]
    lowest = -2.0 * float(LANES // 2 * LANES) ** 0.5
    best = [[jnp.full((count, LANES), lowest, F32) for _ in range(TASKS)] for _ in range(2)]
    best_of(places_of(block_refs, count), count, unit_ref, best)
    for e in range(2):
        for t in range(TASKS):
            best_ref[e, t] = best[e][t]


def last_score_kernel(count, unit_ref, block_ref, best_ref, out_ref, mean_ref):
    best = [[best_ref[e, t] for t in range(TASKS)] for e in range(2)]
    best_of(places_of([block_ref], count), count, unit_ref, best)
    lane = lax.broadcasted_iota(jnp.int32, (1, LANES), 1)
    means = []
    for e in range(2):
        values = [jnp.max(best[e][t], axis=0, keepdims=True) for t in range(TASKS)]
        row = jnp.where(lane == 0, values[0], jnp.where(lane == 1, values[1], values[2]))
        out_ref[pl.ds(e, 1), :] = row[:, :TASKS]
        means.append((values[0] + values[1] + values[2]) * (1.0 / TASKS))
    mean_ref[...] = jnp.where(lane == 0, means[0], means[1])[:, :2]


VMEM = pl.BlockSpec(memory_space=pltpu.VMEM)
SMEM = pl.BlockSpec(memory_space=pltpu.SMEM)
ANY = pl.BlockSpec(memory_space=pl.ANY)
HBM = pl.BlockSpec(memory_space=pltpu.HBM)


def in_hbm(arrays):
    return [pltpu.with_memory_space_constraint(a, pltpu.HBM) for a in arrays]


def params(mib):
    return pltpu.CompilerParams(vmem_limit_bytes=mib * MIB)


def cost(flops, nbytes):
    return pl.CostEstimate(flops=flops, bytes_accessed=nbytes, transcendentals=0)


def shards(
    hidden_state_input,
    attention_mixed_state,
    hidden_state_adjoint,
    attention_values_adjoint,
    sequence_token_counts,
    heldout_sketched_signals,
    benchmark_labels,
    top_rmsnorm_weights,
    top_reducer_matrix,
    top_expander_matrix,
    bottom_reducer_matrix,
    bottom_expander_matrix,
    source_sketch,
    top_reducer_sketch,
    top_expander_sketch,
    top_target_sketch,
    bottom_reducer_sketch,
    bottom_expander_sketch,
    bottom_target_sketch,
):
    me = lax.axis_index("dp").astype(jnp.int32)
    x, mixed, adjoint, values = (
        hidden_state_input,
        attention_mixed_state,
        hidden_state_adjoint,
        attention_values_adjoint,
    )
    tokens, width = x.shape
    rows = top_reducer_matrix.shape[0]
    count = heldout_sketched_signals.shape[0]

    inputs = (
        top_rmsnorm_weights.reshape(width // LANES, LANES),
        top_reducer_matrix,
        bottom_expander_matrix.T,
        bottom_reducer_sketch,
        top_expander_matrix.T,
        bottom_reducer_matrix,
        bottom_expander_sketch.T,
        heldout_sketched_signals,
        benchmark_labels.T,
    )
    own = pl.pallas_call(
        pack_kernel,
        out_shape=jax.ShapeDtypeStruct((3 * rows + (LANES // 2 + 2) * count, LANES), BF16),
        in_specs=[SMEM] + [HBM] * len(inputs),
        out_specs=VMEM,
        scratch_shapes=[pltpu.VMEM(a.shape, a.dtype) for a in inputs]
        + [pltpu.SemaphoreType.DMA((len(inputs),))],
        compiler_params=params(8),
        name="pack",
    )(me.reshape(1), *in_hbm(inputs))

    tie = lax.optimization_barrier
    inputs = (mixed, adjoint, top_target_sketch)
    fetched = pl.pallas_call(
        fetch_kernel,
        out_shape=[jax.ShapeDtypeStruct(a.shape, a.dtype) for a in inputs],
        in_specs=[HBM] * len(inputs),
        out_specs=[VMEM] * len(inputs),
        scratch_shapes=[pltpu.SemaphoreType.DMA((STEPS * len(inputs),))],
        compiler_params=params(16),
        cost_estimate=cost(1, 6 * MIB),
        name="fetch",
    )(*in_hbm(inputs))
    own_late, fetched = tie((own, fetched))
    inputs = (x, values, bottom_target_sketch, top_rmsnorm_weights.reshape(1, width), source_sketch.T)
    upper, upper_values, low_target, source, local = pl.pallas_call(
        local_kernel,
        out_shape=[jax.ShapeDtypeStruct(a.shape, a.dtype) for a in inputs[:3]]
        + [
            jax.ShapeDtypeStruct((width, LANES), BF16),
            jax.ShapeDtypeStruct((tokens, LOCAL_SUMS * LANES), F32),
        ],
        in_specs=[VMEM] + [HBM] * len(inputs),
        out_specs=[VMEM] * 5,
        scratch_shapes=[pltpu.VMEM(a.shape, a.dtype) for a in inputs[3:]]
        + [pltpu.SemaphoreType.DMA((STEPS + 1, 4))],
        compiler_params=params(16),
        cost_estimate=cost(tokens * width * LANES * 4, 7 * MIB),
        name="local_products",
    )(fetched[2], *in_hbm(inputs))
    activations = [upper, *fetched[:2], upper_values, low_target, fetched[2], source]

    stage_scratch = [
        pltpu.VMEM((2 * rows, 2 * LANES), BF16),
        pltpu.VMEM((rows + LANES // 2, 2 * LANES), BF16),
        pltpu.VMEM((2 * rows, LANES), BF16),
    ]

    def stage(away, pieces, sums):
        first = not sums
        start = 1 + len(pieces) + len(activations)
        return pl.pallas_call(
            functools.partial(stage_kernel, away, first),
            out_shape=[
                jax.ShapeDtypeStruct((tokens, SUMS * LANES), F32),
                jax.ShapeDtypeStruct((LANES, 2 * LANES), F32),
            ],
            in_specs=[SMEM] + [VMEM] * (len(pieces) + len(activations) + len(sums)),
            out_specs=[VMEM, VMEM],
            scratch_shapes=stage_scratch,
            input_output_aliases={} if first else {start: 0, start + 1: 1},
            compiler_params=params(16),
            cost_estimate=cost(tokens * rows * LANES * 16, 2 * MIB),
            name="stage",
        )(me.reshape(1), *pieces, *activations, *sums)

    def split(block, *tails):
        tail = block.shape[0] - 3 * rows
        shapes = (3 * rows, LANES), ((1 + len(tails)) * tail, LANES)
        return pl.pallas_call(
            split_kernel,
            out_shape=[jax.ShapeDtypeStruct(shape, BF16) for shape in shapes],
            in_specs=[VMEM] * (1 + len(tails)),
            out_specs=[VMEM, VMEM],
            compiler_params=params(8),
            name="split",
        )(block, *tails)

    half = RING_CHIPS // 2
    held = [own, other_core(own_late)]
    blocks = list(held)
    first, second = hop(own), hop(own_late, from_other=True)
    first, activations = tie((first, activations))
    sums = stage(0, held, [])
    second, sums = tie((second, sums))
    for k in range(1, half):
        held = [first, second]
        crossed = [other_core(first), other_core(second)]
        blocks += [first, crossed[0]]
        if k < half - 1:
            blocks += [second, crossed[1]]
        else:
            first, tails = split(first, tail)
        first = hop(first)
        sums = stage(k, held, sums)
        first, sums = tie((first, sums))
        if k == half - 2:
            second, tail = split(second)
        if k < half - 1:
            second = hop(second)
        sums = stage(-k, crossed, sums)
        if k < half - 1:
            second, sums = tie((second, sums))
    tails = hop(tails)
    small = (top_expander_sketch.T, top_reducer_sketch)
    unit = pl.pallas_call(
        functools.partial(feature_kernel, half),
        out_shape=jax.ShapeDtypeStruct((LANES, LANES), F32),
        in_specs=[SMEM] * 2 + [VMEM] * (2 + len(activations) + 3) + [HBM] * 2,
        out_specs=VMEM,
        scratch_shapes=stage_scratch
        + [pltpu.VMEM(a.shape, a.dtype) for a in small]
        + [pltpu.SemaphoreType.DMA((2,))],
        compiler_params=params(16),
        cost_estimate=cost(1, 1),
        name="features",
    )(
        me.reshape(1),
        sequence_token_counts,
        first,
        other_core(first),
        *activations,
        *sums,
        local,
        *in_hbm(small),
    )
    tails, unit = tie((tails, unit))
    blocks.append(tails)
    best = pl.pallas_call(
        functools.partial(score_kernel, len(blocks), count),
        out_shape=jax.ShapeDtypeStruct((2, TASKS, count, LANES), F32),
        in_specs=[VMEM] * (1 + len(blocks)),
        out_specs=VMEM,
        compiler_params=params(16),
        cost_estimate=cost(4 * MIB, 2 * MIB),
        name="scores",
    )(unit, *blocks)
    task_best, scores = pl.pallas_call(
        functools.partial(last_score_kernel, count),
        out_shape=(jax.ShapeDtypeStruct((2, TASKS), F32), jax.ShapeDtypeStruct((1, 2), F32)),
        in_specs=[VMEM] * 3,
        out_specs=(VMEM, VMEM),
        compiler_params=params(8),
        name="last_scores",
    )(unit, other_core(tails), best)
    return (scores.reshape(2), task_best)


def shards_of_any_slice(
    hidden_state_input,
    attention_mixed_state,
    hidden_state_adjoint,
    attention_values_adjoint,
    sequence_token_counts,
    heldout_sketched_signals,
    benchmark_labels,
    top_rmsnorm_weights,
    top_reducer_matrix,
    top_expander_matrix,
    bottom_reducer_matrix,
    bottom_expander_matrix,
    source_sketch,
    top_reducer_sketch,
    top_expander_sketch,
    top_target_sketch,
    bottom_reducer_sketch,
    bottom_expander_sketch,
    bottom_target_sketch,
    n,
):
    me = lax.axis_index("dp")
    x, mixed, adjoint, values = (
        hidden_state_input,
        attention_mixed_state,
        hidden_state_adjoint,
        attention_values_adjoint,
    )
    tokens, width = x.shape
    rows = top_reducer_matrix.shape[0]
    up_rows = top_expander_matrix.shape[1]
    rank = top_reducer_matrix.shape[1]
    k1 = source_sketch.shape[1]
    gain = top_rmsnorm_weights
    own_gain = lax.dynamic_slice_in_dim(gain, me * rows, rows)

    down_upper = (own_gain[:, None] * top_reducer_matrix.astype(F32)).astype(BF16)
    up_lower = mm(bottom_expander_matrix.T, bottom_reducer_sketch).astype(BF16)
    down_lower = mm(bottom_reducer_matrix, bottom_expander_sketch).astype(BF16)
    packed_lower = jnp.concatenate([down_lower[: rows // 2], down_lower[rows // 2 :]], axis=1)
    factors = jnp.concatenate([down_upper, up_lower, top_expander_matrix.T, packed_lower], axis=0)
    factors = lax.all_gather(factors, "dp")

    val_wide = heldout_sketched_signals.astype(F32)
    val_unit = (
        val_wide * lax.rsqrt(jnp.sum(val_wide * val_wide, axis=1, keepdims=True) + 1e-06)
    ).astype(BF16)
    labels = jnp.broadcast_to(benchmark_labels.astype(BF16), (val_unit.shape[0], 128))
    panel = jnp.concatenate([val_unit.reshape(-1, 128), labels], axis=0)
    panel = lax.all_gather(panel, "dp")
    val_rows = val_unit.shape[0]
    cut = panel.shape[1] - val_rows
    panel_tasks = panel[:, cut:, 0].reshape(n * val_rows, 1).astype(jnp.int32)
    panel = panel[:, :cut].reshape(n * val_rows, val_unit.shape[1])

    wide = x.astype(F32)
    inverse = lax.rsqrt(jnp.mean(wide * wide, axis=1, keepdims=True) + 1e-05)
    gained_sketch = (gain[:, None] * source_sketch.astype(F32)).astype(BF16)
    left_one = inverse * mm(x, gained_sketch)
    left_three = mm(mixed, source_sketch)
    right_two = ALPHA * mm(values, top_target_sketch)

    at = 0
    down_upper = factors[:, at : at + rows].reshape(width, rank)
    at += rows
    up_lower = factors[:, at : at + rows].reshape(width, -1)
    at += rows
    up_upper = factors[:, at : at + up_rows].reshape(-1, rank)
    at += up_rows
    down_lower = factors[:, at:]
    down_lower = jnp.concatenate([down_lower[:, :, :k1], down_lower[:, :, k1:]], axis=1)
    down_lower = down_lower.reshape(width, k1)

    reduced = inverse * mm(x, down_upper)
    left_two = mm(reduced.astype(BF16), top_expander_sketch)
    left_four = mm(mixed, down_lower)
    returned = mm(values, up_upper).astype(BF16)
    right_one = ALPHA * mm(returned, top_reducer_sketch)
    along = (ALPHA / width) * jnp.sum(returned.astype(F32) * reduced, axis=1, keepdims=True)
    targets = jnp.concatenate([up_lower, bottom_target_sketch], axis=1)
    bridge = mm_cols(down_upper, targets).astype(BF16)
    rights_low = mm(adjoint, targets) + inverse * (
        ALPHA * mm(returned, bridge) - (along * inverse) * mm(x, targets)
    )
    rights_low = ALPHA * rights_low
    k2 = up_lower.shape[1]
    lefts = (left_one, left_two, left_three, left_four)
    rights = (right_one, right_two, rights_low[:, :k2], rights_low[:, k2:])

    counts = sequence_token_counts[0]
    ends = jnp.cumsum(counts)
    starts = ends - counts
    places = jnp.arange(tokens, dtype=jnp.int32)[:, None]
    member = (places >= starts[None, :]) & (places < ends[None, :])
    count_ex = counts.shape[0]
    spread = jnp.concatenate(lefts, axis=0).astype(BF16)
    member = jnp.tile(member, (4, 1))
    spread = jnp.concatenate(
        [jnp.where(member[:, e : e + 1], spread, 0) for e in range(count_ex)], axis=1
    )
    feats = mm_cols(spread, jnp.concatenate(rights, axis=0).astype(BF16))
    feats = feats.reshape(count_ex, -1)
    squares = jnp.sum(feats * feats, axis=1, keepdims=True)
    unit_rows = (feats * lax.rsqrt(squares + 1e-06)).astype(BF16)

    score_scale = float(unit_rows.shape[1]) ** 0.5
    similar = score_scale * mm_rows(unit_rows, panel)
    task_mask = panel_tasks == jnp.arange(TASKS, dtype=jnp.int32)[None, :]
    task_best = jnp.max(
        jnp.where(task_mask[None, :, :], similar[:, :, None], -2.0 * score_scale), axis=1
    )
    return (jnp.mean(task_best, axis=1), task_best)


def solution(mesh):
    n = mesh.shape["dp"]
    split = P(("parts", "dp"), None)
    by_row, by_column, whole = P("dp", None), P(None, "dp"), P()
    placed = (
        (split,) * 5
        + (by_row, by_row, whole)
        + (by_row, by_column, by_row, by_column)
        + (whole,) * 7
    )
    ours = shards if n == 2 * RING_CHIPS else functools.partial(shards_of_any_slice, n=n)
    return jax.shard_map(
        ours,
        mesh=mesh,
        in_specs=placed,
        out_specs=(P(("parts", "dp")), split),
        check_vma=False,
    )
```

```python
import functools

import jax
import jax.numpy as jnp
from jax import lax
from jax.experimental import pallas as pl
from jax.experimental.pallas import tpu as pltpu
from jax.sharding import PartitionSpec as P

TASKS = 3
ALPHA = 4.0
F32 = jnp.float32
BF16 = jnp.bfloat16
RING_CHIPS = 8
LANES = 128
STEPS = 4
VALUES, V_TARGET, X_DOWN, X_LOW, J_LOW, J_TARGET, M_DOWN, M_SOURCE, SUMS = range(9)
INVERSE, LEFT_ONE, X_TARGET, LOCAL_SUMS = range(4)
MIB = 1 << 20


def mm(a, b):
    return jnp.dot(a, b, preferred_element_type=F32)


def mm_rows(a, b):
    return lax.dot_general(a, b, (((1,), (1,)), ((), ())), preferred_element_type=F32)


def mm_cols(a, b):
    return lax.dot_general(a, b, (((0,), (0,)), ((), ())), preferred_element_type=F32)


def ring_chip(pos):
    half = RING_CHIPS // 2
    return jnp.where(pos < half, 2 * pos, 2 * (RING_CHIPS - 1 - pos) + 1)


def ring_pos(chip):
    row, side = chip // 2, chip % 2
    return jnp.where(side == 0, row, RING_CHIPS - 1 - row)


def hop(value):
    half = RING_CHIPS // 2
    place = [2 * q if q < half else 2 * (RING_CHIPS - 1 - q) + 1 for q in range(RING_CHIPS)]
    pairs = []
    for q in range(RING_CHIPS):
        pairs.append((2 * place[q], 2 * place[(q + 1) % RING_CHIPS]))
        pairs.append((2 * place[q] + 1, 2 * place[(q - 1) % RING_CHIPS] + 1))
    return lax.ppermute(value, "dp", pairs)


def other_core(value):
    return lax.ppermute(value, "dp", [(d, d ^ 1) for d in range(2 * RING_CHIPS)])


def half_lanes(shape):
    return lax.broadcasted_iota(jnp.int32, shape, 1) < LANES // 2


def diagonal_column(row, first, count):
    shape = (count, row.shape[1])
    lane = lax.broadcasted_iota(jnp.int32, shape, 1)
    at = lax.broadcasted_iota(jnp.int32, shape, 0)
    return jnp.sum(jnp.where(lane == at + first, row, 0.0), axis=1, keepdims=True)


def load(pairs, sems):
    copies = [pltpu.make_async_copy(src, dst, sems.at[i]) for i, (src, dst) in enumerate(pairs)]
    for copy in copies:
        copy.start()
    return copies


def pack_kernel(me_ref, *refs):
    hbm, out_ref, held, sems = refs[:9], refs[9], refs[10:19], refs[19]
    gain_ref, down_up_ref, up_low_ref, sketch_ref, up_up_ref, down_low_ref, expand_ref, val_ref, label_ref = held
    copies = load(zip(hbm, held), sems)
    rows = down_up_ref.shape[0]
    half = LANES // 2
    for copy in copies:
        copy.wait()
    for b in range(rows // half):
        place = me_ref[0] * (rows // half) + b
        row = gain_ref[pl.ds(place // 2, 1), :]
        column = diagonal_column(row, (place % 2) * half, half)
        part = down_up_ref[pl.ds(b * half, half), :].astype(F32)
        out_ref[pl.ds(b * half, half), :] = (column * part).astype(BF16)
    at = rows
    out_ref[pl.ds(at, rows), :] = mm(up_low_ref[...], sketch_ref[...]).astype(BF16)
    at += rows
    out_ref[pl.ds(at, rows // 2), :] = up_up_ref[...]
    at += rows // 2
    expand = expand_ref[...]
    low = mm_rows(down_low_ref[...], jnp.concatenate([expand, expand], axis=0))
    first, second = low[: rows // 2], low[rows // 2 :]
    out_ref[pl.ds(at, rows // 2), :] = jnp.where(half_lanes(first.shape), first, second).astype(BF16)
    at += rows // 2
    wide = val_ref[...].astype(F32)
    count, width = wide.shape
    scale = lax.rsqrt(jnp.sum(wide * wide, axis=1, keepdims=True) + 1e-06)
    unit = wide * scale
    blocks = [unit[:, i * LANES : (i + 1) * LANES] for i in range(width // LANES)]
    row = label_ref[...].astype(F32)
    labels = jnp.broadcast_to(diagonal_column(row, 0, count), (count, LANES))
    blocks += [labels, labels]
    for i in range(0, len(blocks), 2):
        pair = jnp.concatenate(blocks[i : i + 2], axis=0)
        out_ref[pl.ds(at + i * count, 2 * count), :] = pair.astype(BF16)


def local_kernel(*refs):
    x_hbm, mixed_hbm, adjoint_hbm, values_hbm, target_hbm, top_target_hbm, gain_hbm, source_hbm = refs[:8]
    x_ref, mixed_ref, adjoint_ref, values_ref, target_ref, top_target_ref, turned_ref, sums_ref = refs[8:16]
    gain_ref, source_ref, sems = refs[16:]
    tokens, width = x_ref.shape
    span = width // STEPS
    copies = []
    for j in range(STEPS):
        part = pl.ds(j * span, span)
        pairs = (
            (gain_hbm.at[:, part], gain_ref.at[:, part]),
            (source_hbm.at[:, part], source_ref.at[:, part]),
            (x_hbm.at[:, part], x_ref.at[:, part]),
            (target_hbm.at[part], target_ref.at[part]),
        )
        copies.append(load(pairs, sems.at[j]))
    pairs = (
        (adjoint_hbm, adjoint_ref),
        (mixed_hbm, mixed_ref),
        (values_hbm, values_ref),
        (top_target_hbm, top_target_ref),
    )
    later = load(pairs, sems.at[STEPS])
    products = jnp.zeros((tokens, 2 * LANES), F32)
    squares = jnp.zeros((tokens, LANES), F32)
    for j in range(STEPS):
        for copy in copies[j]:
            copy.wait()
        part = slice(j * span, (j + 1) * span)
        x, source = x_ref[:, part], source_ref[:, part].astype(F32)
        gained = source * gain_ref[:, part]
        turned_ref[part, :] = jnp.concatenate([source, source], axis=0).T.astype(BF16)
        gained = jnp.concatenate([gained, gained], axis=0).T.astype(BF16)
        products = products + mm(x, jnp.concatenate([gained, target_ref[part, :]], axis=1))
        for i in range(span // LANES):
            wide = x[:, i * LANES : (i + 1) * LANES].astype(F32)
            squares = squares + wide * wide
    mean = jnp.sum(squares, axis=1, keepdims=True) * (1.0 / width)
    inverse = jnp.broadcast_to(lax.rsqrt(mean + 1e-05), (tokens, LANES))
    for i, value in enumerate((inverse, inverse * products[:, :LANES], products[:, LANES:])):
        sums_ref[:, i * LANES : (i + 1) * LANES] = value
    for copy in later:
        copy.wait()


def add_stage(away, me_ref, pieces, held, old, scratch):
    x_ref, mixed_ref, adjoint_ref, values_ref, target_ref, top_target_ref, source_ref = held
    both, up, down = scratch
    rows = both.shape[0] // 2
    half, pad = rows // 2, LANES // 2
    span = 2 * rows
    me = me_ref[0]
    pos, core = ring_pos(me // 2), me % 2
    chip = ring_chip((pos + away * (2 * core - 1) + RING_CHIPS) % RING_CHIPS)
    odd = chip % 2
    mine = pl.ds(pl.multiple_of(chip * span, LANES), span)
    values_start = (chip // 2) * span + odd * (rows - pad)
    values_part = pl.ds(pl.multiple_of(values_start, LANES), rows + pad)
    side = core if away >= 0 else 1 - core
    up[pl.ds(pl.multiple_of((1 - odd) * rows, 16), pad), :] = jnp.zeros((pad, 2 * LANES), BF16)
    up[pl.ds(pl.multiple_of(odd * pad, 16), rows), pl.ds(LANES, LANES)] = top_target_ref[
        pl.ds(pl.multiple_of(chip * rows, 16), rows), :
    ]
    for piece, c in ((pieces[0], side), (pieces[1], 1 - side)):
        one = pl.ds(pl.multiple_of(c * rows, 16), rows)
        both[one, pl.ds(0, LANES)] = piece[pl.ds(0, rows), :]
        both[one, pl.ds(LANES, LANES)] = piece[pl.ds(rows, rows), :]
        up[pl.ds(pl.multiple_of(odd * pad + c * half, 16), half), pl.ds(0, LANES)] = piece[
            pl.ds(2 * rows, half), :
        ]
        packed = piece[pl.ds(2 * rows + half, half), :].astype(F32)
        turned = pltpu.roll(packed, pad, 1)
        lower = half_lanes(packed.shape)
        down[pl.ds(pl.multiple_of(c * rows, 16), half), :] = jnp.where(lower, packed, turned).astype(BF16)
        down[pl.ds(pl.multiple_of(c * rows + half, 16), half), :] = jnp.where(lower, turned, packed).astype(BF16)

    weights = both[...]
    down_up = weights[:, :LANES]
    lows = jnp.concatenate([weights[:, LANES:], target_ref[mine, :]], axis=1)
    bridge = mm_cols(down_up, lows)
    products = []
    for activation, factor in (
        (values_ref[:, values_part], up[...]),
        (x_ref[:, mine], weights),
        (adjoint_ref[:, mine], lows),
        (mixed_ref[:, mine], jnp.concatenate([down[...], source_ref[mine, :]], axis=1)),
    ):
        product = mm(activation, factor)
        products += [product[:, :LANES], product[:, LANES:]]
    if old:
        old_sums, old_bridge = old
        products = [p + old_sums[:, i * LANES : (i + 1) * LANES] for i, p in enumerate(products)]
        bridge = bridge + old_bridge[...]
    return products, bridge


def stage_kernel(away, first, me_ref, *refs):
    pieces, held, old = refs[:2], refs[2:9], refs[9:-5]
    (new_sums, new_bridge), scratch = refs[-5:-3], refs[-3:]
    products, bridge = add_stage(away, me_ref, pieces, held, old, scratch)
    for i in range(SUMS):
        new_sums[:, i * LANES : (i + 1) * LANES] = products[i]
    new_bridge[...] = bridge


def feature_kernel(away, me_ref, counts_ref, *refs):
    pieces, held, old, local_ref, small_hbm, refs = refs[:2], refs[2:9], refs[9:11], refs[11], refs[12:14], refs[14:]
    out_ref, scratch, (expand_ref, sketch_ref, sems) = refs[0], refs[1:4], refs[4:]
    more = load(zip(small_hbm, (expand_ref, sketch_ref)), sems)
    products, bridge = add_stage(away, me_ref, pieces, held, old, scratch)
    local = [local_ref[:, i * LANES : (i + 1) * LANES] for i in range(LOCAL_SUMS)]
    tokens, width = held[0].shape
    half = LANES // 2
    for copy in more:
        copy.wait()
    inverse = local[INVERSE]
    returned = products[VALUES].astype(BF16)
    back = mm(returned, jnp.concatenate([bridge.astype(BF16), sketch_ref[...]], axis=1))
    right_one = ALPHA * back[:, 2 * LANES :]
    reduced = inverse * products[X_DOWN]
    expand = expand_ref[...]
    left_two = mm_rows(reduced.astype(BF16), jnp.concatenate([expand, expand], axis=0))
    along = (ALPHA / width) * jnp.sum(returned.astype(F32) * reduced, axis=1, keepdims=True)
    along = along * inverse
    right_three = products[J_LOW] + inverse * (ALPHA * back[:, :LANES] - along * products[X_LOW])
    right_four = products[J_TARGET] + inverse * (ALPHA * back[:, LANES : 2 * LANES] - along * local[X_TARGET])
    rights = (right_one, ALPHA * products[V_TARGET], ALPHA * right_three, ALPHA * right_four)
    lefts = (local[LEFT_ONE], left_two, products[M_SOURCE], products[M_DOWN])
    place = lax.broadcasted_iota(jnp.int32, (tokens, LANES), 0)
    one, two = counts_ref[0, 0], counts_ref[0, 1]
    lower = half_lanes((tokens, LANES))
    member = (place >= jnp.where(lower, 0, one)) & (place < jnp.where(lower, one, one + two))
    feats = jnp.zeros((LANES, LANES), F32)
    for left, right in zip(lefts, rights):
        feats = feats + mm_cols(jnp.where(member, left, 0.0).astype(BF16), right.astype(BF16))
    for e in range(2):
        own = feats[e * half : (e + 1) * half]
        squares = jnp.sum(own * own, keepdims=True)
        out_ref[pl.ds(e * half, half), :] = (own * lax.rsqrt(squares + 1e-06)).astype(BF16).astype(F32)


def split_kernel(block_ref, *refs):
    head_ref, tail_ref = refs[-2:]
    cut, tail = head_ref.shape[0], block_ref.shape[0] - head_ref.shape[0]
    head_ref[...] = block_ref[pl.ds(0, cut), :]
    if len(refs) == 3:
        tail_ref[pl.ds(0, tail), :] = refs[0][...]
    tail_ref[pl.ds(tail_ref.shape[0] - tail, tail), :] = block_ref[pl.ds(cut, tail), :]


def best_of(places, count, unit_ref, best):
    half = LANES // 2
    scale = float(half * LANES) ** 0.5
    shape = (count, LANES)
    totals = [[jnp.zeros(shape, F32) for _ in range(2)] for _ in places]
    for i in range(0, half, 2):
        units = [
            [jnp.broadcast_to(unit_ref[pl.ds(e * half + i + k, 1), :], shape) for k in range(2)]
            for e in range(2)
        ]
        for b, (block, start) in enumerate(places):
            wide = block[pl.ds(start + i * count, 2 * count), :].astype(F32)
            for e in range(2):
                totals[b][e] = totals[b][e] + (wide[:count] * units[e][0] + wide[count:] * units[e][1])
    for b, (block, start) in enumerate(places):
        labels = block[pl.ds(start + half * count, 2 * count), :].astype(F32)[:count]
        for e in range(2):
            similar = scale * jnp.sum(totals[b][e], axis=1, keepdims=True)
            for t in range(TASKS):
                best[e][t] = jnp.maximum(best[e][t], jnp.where(labels == float(t), similar, -2.0 * scale))


def places_of(blocks, count):
    size = (LANES // 2 + 2) * count
    places = []
    for block in blocks:
        total = block.shape[0]
        firsts = range(0, total, size) if total % size == 0 else [total - size]
        places += [(block, first) for first in firsts]
    return places


def score_kernel(blocks, count, unit_ref, *refs):
    block_refs, best_ref = refs[:blocks], refs[blocks]
    lowest = -2.0 * float(LANES // 2 * LANES) ** 0.5
    best = [[jnp.full((count, LANES), lowest, F32) for _ in range(TASKS)] for _ in range(2)]
    best_of(places_of(block_refs, count), count, unit_ref, best)
    for e in range(2):
        for t in range(TASKS):
            best_ref[e, t] = best[e][t]


def last_score_kernel(count, unit_ref, block_ref, best_ref, out_ref, mean_ref):
    best = [[best_ref[e, t] for t in range(TASKS)] for e in range(2)]
    best_of(places_of([block_ref], count), count, unit_ref, best)
    lane = lax.broadcasted_iota(jnp.int32, (1, LANES), 1)
    means = []
    for e in range(2):
        values = [jnp.max(best[e][t], axis=0, keepdims=True) for t in range(TASKS)]
        row = jnp.where(lane == 0, values[0], jnp.where(lane == 1, values[1], values[2]))
        out_ref[pl.ds(e, 1), :] = row[:, :TASKS]
        means.append((values[0] + values[1] + values[2]) * (1.0 / TASKS))
    mean_ref[...] = jnp.where(lane == 0, means[0], means[1])[:, :2]


VMEM = pl.BlockSpec(memory_space=pltpu.VMEM)
SMEM = pl.BlockSpec(memory_space=pltpu.SMEM)
ANY = pl.BlockSpec(memory_space=pl.ANY)
HBM = pl.BlockSpec(memory_space=pltpu.HBM)


def in_hbm(arrays):
    return [pltpu.with_memory_space_constraint(a, pltpu.HBM) for a in arrays]


def params(mib):
    return pltpu.CompilerParams(vmem_limit_bytes=mib * MIB)


def cost(flops, nbytes):
    return pl.CostEstimate(flops=flops, bytes_accessed=nbytes, transcendentals=0)


def shards(
    hidden_state_input,
    attention_mixed_state,
    hidden_state_adjoint,
    attention_values_adjoint,
    sequence_token_counts,
    heldout_sketched_signals,
    benchmark_labels,
    top_rmsnorm_weights,
    top_reducer_matrix,
    top_expander_matrix,
    bottom_reducer_matrix,
    bottom_expander_matrix,
    source_sketch,
    top_reducer_sketch,
    top_expander_sketch,
    top_target_sketch,
    bottom_reducer_sketch,
    bottom_expander_sketch,
    bottom_target_sketch,
):
    me = lax.axis_index("dp").astype(jnp.int32)
    x, mixed, adjoint, values = (
        hidden_state_input,
        attention_mixed_state,
        hidden_state_adjoint,
        attention_values_adjoint,
    )
    tokens, width = x.shape
    rows = top_reducer_matrix.shape[0]
    count = heldout_sketched_signals.shape[0]

    inputs = (
        top_rmsnorm_weights.reshape(width // LANES, LANES),
        top_reducer_matrix,
        bottom_expander_matrix.T,
        bottom_reducer_sketch,
        top_expander_matrix.T,
        bottom_reducer_matrix,
        bottom_expander_sketch.T,
        heldout_sketched_signals,
        benchmark_labels.T,
    )
    own = pl.pallas_call(
        pack_kernel,
        out_shape=jax.ShapeDtypeStruct((3 * rows + (LANES // 2 + 2) * count, LANES), BF16),
        in_specs=[SMEM] + [HBM] * len(inputs),
        out_specs=VMEM,
        scratch_shapes=[pltpu.VMEM(a.shape, a.dtype) for a in inputs]
        + [pltpu.SemaphoreType.DMA((len(inputs),))],
        compiler_params=params(8),
        name="pack",
    )(me.reshape(1), *in_hbm(inputs))

    inputs = (
        x,
        mixed,
        adjoint,
        values,
        bottom_target_sketch,
        top_target_sketch,
        top_rmsnorm_weights.reshape(1, width),
        source_sketch.T,
    )
    *activations, local = pl.pallas_call(
        local_kernel,
        out_shape=[jax.ShapeDtypeStruct(a.shape, a.dtype) for a in inputs[:6]]
        + [
            jax.ShapeDtypeStruct((width, LANES), BF16),
            jax.ShapeDtypeStruct((tokens, LOCAL_SUMS * LANES), F32),
        ],
        in_specs=[HBM] * len(inputs),
        out_specs=[VMEM] * 8,
        scratch_shapes=[pltpu.VMEM(a.shape, a.dtype) for a in inputs[6:]]
        + [pltpu.SemaphoreType.DMA((STEPS + 1, 4))],
        compiler_params=params(24),
        cost_estimate=cost(tokens * width * LANES * 6, 14 * MIB),
        name="local_products",
    )(*in_hbm(inputs))

    stage_scratch = [
        pltpu.VMEM((2 * rows, 2 * LANES), BF16),
        pltpu.VMEM((rows + LANES // 2, 2 * LANES), BF16),
        pltpu.VMEM((2 * rows, LANES), BF16),
    ]

    def stage(away, pieces, sums):
        first = not sums
        start = 1 + len(pieces) + len(activations)
        return pl.pallas_call(
            functools.partial(stage_kernel, away, first),
            out_shape=[
                jax.ShapeDtypeStruct((tokens, SUMS * LANES), F32),
                jax.ShapeDtypeStruct((LANES, 2 * LANES), F32),
            ],
            in_specs=[SMEM] + [VMEM] * (len(pieces) + len(activations) + len(sums)),
            out_specs=[VMEM, VMEM],
            scratch_shapes=stage_scratch,
            input_output_aliases={} if first else {start: 0, start + 1: 1},
            compiler_params=params(16),
            cost_estimate=cost(tokens * rows * LANES * 16, 2 * MIB),
            name="stage",
        )(me.reshape(1), *pieces, *activations, *sums)

    def split(block, *tails):
        tail = block.shape[0] - 3 * rows
        shapes = (3 * rows, LANES), ((1 + len(tails)) * tail, LANES)
        return pl.pallas_call(
            split_kernel,
            out_shape=[jax.ShapeDtypeStruct(shape, BF16) for shape in shapes],
            in_specs=[VMEM] * (1 + len(tails)),
            out_specs=[VMEM, VMEM],
            compiler_params=params(8),
            name="split",
        )(block, *tails)

    tie = lax.optimization_barrier
    half = RING_CHIPS // 2
    held = [own, other_core(own)]
    blocks = list(held)
    first, second = hop(held[0]), hop(held[1])
    first, activations = tie((first, activations))
    sums = stage(0, held, [])
    second, sums = tie((second, sums))
    for k in range(1, half):
        held = [first, second]
        crossed = [other_core(first), other_core(second)]
        blocks += [first, crossed[0]]
        if k < half - 1:
            blocks += [second, crossed[1]]
        else:
            first, tails = split(first, tail)
            tails, sums = tie((tails, sums))
        first = hop(first)
        sums = stage(k, held, sums)
        first, sums = tie((first, sums))
        if k == half - 2:
            second, tail = split(second)
        if k < half - 1:
            second = hop(second)
        sums = stage(-k, crossed, sums)
        if k < half - 1:
            second, sums = tie((second, sums))
    tails = hop(tails)
    small = (top_expander_sketch.T, top_reducer_sketch)
    unit = pl.pallas_call(
        functools.partial(feature_kernel, half),
        out_shape=jax.ShapeDtypeStruct((LANES, LANES), F32),
        in_specs=[SMEM] * 2 + [VMEM] * (2 + len(activations) + 3) + [HBM] * 2,
        out_specs=VMEM,
        scratch_shapes=stage_scratch
        + [pltpu.VMEM(a.shape, a.dtype) for a in small]
        + [pltpu.SemaphoreType.DMA((2,))],
        compiler_params=params(16),
        cost_estimate=cost(1, 1),
        name="features",
    )(
        me.reshape(1),
        sequence_token_counts,
        first,
        other_core(first),
        *activations,
        *sums,
        local,
        *in_hbm(small),
    )
    tails, unit = tie((tails, unit))
    blocks.append(tails)
    best = pl.pallas_call(
        functools.partial(score_kernel, len(blocks), count),
        out_shape=jax.ShapeDtypeStruct((2, TASKS, count, LANES), F32),
        in_specs=[VMEM] * (1 + len(blocks)),
        out_specs=VMEM,
        compiler_params=params(16),
        cost_estimate=cost(4 * MIB, 2 * MIB),
        name="scores",
    )(unit, *blocks)
    task_best, scores = pl.pallas_call(
        functools.partial(last_score_kernel, count),
        out_shape=(jax.ShapeDtypeStruct((2, TASKS), F32), jax.ShapeDtypeStruct((1, 2), F32)),
        in_specs=[VMEM] * 3,
        out_specs=(VMEM, VMEM),
        compiler_params=params(8),
        name="last_scores",
    )(unit, other_core(tails), best)
    return (scores.reshape(2), task_best)


def shards_of_any_slice(
    hidden_state_input,
    attention_mixed_state,
    hidden_state_adjoint,
    attention_values_adjoint,
    sequence_token_counts,
    heldout_sketched_signals,
    benchmark_labels,
    top_rmsnorm_weights,
    top_reducer_matrix,
    top_expander_matrix,
    bottom_reducer_matrix,
    bottom_expander_matrix,
    source_sketch,
    top_reducer_sketch,
    top_expander_sketch,
    top_target_sketch,
    bottom_reducer_sketch,
    bottom_expander_sketch,
    bottom_target_sketch,
    n,
):
    me = lax.axis_index("dp")
    x, mixed, adjoint, values = (
        hidden_state_input,
        attention_mixed_state,
        hidden_state_adjoint,
        attention_values_adjoint,
    )
    tokens, width = x.shape
    rows = top_reducer_matrix.shape[0]
    up_rows = top_expander_matrix.shape[1]
    rank = top_reducer_matrix.shape[1]
    k1 = source_sketch.shape[1]
    gain = top_rmsnorm_weights
    own_gain = lax.dynamic_slice_in_dim(gain, me * rows, rows)

    down_upper = (own_gain[:, None] * top_reducer_matrix.astype(F32)).astype(BF16)
    up_lower = mm(bottom_expander_matrix.T, bottom_reducer_sketch).astype(BF16)
    down_lower = mm(bottom_reducer_matrix, bottom_expander_sketch).astype(BF16)
    packed_lower = jnp.concatenate([down_lower[: rows // 2], down_lower[rows // 2 :]], axis=1)
    factors = jnp.concatenate([down_upper, up_lower, top_expander_matrix.T, packed_lower], axis=0)
    factors = lax.all_gather(factors, "dp")

    val_wide = heldout_sketched_signals.astype(F32)
    val_unit = (
        val_wide * lax.rsqrt(jnp.sum(val_wide * val_wide, axis=1, keepdims=True) + 1e-06)
    ).astype(BF16)
    labels = jnp.broadcast_to(benchmark_labels.astype(BF16), (val_unit.shape[0], 128))
    panel = jnp.concatenate([val_unit.reshape(-1, 128), labels], axis=0)
    panel = lax.all_gather(panel, "dp")
    val_rows = val_unit.shape[0]
    cut = panel.shape[1] - val_rows
    panel_tasks = panel[:, cut:, 0].reshape(n * val_rows, 1).astype(jnp.int32)
    panel = panel[:, :cut].reshape(n * val_rows, val_unit.shape[1])

    wide = x.astype(F32)
    inverse = lax.rsqrt(jnp.mean(wide * wide, axis=1, keepdims=True) + 1e-05)
    gained_sketch = (gain[:, None] * source_sketch.astype(F32)).astype(BF16)
    left_one = inverse * mm(x, gained_sketch)
    left_three = mm(mixed, source_sketch)
    right_two = ALPHA * mm(values, top_target_sketch)

    at = 0
    down_upper = factors[:, at : at + rows].reshape(width, rank)
    at += rows
    up_lower = factors[:, at : at + rows].reshape(width, -1)
    at += rows
    up_upper = factors[:, at : at + up_rows].reshape(-1, rank)
    at += up_rows
    down_lower = factors[:, at:]
    down_lower = jnp.concatenate([down_lower[:, :, :k1], down_lower[:, :, k1:]], axis=1)
    down_lower = down_lower.reshape(width, k1)

    reduced = inverse * mm(x, down_upper)
    left_two = mm(reduced.astype(BF16), top_expander_sketch)
    left_four = mm(mixed, down_lower)
    returned = mm(values, up_upper).astype(BF16)
    right_one = ALPHA * mm(returned, top_reducer_sketch)
    along = (ALPHA / width) * jnp.sum(returned.astype(F32) * reduced, axis=1, keepdims=True)
    targets = jnp.concatenate([up_lower, bottom_target_sketch], axis=1)
    bridge = mm_cols(down_upper, targets).astype(BF16)
    rights_low = mm(adjoint, targets) + inverse * (
        ALPHA * mm(returned, bridge) - (along * inverse) * mm(x, targets)
    )
    rights_low = ALPHA * rights_low
    k2 = up_lower.shape[1]
    lefts = (left_one, left_two, left_three, left_four)
    rights = (right_one, right_two, rights_low[:, :k2], rights_low[:, k2:])

    counts = sequence_token_counts[0]
    ends = jnp.cumsum(counts)
    starts = ends - counts
    places = jnp.arange(tokens, dtype=jnp.int32)[:, None]
    member = (places >= starts[None, :]) & (places < ends[None, :])
    count_ex = counts.shape[0]
    spread = jnp.concatenate(lefts, axis=0).astype(BF16)
    member = jnp.tile(member, (4, 1))
    spread = jnp.concatenate(
        [jnp.where(member[:, e : e + 1], spread, 0) for e in range(count_ex)], axis=1
    )
    feats = mm_cols(spread, jnp.concatenate(rights, axis=0).astype(BF16))
    feats = feats.reshape(count_ex, -1)
    squares = jnp.sum(feats * feats, axis=1, keepdims=True)
    unit_rows = (feats * lax.rsqrt(squares + 1e-06)).astype(BF16)

    score_scale = float(unit_rows.shape[1]) ** 0.5
    similar = score_scale * mm_rows(unit_rows, panel)
    task_mask = panel_tasks == jnp.arange(TASKS, dtype=jnp.int32)[None, :]
    task_best = jnp.max(
        jnp.where(task_mask[None, :, :], similar[:, :, None], -2.0 * score_scale), axis=1
    )
    return (jnp.mean(task_best, axis=1), task_best)


def solution(mesh):
    n = mesh.shape["dp"]
    split = P(("parts", "dp"), None)
    by_row, by_column, whole = P("dp", None), P(None, "dp"), P()
    placed = (
        (split,) * 5
        + (by_row, by_row, whole)
        + (by_row, by_column, by_row, by_column)
        + (whole,) * 7
    )
    ours = shards if n == 2 * RING_CHIPS else functools.partial(shards_of_any_slice, n=n)
    return jax.shard_map(
        ours,
        mesh=mesh,
        in_specs=placed,
        out_specs=(P(("parts", "dp")), split),
        check_vma=False,
    )
```

```python
import functools

import jax
import jax.numpy as jnp
from jax import lax
from jax.experimental import pallas as pl
from jax.experimental.pallas import tpu as pltpu
from jax.sharding import PartitionSpec as P

TASKS = 3
ALPHA = 4.0
F32 = jnp.float32
BF16 = jnp.bfloat16
RING_CHIPS = 8
LANES = 128
STEPS = 4
VALUES, V_TARGET, X_DOWN, X_LOW, J_LOW, J_TARGET, M_DOWN, M_SOURCE, SUMS = range(9)
INVERSE, LEFT_ONE, X_TARGET, LOCAL_SUMS = range(4)
MIB = 1 << 20


def mm(a, b):
    return jnp.dot(a, b, preferred_element_type=F32)


def mm_rows(a, b):
    return lax.dot_general(a, b, (((1,), (1,)), ((), ())), preferred_element_type=F32)


def mm_cols(a, b):
    return lax.dot_general(a, b, (((0,), (0,)), ((), ())), preferred_element_type=F32)


def ring_chip(pos):
    half = RING_CHIPS // 2
    return jnp.where(pos < half, 2 * pos, 2 * (RING_CHIPS - 1 - pos) + 1)


def ring_pos(chip):
    row, side = chip // 2, chip % 2
    return jnp.where(side == 0, row, RING_CHIPS - 1 - row)


def hop(value):
    half = RING_CHIPS // 2
    place = [2 * q if q < half else 2 * (RING_CHIPS - 1 - q) + 1 for q in range(RING_CHIPS)]
    pairs = []
    for q in range(RING_CHIPS):
        pairs.append((2 * place[q], 2 * place[(q + 1) % RING_CHIPS]))
        pairs.append((2 * place[q] + 1, 2 * place[(q - 1) % RING_CHIPS] + 1))
    return lax.ppermute(value, "dp", pairs)


def other_core(value):
    return lax.ppermute(value, "dp", [(d, d ^ 1) for d in range(2 * RING_CHIPS)])


def half_lanes(shape):
    return lax.broadcasted_iota(jnp.int32, shape, 1) < LANES // 2


def diagonal_column(row, first, count):
    shape = (count, row.shape[1])
    lane = lax.broadcasted_iota(jnp.int32, shape, 1)
    at = lax.broadcasted_iota(jnp.int32, shape, 0)
    return jnp.sum(jnp.where(lane == at + first, row, 0.0), axis=1, keepdims=True)


def load(pairs, sems):
    copies = [pltpu.make_async_copy(src, dst, sems.at[i]) for i, (src, dst) in enumerate(pairs)]
    for copy in copies:
        copy.start()
    return copies


def pack_kernel(me_ref, *refs):
    up_up_hbm, hbm, out_ref, held, sems = refs[0], refs[1:9], refs[9], refs[10:18], refs[18]
    val_ref, down_up_ref, up_low_ref, down_low_ref, gain_ref, sketch_ref, expand_ref, label_ref = held
    rows = down_up_ref.shape[0]
    half = LANES // 2
    direct = (up_up_hbm, out_ref.at[pl.ds(2 * rows, rows // 2)])
    for copy in load((*zip(hbm, held), direct), sems):
        copy.wait()
    for b in range(rows // half):
        place = me_ref[0] * (rows // half) + b
        row = gain_ref[pl.ds(place // 2, 1), :]
        column = diagonal_column(row, (place % 2) * half, half)
        part = down_up_ref[pl.ds(b * half, half), :].astype(F32)
        out_ref[pl.ds(b * half, half), :] = (column * part).astype(BF16)
    at = rows
    out_ref[pl.ds(at, rows), :] = mm(up_low_ref[...], sketch_ref[...]).astype(BF16)
    at += rows + rows // 2
    expand = expand_ref[...]
    low = mm_rows(down_low_ref[...], jnp.concatenate([expand, expand], axis=0))
    first, second = low[: rows // 2], low[rows // 2 :]
    out_ref[pl.ds(at, rows // 2), :] = jnp.where(half_lanes(first.shape), first, second).astype(BF16)
    at += rows // 2
    wide = val_ref[...].astype(F32)
    count, width = wide.shape
    scale = lax.rsqrt(jnp.sum(wide * wide, axis=1, keepdims=True) + 1e-06)
    unit = wide * scale
    blocks = [unit[:, i * LANES : (i + 1) * LANES] for i in range(width // LANES)]
    row = label_ref[...].astype(F32)
    labels = jnp.broadcast_to(diagonal_column(row, 0, count), (count, LANES))
    blocks += [labels, labels]
    for i in range(0, len(blocks), 2):
        pair = jnp.concatenate(blocks[i : i + 2], axis=0)
        out_ref[pl.ds(at + i * count, 2 * count), :] = pair.astype(BF16)


def local_kernel(*refs):
    x_hbm, mixed_hbm, adjoint_hbm, values_hbm, target_hbm, top_target_hbm, gain_hbm, source_hbm = refs[:8]
    x_ref, mixed_ref, adjoint_ref, values_ref, target_ref, top_target_ref, turned_ref, sums_ref = refs[8:16]
    gain_ref, source_ref, sems = refs[16:]
    tokens, width = x_ref.shape
    span = width // STEPS
    copies = []
    for j in range(STEPS):
        part = pl.ds(j * span, span)
        pairs = (
            (gain_hbm.at[:, part], gain_ref.at[:, part]),
            (source_hbm.at[:, part], source_ref.at[:, part]),
            (x_hbm.at[:, part], x_ref.at[:, part]),
            (target_hbm.at[part], target_ref.at[part]),
        )
        copies.append(load(pairs, sems.at[j]))
    pairs = (
        (adjoint_hbm, adjoint_ref),
        (mixed_hbm, mixed_ref),
        (values_hbm, values_ref),
        (top_target_hbm, top_target_ref),
    )
    later = load(pairs, sems.at[STEPS])
    products = jnp.zeros((tokens, 2 * LANES), F32)
    squares = jnp.zeros((tokens, LANES), F32)
    for j in range(STEPS):
        for copy in copies[j]:
            copy.wait()
        part = slice(j * span, (j + 1) * span)
        x, source = x_ref[:, part], source_ref[:, part].astype(F32)
        gained = source * gain_ref[:, part]
        turned_ref[part, :] = jnp.concatenate([source, source], axis=0).T.astype(BF16)
        gained = jnp.concatenate([gained, gained], axis=0).T.astype(BF16)
        products = products + mm(x, jnp.concatenate([gained, target_ref[part, :]], axis=1))
        for i in range(span // LANES):
            wide = x[:, i * LANES : (i + 1) * LANES].astype(F32)
            squares = squares + wide * wide
    mean = jnp.sum(squares, axis=1, keepdims=True) * (1.0 / width)
    inverse = jnp.broadcast_to(lax.rsqrt(mean + 1e-05), (tokens, LANES))
    for i, value in enumerate((inverse, inverse * products[:, :LANES], products[:, LANES:])):
        sums_ref[:, i * LANES : (i + 1) * LANES] = value
    for copy in later:
        copy.wait()


def add_stage(away, me_ref, pieces, held, old, scratch):
    x_ref, mixed_ref, adjoint_ref, values_ref, target_ref, top_target_ref, source_ref = held
    both, up, down = scratch
    rows = both.shape[0] // 2
    half, pad = rows // 2, LANES // 2
    span = 2 * rows
    me = me_ref[0]
    pos, core = ring_pos(me // 2), me % 2
    chip = ring_chip((pos + away * (2 * core - 1) + RING_CHIPS) % RING_CHIPS)
    odd = chip % 2
    mine = pl.ds(pl.multiple_of(chip * span, LANES), span)
    values_start = (chip // 2) * span + odd * (rows - pad)
    values_part = pl.ds(pl.multiple_of(values_start, LANES), rows + pad)
    side = core if away >= 0 else 1 - core
    up[pl.ds(pl.multiple_of((1 - odd) * rows, 16), pad), :] = jnp.zeros((pad, 2 * LANES), BF16)
    up[pl.ds(pl.multiple_of(odd * pad, 16), rows), pl.ds(LANES, LANES)] = top_target_ref[
        pl.ds(pl.multiple_of(chip * rows, 16), rows), :
    ]
    for piece, c in ((pieces[0], side), (pieces[1], 1 - side)):
        one = pl.ds(pl.multiple_of(c * rows, 16), rows)
        both[one, pl.ds(0, LANES)] = piece[pl.ds(0, rows), :]
        both[one, pl.ds(LANES, LANES)] = piece[pl.ds(rows, rows), :]
        up[pl.ds(pl.multiple_of(odd * pad + c * half, 16), half), pl.ds(0, LANES)] = piece[
            pl.ds(2 * rows, half), :
        ]
        packed = piece[pl.ds(2 * rows + half, half), :].astype(F32)
        turned = pltpu.roll(packed, pad, 1)
        lower = half_lanes(packed.shape)
        down[pl.ds(pl.multiple_of(c * rows, 16), half), :] = jnp.where(lower, packed, turned).astype(BF16)
        down[pl.ds(pl.multiple_of(c * rows + half, 16), half), :] = jnp.where(lower, turned, packed).astype(BF16)

    weights = both[...]
    down_up = weights[:, :LANES]
    lows = jnp.concatenate([weights[:, LANES:], target_ref[mine, :]], axis=1)
    bridge = mm_cols(down_up, lows)
    products = []
    for activation, factor in (
        (values_ref[:, values_part], up[...]),
        (x_ref[:, mine], weights),
        (adjoint_ref[:, mine], lows),
        (mixed_ref[:, mine], jnp.concatenate([down[...], source_ref[mine, :]], axis=1)),
    ):
        product = mm(activation, factor)
        products += [product[:, :LANES], product[:, LANES:]]
    if old:
        old_sums, old_bridge = old
        products = [p + old_sums[:, i * LANES : (i + 1) * LANES] for i, p in enumerate(products)]
        bridge = bridge + old_bridge[...]
    return products, bridge


def stage_kernel(away, first, me_ref, *refs):
    pieces, held, old = refs[:2], refs[2:9], refs[9:-5]
    (new_sums, new_bridge), scratch = refs[-5:-3], refs[-3:]
    products, bridge = add_stage(away, me_ref, pieces, held, old, scratch)
    for i in range(SUMS):
        new_sums[:, i * LANES : (i + 1) * LANES] = products[i]
    new_bridge[...] = bridge


def feature_kernel(away, me_ref, counts_ref, *refs):
    pieces, held, old, local_ref, small_hbm, refs = refs[:2], refs[2:9], refs[9:11], refs[11], refs[12:14], refs[14:]
    out_ref, scratch, (expand_ref, sketch_ref, sems) = refs[0], refs[1:4], refs[4:]
    more = load(zip(small_hbm, (expand_ref, sketch_ref)), sems)
    products, bridge = add_stage(away, me_ref, pieces, held, old, scratch)
    local = [local_ref[:, i * LANES : (i + 1) * LANES] for i in range(LOCAL_SUMS)]
    tokens, width = held[0].shape
    half = LANES // 2
    for copy in more:
        copy.wait()
    inverse = local[INVERSE]
    returned = products[VALUES].astype(BF16)
    back = mm(returned, jnp.concatenate([bridge.astype(BF16), sketch_ref[...]], axis=1))
    right_one = ALPHA * back[:, 2 * LANES :]
    reduced = inverse * products[X_DOWN]
    expand = expand_ref[...]
    left_two = mm_rows(reduced.astype(BF16), jnp.concatenate([expand, expand], axis=0))
    along = (ALPHA / width) * jnp.sum(returned.astype(F32) * reduced, axis=1, keepdims=True)
    along = along * inverse
    right_three = products[J_LOW] + inverse * (ALPHA * back[:, :LANES] - along * products[X_LOW])
    right_four = products[J_TARGET] + inverse * (ALPHA * back[:, LANES : 2 * LANES] - along * local[X_TARGET])
    rights = (right_one, ALPHA * products[V_TARGET], ALPHA * right_three, ALPHA * right_four)
    lefts = (local[LEFT_ONE], left_two, products[M_SOURCE], products[M_DOWN])
    place = lax.broadcasted_iota(jnp.int32, (tokens, LANES), 0)
    one, two = counts_ref[0, 0], counts_ref[0, 1]
    lower = half_lanes((tokens, LANES))
    member = (place >= jnp.where(lower, 0, one)) & (place < jnp.where(lower, one, one + two))
    feats = jnp.zeros((LANES, LANES), F32)
    for left, right in zip(lefts, rights):
        feats = feats + mm_cols(jnp.where(member, left, 0.0).astype(BF16), right.astype(BF16))
    for e in range(2):
        own = feats[e * half : (e + 1) * half]
        squares = jnp.sum(own * own, keepdims=True)
        out_ref[pl.ds(e * half, half), :] = (own * lax.rsqrt(squares + 1e-06)).astype(BF16).astype(F32)


def split_kernel(block_ref, *refs):
    head_ref, tail_ref = refs[-2:]
    cut, tail = head_ref.shape[0], block_ref.shape[0] - head_ref.shape[0]
    head_ref[...] = block_ref[pl.ds(0, cut), :]
    if len(refs) == 3:
        tail_ref[pl.ds(0, tail), :] = refs[0][...]
    tail_ref[pl.ds(tail_ref.shape[0] - tail, tail), :] = block_ref[pl.ds(cut, tail), :]


def best_of(places, count, unit_ref, best):
    half = LANES // 2
    scale = float(half * LANES) ** 0.5
    shape = (count, LANES)
    totals = [[jnp.zeros(shape, F32) for _ in range(2)] for _ in places]
    for i in range(0, half, 2):
        units = [
            [jnp.broadcast_to(unit_ref[pl.ds(e * half + i + k, 1), :], shape) for k in range(2)]
            for e in range(2)
        ]
        for b, (block, start) in enumerate(places):
            wide = block[pl.ds(start + i * count, 2 * count), :].astype(F32)
            for e in range(2):
                totals[b][e] = totals[b][e] + (wide[:count] * units[e][0] + wide[count:] * units[e][1])
    for b, (block, start) in enumerate(places):
        labels = block[pl.ds(start + half * count, 2 * count), :].astype(F32)[:count]
        for e in range(2):
            similar = scale * jnp.sum(totals[b][e], axis=1, keepdims=True)
            for t in range(TASKS):
                best[e][t] = jnp.maximum(best[e][t], jnp.where(labels == float(t), similar, -2.0 * scale))


def places_of(blocks, count):
    size = (LANES // 2 + 2) * count
    places = []
    for block in blocks:
        total = block.shape[0]
        firsts = range(0, total, size) if total % size == 0 else [total - size]
        places += [(block, first) for first in firsts]
    return places


def score_kernel(blocks, count, unit_ref, *refs):
    block_refs, best_ref = refs[:blocks], refs[blocks]
    lowest = -2.0 * float(LANES // 2 * LANES) ** 0.5
    best = [[jnp.full((count, LANES), lowest, F32) for _ in range(TASKS)] for _ in range(2)]
    best_of(places_of(block_refs, count), count, unit_ref, best)
    for e in range(2):
        for t in range(TASKS):
            best_ref[e, t] = best[e][t]


def last_score_kernel(count, unit_ref, block_ref, best_ref, out_ref, mean_ref):
    best = [[best_ref[e, t] for t in range(TASKS)] for e in range(2)]
    best_of(places_of([block_ref], count), count, unit_ref, best)
    lane = lax.broadcasted_iota(jnp.int32, (1, LANES), 1)
    means = []
    for e in range(2):
        values = [jnp.max(best[e][t], axis=0, keepdims=True) for t in range(TASKS)]
        row = jnp.where(lane == 0, values[0], jnp.where(lane == 1, values[1], values[2]))
        out_ref[pl.ds(e, 1), :] = row[:, :TASKS]
        means.append((values[0] + values[1] + values[2]) * (1.0 / TASKS))
    mean_ref[...] = jnp.where(lane == 0, means[0], means[1])[:, :2]


VMEM = pl.BlockSpec(memory_space=pltpu.VMEM)
SMEM = pl.BlockSpec(memory_space=pltpu.SMEM)
ANY = pl.BlockSpec(memory_space=pl.ANY)
HBM = pl.BlockSpec(memory_space=pltpu.HBM)


def in_hbm(arrays):
    return [pltpu.with_memory_space_constraint(a, pltpu.HBM) for a in arrays]


def params(mib):
    return pltpu.CompilerParams(vmem_limit_bytes=mib * MIB)


def cost(flops, nbytes):
    return pl.CostEstimate(flops=flops, bytes_accessed=nbytes, transcendentals=0)


def shards(
    hidden_state_input,
    attention_mixed_state,
    hidden_state_adjoint,
    attention_values_adjoint,
    sequence_token_counts,
    heldout_sketched_signals,
    benchmark_labels,
    top_rmsnorm_weights,
    top_reducer_matrix,
    top_expander_matrix,
    bottom_reducer_matrix,
    bottom_expander_matrix,
    source_sketch,
    top_reducer_sketch,
    top_expander_sketch,
    top_target_sketch,
    bottom_reducer_sketch,
    bottom_expander_sketch,
    bottom_target_sketch,
):
    me = lax.axis_index("dp").astype(jnp.int32)
    x, mixed, adjoint, values = (
        hidden_state_input,
        attention_mixed_state,
        hidden_state_adjoint,
        attention_values_adjoint,
    )
    tokens, width = x.shape
    rows = top_reducer_matrix.shape[0]
    count = heldout_sketched_signals.shape[0]

    inputs = (
        top_expander_matrix.T,
        heldout_sketched_signals,
        top_reducer_matrix,
        bottom_expander_matrix.T,
        bottom_reducer_matrix,
        top_rmsnorm_weights.reshape(width // LANES, LANES),
        bottom_reducer_sketch,
        bottom_expander_sketch.T,
        benchmark_labels.T,
    )
    own = pl.pallas_call(
        pack_kernel,
        out_shape=jax.ShapeDtypeStruct((3 * rows + (LANES // 2 + 2) * count, LANES), BF16),
        in_specs=[SMEM] + [HBM] * len(inputs),
        out_specs=VMEM,
        scratch_shapes=[pltpu.VMEM(a.shape, a.dtype) for a in inputs[1:]]
        + [pltpu.SemaphoreType.DMA((len(inputs),))],
        compiler_params=params(8),
        name="pack",
    )(me.reshape(1), *in_hbm(inputs))

    inputs = (
        x,
        mixed,
        adjoint,
        values,
        bottom_target_sketch,
        top_target_sketch,
        top_rmsnorm_weights.reshape(1, width),
        source_sketch.T,
    )
    *activations, local = pl.pallas_call(
        local_kernel,
        out_shape=[jax.ShapeDtypeStruct(a.shape, a.dtype) for a in inputs[:6]]
        + [
            jax.ShapeDtypeStruct((width, LANES), BF16),
            jax.ShapeDtypeStruct((tokens, LOCAL_SUMS * LANES), F32),
        ],
        in_specs=[HBM] * len(inputs),
        out_specs=[VMEM] * 8,
        scratch_shapes=[pltpu.VMEM(a.shape, a.dtype) for a in inputs[6:]]
        + [pltpu.SemaphoreType.DMA((STEPS + 1, 4))],
        compiler_params=params(24),
        cost_estimate=cost(tokens * width * LANES * 6, 14 * MIB),
        name="local_products",
    )(*in_hbm(inputs))

    stage_scratch = [
        pltpu.VMEM((2 * rows, 2 * LANES), BF16),
        pltpu.VMEM((rows + LANES // 2, 2 * LANES), BF16),
        pltpu.VMEM((2 * rows, LANES), BF16),
    ]

    def stage(away, pieces, sums):
        first = not sums
        start = 1 + len(pieces) + len(activations)
        return pl.pallas_call(
            functools.partial(stage_kernel, away, first),
            out_shape=[
                jax.ShapeDtypeStruct((tokens, SUMS * LANES), F32),
                jax.ShapeDtypeStruct((LANES, 2 * LANES), F32),
            ],
            in_specs=[SMEM] + [VMEM] * (len(pieces) + len(activations) + len(sums)),
            out_specs=[VMEM, VMEM],
            scratch_shapes=stage_scratch,
            input_output_aliases={} if first else {start: 0, start + 1: 1},
            compiler_params=params(16),
            cost_estimate=cost(tokens * rows * LANES * 16, 2 * MIB),
            name="stage",
        )(me.reshape(1), *pieces, *activations, *sums)

    def split(block, *tails):
        tail = block.shape[0] - 3 * rows
        shapes = (3 * rows, LANES), ((1 + len(tails)) * tail, LANES)
        return pl.pallas_call(
            split_kernel,
            out_shape=[jax.ShapeDtypeStruct(shape, BF16) for shape in shapes],
            in_specs=[VMEM] * (1 + len(tails)),
            out_specs=[VMEM, VMEM],
            compiler_params=params(8),
            name="split",
        )(block, *tails)

    tie = lax.optimization_barrier
    half = RING_CHIPS // 2
    held = [own, other_core(own)]
    blocks = list(held)
    first, second = hop(held[0]), hop(held[1])
    first, activations = tie((first, activations))
    sums = stage(0, held, [])
    second, sums = tie((second, sums))
    for k in range(1, half):
        held = [first, second]
        crossed = [other_core(first), other_core(second)]
        blocks += [first, crossed[0]]
        if k < half - 1:
            blocks += [second, crossed[1]]
        else:
            first, tails = split(first, tail)
        first = hop(first)
        sums = stage(k, held, sums)
        if k == half - 1:
            tails, sums = tie((tails, sums))
        first, sums = tie((first, sums))
        if k == half - 2:
            second, tail = split(second)
        if k < half - 1:
            second = hop(second)
        sums = stage(-k, crossed, sums)
        if k < half - 1:
            second, sums = tie((second, sums))
    tails = hop(tails)
    small = (top_expander_sketch.T, top_reducer_sketch)
    unit = pl.pallas_call(
        functools.partial(feature_kernel, half),
        out_shape=jax.ShapeDtypeStruct((LANES, LANES), F32),
        in_specs=[SMEM] * 2 + [VMEM] * (2 + len(activations) + 3) + [HBM] * 2,
        out_specs=VMEM,
        scratch_shapes=stage_scratch
        + [pltpu.VMEM(a.shape, a.dtype) for a in small]
        + [pltpu.SemaphoreType.DMA((2,))],
        compiler_params=params(16),
        cost_estimate=cost(1, 1),
        name="features",
    )(
        me.reshape(1),
        sequence_token_counts,
        first,
        other_core(first),
        *activations,
        *sums,
        local,
        *in_hbm(small),
    )
    tails, unit = tie((tails, unit))
    blocks.append(tails)
    best = pl.pallas_call(
        functools.partial(score_kernel, len(blocks), count),
        out_shape=jax.ShapeDtypeStruct((2, TASKS, count, LANES), F32),
        in_specs=[VMEM] * (1 + len(blocks)),
        out_specs=VMEM,
        compiler_params=params(16),
        cost_estimate=cost(4 * MIB, 2 * MIB),
        name="scores",
    )(unit, *blocks)
    task_best, scores = pl.pallas_call(
        functools.partial(last_score_kernel, count),
        out_shape=(jax.ShapeDtypeStruct((2, TASKS), F32), jax.ShapeDtypeStruct((1, 2), F32)),
        in_specs=[VMEM] * 3,
        out_specs=(VMEM, VMEM),
        compiler_params=params(8),
        name="last_scores",
    )(unit, other_core(tails), best)
    return (scores.reshape(2), task_best)


def shards_of_any_slice(
    hidden_state_input,
    attention_mixed_state,
    hidden_state_adjoint,
    attention_values_adjoint,
    sequence_token_counts,
    heldout_sketched_signals,
    benchmark_labels,
    top_rmsnorm_weights,
    top_reducer_matrix,
    top_expander_matrix,
    bottom_reducer_matrix,
    bottom_expander_matrix,
    source_sketch,
    top_reducer_sketch,
    top_expander_sketch,
    top_target_sketch,
    bottom_reducer_sketch,
    bottom_expander_sketch,
    bottom_target_sketch,
    n,
):
    me = lax.axis_index("dp")
    x, mixed, adjoint, values = (
        hidden_state_input,
        attention_mixed_state,
        hidden_state_adjoint,
        attention_values_adjoint,
    )
    tokens, width = x.shape
    rows = top_reducer_matrix.shape[0]
    up_rows = top_expander_matrix.shape[1]
    rank = top_reducer_matrix.shape[1]
    k1 = source_sketch.shape[1]
    gain = top_rmsnorm_weights
    own_gain = lax.dynamic_slice_in_dim(gain, me * rows, rows)

    down_upper = (own_gain[:, None] * top_reducer_matrix.astype(F32)).astype(BF16)
    up_lower = mm(bottom_expander_matrix.T, bottom_reducer_sketch).astype(BF16)
    down_lower = mm(bottom_reducer_matrix, bottom_expander_sketch).astype(BF16)
    packed_lower = jnp.concatenate([down_lower[: rows // 2], down_lower[rows // 2 :]], axis=1)
    factors = jnp.concatenate([down_upper, up_lower, top_expander_matrix.T, packed_lower], axis=0)
    factors = lax.all_gather(factors, "dp")

    val_wide = heldout_sketched_signals.astype(F32)
    val_unit = (
        val_wide * lax.rsqrt(jnp.sum(val_wide * val_wide, axis=1, keepdims=True) + 1e-06)
    ).astype(BF16)
    labels = jnp.broadcast_to(benchmark_labels.astype(BF16), (val_unit.shape[0], 128))
    panel = jnp.concatenate([val_unit.reshape(-1, 128), labels], axis=0)
    panel = lax.all_gather(panel, "dp")
    val_rows = val_unit.shape[0]
    cut = panel.shape[1] - val_rows
    panel_tasks = panel[:, cut:, 0].reshape(n * val_rows, 1).astype(jnp.int32)
    panel = panel[:, :cut].reshape(n * val_rows, val_unit.shape[1])

    wide = x.astype(F32)
    inverse = lax.rsqrt(jnp.mean(wide * wide, axis=1, keepdims=True) + 1e-05)
    gained_sketch = (gain[:, None] * source_sketch.astype(F32)).astype(BF16)
    left_one = inverse * mm(x, gained_sketch)
    left_three = mm(mixed, source_sketch)
    right_two = ALPHA * mm(values, top_target_sketch)

    at = 0
    down_upper = factors[:, at : at + rows].reshape(width, rank)
    at += rows
    up_lower = factors[:, at : at + rows].reshape(width, -1)
    at += rows
    up_upper = factors[:, at : at + up_rows].reshape(-1, rank)
    at += up_rows
    down_lower = factors[:, at:]
    down_lower = jnp.concatenate([down_lower[:, :, :k1], down_lower[:, :, k1:]], axis=1)
    down_lower = down_lower.reshape(width, k1)

    reduced = inverse * mm(x, down_upper)
    left_two = mm(reduced.astype(BF16), top_expander_sketch)
    left_four = mm(mixed, down_lower)
    returned = mm(values, up_upper).astype(BF16)
    right_one = ALPHA * mm(returned, top_reducer_sketch)
    along = (ALPHA / width) * jnp.sum(returned.astype(F32) * reduced, axis=1, keepdims=True)
    targets = jnp.concatenate([up_lower, bottom_target_sketch], axis=1)
    bridge = mm_cols(down_upper, targets).astype(BF16)
    rights_low = mm(adjoint, targets) + inverse * (
        ALPHA * mm(returned, bridge) - (along * inverse) * mm(x, targets)
    )
    rights_low = ALPHA * rights_low
    k2 = up_lower.shape[1]
    lefts = (left_one, left_two, left_three, left_four)
    rights = (right_one, right_two, rights_low[:, :k2], rights_low[:, k2:])

    counts = sequence_token_counts[0]
    ends = jnp.cumsum(counts)
    starts = ends - counts
    places = jnp.arange(tokens, dtype=jnp.int32)[:, None]
    member = (places >= starts[None, :]) & (places < ends[None, :])
    count_ex = counts.shape[0]
    spread = jnp.concatenate(lefts, axis=0).astype(BF16)
    member = jnp.tile(member, (4, 1))
    spread = jnp.concatenate(
        [jnp.where(member[:, e : e + 1], spread, 0) for e in range(count_ex)], axis=1
    )
    feats = mm_cols(spread, jnp.concatenate(rights, axis=0).astype(BF16))
    feats = feats.reshape(count_ex, -1)
    squares = jnp.sum(feats * feats, axis=1, keepdims=True)
    unit_rows = (feats * lax.rsqrt(squares + 1e-06)).astype(BF16)

    score_scale = float(unit_rows.shape[1]) ** 0.5
    similar = score_scale * mm_rows(unit_rows, panel)
    task_mask = panel_tasks == jnp.arange(TASKS, dtype=jnp.int32)[None, :]
    task_best = jnp.max(
        jnp.where(task_mask[None, :, :], similar[:, :, None], -2.0 * score_scale), axis=1
    )
    return (jnp.mean(task_best, axis=1), task_best)


def solution(mesh):
    n = mesh.shape["dp"]
    split = P(("parts", "dp"), None)
    by_row, by_column, whole = P("dp", None), P(None, "dp"), P()
    placed = (
        (split,) * 5
        + (by_row, by_row, whole)
        + (by_row, by_column, by_row, by_column)
        + (whole,) * 7
    )
    ours = shards if n == 2 * RING_CHIPS else functools.partial(shards_of_any_slice, n=n)
    return jax.shard_map(
        ours,
        mesh=mesh,
        in_specs=placed,
        out_specs=(P(("parts", "dp")), split),
        check_vma=False,
    )
```

```python
import functools

import jax
import jax.numpy as jnp
from jax import lax
from jax.experimental import pallas as pl
from jax.experimental.pallas import tpu as pltpu
from jax.sharding import PartitionSpec as P

TASKS = 3
ALPHA = 4.0
F32 = jnp.float32
BF16 = jnp.bfloat16
RING_CHIPS = 8
LANES = 128
STEPS = 4
VALUES, V_TARGET, X_DOWN, X_LOW, J_LOW, J_TARGET, M_DOWN, M_SOURCE, SUMS = range(9)
INVERSE, LEFT_ONE, X_TARGET, LOCAL_SUMS = range(4)
MIB = 1 << 20


def mm(a, b):
    return jnp.dot(a, b, preferred_element_type=F32)


def mm_rows(a, b):
    return lax.dot_general(a, b, (((1,), (1,)), ((), ())), preferred_element_type=F32)


def mm_cols(a, b):
    return lax.dot_general(a, b, (((0,), (0,)), ((), ())), preferred_element_type=F32)


def ring_chip(pos):
    half = RING_CHIPS // 2
    return jnp.where(pos < half, 2 * pos, 2 * (RING_CHIPS - 1 - pos) + 1)


def ring_pos(chip):
    row, side = chip // 2, chip % 2
    return jnp.where(side == 0, row, RING_CHIPS - 1 - row)


def hop(value):
    half = RING_CHIPS // 2
    place = [2 * q if q < half else 2 * (RING_CHIPS - 1 - q) + 1 for q in range(RING_CHIPS)]
    pairs = []
    for q in range(RING_CHIPS):
        pairs.append((2 * place[q], 2 * place[(q + 1) % RING_CHIPS]))
        pairs.append((2 * place[q] + 1, 2 * place[(q - 1) % RING_CHIPS] + 1))
    return lax.ppermute(value, "dp", pairs)


def other_core(value):
    return lax.ppermute(value, "dp", [(d, d ^ 1) for d in range(2 * RING_CHIPS)])


def half_lanes(shape):
    return lax.broadcasted_iota(jnp.int32, shape, 1) < LANES // 2


def diagonal_column(row, first, count):
    shape = (count, row.shape[1])
    lane = lax.broadcasted_iota(jnp.int32, shape, 1)
    at = lax.broadcasted_iota(jnp.int32, shape, 0)
    return jnp.sum(jnp.where(lane == at + first, row, 0.0), axis=1, keepdims=True)


def load(pairs, sems):
    copies = [pltpu.make_async_copy(src, dst, sems.at[i]) for i, (src, dst) in enumerate(pairs)]
    for copy in copies:
        copy.start()
    return copies


def pack_kernel(me_ref, *refs):
    up_up_hbm, hbm, out_ref, held, sems = refs[0], refs[1:9], refs[9], refs[10:18], refs[18]
    val_ref, down_up_ref, up_low_ref, down_low_ref, gain_ref, sketch_ref, expand_ref, label_ref = held
    rows = down_up_ref.shape[0]
    half = LANES // 2
    direct = (up_up_hbm, out_ref.at[pl.ds(2 * rows, rows // 2)])
    for copy in load((*zip(hbm, held), direct), sems):
        copy.wait()
    for b in range(rows // half):
        place = me_ref[0] * (rows // half) + b
        row = gain_ref[pl.ds(place // 2, 1), :]
        column = diagonal_column(row, (place % 2) * half, half)
        part = down_up_ref[pl.ds(b * half, half), :].astype(F32)
        out_ref[pl.ds(b * half, half), :] = (column * part).astype(BF16)
    at = rows
    out_ref[pl.ds(at, rows), :] = mm(up_low_ref[...], sketch_ref[...]).astype(BF16)
    at += rows + rows // 2
    expand = expand_ref[...]
    low = mm_rows(down_low_ref[...], jnp.concatenate([expand, expand], axis=0))
    first, second = low[: rows // 2], low[rows // 2 :]
    out_ref[pl.ds(at, rows // 2), :] = jnp.where(half_lanes(first.shape), first, second).astype(BF16)
    at += rows // 2
    wide = val_ref[...].astype(F32)
    count, width = wide.shape
    scale = lax.rsqrt(jnp.sum(wide * wide, axis=1, keepdims=True) + 1e-06)
    unit = wide * scale
    blocks = [unit[:, i * LANES : (i + 1) * LANES] for i in range(width // LANES)]
    row = label_ref[...].astype(F32)
    labels = jnp.broadcast_to(diagonal_column(row, 0, count), (count, LANES))
    blocks += [labels, labels]
    for i in range(0, len(blocks), 2):
        pair = jnp.concatenate(blocks[i : i + 2], axis=0)
        out_ref[pl.ds(at + i * count, 2 * count), :] = pair.astype(BF16)


def local_kernel(*refs):
    x_hbm, mixed_hbm, adjoint_hbm, values_hbm, target_hbm, top_target_hbm = refs[:6]
    small_hbm, gain_hbm, source_hbm = refs[6:8], refs[8], refs[9]
    x_ref, mixed_ref, adjoint_ref, values_ref, target_ref, top_target_ref = refs[10:16]
    small_refs, turned_ref, sums_ref = refs[16:18], refs[18], refs[19]
    gain_ref, source_ref, sems = refs[20:]
    tokens, width = x_ref.shape
    span = width // STEPS
    copies = []
    for j in range(STEPS):
        part = pl.ds(j * span, span)
        pairs = (
            (gain_hbm.at[:, part], gain_ref.at[:, part]),
            (source_hbm.at[:, part], source_ref.at[:, part]),
            (x_hbm.at[:, part], x_ref.at[:, part]),
            (target_hbm.at[part], target_ref.at[part]),
        )
        copies.append(load(pairs, sems.at[j]))
    pairs = (
        (adjoint_hbm, adjoint_ref),
        (mixed_hbm, mixed_ref),
        (values_hbm, values_ref),
        (top_target_hbm, top_target_ref),
        *zip(small_hbm, small_refs),
    )
    later = load(pairs, sems.at[STEPS])
    products = jnp.zeros((tokens, 2 * LANES), F32)
    squares = jnp.zeros((tokens, LANES), F32)
    for j in range(STEPS):
        for copy in copies[j]:
            copy.wait()
        part = slice(j * span, (j + 1) * span)
        x, source = x_ref[:, part], source_ref[:, part].astype(F32)
        gained = source * gain_ref[:, part]
        turned_ref[part, :] = jnp.concatenate([source, source], axis=0).T.astype(BF16)
        gained = jnp.concatenate([gained, gained], axis=0).T.astype(BF16)
        products = products + mm(x, jnp.concatenate([gained, target_ref[part, :]], axis=1))
        for i in range(span // LANES):
            wide = x[:, i * LANES : (i + 1) * LANES].astype(F32)
            squares = squares + wide * wide
    mean = jnp.sum(squares, axis=1, keepdims=True) * (1.0 / width)
    inverse = jnp.broadcast_to(lax.rsqrt(mean + 1e-05), (tokens, LANES))
    for i, value in enumerate((inverse, inverse * products[:, :LANES], products[:, LANES:])):
        sums_ref[:, i * LANES : (i + 1) * LANES] = value
    for copy in later:
        copy.wait()


def add_stage(away, me_ref, pieces, held, old, scratch):
    x_ref, mixed_ref, adjoint_ref, values_ref, target_ref, top_target_ref, source_ref = held
    both, up, down = scratch
    rows = both.shape[0] // 2
    half, pad = rows // 2, LANES // 2
    span = 2 * rows
    me = me_ref[0]
    pos, core = ring_pos(me // 2), me % 2
    chip = ring_chip((pos + away * (2 * core - 1) + RING_CHIPS) % RING_CHIPS)
    odd = chip % 2
    mine = pl.ds(pl.multiple_of(chip * span, LANES), span)
    values_start = (chip // 2) * span + odd * (rows - pad)
    values_part = pl.ds(pl.multiple_of(values_start, LANES), rows + pad)
    side = core if away >= 0 else 1 - core
    up[pl.ds(pl.multiple_of((1 - odd) * rows, 16), pad), :] = jnp.zeros((pad, 2 * LANES), BF16)
    up[pl.ds(pl.multiple_of(odd * pad, 16), rows), pl.ds(LANES, LANES)] = top_target_ref[
        pl.ds(pl.multiple_of(chip * rows, 16), rows), :
    ]
    for piece, c in ((pieces[0], side), (pieces[1], 1 - side)):
        one = pl.ds(pl.multiple_of(c * rows, 16), rows)
        both[one, pl.ds(0, LANES)] = piece[pl.ds(0, rows), :]
        both[one, pl.ds(LANES, LANES)] = piece[pl.ds(rows, rows), :]
        up[pl.ds(pl.multiple_of(odd * pad + c * half, 16), half), pl.ds(0, LANES)] = piece[
            pl.ds(2 * rows, half), :
        ]
        packed = piece[pl.ds(2 * rows + half, half), :].astype(F32)
        turned = pltpu.roll(packed, pad, 1)
        lower = half_lanes(packed.shape)
        down[pl.ds(pl.multiple_of(c * rows, 16), half), :] = jnp.where(lower, packed, turned).astype(BF16)
        down[pl.ds(pl.multiple_of(c * rows + half, 16), half), :] = jnp.where(lower, turned, packed).astype(BF16)

    weights = both[...]
    down_up = weights[:, :LANES]
    lows = jnp.concatenate([weights[:, LANES:], target_ref[mine, :]], axis=1)
    bridge = mm_cols(down_up, lows)
    products = []
    for activation, factor in (
        (values_ref[:, values_part], up[...]),
        (x_ref[:, mine], weights),
        (adjoint_ref[:, mine], lows),
        (mixed_ref[:, mine], jnp.concatenate([down[...], source_ref[mine, :]], axis=1)),
    ):
        product = mm(activation, factor)
        products += [product[:, :LANES], product[:, LANES:]]
    if old:
        old_sums, old_bridge = old
        products = [p + old_sums[:, i * LANES : (i + 1) * LANES] for i, p in enumerate(products)]
        bridge = bridge + old_bridge[...]
    return products, bridge


def add_half(away, other, me_ref, piece, held, old, scratch):
    x_ref, mixed_ref, adjoint_ref, values_ref, target_ref, top_target_ref, source_ref = held
    wide, down, up = scratch
    pad = LANES // 2
    rows = wide.shape[0] - pad
    half, span = rows // 2, 2 * rows
    me = me_ref[0]
    pos, core = ring_pos(me // 2), me % 2
    chip = ring_chip((pos + away * (2 * core - 1) + RING_CHIPS) % RING_CHIPS)
    side = 1 - core if other else core
    odd = chip % 2
    mine = pl.ds(pl.multiple_of(chip * span + side * (rows - pad), LANES), rows + pad)
    inside = pl.ds(pl.multiple_of(side * pad, 16), rows)
    outside = pl.ds(pl.multiple_of((1 - side) * rows, 16), pad)
    block = pl.ds(pl.multiple_of(chip * span + side * rows, 16), rows)
    values_start = (chip // 2) * span + odd * (rows - pad)
    values_part = pl.ds(pl.multiple_of(values_start, LANES), rows + pad)
    values_inside = pl.ds(pl.multiple_of(odd * pad + side * half, 16), half)
    values_block = pl.ds(pl.multiple_of(chip * rows + side * half, 16), half)
    wide[outside, :] = jnp.zeros((pad, wide.shape[1]), BF16)
    down[outside, :] = jnp.zeros((pad, down.shape[1]), BF16)
    up[...] = jnp.zeros(up.shape, BF16)
    wide[inside, pl.ds(0, LANES)] = piece[pl.ds(0, rows), :]
    wide[inside, pl.ds(LANES, LANES)] = piece[pl.ds(rows, rows), :]
    wide[inside, pl.ds(2 * LANES, LANES)] = target_ref[block, :]
    up[values_inside, pl.ds(0, LANES)] = piece[pl.ds(2 * rows, half), :]
    up[values_inside, pl.ds(LANES, LANES)] = top_target_ref[values_block, :]
    packed = piece[pl.ds(2 * rows + half, half), :].astype(F32)
    turned = pltpu.roll(packed, pad, 1)
    lower = half_lanes(packed.shape)
    at = side * pad
    down[pl.ds(pl.multiple_of(at, 16), half), pl.ds(0, LANES)] = jnp.where(lower, packed, turned).astype(BF16)
    down[pl.ds(pl.multiple_of(at + half, 16), half), pl.ds(0, LANES)] = jnp.where(lower, turned, packed).astype(BF16)
    down[inside, pl.ds(LANES, LANES)] = source_ref[block, :]

    weights = wide[...]
    bridge = mm_cols(weights[:, :LANES], weights[:, LANES:])
    products = []
    for activation, factor in (
        (values_ref[:, values_part], up[...]),
        (x_ref[:, mine], weights[:, : 2 * LANES]),
        (adjoint_ref[:, mine], weights[:, LANES:]),
        (mixed_ref[:, mine], down[...]),
    ):
        product = mm(activation, factor)
        products += [product[:, :LANES], product[:, LANES:]]
    old_sums, old_bridge = old
    products = [p + old_sums[:, i * LANES : (i + 1) * LANES] for i, p in enumerate(products)]
    return products, bridge + old_bridge[...]


def half_kernel(away, me_ref, *refs):
    piece, held, old = refs[0], refs[1:8], refs[8:10]
    (new_sums, new_bridge), scratch = refs[10:12], refs[12:]
    products, bridge = add_half(away, False, me_ref, piece, held, old, scratch)
    for i in range(SUMS):
        new_sums[:, i * LANES : (i + 1) * LANES] = products[i]
    new_bridge[...] = bridge


def stage_kernel(away, first, me_ref, *refs):
    pieces, held, old = refs[:2], refs[2:9], refs[9:-5]
    (new_sums, new_bridge), scratch = refs[-5:-3], refs[-3:]
    products, bridge = add_stage(away, me_ref, pieces, held, old, scratch)
    for i in range(SUMS):
        new_sums[:, i * LANES : (i + 1) * LANES] = products[i]
    new_bridge[...] = bridge


def feature_kernel(away, me_ref, counts_ref, *refs):
    piece, held, old, local_ref, expand_ref, sketch_ref = refs[0], refs[1:8], refs[8:10], *refs[10:13]
    out_ref, scratch = refs[13], refs[14:]
    products, bridge = add_half(away, True, me_ref, piece, held, old, scratch)
    local = [local_ref[:, i * LANES : (i + 1) * LANES] for i in range(LOCAL_SUMS)]
    tokens, width = held[0].shape
    half = LANES // 2
    inverse = local[INVERSE]
    returned = products[VALUES].astype(BF16)
    back = mm(returned, jnp.concatenate([bridge.astype(BF16), sketch_ref[...]], axis=1))
    right_one = ALPHA * back[:, 2 * LANES :]
    reduced = inverse * products[X_DOWN]
    expand = expand_ref[...]
    left_two = mm_rows(reduced.astype(BF16), jnp.concatenate([expand, expand], axis=0))
    along = (ALPHA / width) * jnp.sum(returned.astype(F32) * reduced, axis=1, keepdims=True)
    along = along * inverse
    right_three = products[J_LOW] + inverse * (ALPHA * back[:, :LANES] - along * products[X_LOW])
    right_four = products[J_TARGET] + inverse * (ALPHA * back[:, LANES : 2 * LANES] - along * local[X_TARGET])
    rights = (right_one, ALPHA * products[V_TARGET], ALPHA * right_three, ALPHA * right_four)
    lefts = (local[LEFT_ONE], left_two, products[M_SOURCE], products[M_DOWN])
    place = lax.broadcasted_iota(jnp.int32, (tokens, LANES), 0)
    one, two = counts_ref[0, 0], counts_ref[0, 1]
    lower = half_lanes((tokens, LANES))
    member = (place >= jnp.where(lower, 0, one)) & (place < jnp.where(lower, one, one + two))
    feats = jnp.zeros((LANES, LANES), F32)
    for left, right in zip(lefts, rights):
        feats = feats + mm_cols(jnp.where(member, left, 0.0).astype(BF16), right.astype(BF16))
    for e in range(2):
        own = feats[e * half : (e + 1) * half]
        squares = jnp.sum(own * own, keepdims=True)
        out_ref[pl.ds(e * half, half), :] = (own * lax.rsqrt(squares + 1e-06)).astype(BF16).astype(F32)


def split_kernel(block_ref, *refs):
    head_ref, tail_ref = refs[-2:]
    cut, tail = head_ref.shape[0], block_ref.shape[0] - head_ref.shape[0]
    head_ref[...] = block_ref[pl.ds(0, cut), :]
    if len(refs) == 3:
        tail_ref[pl.ds(0, tail), :] = refs[0][...]
    tail_ref[pl.ds(tail_ref.shape[0] - tail, tail), :] = block_ref[pl.ds(cut, tail), :]


def best_of(places, count, unit_ref, best):
    half = LANES // 2
    scale = float(half * LANES) ** 0.5
    shape = (count, LANES)
    totals = [[jnp.zeros(shape, F32) for _ in range(2)] for _ in places]
    for i in range(0, half, 2):
        units = [
            [jnp.broadcast_to(unit_ref[pl.ds(e * half + i + k, 1), :], shape) for k in range(2)]
            for e in range(2)
        ]
        for b, (block, start) in enumerate(places):
            wide = block[pl.ds(start + i * count, 2 * count), :].astype(F32)
            for e in range(2):
                totals[b][e] = totals[b][e] + (wide[:count] * units[e][0] + wide[count:] * units[e][1])
    for b, (block, start) in enumerate(places):
        labels = block[pl.ds(start + half * count, 2 * count), :].astype(F32)[:count]
        for e in range(2):
            similar = scale * jnp.sum(totals[b][e], axis=1, keepdims=True)
            for t in range(TASKS):
                best[e][t] = jnp.maximum(best[e][t], jnp.where(labels == float(t), similar, -2.0 * scale))


def places_of(blocks, count):
    size = (LANES // 2 + 2) * count
    places = []
    for block in blocks:
        total = block.shape[0]
        firsts = range(0, total, size) if total % size == 0 else [total - size]
        places += [(block, first) for first in firsts]
    return places


def score_kernel(blocks, count, unit_ref, *refs):
    block_refs, best_ref = refs[:blocks], refs[blocks]
    lowest = -2.0 * float(LANES // 2 * LANES) ** 0.5
    best = [[jnp.full((count, LANES), lowest, F32) for _ in range(TASKS)] for _ in range(2)]
    best_of(places_of(block_refs, count), count, unit_ref, best)
    for e in range(2):
        for t in range(TASKS):
            best_ref[e, t] = best[e][t]


def last_score_kernel(count, unit_ref, block_ref, best_ref, out_ref, mean_ref):
    best = [[best_ref[e, t] for t in range(TASKS)] for e in range(2)]
    best_of(places_of([block_ref], count), count, unit_ref, best)
    lane = lax.broadcasted_iota(jnp.int32, (1, LANES), 1)
    means = []
    for e in range(2):
        values = [jnp.max(best[e][t], axis=0, keepdims=True) for t in range(TASKS)]
        row = jnp.where(lane == 0, values[0], jnp.where(lane == 1, values[1], values[2]))
        out_ref[pl.ds(e, 1), :] = row[:, :TASKS]
        means.append((values[0] + values[1] + values[2]) * (1.0 / TASKS))
    mean_ref[...] = jnp.where(lane == 0, means[0], means[1])[:, :2]


VMEM = pl.BlockSpec(memory_space=pltpu.VMEM)
SMEM = pl.BlockSpec(memory_space=pltpu.SMEM)
ANY = pl.BlockSpec(memory_space=pl.ANY)
HBM = pl.BlockSpec(memory_space=pltpu.HBM)


def in_hbm(arrays):
    return [pltpu.with_memory_space_constraint(a, pltpu.HBM) for a in arrays]


def params(mib):
    return pltpu.CompilerParams(vmem_limit_bytes=mib * MIB)


def cost(flops, nbytes):
    return pl.CostEstimate(flops=flops, bytes_accessed=nbytes, transcendentals=0)


def shards(
    hidden_state_input,
    attention_mixed_state,
    hidden_state_adjoint,
    attention_values_adjoint,
    sequence_token_counts,
    heldout_sketched_signals,
    benchmark_labels,
    top_rmsnorm_weights,
    top_reducer_matrix,
    top_expander_matrix,
    bottom_reducer_matrix,
    bottom_expander_matrix,
    source_sketch,
    top_reducer_sketch,
    top_expander_sketch,
    top_target_sketch,
    bottom_reducer_sketch,
    bottom_expander_sketch,
    bottom_target_sketch,
):
    me = lax.axis_index("dp").astype(jnp.int32)
    x, mixed, adjoint, values = (
        hidden_state_input,
        attention_mixed_state,
        hidden_state_adjoint,
        attention_values_adjoint,
    )
    tokens, width = x.shape
    rows = top_reducer_matrix.shape[0]
    count = heldout_sketched_signals.shape[0]

    inputs = (
        top_expander_matrix.T,
        heldout_sketched_signals,
        top_reducer_matrix,
        bottom_expander_matrix.T,
        bottom_reducer_matrix,
        top_rmsnorm_weights.reshape(width // LANES, LANES),
        bottom_reducer_sketch,
        bottom_expander_sketch.T,
        benchmark_labels.T,
    )
    own = pl.pallas_call(
        pack_kernel,
        out_shape=jax.ShapeDtypeStruct((3 * rows + (LANES // 2 + 2) * count, LANES), BF16),
        in_specs=[SMEM] + [HBM] * len(inputs),
        out_specs=VMEM,
        scratch_shapes=[pltpu.VMEM(a.shape, a.dtype) for a in inputs[1:]]
        + [pltpu.SemaphoreType.DMA((len(inputs),))],
        compiler_params=params(8),
        name="pack",
    )(me.reshape(1), *in_hbm(inputs))

    inputs = (
        x,
        mixed,
        adjoint,
        values,
        bottom_target_sketch,
        top_target_sketch,
        top_expander_sketch.T,
        top_reducer_sketch,
        top_rmsnorm_weights.reshape(1, width),
        source_sketch.T,
    )
    *activations, local = pl.pallas_call(
        local_kernel,
        out_shape=[jax.ShapeDtypeStruct(a.shape, a.dtype) for a in inputs[:8]]
        + [
            jax.ShapeDtypeStruct((width, LANES), BF16),
            jax.ShapeDtypeStruct((tokens, LOCAL_SUMS * LANES), F32),
        ],
        in_specs=[HBM] * len(inputs),
        out_specs=[VMEM] * 10,
        scratch_shapes=[pltpu.VMEM(a.shape, a.dtype) for a in inputs[8:]]
        + [pltpu.SemaphoreType.DMA((STEPS + 1, 6))],
        compiler_params=params(24),
        cost_estimate=cost(tokens * width * LANES * 6, 14 * MIB),
        name="local_products",
    )(*in_hbm(inputs))
    activations, small = [*activations[:6], activations[8]], activations[6:8]

    stage_scratch = [
        pltpu.VMEM((2 * rows, 2 * LANES), BF16),
        pltpu.VMEM((rows + LANES // 2, 2 * LANES), BF16),
        pltpu.VMEM((2 * rows, LANES), BF16),
    ]

    def stage(away, pieces, sums):
        first = not sums
        start = 1 + len(pieces) + len(activations)
        return pl.pallas_call(
            functools.partial(stage_kernel, away, first),
            out_shape=[
                jax.ShapeDtypeStruct((tokens, SUMS * LANES), F32),
                jax.ShapeDtypeStruct((LANES, 2 * LANES), F32),
            ],
            in_specs=[SMEM] + [VMEM] * (len(pieces) + len(activations) + len(sums)),
            out_specs=[VMEM, VMEM],
            scratch_shapes=stage_scratch,
            input_output_aliases={} if first else {start: 0, start + 1: 1},
            compiler_params=params(16),
            cost_estimate=cost(tokens * rows * LANES * 16, 2 * MIB),
            name="stage",
        )(me.reshape(1), *pieces, *activations, *sums)

    def split(block, *tails):
        tail = block.shape[0] - 3 * rows
        shapes = (3 * rows, LANES), ((1 + len(tails)) * tail, LANES)
        return pl.pallas_call(
            split_kernel,
            out_shape=[jax.ShapeDtypeStruct(shape, BF16) for shape in shapes],
            in_specs=[VMEM] * (1 + len(tails)),
            out_specs=[VMEM, VMEM],
            compiler_params=params(8),
            name="split",
        )(block, *tails)

    tie = lax.optimization_barrier
    half = RING_CHIPS // 2
    held = [own, other_core(own)]
    blocks = list(held)
    first, second = hop(held[0]), hop(held[1])
    first, activations = tie((first, activations))
    sums = stage(0, held, [])
    second, sums = tie((second, sums))
    for k in range(1, half):
        held = [first, second]
        crossed = [other_core(first), other_core(second)]
        blocks += [first, crossed[0]]
        if k < half - 1:
            blocks += [second, crossed[1]]
        else:
            first, tails = split(first, tail)
        first = hop(first)
        sums = stage(k, held, sums)
        if k == half - 1:
            tails, sums = tie((tails, sums))
        first, sums = tie((first, sums))
        if k == half - 2:
            second, tail = split(second)
        if k < half - 1:
            second = hop(second)
        sums = stage(-k, crossed, sums)
        if k < half - 1:
            second, sums = tie((second, sums))
    tails = hop(tails)
    half_scratch = [
        pltpu.VMEM((rows + LANES // 2, 3 * LANES), BF16),
        pltpu.VMEM((rows + LANES // 2, 2 * LANES), BF16),
        pltpu.VMEM((rows + LANES // 2, 2 * LANES), BF16),
    ]
    crossed = other_core(first)
    start = 2 + len(activations)
    sums = pl.pallas_call(
        functools.partial(half_kernel, half),
        out_shape=[jax.ShapeDtypeStruct(a.shape, a.dtype) for a in sums],
        in_specs=[SMEM] + [VMEM] * (1 + len(activations) + 2),
        out_specs=[VMEM, VMEM],
        scratch_shapes=half_scratch,
        input_output_aliases={start: 0, start + 1: 1},
        compiler_params=params(16),
        cost_estimate=cost(tokens * rows * LANES * 8, MIB),
        name="half_stage",
    )(me.reshape(1), first, *activations, *sums)
    unit = pl.pallas_call(
        functools.partial(feature_kernel, half),
        out_shape=jax.ShapeDtypeStruct((LANES, LANES), F32),
        in_specs=[SMEM] * 2 + [VMEM] * (1 + len(activations) + 5),
        out_specs=VMEM,
        scratch_shapes=half_scratch,
        compiler_params=params(16),
        cost_estimate=cost(1, 1),
        name="features",
    )(me.reshape(1), sequence_token_counts, crossed, *activations, *sums, local, *small)
    tails, unit = tie((tails, unit))
    blocks.append(tails)
    best = pl.pallas_call(
        functools.partial(score_kernel, len(blocks), count),
        out_shape=jax.ShapeDtypeStruct((2, TASKS, count, LANES), F32),
        in_specs=[VMEM] * (1 + len(blocks)),
        out_specs=VMEM,
        compiler_params=params(16),
        cost_estimate=cost(4 * MIB, 2 * MIB),
        name="scores",
    )(unit, *blocks)
    task_best, scores = pl.pallas_call(
        functools.partial(last_score_kernel, count),
        out_shape=(jax.ShapeDtypeStruct((2, TASKS), F32), jax.ShapeDtypeStruct((1, 2), F32)),
        in_specs=[VMEM] * 3,
        out_specs=(VMEM, VMEM),
        compiler_params=params(8),
        name="last_scores",
    )(unit, other_core(tails), best)
    return (scores.reshape(2), task_best)


def shards_of_any_slice(
    hidden_state_input,
    attention_mixed_state,
    hidden_state_adjoint,
    attention_values_adjoint,
    sequence_token_counts,
    heldout_sketched_signals,
    benchmark_labels,
    top_rmsnorm_weights,
    top_reducer_matrix,
    top_expander_matrix,
    bottom_reducer_matrix,
    bottom_expander_matrix,
    source_sketch,
    top_reducer_sketch,
    top_expander_sketch,
    top_target_sketch,
    bottom_reducer_sketch,
    bottom_expander_sketch,
    bottom_target_sketch,
    n,
):
    me = lax.axis_index("dp")
    x, mixed, adjoint, values = (
        hidden_state_input,
        attention_mixed_state,
        hidden_state_adjoint,
        attention_values_adjoint,
    )
    tokens, width = x.shape
    rows = top_reducer_matrix.shape[0]
    up_rows = top_expander_matrix.shape[1]
    rank = top_reducer_matrix.shape[1]
    k1 = source_sketch.shape[1]
    gain = top_rmsnorm_weights
    own_gain = lax.dynamic_slice_in_dim(gain, me * rows, rows)

    down_upper = (own_gain[:, None] * top_reducer_matrix.astype(F32)).astype(BF16)
    up_lower = mm(bottom_expander_matrix.T, bottom_reducer_sketch).astype(BF16)
    down_lower = mm(bottom_reducer_matrix, bottom_expander_sketch).astype(BF16)
    packed_lower = jnp.concatenate([down_lower[: rows // 2], down_lower[rows // 2 :]], axis=1)
    factors = jnp.concatenate([down_upper, up_lower, top_expander_matrix.T, packed_lower], axis=0)
    factors = lax.all_gather(factors, "dp")

    val_wide = heldout_sketched_signals.astype(F32)
    val_unit = (
        val_wide * lax.rsqrt(jnp.sum(val_wide * val_wide, axis=1, keepdims=True) + 1e-06)
    ).astype(BF16)
    labels = jnp.broadcast_to(benchmark_labels.astype(BF16), (val_unit.shape[0], 128))
    panel = jnp.concatenate([val_unit.reshape(-1, 128), labels], axis=0)
    panel = lax.all_gather(panel, "dp")
    val_rows = val_unit.shape[0]
    cut = panel.shape[1] - val_rows
    panel_tasks = panel[:, cut:, 0].reshape(n * val_rows, 1).astype(jnp.int32)
    panel = panel[:, :cut].reshape(n * val_rows, val_unit.shape[1])

    wide = x.astype(F32)
    inverse = lax.rsqrt(jnp.mean(wide * wide, axis=1, keepdims=True) + 1e-05)
    gained_sketch = (gain[:, None] * source_sketch.astype(F32)).astype(BF16)
    left_one = inverse * mm(x, gained_sketch)
    left_three = mm(mixed, source_sketch)
    right_two = ALPHA * mm(values, top_target_sketch)

    at = 0
    down_upper = factors[:, at : at + rows].reshape(width, rank)
    at += rows
    up_lower = factors[:, at : at + rows].reshape(width, -1)
    at += rows
    up_upper = factors[:, at : at + up_rows].reshape(-1, rank)
    at += up_rows
    down_lower = factors[:, at:]
    down_lower = jnp.concatenate([down_lower[:, :, :k1], down_lower[:, :, k1:]], axis=1)
    down_lower = down_lower.reshape(width, k1)

    reduced = inverse * mm(x, down_upper)
    left_two = mm(reduced.astype(BF16), top_expander_sketch)
    left_four = mm(mixed, down_lower)
    returned = mm(values, up_upper).astype(BF16)
    right_one = ALPHA * mm(returned, top_reducer_sketch)
    along = (ALPHA / width) * jnp.sum(returned.astype(F32) * reduced, axis=1, keepdims=True)
    targets = jnp.concatenate([up_lower, bottom_target_sketch], axis=1)
    bridge = mm_cols(down_upper, targets).astype(BF16)
    rights_low = mm(adjoint, targets) + inverse * (
        ALPHA * mm(returned, bridge) - (along * inverse) * mm(x, targets)
    )
    rights_low = ALPHA * rights_low
    k2 = up_lower.shape[1]
    lefts = (left_one, left_two, left_three, left_four)
    rights = (right_one, right_two, rights_low[:, :k2], rights_low[:, k2:])

    counts = sequence_token_counts[0]
    ends = jnp.cumsum(counts)
    starts = ends - counts
    places = jnp.arange(tokens, dtype=jnp.int32)[:, None]
    member = (places >= starts[None, :]) & (places < ends[None, :])
    count_ex = counts.shape[0]
    spread = jnp.concatenate(lefts, axis=0).astype(BF16)
    member = jnp.tile(member, (4, 1))
    spread = jnp.concatenate(
        [jnp.where(member[:, e : e + 1], spread, 0) for e in range(count_ex)], axis=1
    )
    feats = mm_cols(spread, jnp.concatenate(rights, axis=0).astype(BF16))
    feats = feats.reshape(count_ex, -1)
    squares = jnp.sum(feats * feats, axis=1, keepdims=True)
    unit_rows = (feats * lax.rsqrt(squares + 1e-06)).astype(BF16)

    score_scale = float(unit_rows.shape[1]) ** 0.5
    similar = score_scale * mm_rows(unit_rows, panel)
    task_mask = panel_tasks == jnp.arange(TASKS, dtype=jnp.int32)[None, :]
    task_best = jnp.max(
        jnp.where(task_mask[None, :, :], similar[:, :, None], -2.0 * score_scale), axis=1
    )
    return (jnp.mean(task_best, axis=1), task_best)


def solution(mesh):
    n = mesh.shape["dp"]
    split = P(("parts", "dp"), None)
    by_row, by_column, whole = P("dp", None), P(None, "dp"), P()
    placed = (
        (split,) * 5
        + (by_row, by_row, whole)
        + (by_row, by_column, by_row, by_column)
        + (whole,) * 7
    )
    ours = shards if n == 2 * RING_CHIPS else functools.partial(shards_of_any_slice, n=n)
    return jax.shard_map(
        ours,
        mesh=mesh,
        in_specs=placed,
        out_specs=(P(("parts", "dp")), split),
        check_vma=False,
    )
```

```python
import functools

import jax
import jax.numpy as jnp
from jax import lax
from jax.experimental import pallas as pl
from jax.experimental.pallas import tpu as pltpu
from jax.sharding import PartitionSpec as P

TASKS = 3
ALPHA = 4.0
F32 = jnp.float32
BF16 = jnp.bfloat16
RING_CHIPS = 8
LANES = 128
STEPS = 4
VALUES, V_TARGET, X_DOWN, X_LOW, J_LOW, J_TARGET, M_DOWN, M_SOURCE, SUMS = range(9)
INVERSE, LEFT_ONE, X_TARGET, LOCAL_SUMS = range(4)
MIB = 1 << 20


def mm(a, b):
    return jnp.dot(a, b, preferred_element_type=F32)


def mm_rows(a, b):
    return lax.dot_general(a, b, (((1,), (1,)), ((), ())), preferred_element_type=F32)


def mm_cols(a, b):
    return lax.dot_general(a, b, (((0,), (0,)), ((), ())), preferred_element_type=F32)


def ring_chip(pos):
    half = RING_CHIPS // 2
    return jnp.where(pos < half, 2 * pos, 2 * (RING_CHIPS - 1 - pos) + 1)


def ring_pos(chip):
    row, side = chip // 2, chip % 2
    return jnp.where(side == 0, row, RING_CHIPS - 1 - row)


def hop(value):
    half = RING_CHIPS // 2
    place = [2 * q if q < half else 2 * (RING_CHIPS - 1 - q) + 1 for q in range(RING_CHIPS)]
    pairs = []
    for q in range(RING_CHIPS):
        pairs.append((2 * place[q], 2 * place[(q + 1) % RING_CHIPS]))
        pairs.append((2 * place[q] + 1, 2 * place[(q - 1) % RING_CHIPS] + 1))
    return lax.ppermute(value, "dp", pairs)


def other_core(value):
    return lax.ppermute(value, "dp", [(d, d ^ 1) for d in range(2 * RING_CHIPS)])


def half_lanes(shape):
    return lax.broadcasted_iota(jnp.int32, shape, 1) < LANES // 2


def diagonal_column(row, first, count):
    shape = (count, row.shape[1])
    lane = lax.broadcasted_iota(jnp.int32, shape, 1)
    at = lax.broadcasted_iota(jnp.int32, shape, 0)
    return jnp.sum(jnp.where(lane == at + first, row, 0.0), axis=1, keepdims=True)


def load(pairs, sems):
    copies = [pltpu.make_async_copy(src, dst, sems.at[i]) for i, (src, dst) in enumerate(pairs)]
    for copy in copies:
        copy.start()
    return copies


def pack_kernel(me_ref, *refs):
    up_up_hbm, hbm, out_ref, held, sems = refs[0], refs[1:9], refs[9], refs[10:18], refs[18]
    val_ref, down_up_ref, up_low_ref, down_low_ref, gain_ref, sketch_ref, expand_ref, label_ref = held
    rows = down_up_ref.shape[0]
    half = LANES // 2
    direct = (up_up_hbm, out_ref.at[pl.ds(2 * rows, rows // 2)])
    for copy in load((*zip(hbm, held), direct), sems):
        copy.wait()
    for b in range(rows // half):
        place = me_ref[0] * (rows // half) + b
        row = gain_ref[pl.ds(place // 2, 1), :]
        column = diagonal_column(row, (place % 2) * half, half)
        part = down_up_ref[pl.ds(b * half, half), :].astype(F32)
        out_ref[pl.ds(b * half, half), :] = (column * part).astype(BF16)
    at = rows
    out_ref[pl.ds(at, rows), :] = mm(up_low_ref[...], sketch_ref[...]).astype(BF16)
    at += rows + rows // 2
    expand = expand_ref[...]
    low = mm_rows(down_low_ref[...], jnp.concatenate([expand, expand], axis=0))
    first, second = low[: rows // 2], low[rows // 2 :]
    out_ref[pl.ds(at, rows // 2), :] = jnp.where(half_lanes(first.shape), first, second).astype(BF16)
    at += rows // 2
    wide = val_ref[...].astype(F32)
    count, width = wide.shape
    scale = lax.rsqrt(jnp.sum(wide * wide, axis=1, keepdims=True) + 1e-06)
    unit = wide * scale
    blocks = [unit[:, i * LANES : (i + 1) * LANES] for i in range(width // LANES)]
    row = label_ref[...].astype(F32)
    labels = jnp.broadcast_to(diagonal_column(row, 0, count), (count, LANES))
    blocks += [labels, labels]
    for i in range(0, len(blocks), 2):
        pair = jnp.concatenate(blocks[i : i + 2], axis=0)
        out_ref[pl.ds(at + i * count, 2 * count), :] = pair.astype(BF16)


def local_kernel(*refs):
    x_hbm, mixed_hbm, adjoint_hbm, values_hbm, target_hbm, top_target_hbm = refs[:6]
    small_hbm, gain_hbm, source_hbm = refs[6:8], refs[8], refs[9]
    x_ref, mixed_ref, adjoint_ref, values_ref, target_ref, top_target_ref = refs[10:16]
    small_refs, turned_ref, sums_ref = refs[16:18], refs[18], refs[19]
    gain_ref, source_ref, sems = refs[20:]
    tokens, width = x_ref.shape
    span = width // STEPS
    copies = []
    for j in range(STEPS):
        part = pl.ds(j * span, span)
        pairs = (
            (gain_hbm.at[:, part], gain_ref.at[:, part]),
            (source_hbm.at[:, part], source_ref.at[:, part]),
            (x_hbm.at[:, part], x_ref.at[:, part]),
            (target_hbm.at[part], target_ref.at[part]),
        )
        copies.append(load(pairs, sems.at[j]))
    pairs = (
        (adjoint_hbm, adjoint_ref),
        (mixed_hbm, mixed_ref),
        (values_hbm, values_ref),
        (top_target_hbm, top_target_ref),
        *zip(small_hbm, small_refs),
    )
    later = load(pairs, sems.at[STEPS])
    products = jnp.zeros((tokens, 2 * LANES), F32)
    squares = jnp.zeros((tokens, LANES), F32)
    for j in range(STEPS):
        for copy in copies[j]:
            copy.wait()
        part = slice(j * span, (j + 1) * span)
        x, source = x_ref[:, part], source_ref[:, part].astype(F32)
        gained = source * gain_ref[:, part]
        turned_ref[part, :] = jnp.concatenate([source, source], axis=0).T.astype(BF16)
        gained = jnp.concatenate([gained, gained], axis=0).T.astype(BF16)
        products = products + mm(x, jnp.concatenate([gained, target_ref[part, :]], axis=1))
        for i in range(span // LANES):
            wide = x[:, i * LANES : (i + 1) * LANES].astype(F32)
            squares = squares + wide * wide
    mean = jnp.sum(squares, axis=1, keepdims=True) * (1.0 / width)
    inverse = jnp.broadcast_to(lax.rsqrt(mean + 1e-05), (tokens, LANES))
    for i, value in enumerate((inverse, inverse * products[:, :LANES], products[:, LANES:])):
        sums_ref[:, i * LANES : (i + 1) * LANES] = value
    for copy in later:
        copy.wait()


def add_stage(away, me_ref, pieces, held, old, scratch):
    x_ref, mixed_ref, adjoint_ref, values_ref, target_ref, top_target_ref, source_ref = held
    both, up, down = scratch
    rows = both.shape[0] // 2
    half, pad = rows // 2, LANES // 2
    span = 2 * rows
    me = me_ref[0]
    pos, core = ring_pos(me // 2), me % 2
    chip = ring_chip((pos + away * (2 * core - 1) + RING_CHIPS) % RING_CHIPS)
    odd = chip % 2
    mine = pl.ds(pl.multiple_of(chip * span, LANES), span)
    values_start = (chip // 2) * span + odd * (rows - pad)
    values_part = pl.ds(pl.multiple_of(values_start, LANES), rows + pad)
    side = core if away >= 0 else 1 - core
    up[pl.ds(pl.multiple_of((1 - odd) * rows, 16), pad), :] = jnp.zeros((pad, 2 * LANES), BF16)
    up[pl.ds(pl.multiple_of(odd * pad, 16), rows), pl.ds(LANES, LANES)] = top_target_ref[
        pl.ds(pl.multiple_of(chip * rows, 16), rows), :
    ]
    for piece, c in ((pieces[0], side), (pieces[1], 1 - side)):
        one = pl.ds(pl.multiple_of(c * rows, 16), rows)
        both[one, pl.ds(0, LANES)] = piece[pl.ds(0, rows), :]
        both[one, pl.ds(LANES, LANES)] = piece[pl.ds(rows, rows), :]
        up[pl.ds(pl.multiple_of(odd * pad + c * half, 16), half), pl.ds(0, LANES)] = piece[
            pl.ds(2 * rows, half), :
        ]
        packed = piece[pl.ds(2 * rows + half, half), :].astype(F32)
        turned = pltpu.roll(packed, pad, 1)
        lower = half_lanes(packed.shape)
        down[pl.ds(pl.multiple_of(c * rows, 16), half), :] = jnp.where(lower, packed, turned).astype(BF16)
        down[pl.ds(pl.multiple_of(c * rows + half, 16), half), :] = jnp.where(lower, turned, packed).astype(BF16)

    weights = both[...]
    down_up = weights[:, :LANES]
    lows = jnp.concatenate([weights[:, LANES:], target_ref[mine, :]], axis=1)
    bridge = mm_cols(down_up, lows)
    products = []
    for activation, factor in (
        (values_ref[:, values_part], up[...]),
        (x_ref[:, mine], weights),
        (adjoint_ref[:, mine], lows),
        (mixed_ref[:, mine], jnp.concatenate([down[...], source_ref[mine, :]], axis=1)),
    ):
        product = mm(activation, factor)
        products += [product[:, :LANES], product[:, LANES:]]
    if old:
        old_sums, old_bridge = old
        products = [p + old_sums[:, i * LANES : (i + 1) * LANES] for i, p in enumerate(products)]
        bridge = bridge + old_bridge[...]
    return products, bridge


def add_half(away, other, me_ref, piece, held, old, scratch):
    x_ref, mixed_ref, adjoint_ref, values_ref, target_ref, top_target_ref, source_ref = held
    wide, down, up = scratch
    pad = LANES // 2
    rows = wide.shape[0] - pad
    half, span = rows // 2, 2 * rows
    me = me_ref[0]
    pos, core = ring_pos(me // 2), me % 2
    chip = ring_chip((pos + away * (2 * core - 1) + RING_CHIPS) % RING_CHIPS)
    side = 1 - core if other else core
    odd = chip % 2
    mine = pl.ds(pl.multiple_of(chip * span + side * (rows - pad), LANES), rows + pad)
    inside = pl.ds(pl.multiple_of(side * pad, 16), rows)
    outside = pl.ds(pl.multiple_of((1 - side) * rows, 16), pad)
    block = pl.ds(pl.multiple_of(chip * span + side * rows, 16), rows)
    values_start = (chip // 2) * span + odd * (rows - pad)
    values_part = pl.ds(pl.multiple_of(values_start, LANES), rows + pad)
    values_inside = pl.ds(pl.multiple_of(odd * pad + side * half, 16), half)
    values_block = pl.ds(pl.multiple_of(chip * rows + side * half, 16), half)
    wide[outside, :] = jnp.zeros((pad, wide.shape[1]), BF16)
    down[outside, :] = jnp.zeros((pad, down.shape[1]), BF16)
    up[...] = jnp.zeros(up.shape, BF16)
    wide[inside, pl.ds(0, LANES)] = piece[pl.ds(0, rows), :]
    wide[inside, pl.ds(LANES, LANES)] = piece[pl.ds(rows, rows), :]
    wide[inside, pl.ds(2 * LANES, LANES)] = target_ref[block, :]
    up[values_inside, pl.ds(0, LANES)] = piece[pl.ds(2 * rows, half), :]
    up[values_inside, pl.ds(LANES, LANES)] = top_target_ref[values_block, :]
    packed = piece[pl.ds(2 * rows + half, half), :].astype(F32)
    turned = pltpu.roll(packed, pad, 1)
    lower = half_lanes(packed.shape)
    at = side * pad
    down[pl.ds(pl.multiple_of(at, 16), half), pl.ds(0, LANES)] = jnp.where(lower, packed, turned).astype(BF16)
    down[pl.ds(pl.multiple_of(at + half, 16), half), pl.ds(0, LANES)] = jnp.where(lower, turned, packed).astype(BF16)
    down[inside, pl.ds(LANES, LANES)] = source_ref[block, :]

    weights = wide[...]
    bridge = mm_cols(weights[:, :LANES], weights[:, LANES:])
    products = []
    for activation, factor in (
        (values_ref[:, values_part], up[...]),
        (x_ref[:, mine], weights[:, : 2 * LANES]),
        (adjoint_ref[:, mine], weights[:, LANES:]),
        (mixed_ref[:, mine], down[...]),
    ):
        product = mm(activation, factor)
        products += [product[:, :LANES], product[:, LANES:]]
    old_sums, old_bridge = old
    products = [p + old_sums[:, i * LANES : (i + 1) * LANES] for i, p in enumerate(products)]
    return products, bridge + old_bridge[...]


def half_kernel(away, me_ref, *refs):
    piece, held, old = refs[0], refs[1:8], refs[8:10]
    (new_sums, new_bridge), scratch = refs[10:12], refs[12:]
    products, bridge = add_half(away, False, me_ref, piece, held, old, scratch)
    for i in range(SUMS):
        new_sums[:, i * LANES : (i + 1) * LANES] = products[i]
    new_bridge[...] = bridge


def stage_kernel(away, first, me_ref, *refs):
    pieces, held, old = refs[:2], refs[2:9], refs[9:-5]
    (new_sums, new_bridge), scratch = refs[-5:-3], refs[-3:]
    products, bridge = add_stage(away, me_ref, pieces, held, old, scratch)
    for i in range(SUMS):
        new_sums[:, i * LANES : (i + 1) * LANES] = products[i]
    new_bridge[...] = bridge


def feature_kernel(away, me_ref, counts_ref, *refs):
    piece, held, old, local_ref, expand_ref, sketch_ref = refs[0], refs[1:8], refs[8:10], *refs[10:13]
    out_ref, scratch = refs[13], refs[14:]
    products, bridge = add_half(away, True, me_ref, piece, held, old, scratch)
    local = [local_ref[:, i * LANES : (i + 1) * LANES] for i in range(LOCAL_SUMS)]
    tokens, width = held[0].shape
    half = LANES // 2
    inverse = local[INVERSE]
    returned = products[VALUES].astype(BF16)
    back = mm(returned, jnp.concatenate([bridge.astype(BF16), sketch_ref[...]], axis=1))
    right_one = ALPHA * back[:, 2 * LANES :]
    reduced = inverse * products[X_DOWN]
    expand = expand_ref[...]
    left_two = mm_rows(reduced.astype(BF16), jnp.concatenate([expand, expand], axis=0))
    along = (ALPHA / width) * jnp.sum(returned.astype(F32) * reduced, axis=1, keepdims=True)
    along = along * inverse
    right_three = products[J_LOW] + inverse * (ALPHA * back[:, :LANES] - along * products[X_LOW])
    right_four = products[J_TARGET] + inverse * (ALPHA * back[:, LANES : 2 * LANES] - along * local[X_TARGET])
    rights = (right_one, ALPHA * products[V_TARGET], ALPHA * right_three, ALPHA * right_four)
    lefts = (local[LEFT_ONE], left_two, products[M_SOURCE], products[M_DOWN])
    place = lax.broadcasted_iota(jnp.int32, (tokens, LANES), 0)
    one, two = counts_ref[0, 0], counts_ref[0, 1]
    lower = half_lanes((tokens, LANES))
    member = (place >= jnp.where(lower, 0, one)) & (place < jnp.where(lower, one, one + two))
    feats = jnp.zeros((LANES, LANES), F32)
    for left, right in zip(lefts, rights):
        feats = feats + mm_cols(jnp.where(member, left, 0.0).astype(BF16), right.astype(BF16))
    for e in range(2):
        own = feats[e * half : (e + 1) * half]
        squares = jnp.sum(own * own, keepdims=True)
        out_ref[pl.ds(e * half, half), :] = (own * lax.rsqrt(squares + 1e-06)).astype(BF16).astype(F32)


def split_kernel(block_ref, *refs):
    head_ref, tail_ref = refs[-2:]
    cut, tail = head_ref.shape[0], block_ref.shape[0] - head_ref.shape[0]
    head_ref[...] = block_ref[pl.ds(0, cut), :]
    if len(refs) == 3:
        tail_ref[pl.ds(0, tail), :] = refs[0][...]
    tail_ref[pl.ds(tail_ref.shape[0] - tail, tail), :] = block_ref[pl.ds(cut, tail), :]


def best_of(places, count, unit_ref, best):
    half = LANES // 2
    scale = float(half * LANES) ** 0.5
    shape = (count, LANES)
    totals = [[jnp.zeros(shape, F32) for _ in range(2)] for _ in places]
    for i in range(0, half, 2):
        units = [
            [jnp.broadcast_to(unit_ref[pl.ds(e * half + i + k, 1), :], shape) for k in range(2)]
            for e in range(2)
        ]
        for b, (block, start) in enumerate(places):
            wide = block[pl.ds(start + i * count, 2 * count), :].astype(F32)
            for e in range(2):
                totals[b][e] = totals[b][e] + (wide[:count] * units[e][0] + wide[count:] * units[e][1])
    for b, (block, start) in enumerate(places):
        labels = block[pl.ds(start + half * count, 2 * count), :].astype(F32)[:count]
        for e in range(2):
            similar = scale * jnp.sum(totals[b][e], axis=1, keepdims=True)
            for t in range(TASKS):
                best[e][t] = jnp.maximum(best[e][t], jnp.where(labels == float(t), similar, -2.0 * scale))


def places_of(blocks, count):
    size = (LANES // 2 + 2) * count
    places = []
    for block in blocks:
        total = block.shape[0]
        firsts = range(0, total, size) if total % size == 0 else [total - size]
        places += [(block, first) for first in firsts]
    return places


def score_kernel(blocks, count, unit_ref, *refs):
    block_refs, best_ref = refs[:blocks], refs[blocks]
    lowest = -2.0 * float(LANES // 2 * LANES) ** 0.5
    best = [[jnp.full((count, LANES), lowest, F32) for _ in range(TASKS)] for _ in range(2)]
    best_of(places_of(block_refs, count), count, unit_ref, best)
    for e in range(2):
        for t in range(TASKS):
            best_ref[e, t] = best[e][t]


def last_score_kernel(count, unit_ref, block_ref, best_ref, out_ref, mean_ref):
    best = [[best_ref[e, t] for t in range(TASKS)] for e in range(2)]
    best_of(places_of([block_ref], count), count, unit_ref, best)
    lane = lax.broadcasted_iota(jnp.int32, (1, LANES), 1)
    means = []
    for e in range(2):
        values = [jnp.max(best[e][t], axis=0, keepdims=True) for t in range(TASKS)]
        row = jnp.where(lane == 0, values[0], jnp.where(lane == 1, values[1], values[2]))
        out_ref[pl.ds(e, 1), :] = row[:, :TASKS]
        means.append((values[0] + values[1] + values[2]) * (1.0 / TASKS))
    mean_ref[...] = jnp.where(lane == 0, means[0], means[1])[:, :2]


VMEM = pl.BlockSpec(memory_space=pltpu.VMEM)
SMEM = pl.BlockSpec(memory_space=pltpu.SMEM)
ANY = pl.BlockSpec(memory_space=pl.ANY)
HBM = pl.BlockSpec(memory_space=pltpu.HBM)


def in_hbm(arrays):
    return [pltpu.with_memory_space_constraint(a, pltpu.HBM) for a in arrays]


def params(mib):
    return pltpu.CompilerParams(vmem_limit_bytes=mib * MIB)


def cost(flops, nbytes):
    return pl.CostEstimate(flops=flops, bytes_accessed=nbytes, transcendentals=0)


def shards(
    hidden_state_input,
    attention_mixed_state,
    hidden_state_adjoint,
    attention_values_adjoint,
    sequence_token_counts,
    heldout_sketched_signals,
    benchmark_labels,
    top_rmsnorm_weights,
    top_reducer_matrix,
    top_expander_matrix,
    bottom_reducer_matrix,
    bottom_expander_matrix,
    source_sketch,
    top_reducer_sketch,
    top_expander_sketch,
    top_target_sketch,
    bottom_reducer_sketch,
    bottom_expander_sketch,
    bottom_target_sketch,
):
    me = lax.axis_index("dp").astype(jnp.int32)
    x, mixed, adjoint, values = (
        hidden_state_input,
        attention_mixed_state,
        hidden_state_adjoint,
        attention_values_adjoint,
    )
    tokens, width = x.shape
    rows = top_reducer_matrix.shape[0]
    count = heldout_sketched_signals.shape[0]

    inputs = (
        top_expander_matrix.T,
        heldout_sketched_signals,
        top_reducer_matrix,
        bottom_expander_matrix.T,
        bottom_reducer_matrix,
        top_rmsnorm_weights.reshape(width // LANES, LANES),
        bottom_reducer_sketch,
        bottom_expander_sketch.T,
        benchmark_labels.T,
    )
    own = pl.pallas_call(
        pack_kernel,
        out_shape=jax.ShapeDtypeStruct((3 * rows + (LANES // 2 + 2) * count, LANES), BF16),
        in_specs=[SMEM] + [HBM] * len(inputs),
        out_specs=VMEM,
        scratch_shapes=[pltpu.VMEM(a.shape, a.dtype) for a in inputs[1:]]
        + [pltpu.SemaphoreType.DMA((len(inputs),))],
        compiler_params=params(8),
        name="pack",
    )(me.reshape(1), *in_hbm(inputs))

    inputs = (
        x,
        mixed,
        adjoint,
        values,
        bottom_target_sketch,
        top_target_sketch,
        top_expander_sketch.T,
        top_reducer_sketch,
        top_rmsnorm_weights.reshape(1, width),
        source_sketch.T,
    )
    *activations, local = pl.pallas_call(
        local_kernel,
        out_shape=[jax.ShapeDtypeStruct(a.shape, a.dtype) for a in inputs[:8]]
        + [
            jax.ShapeDtypeStruct((width, LANES), BF16),
            jax.ShapeDtypeStruct((tokens, LOCAL_SUMS * LANES), F32),
        ],
        in_specs=[HBM] * len(inputs),
        out_specs=[VMEM] * 10,
        scratch_shapes=[pltpu.VMEM(a.shape, a.dtype) for a in inputs[8:]]
        + [pltpu.SemaphoreType.DMA((STEPS + 1, 6))],
        compiler_params=params(24),
        cost_estimate=cost(tokens * width * LANES * 6, 14 * MIB),
        name="local_products",
    )(*in_hbm(inputs))
    activations, small = [*activations[:6], activations[8]], activations[6:8]

    stage_scratch = [
        pltpu.VMEM((2 * rows, 2 * LANES), BF16),
        pltpu.VMEM((rows + LANES // 2, 2 * LANES), BF16),
        pltpu.VMEM((2 * rows, LANES), BF16),
    ]

    def stage(away, pieces, sums):
        first = not sums
        start = 1 + len(pieces) + len(activations)
        return pl.pallas_call(
            functools.partial(stage_kernel, away, first),
            out_shape=[
                jax.ShapeDtypeStruct((tokens, SUMS * LANES), F32),
                jax.ShapeDtypeStruct((LANES, 2 * LANES), F32),
            ],
            in_specs=[SMEM] + [VMEM] * (len(pieces) + len(activations) + len(sums)),
            out_specs=[VMEM, VMEM],
            scratch_shapes=stage_scratch,
            input_output_aliases={} if first else {start: 0, start + 1: 1},
            compiler_params=params(16),
            cost_estimate=cost(tokens * rows * LANES * 16, 2 * MIB),
            name="stage",
        )(me.reshape(1), *pieces, *activations, *sums)

    def split(block, *tails):
        tail = block.shape[0] - 3 * rows
        shapes = (3 * rows, LANES), ((1 + len(tails)) * tail, LANES)
        return pl.pallas_call(
            split_kernel,
            out_shape=[jax.ShapeDtypeStruct(shape, BF16) for shape in shapes],
            in_specs=[VMEM] * (1 + len(tails)),
            out_specs=[VMEM, VMEM],
            compiler_params=params(8),
            name="split",
        )(block, *tails)

    tie = lax.optimization_barrier
    half = RING_CHIPS // 2
    held = [own, other_core(own)]
    blocks = list(held)
    first, second = hop(held[0]), hop(held[1])
    first, activations = tie((first, activations))
    sums = stage(0, held, [])
    second, sums = tie((second, sums))
    for k in range(1, half):
        held = [first, second]
        crossed = [other_core(first), other_core(second)]
        blocks += [first, crossed[0]]
        if k < half - 1:
            blocks += [second, crossed[1]]
        else:
            first, tails = split(first, tail)
            tails, sums = tie((tails, sums))
        first = hop(first)
        sums = stage(k, held, sums)
        first, sums = tie((first, sums))
        if k == half - 2:
            second, tail = split(second)
        if k < half - 1:
            second = hop(second)
        sums = stage(-k, crossed, sums)
        if k < half - 1:
            second, sums = tie((second, sums))
    tails = hop(tails)
    half_scratch = [
        pltpu.VMEM((rows + LANES // 2, 3 * LANES), BF16),
        pltpu.VMEM((rows + LANES // 2, 2 * LANES), BF16),
        pltpu.VMEM((rows + LANES // 2, 2 * LANES), BF16),
    ]
    crossed = other_core(first)
    start = 2 + len(activations)
    sums = pl.pallas_call(
        functools.partial(half_kernel, half),
        out_shape=[jax.ShapeDtypeStruct(a.shape, a.dtype) for a in sums],
        in_specs=[SMEM] + [VMEM] * (1 + len(activations) + 2),
        out_specs=[VMEM, VMEM],
        scratch_shapes=half_scratch,
        input_output_aliases={start: 0, start + 1: 1},
        compiler_params=params(16),
        cost_estimate=cost(tokens * rows * LANES * 8, MIB),
        name="half_stage",
    )(me.reshape(1), first, *activations, *sums)
    unit = pl.pallas_call(
        functools.partial(feature_kernel, half),
        out_shape=jax.ShapeDtypeStruct((LANES, LANES), F32),
        in_specs=[SMEM] * 2 + [VMEM] * (1 + len(activations) + 5),
        out_specs=VMEM,
        scratch_shapes=half_scratch,
        compiler_params=params(16),
        cost_estimate=cost(1, 1),
        name="features",
    )(me.reshape(1), sequence_token_counts, crossed, *activations, *sums, local, *small)
    tails, unit = tie((tails, unit))
    blocks.append(tails)
    best = pl.pallas_call(
        functools.partial(score_kernel, len(blocks), count),
        out_shape=jax.ShapeDtypeStruct((2, TASKS, count, LANES), F32),
        in_specs=[VMEM] * (1 + len(blocks)),
        out_specs=VMEM,
        compiler_params=params(16),
        cost_estimate=cost(4 * MIB, 2 * MIB),
        name="scores",
    )(unit, *blocks)
    task_best, scores = pl.pallas_call(
        functools.partial(last_score_kernel, count),
        out_shape=(jax.ShapeDtypeStruct((2, TASKS), F32), jax.ShapeDtypeStruct((1, 2), F32)),
        in_specs=[VMEM] * 3,
        out_specs=(VMEM, VMEM),
        compiler_params=params(8),
        name="last_scores",
    )(unit, other_core(tails), best)
    return (scores.reshape(2), task_best)


def shards_of_any_slice(
    hidden_state_input,
    attention_mixed_state,
    hidden_state_adjoint,
    attention_values_adjoint,
    sequence_token_counts,
    heldout_sketched_signals,
    benchmark_labels,
    top_rmsnorm_weights,
    top_reducer_matrix,
    top_expander_matrix,
    bottom_reducer_matrix,
    bottom_expander_matrix,
    source_sketch,
    top_reducer_sketch,
    top_expander_sketch,
    top_target_sketch,
    bottom_reducer_sketch,
    bottom_expander_sketch,
    bottom_target_sketch,
    n,
):
    me = lax.axis_index("dp")
    x, mixed, adjoint, values = (
        hidden_state_input,
        attention_mixed_state,
        hidden_state_adjoint,
        attention_values_adjoint,
    )
    tokens, width = x.shape
    rows = top_reducer_matrix.shape[0]
    up_rows = top_expander_matrix.shape[1]
    rank = top_reducer_matrix.shape[1]
    k1 = source_sketch.shape[1]
    gain = top_rmsnorm_weights
    own_gain = lax.dynamic_slice_in_dim(gain, me * rows, rows)

    down_upper = (own_gain[:, None] * top_reducer_matrix.astype(F32)).astype(BF16)
    up_lower = mm(bottom_expander_matrix.T, bottom_reducer_sketch).astype(BF16)
    down_lower = mm(bottom_reducer_matrix, bottom_expander_sketch).astype(BF16)
    packed_lower = jnp.concatenate([down_lower[: rows // 2], down_lower[rows // 2 :]], axis=1)
    factors = jnp.concatenate([down_upper, up_lower, top_expander_matrix.T, packed_lower], axis=0)
    factors = lax.all_gather(factors, "dp")

    val_wide = heldout_sketched_signals.astype(F32)
    val_unit = (
        val_wide * lax.rsqrt(jnp.sum(val_wide * val_wide, axis=1, keepdims=True) + 1e-06)
    ).astype(BF16)
    labels = jnp.broadcast_to(benchmark_labels.astype(BF16), (val_unit.shape[0], 128))
    panel = jnp.concatenate([val_unit.reshape(-1, 128), labels], axis=0)
    panel = lax.all_gather(panel, "dp")
    val_rows = val_unit.shape[0]
    cut = panel.shape[1] - val_rows
    panel_tasks = panel[:, cut:, 0].reshape(n * val_rows, 1).astype(jnp.int32)
    panel = panel[:, :cut].reshape(n * val_rows, val_unit.shape[1])

    wide = x.astype(F32)
    inverse = lax.rsqrt(jnp.mean(wide * wide, axis=1, keepdims=True) + 1e-05)
    gained_sketch = (gain[:, None] * source_sketch.astype(F32)).astype(BF16)
    left_one = inverse * mm(x, gained_sketch)
    left_three = mm(mixed, source_sketch)
    right_two = ALPHA * mm(values, top_target_sketch)

    at = 0
    down_upper = factors[:, at : at + rows].reshape(width, rank)
    at += rows
    up_lower = factors[:, at : at + rows].reshape(width, -1)
    at += rows
    up_upper = factors[:, at : at + up_rows].reshape(-1, rank)
    at += up_rows
    down_lower = factors[:, at:]
    down_lower = jnp.concatenate([down_lower[:, :, :k1], down_lower[:, :, k1:]], axis=1)
    down_lower = down_lower.reshape(width, k1)

    reduced = inverse * mm(x, down_upper)
    left_two = mm(reduced.astype(BF16), top_expander_sketch)
    left_four = mm(mixed, down_lower)
    returned = mm(values, up_upper).astype(BF16)
    right_one = ALPHA * mm(returned, top_reducer_sketch)
    along = (ALPHA / width) * jnp.sum(returned.astype(F32) * reduced, axis=1, keepdims=True)
    targets = jnp.concatenate([up_lower, bottom_target_sketch], axis=1)
    bridge = mm_cols(down_upper, targets).astype(BF16)
    rights_low = mm(adjoint, targets) + inverse * (
        ALPHA * mm(returned, bridge) - (along * inverse) * mm(x, targets)
    )
    rights_low = ALPHA * rights_low
    k2 = up_lower.shape[1]
    lefts = (left_one, left_two, left_three, left_four)
    rights = (right_one, right_two, rights_low[:, :k2], rights_low[:, k2:])

    counts = sequence_token_counts[0]
    ends = jnp.cumsum(counts)
    starts = ends - counts
    places = jnp.arange(tokens, dtype=jnp.int32)[:, None]
    member = (places >= starts[None, :]) & (places < ends[None, :])
    count_ex = counts.shape[0]
    spread = jnp.concatenate(lefts, axis=0).astype(BF16)
    member = jnp.tile(member, (4, 1))
    spread = jnp.concatenate(
        [jnp.where(member[:, e : e + 1], spread, 0) for e in range(count_ex)], axis=1
    )
    feats = mm_cols(spread, jnp.concatenate(rights, axis=0).astype(BF16))
    feats = feats.reshape(count_ex, -1)
    squares = jnp.sum(feats * feats, axis=1, keepdims=True)
    unit_rows = (feats * lax.rsqrt(squares + 1e-06)).astype(BF16)

    score_scale = float(unit_rows.shape[1]) ** 0.5
    similar = score_scale * mm_rows(unit_rows, panel)
    task_mask = panel_tasks == jnp.arange(TASKS, dtype=jnp.int32)[None, :]
    task_best = jnp.max(
        jnp.where(task_mask[None, :, :], similar[:, :, None], -2.0 * score_scale), axis=1
    )
    return (jnp.mean(task_best, axis=1), task_best)


def solution(mesh):
    n = mesh.shape["dp"]
    split = P(("parts", "dp"), None)
    by_row, by_column, whole = P("dp", None), P(None, "dp"), P()
    placed = (
        (split,) * 5
        + (by_row, by_row, whole)
        + (by_row, by_column, by_row, by_column)
        + (whole,) * 7
    )
    ours = shards if n == 2 * RING_CHIPS else functools.partial(shards_of_any_slice, n=n)
    return jax.shard_map(
        ours,
        mesh=mesh,
        in_specs=placed,
        out_specs=(P(("parts", "dp")), split),
        check_vma=False,
    )
```

```python
import functools

import jax
import jax.numpy as jnp
from jax import lax
from jax.experimental import pallas as pl
from jax.experimental.pallas import tpu as pltpu
from jax.sharding import PartitionSpec as P

TASKS = 3
ALPHA = 4.0
F32 = jnp.float32
BF16 = jnp.bfloat16
RING_CHIPS = 8
LANES = 128
STEPS = 4
VALUES, V_TARGET, X_DOWN, X_LOW, J_LOW, J_TARGET, M_DOWN, M_SOURCE, SUMS = range(9)
INVERSE, LEFT_ONE, X_TARGET, LOCAL_SUMS = range(4)
MIB = 1 << 20


def mm(a, b):
    return jnp.dot(a, b, preferred_element_type=F32)


def mm_rows(a, b):
    return lax.dot_general(a, b, (((1,), (1,)), ((), ())), preferred_element_type=F32)


def mm_cols(a, b):
    return lax.dot_general(a, b, (((0,), (0,)), ((), ())), preferred_element_type=F32)


def ring_chip(pos):
    half = RING_CHIPS // 2
    return jnp.where(pos < half, 2 * pos, 2 * (RING_CHIPS - 1 - pos) + 1)


def ring_pos(chip):
    row, side = chip // 2, chip % 2
    return jnp.where(side == 0, row, RING_CHIPS - 1 - row)


def hop(value):
    half = RING_CHIPS // 2
    place = [2 * q if q < half else 2 * (RING_CHIPS - 1 - q) + 1 for q in range(RING_CHIPS)]
    pairs = []
    for q in range(RING_CHIPS):
        pairs.append((2 * place[q], 2 * place[(q + 1) % RING_CHIPS]))
        pairs.append((2 * place[q] + 1, 2 * place[(q - 1) % RING_CHIPS] + 1))
    return lax.ppermute(value, "dp", pairs)


def other_core(value):
    return lax.ppermute(value, "dp", [(d, d ^ 1) for d in range(2 * RING_CHIPS)])


def half_lanes(shape):
    return lax.broadcasted_iota(jnp.int32, shape, 1) < LANES // 2


def diagonal_column(row, first, count):
    shape = (count, row.shape[1])
    lane = lax.broadcasted_iota(jnp.int32, shape, 1)
    at = lax.broadcasted_iota(jnp.int32, shape, 0)
    return jnp.sum(jnp.where(lane == at + first, row, 0.0), axis=1, keepdims=True)


def load(pairs, sems):
    copies = [pltpu.make_async_copy(src, dst, sems.at[i]) for i, (src, dst) in enumerate(pairs)]
    for copy in copies:
        copy.start()
    return copies


def pack_kernel(me_ref, *refs):
    up_up_hbm, hbm, out_ref, held, sems = refs[0], refs[1:9], refs[9], refs[10:18], refs[18]
    val_ref, down_up_ref, up_low_ref, down_low_ref, gain_ref, sketch_ref, expand_ref, label_ref = held
    rows = down_up_ref.shape[0]
    half = LANES // 2
    direct = (up_up_hbm, out_ref.at[pl.ds(2 * rows, rows // 2)])
    for copy in load((*zip(hbm, held), direct), sems):
        copy.wait()
    for b in range(rows // half):
        place = me_ref[0] * (rows // half) + b
        row = gain_ref[pl.ds(place // 2, 1), :]
        column = diagonal_column(row, (place % 2) * half, half)
        part = down_up_ref[pl.ds(b * half, half), :].astype(F32)
        out_ref[pl.ds(b * half, half), :] = (column * part).astype(BF16)
    at = rows
    out_ref[pl.ds(at, rows), :] = mm(up_low_ref[...], sketch_ref[...]).astype(BF16)
    at += rows + rows // 2
    expand = expand_ref[...]
    low = mm_rows(down_low_ref[...], jnp.concatenate([expand, expand], axis=0))
    first, second = low[: rows // 2], low[rows // 2 :]
    out_ref[pl.ds(at, rows // 2), :] = jnp.where(half_lanes(first.shape), first, second).astype(BF16)
    at += rows // 2
    wide = val_ref[...].astype(F32)
    count, width = wide.shape
    scale = lax.rsqrt(jnp.sum(wide * wide, axis=1, keepdims=True) + 1e-06)
    unit = wide * scale
    blocks = [unit[:, i * LANES : (i + 1) * LANES] for i in range(width // LANES)]
    row = label_ref[...].astype(F32)
    labels = jnp.broadcast_to(diagonal_column(row, 0, count), (count, LANES))
    blocks += [labels, labels]
    for i in range(0, len(blocks), 2):
        pair = jnp.concatenate(blocks[i : i + 2], axis=0)
        out_ref[pl.ds(at + i * count, 2 * count), :] = pair.astype(BF16)


def local_kernel(*refs):
    x_hbm, mixed_hbm, adjoint_hbm, values_hbm, target_hbm, top_target_hbm = refs[:6]
    small_hbm, gain_hbm, source_hbm = refs[6:8], refs[8], refs[9]
    x_ref, mixed_ref, adjoint_ref, values_ref, target_ref, top_target_ref = refs[10:16]
    small_refs, turned_ref, sums_ref = refs[16:18], refs[18], refs[19]
    gain_ref, source_ref, sems = refs[20:]
    tokens, width = x_ref.shape
    span = width // STEPS
    copies = []
    for j in range(STEPS):
        part = pl.ds(j * span, span)
        pairs = (
            (gain_hbm.at[:, part], gain_ref.at[:, part]),
            (source_hbm.at[:, part], source_ref.at[:, part]),
            (x_hbm.at[:, part], x_ref.at[:, part]),
            (target_hbm.at[part], target_ref.at[part]),
        )
        copies.append(load(pairs, sems.at[j]))
    pairs = (
        (adjoint_hbm, adjoint_ref),
        (mixed_hbm, mixed_ref),
        (values_hbm, values_ref),
        (top_target_hbm, top_target_ref),
        *zip(small_hbm, small_refs),
    )
    later = load(pairs, sems.at[STEPS])
    products = jnp.zeros((tokens, 2 * LANES), F32)
    squares = jnp.zeros((tokens, LANES), F32)
    for j in range(STEPS):
        for copy in copies[j]:
            copy.wait()
        part = slice(j * span, (j + 1) * span)
        x, source = x_ref[:, part], source_ref[:, part].astype(F32)
        gained = source * gain_ref[:, part]
        turned_ref[part, :] = jnp.concatenate([source, source], axis=0).T.astype(BF16)
        gained = jnp.concatenate([gained, gained], axis=0).T.astype(BF16)
        products = products + mm(x, jnp.concatenate([gained, target_ref[part, :]], axis=1))
        for i in range(span // LANES):
            wide = x[:, i * LANES : (i + 1) * LANES].astype(F32)
            squares = squares + wide * wide
    mean = jnp.sum(squares, axis=1, keepdims=True) * (1.0 / width)
    inverse = jnp.broadcast_to(lax.rsqrt(mean + 1e-05), (tokens, LANES))
    for i, value in enumerate((inverse, inverse * products[:, :LANES], products[:, LANES:])):
        sums_ref[:, i * LANES : (i + 1) * LANES] = value
    for copy in later:
        copy.wait()


def add_stage(away, me_ref, pieces, held, old, scratch):
    x_ref, mixed_ref, adjoint_ref, values_ref, target_ref, top_target_ref, source_ref = held
    both, up, down = scratch
    rows = both.shape[0] // 2
    half, pad = rows // 2, LANES // 2
    span = 2 * rows
    me = me_ref[0]
    pos, core = ring_pos(me // 2), me % 2
    chip = ring_chip((pos + away * (2 * core - 1) + RING_CHIPS) % RING_CHIPS)
    odd = chip % 2
    mine = pl.ds(pl.multiple_of(chip * span, LANES), span)
    values_start = (chip // 2) * span + odd * (rows - pad)
    values_part = pl.ds(pl.multiple_of(values_start, LANES), rows + pad)
    side = core if away >= 0 else 1 - core
    up[pl.ds(pl.multiple_of((1 - odd) * rows, 16), pad), :] = jnp.zeros((pad, 2 * LANES), BF16)
    up[pl.ds(pl.multiple_of(odd * pad, 16), rows), pl.ds(LANES, LANES)] = top_target_ref[
        pl.ds(pl.multiple_of(chip * rows, 16), rows), :
    ]
    for piece, c in ((pieces[0], side), (pieces[1], 1 - side)):
        one = pl.ds(pl.multiple_of(c * rows, 16), rows)
        both[one, pl.ds(0, LANES)] = piece[pl.ds(0, rows), :]
        both[one, pl.ds(LANES, LANES)] = piece[pl.ds(rows, rows), :]
        up[pl.ds(pl.multiple_of(odd * pad + c * half, 16), half), pl.ds(0, LANES)] = piece[
            pl.ds(2 * rows, half), :
        ]
        packed = piece[pl.ds(2 * rows + half, half), :].astype(F32)
        turned = pltpu.roll(packed, pad, 1)
        lower = half_lanes(packed.shape)
        down[pl.ds(pl.multiple_of(c * rows, 16), half), :] = jnp.where(lower, packed, turned).astype(BF16)
        down[pl.ds(pl.multiple_of(c * rows + half, 16), half), :] = jnp.where(lower, turned, packed).astype(BF16)

    weights = both[...]
    down_up = weights[:, :LANES]
    lows = jnp.concatenate([weights[:, LANES:], target_ref[mine, :]], axis=1)
    bridge = mm_cols(down_up, lows)
    products = []
    for activation, factor in (
        (values_ref[:, values_part], up[...]),
        (x_ref[:, mine], weights),
        (adjoint_ref[:, mine], lows),
        (mixed_ref[:, mine], jnp.concatenate([down[...], source_ref[mine, :]], axis=1)),
    ):
        product = mm(activation, factor)
        products += [product[:, :LANES], product[:, LANES:]]
    if old:
        products = [p + q for p, q in zip(products, old[0])]
        bridge = bridge + old[1]
    return products, bridge


def read_sums(refs):
    return [refs[0][:, i * LANES : (i + 1) * LANES] for i in range(SUMS)], refs[1][...]


def add_half(away, other, me_ref, piece, held, old, scratch):
    x_ref, mixed_ref, adjoint_ref, values_ref, target_ref, top_target_ref, source_ref = held
    wide, down, up = scratch
    pad = LANES // 2
    rows = wide.shape[0] - pad
    half, span = rows // 2, 2 * rows
    me = me_ref[0]
    pos, core = ring_pos(me // 2), me % 2
    chip = ring_chip((pos + away * (2 * core - 1) + RING_CHIPS) % RING_CHIPS)
    side = 1 - core if other else core
    odd = chip % 2
    mine = pl.ds(pl.multiple_of(chip * span + side * (rows - pad), LANES), rows + pad)
    inside = pl.ds(pl.multiple_of(side * pad, 16), rows)
    outside = pl.ds(pl.multiple_of((1 - side) * rows, 16), pad)
    block = pl.ds(pl.multiple_of(chip * span + side * rows, 16), rows)
    values_start = (chip // 2) * span + odd * (rows - pad)
    values_part = pl.ds(pl.multiple_of(values_start, LANES), rows + pad)
    values_inside = pl.ds(pl.multiple_of(odd * pad + side * half, 16), half)
    values_block = pl.ds(pl.multiple_of(chip * rows + side * half, 16), half)
    wide[outside, :] = jnp.zeros((pad, wide.shape[1]), BF16)
    down[outside, :] = jnp.zeros((pad, down.shape[1]), BF16)
    up[...] = jnp.zeros(up.shape, BF16)
    wide[inside, pl.ds(0, LANES)] = piece[pl.ds(0, rows), :]
    wide[inside, pl.ds(LANES, LANES)] = piece[pl.ds(rows, rows), :]
    wide[inside, pl.ds(2 * LANES, LANES)] = target_ref[block, :]
    up[values_inside, pl.ds(0, LANES)] = piece[pl.ds(2 * rows, half), :]
    up[values_inside, pl.ds(LANES, LANES)] = top_target_ref[values_block, :]
    packed = piece[pl.ds(2 * rows + half, half), :].astype(F32)
    turned = pltpu.roll(packed, pad, 1)
    lower = half_lanes(packed.shape)
    at = side * pad
    down[pl.ds(pl.multiple_of(at, 16), half), pl.ds(0, LANES)] = jnp.where(lower, packed, turned).astype(BF16)
    down[pl.ds(pl.multiple_of(at + half, 16), half), pl.ds(0, LANES)] = jnp.where(lower, turned, packed).astype(BF16)
    down[inside, pl.ds(LANES, LANES)] = source_ref[block, :]

    weights = wide[...]
    bridge = mm_cols(weights[:, :LANES], weights[:, LANES:])
    products = []
    for activation, factor in (
        (values_ref[:, values_part], up[...]),
        (x_ref[:, mine], weights[:, : 2 * LANES]),
        (adjoint_ref[:, mine], weights[:, LANES:]),
        (mixed_ref[:, mine], down[...]),
    ):
        product = mm(activation, factor)
        products += [product[:, :LANES], product[:, LANES:]]
    return [p + q for p, q in zip(products, old[0])], bridge + old[1]


def stage_and_half_kernel(away, half_away, me_ref, *refs):
    pieces, piece, held, old = refs[:2], refs[2], refs[3:10], refs[10:12]
    (new_sums, new_bridge), scratch, half_scratch = refs[12:14], refs[14:17], refs[17:]
    sums = add_stage(away, me_ref, pieces, held, read_sums(old), scratch)
    products, bridge = add_half(half_away, False, me_ref, piece, held, sums, half_scratch)
    for i in range(SUMS):
        new_sums[:, i * LANES : (i + 1) * LANES] = products[i]
    new_bridge[...] = bridge


def stage_kernel(away, first, me_ref, *refs):
    pieces, held, old = refs[:2], refs[2:9], refs[9:-5]
    (new_sums, new_bridge), scratch = refs[-5:-3], refs[-3:]
    products, bridge = add_stage(away, me_ref, pieces, held, read_sums(old) if old else (), scratch)
    for i in range(SUMS):
        new_sums[:, i * LANES : (i + 1) * LANES] = products[i]
    new_bridge[...] = bridge


def feature_kernel(away, me_ref, counts_ref, *refs):
    piece, held, old, local_ref, expand_ref, sketch_ref = refs[0], refs[1:8], refs[8:10], *refs[10:13]
    out_ref, scratch = refs[13], refs[14:]
    products, bridge = add_half(away, True, me_ref, piece, held, read_sums(old), scratch)
    local = [local_ref[:, i * LANES : (i + 1) * LANES] for i in range(LOCAL_SUMS)]
    tokens, width = held[0].shape
    half = LANES // 2
    inverse = local[INVERSE]
    returned = products[VALUES].astype(BF16)
    back = mm(returned, jnp.concatenate([bridge.astype(BF16), sketch_ref[...]], axis=1))
    right_one = ALPHA * back[:, 2 * LANES :]
    reduced = inverse * products[X_DOWN]
    expand = expand_ref[...]
    left_two = mm_rows(reduced.astype(BF16), jnp.concatenate([expand, expand], axis=0))
    along = (ALPHA / width) * jnp.sum(returned.astype(F32) * reduced, axis=1, keepdims=True)
    along = along * inverse
    right_three = products[J_LOW] + inverse * (ALPHA * back[:, :LANES] - along * products[X_LOW])
    right_four = products[J_TARGET] + inverse * (ALPHA * back[:, LANES : 2 * LANES] - along * local[X_TARGET])
    rights = (right_one, ALPHA * products[V_TARGET], ALPHA * right_three, ALPHA * right_four)
    lefts = (local[LEFT_ONE], left_two, products[M_SOURCE], products[M_DOWN])
    place = lax.broadcasted_iota(jnp.int32, (tokens, LANES), 0)
    one, two = counts_ref[0, 0], counts_ref[0, 1]
    lower = half_lanes((tokens, LANES))
    member = (place >= jnp.where(lower, 0, one)) & (place < jnp.where(lower, one, one + two))
    feats = jnp.zeros((LANES, LANES), F32)
    for left, right in zip(lefts, rights):
        feats = feats + mm_cols(jnp.where(member, left, 0.0).astype(BF16), right.astype(BF16))
    for e in range(2):
        own = feats[e * half : (e + 1) * half]
        squares = jnp.sum(own * own, keepdims=True)
        out_ref[pl.ds(e * half, half), :] = (own * lax.rsqrt(squares + 1e-06)).astype(BF16).astype(F32)


def split_kernel(block_ref, *refs):
    head_ref, tail_ref = refs[-2:]
    cut, tail = head_ref.shape[0], block_ref.shape[0] - head_ref.shape[0]
    head_ref[...] = block_ref[pl.ds(0, cut), :]
    if len(refs) == 3:
        tail_ref[pl.ds(0, tail), :] = refs[0][...]
    tail_ref[pl.ds(tail_ref.shape[0] - tail, tail), :] = block_ref[pl.ds(cut, tail), :]


def best_of(places, count, unit_ref, best):
    half = LANES // 2
    scale = float(half * LANES) ** 0.5
    shape = (count, LANES)
    totals = [[jnp.zeros(shape, F32) for _ in range(2)] for _ in places]
    for i in range(0, half, 2):
        units = [
            [jnp.broadcast_to(unit_ref[pl.ds(e * half + i + k, 1), :], shape) for k in range(2)]
            for e in range(2)
        ]
        for b, (block, start) in enumerate(places):
            wide = block[pl.ds(start + i * count, 2 * count), :].astype(F32)
            for e in range(2):
                totals[b][e] = totals[b][e] + (wide[:count] * units[e][0] + wide[count:] * units[e][1])
    for b, (block, start) in enumerate(places):
        labels = block[pl.ds(start + half * count, 2 * count), :].astype(F32)[:count]
        for e in range(2):
            similar = scale * jnp.sum(totals[b][e], axis=1, keepdims=True)
            for t in range(TASKS):
                best[e][t] = jnp.maximum(best[e][t], jnp.where(labels == float(t), similar, -2.0 * scale))


def places_of(blocks, count):
    size = (LANES // 2 + 2) * count
    places = []
    for block in blocks:
        total = block.shape[0]
        firsts = range(0, total, size) if total % size == 0 else [total - size]
        places += [(block, first) for first in firsts]
    return places


def score_kernel(blocks, count, unit_ref, *refs):
    block_refs, best_ref = refs[:blocks], refs[blocks]
    lowest = -2.0 * float(LANES // 2 * LANES) ** 0.5
    best = [[jnp.full((count, LANES), lowest, F32) for _ in range(TASKS)] for _ in range(2)]
    best_of(places_of(block_refs, count), count, unit_ref, best)
    for e in range(2):
        for t in range(TASKS):
            best_ref[e, t] = best[e][t]


def last_score_kernel(count, unit_ref, block_ref, best_ref, out_ref, mean_ref):
    best = [[best_ref[e, t] for t in range(TASKS)] for e in range(2)]
    best_of(places_of([block_ref], count), count, unit_ref, best)
    lane = lax.broadcasted_iota(jnp.int32, (1, LANES), 1)
    means = []
    for e in range(2):
        values = [jnp.max(best[e][t], axis=0, keepdims=True) for t in range(TASKS)]
        row = jnp.where(lane == 0, values[0], jnp.where(lane == 1, values[1], values[2]))
        out_ref[pl.ds(e, 1), :] = row[:, :TASKS]
        means.append((values[0] + values[1] + values[2]) * (1.0 / TASKS))
    mean_ref[...] = jnp.where(lane == 0, means[0], means[1])[:, :2]


VMEM = pl.BlockSpec(memory_space=pltpu.VMEM)
SMEM = pl.BlockSpec(memory_space=pltpu.SMEM)
ANY = pl.BlockSpec(memory_space=pl.ANY)
HBM = pl.BlockSpec(memory_space=pltpu.HBM)


def in_hbm(arrays):
    return [pltpu.with_memory_space_constraint(a, pltpu.HBM) for a in arrays]


def params(mib):
    return pltpu.CompilerParams(vmem_limit_bytes=mib * MIB)


def cost(flops, nbytes):
    return pl.CostEstimate(flops=flops, bytes_accessed=nbytes, transcendentals=0)


def shards(
    hidden_state_input,
    attention_mixed_state,
    hidden_state_adjoint,
    attention_values_adjoint,
    sequence_token_counts,
    heldout_sketched_signals,
    benchmark_labels,
    top_rmsnorm_weights,
    top_reducer_matrix,
    top_expander_matrix,
    bottom_reducer_matrix,
    bottom_expander_matrix,
    source_sketch,
    top_reducer_sketch,
    top_expander_sketch,
    top_target_sketch,
    bottom_reducer_sketch,
    bottom_expander_sketch,
    bottom_target_sketch,
):
    me = lax.axis_index("dp").astype(jnp.int32)
    x, mixed, adjoint, values = (
        hidden_state_input,
        attention_mixed_state,
        hidden_state_adjoint,
        attention_values_adjoint,
    )
    tokens, width = x.shape
    rows = top_reducer_matrix.shape[0]
    count = heldout_sketched_signals.shape[0]

    inputs = (
        top_expander_matrix.T,
        heldout_sketched_signals,
        top_reducer_matrix,
        bottom_expander_matrix.T,
        bottom_reducer_matrix,
        top_rmsnorm_weights.reshape(width // LANES, LANES),
        bottom_reducer_sketch,
        bottom_expander_sketch.T,
        benchmark_labels.T,
    )
    own = pl.pallas_call(
        pack_kernel,
        out_shape=jax.ShapeDtypeStruct((3 * rows + (LANES // 2 + 2) * count, LANES), BF16),
        in_specs=[SMEM] + [HBM] * len(inputs),
        out_specs=VMEM,
        scratch_shapes=[pltpu.VMEM(a.shape, a.dtype) for a in inputs[1:]]
        + [pltpu.SemaphoreType.DMA((len(inputs),))],
        compiler_params=params(8),
        name="pack",
    )(me.reshape(1), *in_hbm(inputs))

    inputs = (
        x,
        mixed,
        adjoint,
        values,
        bottom_target_sketch,
        top_target_sketch,
        top_expander_sketch.T,
        top_reducer_sketch,
        top_rmsnorm_weights.reshape(1, width),
        source_sketch.T,
    )
    *activations, local = pl.pallas_call(
        local_kernel,
        out_shape=[jax.ShapeDtypeStruct(a.shape, a.dtype) for a in inputs[:8]]
        + [
            jax.ShapeDtypeStruct((width, LANES), BF16),
            jax.ShapeDtypeStruct((tokens, LOCAL_SUMS * LANES), F32),
        ],
        in_specs=[HBM] * len(inputs),
        out_specs=[VMEM] * 10,
        scratch_shapes=[pltpu.VMEM(a.shape, a.dtype) for a in inputs[8:]]
        + [pltpu.SemaphoreType.DMA((STEPS + 1, 6))],
        compiler_params=params(24),
        cost_estimate=cost(tokens * width * LANES * 6, 14 * MIB),
        name="local_products",
    )(*in_hbm(inputs))
    activations, small = [*activations[:6], activations[8]], activations[6:8]

    stage_scratch = [
        pltpu.VMEM((2 * rows, 2 * LANES), BF16),
        pltpu.VMEM((rows + LANES // 2, 2 * LANES), BF16),
        pltpu.VMEM((2 * rows, LANES), BF16),
    ]

    def stage(away, pieces, sums):
        first = not sums
        start = 1 + len(pieces) + len(activations)
        return pl.pallas_call(
            functools.partial(stage_kernel, away, first),
            out_shape=[
                jax.ShapeDtypeStruct((tokens, SUMS * LANES), F32),
                jax.ShapeDtypeStruct((LANES, 2 * LANES), F32),
            ],
            in_specs=[SMEM] + [VMEM] * (len(pieces) + len(activations) + len(sums)),
            out_specs=[VMEM, VMEM],
            scratch_shapes=stage_scratch,
            input_output_aliases={} if first else {start: 0, start + 1: 1},
            compiler_params=params(16),
            cost_estimate=cost(tokens * rows * LANES * 16, 2 * MIB),
            name="stage",
        )(me.reshape(1), *pieces, *activations, *sums)

    def split(block, *tails):
        tail = block.shape[0] - 3 * rows
        shapes = (3 * rows, LANES), ((1 + len(tails)) * tail, LANES)
        return pl.pallas_call(
            split_kernel,
            out_shape=[jax.ShapeDtypeStruct(shape, BF16) for shape in shapes],
            in_specs=[VMEM] * (1 + len(tails)),
            out_specs=[VMEM, VMEM],
            compiler_params=params(8),
            name="split",
        )(block, *tails)

    tie = lax.optimization_barrier
    half = RING_CHIPS // 2
    held = [own, other_core(own)]
    blocks = list(held)
    first, second = hop(held[0]), hop(held[1])
    first, activations = tie((first, activations))
    sums = stage(0, held, [])
    second, sums = tie((second, sums))
    for k in range(1, half):
        held = [first, second]
        crossed = [other_core(first), other_core(second)]
        blocks += [first, crossed[0]]
        if k < half - 1:
            blocks += [second, crossed[1]]
        else:
            first, tails = split(first, tail)
            tails, sums = tie((tails, sums))
        first = hop(first)
        sums = stage(k, held, sums)
        first, sums = tie((first, sums))
        if k == half - 2:
            second, tail = split(second)
        if k < half - 1:
            second = hop(second)
        if k < half - 1:
            sums = stage(-k, crossed, sums)
            second, sums = tie((second, sums))
    tails = hop(tails)
    half_scratch = [
        pltpu.VMEM((rows + LANES // 2, 3 * LANES), BF16),
        pltpu.VMEM((rows + LANES // 2, 2 * LANES), BF16),
        pltpu.VMEM((rows + LANES // 2, 2 * LANES), BF16),
    ]
    start = 4 + len(activations)
    sums = pl.pallas_call(
        functools.partial(stage_and_half_kernel, 1 - half, half),
        out_shape=[jax.ShapeDtypeStruct(a.shape, a.dtype) for a in sums],
        in_specs=[SMEM] + [VMEM] * (3 + len(activations) + 2),
        out_specs=[VMEM, VMEM],
        scratch_shapes=stage_scratch + half_scratch,
        input_output_aliases={start: 0, start + 1: 1},
        compiler_params=params(16),
        cost_estimate=cost(tokens * rows * LANES * 24, 3 * MIB),
        name="stage_and_half",
    )(me.reshape(1), *crossed, first, *activations, *sums)
    crossed = other_core(first)
    unit = pl.pallas_call(
        functools.partial(feature_kernel, half),
        out_shape=jax.ShapeDtypeStruct((LANES, LANES), F32),
        in_specs=[SMEM] * 2 + [VMEM] * (1 + len(activations) + 5),
        out_specs=VMEM,
        scratch_shapes=half_scratch,
        compiler_params=params(16),
        cost_estimate=cost(1, 1),
        name="features",
    )(me.reshape(1), sequence_token_counts, crossed, *activations, *sums, local, *small)
    tails, unit = tie((tails, unit))
    blocks.append(tails)
    best = pl.pallas_call(
        functools.partial(score_kernel, len(blocks), count),
        out_shape=jax.ShapeDtypeStruct((2, TASKS, count, LANES), F32),
        in_specs=[VMEM] * (1 + len(blocks)),
        out_specs=VMEM,
        compiler_params=params(16),
        cost_estimate=cost(4 * MIB, 2 * MIB),
        name="scores",
    )(unit, *blocks)
    task_best, scores = pl.pallas_call(
        functools.partial(last_score_kernel, count),
        out_shape=(jax.ShapeDtypeStruct((2, TASKS), F32), jax.ShapeDtypeStruct((1, 2), F32)),
        in_specs=[VMEM] * 3,
        out_specs=(VMEM, VMEM),
        compiler_params=params(8),
        name="last_scores",
    )(unit, other_core(tails), best)
    return (scores.reshape(2), task_best)


def shards_of_any_slice(
    hidden_state_input,
    attention_mixed_state,
    hidden_state_adjoint,
    attention_values_adjoint,
    sequence_token_counts,
    heldout_sketched_signals,
    benchmark_labels,
    top_rmsnorm_weights,
    top_reducer_matrix,
    top_expander_matrix,
    bottom_reducer_matrix,
    bottom_expander_matrix,
    source_sketch,
    top_reducer_sketch,
    top_expander_sketch,
    top_target_sketch,
    bottom_reducer_sketch,
    bottom_expander_sketch,
    bottom_target_sketch,
    n,
):
    me = lax.axis_index("dp")
    x, mixed, adjoint, values = (
        hidden_state_input,
        attention_mixed_state,
        hidden_state_adjoint,
        attention_values_adjoint,
    )
    tokens, width = x.shape
    rows = top_reducer_matrix.shape[0]
    up_rows = top_expander_matrix.shape[1]
    rank = top_reducer_matrix.shape[1]
    k1 = source_sketch.shape[1]
    gain = top_rmsnorm_weights
    own_gain = lax.dynamic_slice_in_dim(gain, me * rows, rows)

    down_upper = (own_gain[:, None] * top_reducer_matrix.astype(F32)).astype(BF16)
    up_lower = mm(bottom_expander_matrix.T, bottom_reducer_sketch).astype(BF16)
    down_lower = mm(bottom_reducer_matrix, bottom_expander_sketch).astype(BF16)
    packed_lower = jnp.concatenate([down_lower[: rows // 2], down_lower[rows // 2 :]], axis=1)
    factors = jnp.concatenate([down_upper, up_lower, top_expander_matrix.T, packed_lower], axis=0)
    factors = lax.all_gather(factors, "dp")

    val_wide = heldout_sketched_signals.astype(F32)
    val_unit = (
        val_wide * lax.rsqrt(jnp.sum(val_wide * val_wide, axis=1, keepdims=True) + 1e-06)
    ).astype(BF16)
    labels = jnp.broadcast_to(benchmark_labels.astype(BF16), (val_unit.shape[0], 128))
    panel = jnp.concatenate([val_unit.reshape(-1, 128), labels], axis=0)
    panel = lax.all_gather(panel, "dp")
    val_rows = val_unit.shape[0]
    cut = panel.shape[1] - val_rows
    panel_tasks = panel[:, cut:, 0].reshape(n * val_rows, 1).astype(jnp.int32)
    panel = panel[:, :cut].reshape(n * val_rows, val_unit.shape[1])

    wide = x.astype(F32)
    inverse = lax.rsqrt(jnp.mean(wide * wide, axis=1, keepdims=True) + 1e-05)
    gained_sketch = (gain[:, None] * source_sketch.astype(F32)).astype(BF16)
    left_one = inverse * mm(x, gained_sketch)
    left_three = mm(mixed, source_sketch)
    right_two = ALPHA * mm(values, top_target_sketch)

    at = 0
    down_upper = factors[:, at : at + rows].reshape(width, rank)
    at += rows
    up_lower = factors[:, at : at + rows].reshape(width, -1)
    at += rows
    up_upper = factors[:, at : at + up_rows].reshape(-1, rank)
    at += up_rows
    down_lower = factors[:, at:]
    down_lower = jnp.concatenate([down_lower[:, :, :k1], down_lower[:, :, k1:]], axis=1)
    down_lower = down_lower.reshape(width, k1)

    reduced = inverse * mm(x, down_upper)
    left_two = mm(reduced.astype(BF16), top_expander_sketch)
    left_four = mm(mixed, down_lower)
    returned = mm(values, up_upper).astype(BF16)
    right_one = ALPHA * mm(returned, top_reducer_sketch)
    along = (ALPHA / width) * jnp.sum(returned.astype(F32) * reduced, axis=1, keepdims=True)
    targets = jnp.concatenate([up_lower, bottom_target_sketch], axis=1)
    bridge = mm_cols(down_upper, targets).astype(BF16)
    rights_low = mm(adjoint, targets) + inverse * (
        ALPHA * mm(returned, bridge) - (along * inverse) * mm(x, targets)
    )
    rights_low = ALPHA * rights_low
    k2 = up_lower.shape[1]
    lefts = (left_one, left_two, left_three, left_four)
    rights = (right_one, right_two, rights_low[:, :k2], rights_low[:, k2:])

    counts = sequence_token_counts[0]
    ends = jnp.cumsum(counts)
    starts = ends - counts
    places = jnp.arange(tokens, dtype=jnp.int32)[:, None]
    member = (places >= starts[None, :]) & (places < ends[None, :])
    count_ex = counts.shape[0]
    spread = jnp.concatenate(lefts, axis=0).astype(BF16)
    member = jnp.tile(member, (4, 1))
    spread = jnp.concatenate(
        [jnp.where(member[:, e : e + 1], spread, 0) for e in range(count_ex)], axis=1
    )
    feats = mm_cols(spread, jnp.concatenate(rights, axis=0).astype(BF16))
    feats = feats.reshape(count_ex, -1)
    squares = jnp.sum(feats * feats, axis=1, keepdims=True)
    unit_rows = (feats * lax.rsqrt(squares + 1e-06)).astype(BF16)

    score_scale = float(unit_rows.shape[1]) ** 0.5
    similar = score_scale * mm_rows(unit_rows, panel)
    task_mask = panel_tasks == jnp.arange(TASKS, dtype=jnp.int32)[None, :]
    task_best = jnp.max(
        jnp.where(task_mask[None, :, :], similar[:, :, None], -2.0 * score_scale), axis=1
    )
    return (jnp.mean(task_best, axis=1), task_best)


def solution(mesh):
    n = mesh.shape["dp"]
    split = P(("parts", "dp"), None)
    by_row, by_column, whole = P("dp", None), P(None, "dp"), P()
    placed = (
        (split,) * 5
        + (by_row, by_row, whole)
        + (by_row, by_column, by_row, by_column)
        + (whole,) * 7
    )
    ours = shards if n == 2 * RING_CHIPS else functools.partial(shards_of_any_slice, n=n)
    return jax.shard_map(
        ours,
        mesh=mesh,
        in_specs=placed,
        out_specs=(P(("parts", "dp")), split),
        check_vma=False,
    )
```

```python
import functools

import jax
import jax.numpy as jnp
from jax import lax
from jax.experimental import pallas as pl
from jax.experimental.pallas import tpu as pltpu
from jax.sharding import PartitionSpec as P

TASKS = 3
ALPHA = 4.0
F32 = jnp.float32
BF16 = jnp.bfloat16
RING_CHIPS = 8
LANES = 128
STEPS = 4
VALUES, V_TARGET, X_DOWN, X_LOW, J_LOW, J_TARGET, M_DOWN, M_SOURCE, SUMS = range(9)
INVERSE, LEFT_ONE, X_TARGET, LOCAL_SUMS = range(4)
MIB = 1 << 20


def mm(a, b):
    return jnp.dot(a, b, preferred_element_type=F32)


def mm_rows(a, b):
    return lax.dot_general(a, b, (((1,), (1,)), ((), ())), preferred_element_type=F32)


def mm_cols(a, b):
    return lax.dot_general(a, b, (((0,), (0,)), ((), ())), preferred_element_type=F32)


def ring_chip(pos):
    half = RING_CHIPS // 2
    return jnp.where(pos < half, 2 * pos, 2 * (RING_CHIPS - 1 - pos) + 1)


def ring_pos(chip):
    row, side = chip // 2, chip % 2
    return jnp.where(side == 0, row, RING_CHIPS - 1 - row)


def hop(value):
    half = RING_CHIPS // 2
    place = [2 * q if q < half else 2 * (RING_CHIPS - 1 - q) + 1 for q in range(RING_CHIPS)]
    pairs = []
    for q in range(RING_CHIPS):
        pairs.append((2 * place[q], 2 * place[(q + 1) % RING_CHIPS]))
        pairs.append((2 * place[q] + 1, 2 * place[(q - 1) % RING_CHIPS] + 1))
    return lax.ppermute(value, "dp", pairs)


def other_core(value):
    return lax.ppermute(value, "dp", [(d, d ^ 1) for d in range(2 * RING_CHIPS)])


def half_lanes(shape):
    return lax.broadcasted_iota(jnp.int32, shape, 1) < LANES // 2


def diagonal_column(row, first, count):
    shape = (count, row.shape[1])
    lane = lax.broadcasted_iota(jnp.int32, shape, 1)
    at = lax.broadcasted_iota(jnp.int32, shape, 0)
    return jnp.sum(jnp.where(lane == at + first, row, 0.0), axis=1, keepdims=True)


def load(pairs, sems):
    copies = [pltpu.make_async_copy(src, dst, sems.at[i]) for i, (src, dst) in enumerate(pairs)]
    for copy in copies:
        copy.start()
    return copies


def pack_kernel(me_ref, *refs):
    up_up_hbm, hbm, out_ref, held, sems = refs[0], refs[1:9], refs[9], refs[10:18], refs[18]
    val_ref, down_up_ref, up_low_ref, down_low_ref, gain_ref, sketch_ref, expand_ref, label_ref = held
    rows = down_up_ref.shape[0]
    half = LANES // 2
    direct = (up_up_hbm, out_ref.at[pl.ds(2 * rows, rows // 2)])
    for copy in load((*zip(hbm, held), direct), sems):
        copy.wait()
    for b in range(rows // half):
        place = me_ref[0] * (rows // half) + b
        row = gain_ref[pl.ds(place // 2, 1), :]
        column = diagonal_column(row, (place % 2) * half, half)
        part = down_up_ref[pl.ds(b * half, half), :].astype(F32)
        out_ref[pl.ds(b * half, half), :] = (column * part).astype(BF16)
    at = rows
    out_ref[pl.ds(at, rows), :] = mm(up_low_ref[...], sketch_ref[...]).astype(BF16)
    at += rows + rows // 2
    expand = expand_ref[...]
    low = mm_rows(down_low_ref[...], jnp.concatenate([expand, expand], axis=0))
    first, second = low[: rows // 2], low[rows // 2 :]
    out_ref[pl.ds(at, rows // 2), :] = jnp.where(half_lanes(first.shape), first, second).astype(BF16)
    at += rows // 2
    wide = val_ref[...].astype(F32)
    count, width = wide.shape
    scale = lax.rsqrt(jnp.sum(wide * wide, axis=1, keepdims=True) + 1e-06)
    unit = wide * scale
    blocks = [unit[:, i * LANES : (i + 1) * LANES] for i in range(width // LANES)]
    row = label_ref[...].astype(F32)
    labels = jnp.broadcast_to(diagonal_column(row, 0, count), (count, LANES))
    blocks += [labels, labels]
    for i in range(0, len(blocks), 2):
        pair = jnp.concatenate(blocks[i : i + 2], axis=0)
        out_ref[pl.ds(at + i * count, 2 * count), :] = pair.astype(BF16)


def local_kernel(*refs):
    x_hbm, mixed_hbm, adjoint_hbm, values_hbm, target_hbm, top_target_hbm = refs[:6]
    small_hbm, gain_hbm, source_hbm = refs[6:8], refs[8], refs[9]
    x_ref, mixed_ref, adjoint_ref, values_ref, target_ref, top_target_ref = refs[10:16]
    small_refs, turned_ref, sums_ref = refs[16:18], refs[18], refs[19]
    gain_ref, source_ref, sems = refs[20:]
    tokens, width = x_ref.shape
    span = width // STEPS
    copies = []
    for j in range(STEPS):
        part = pl.ds(j * span, span)
        pairs = (
            (gain_hbm.at[:, part], gain_ref.at[:, part]),
            (source_hbm.at[:, part], source_ref.at[:, part]),
            (x_hbm.at[:, part], x_ref.at[:, part]),
            (target_hbm.at[part], target_ref.at[part]),
        )
        copies.append(load(pairs, sems.at[j]))
    pairs = (
        (adjoint_hbm, adjoint_ref),
        (mixed_hbm, mixed_ref),
        (values_hbm, values_ref),
        (top_target_hbm, top_target_ref),
        *zip(small_hbm, small_refs),
    )
    later = load(pairs, sems.at[STEPS])
    products = jnp.zeros((tokens, 2 * LANES), F32)
    squares = jnp.zeros((tokens, LANES), F32)
    for j in range(STEPS):
        for copy in copies[j]:
            copy.wait()
        part = slice(j * span, (j + 1) * span)
        x, source = x_ref[:, part], source_ref[:, part].astype(F32)
        gained = source * gain_ref[:, part]
        turned_ref[part, :] = jnp.concatenate([source, source], axis=0).T.astype(BF16)
        gained = jnp.concatenate([gained, gained], axis=0).T.astype(BF16)
        products = products + mm(x, jnp.concatenate([gained, target_ref[part, :]], axis=1))
        for i in range(span // LANES):
            wide = x[:, i * LANES : (i + 1) * LANES].astype(F32)
            squares = squares + wide * wide
    mean = jnp.sum(squares, axis=1, keepdims=True) * (1.0 / width)
    inverse = jnp.broadcast_to(lax.rsqrt(mean + 1e-05), (tokens, LANES))
    for i, value in enumerate((inverse, inverse * products[:, :LANES], products[:, LANES:])):
        sums_ref[:, i * LANES : (i + 1) * LANES] = value
    for copy in later:
        copy.wait()


def add_stage(away, me_ref, pieces, held, old, scratch):
    x_ref, mixed_ref, adjoint_ref, values_ref, target_ref, top_target_ref, source_ref = held
    both, up, down = scratch
    rows = both.shape[0] // 2
    half, pad = rows // 2, LANES // 2
    span = 2 * rows
    me = me_ref[0]
    pos, core = ring_pos(me // 2), me % 2
    chip = ring_chip((pos + away * (2 * core - 1) + RING_CHIPS) % RING_CHIPS)
    odd = chip % 2
    mine = pl.ds(pl.multiple_of(chip * span, LANES), span)
    values_start = (chip // 2) * span + odd * (rows - pad)
    values_part = pl.ds(pl.multiple_of(values_start, LANES), rows + pad)
    side = core if away >= 0 else 1 - core
    up[pl.ds(pl.multiple_of((1 - odd) * rows, 16), pad), :] = jnp.zeros((pad, 2 * LANES), BF16)
    up[pl.ds(pl.multiple_of(odd * pad, 16), rows), pl.ds(LANES, LANES)] = top_target_ref[
        pl.ds(pl.multiple_of(chip * rows, 16), rows), :
    ]
    for piece, c in ((pieces[0], side), (pieces[1], 1 - side)):
        one = pl.ds(pl.multiple_of(c * rows, 16), rows)
        both[one, pl.ds(0, LANES)] = piece[pl.ds(0, rows), :]
        both[one, pl.ds(LANES, LANES)] = piece[pl.ds(rows, rows), :]
        up[pl.ds(pl.multiple_of(odd * pad + c * half, 16), half), pl.ds(0, LANES)] = piece[
            pl.ds(2 * rows, half), :
        ]
        packed = piece[pl.ds(2 * rows + half, half), :].astype(F32)
        turned = pltpu.roll(packed, pad, 1)
        lower = half_lanes(packed.shape)
        down[pl.ds(pl.multiple_of(c * rows, 16), half), :] = jnp.where(lower, packed, turned).astype(BF16)
        down[pl.ds(pl.multiple_of(c * rows + half, 16), half), :] = jnp.where(lower, turned, packed).astype(BF16)

    weights = both[...]
    down_up = weights[:, :LANES]
    lows = jnp.concatenate([weights[:, LANES:], target_ref[mine, :]], axis=1)
    bridge = mm_cols(down_up, lows)
    products = []
    for activation, factor in (
        (values_ref[:, values_part], up[...]),
        (x_ref[:, mine], weights),
        (adjoint_ref[:, mine], lows),
        (mixed_ref[:, mine], jnp.concatenate([down[...], source_ref[mine, :]], axis=1)),
    ):
        product = mm(activation, factor)
        products += [product[:, :LANES], product[:, LANES:]]
    if old:
        products = [p + q for p, q in zip(products, old[0])]
        bridge = bridge + old[1]
    return products, bridge


def read_sums(refs):
    return [refs[0][:, i * LANES : (i + 1) * LANES] for i in range(SUMS)], refs[1][...]


def add_half(away, other, me_ref, piece, held, old, scratch):
    x_ref, mixed_ref, adjoint_ref, values_ref, target_ref, top_target_ref, source_ref = held
    wide, down, up = scratch
    pad = LANES // 2
    rows = wide.shape[0] - pad
    half, span = rows // 2, 2 * rows
    me = me_ref[0]
    pos, core = ring_pos(me // 2), me % 2
    chip = ring_chip((pos + away * (2 * core - 1) + RING_CHIPS) % RING_CHIPS)
    side = 1 - core if other else core
    odd = chip % 2
    mine = pl.ds(pl.multiple_of(chip * span + side * (rows - pad), LANES), rows + pad)
    inside = pl.ds(pl.multiple_of(side * pad, 16), rows)
    outside = pl.ds(pl.multiple_of((1 - side) * rows, 16), pad)
    block = pl.ds(pl.multiple_of(chip * span + side * rows, 16), rows)
    values_start = (chip // 2) * span + odd * (rows - pad)
    values_part = pl.ds(pl.multiple_of(values_start, LANES), rows + pad)
    values_inside = pl.ds(pl.multiple_of(odd * pad + side * half, 16), half)
    values_block = pl.ds(pl.multiple_of(chip * rows + side * half, 16), half)
    wide[outside, :] = jnp.zeros((pad, wide.shape[1]), BF16)
    down[outside, :] = jnp.zeros((pad, down.shape[1]), BF16)
    up[...] = jnp.zeros(up.shape, BF16)
    wide[inside, pl.ds(0, LANES)] = piece[pl.ds(0, rows), :]
    wide[inside, pl.ds(LANES, LANES)] = piece[pl.ds(rows, rows), :]
    wide[inside, pl.ds(2 * LANES, LANES)] = target_ref[block, :]
    up[values_inside, pl.ds(0, LANES)] = piece[pl.ds(2 * rows, half), :]
    up[values_inside, pl.ds(LANES, LANES)] = top_target_ref[values_block, :]
    packed = piece[pl.ds(2 * rows + half, half), :].astype(F32)
    turned = pltpu.roll(packed, pad, 1)
    lower = half_lanes(packed.shape)
    at = side * pad
    down[pl.ds(pl.multiple_of(at, 16), half), pl.ds(0, LANES)] = jnp.where(lower, packed, turned).astype(BF16)
    down[pl.ds(pl.multiple_of(at + half, 16), half), pl.ds(0, LANES)] = jnp.where(lower, turned, packed).astype(BF16)
    down[inside, pl.ds(LANES, LANES)] = source_ref[block, :]

    weights = wide[...]
    bridge = mm_cols(weights[:, :LANES], weights[:, LANES:])
    products = []
    for activation, factor in (
        (values_ref[:, values_part], up[...]),
        (x_ref[:, mine], weights[:, : 2 * LANES]),
        (adjoint_ref[:, mine], weights[:, LANES:]),
        (mixed_ref[:, mine], down[...]),
    ):
        product = mm(activation, factor)
        products += [product[:, :LANES], product[:, LANES:]]
    return [p + q for p, q in zip(products, old[0])], bridge + old[1]


def stage_and_half_kernel(away, half_away, me_ref, *refs):
    pieces, piece, held, old = refs[:2], refs[2], refs[3:10], refs[10:12]
    (new_sums, new_bridge), scratch, half_scratch = refs[12:14], refs[14:17], refs[17:]
    sums = add_stage(away, me_ref, pieces, held, read_sums(old), scratch)
    products, bridge = add_half(half_away, False, me_ref, piece, held, sums, half_scratch)
    for i in range(SUMS):
        new_sums[:, i * LANES : (i + 1) * LANES] = products[i]
    new_bridge[...] = bridge


def half_kernel(away, me_ref, *refs):
    piece, held, old = refs[0], refs[1:8], refs[8:10]
    (new_sums, new_bridge), scratch = refs[10:12], refs[12:]
    products, bridge = add_half(away, True, me_ref, piece, held, read_sums(old), scratch)
    for i in range(SUMS):
        new_sums[:, i * LANES : (i + 1) * LANES] = products[i]
    new_bridge[...] = bridge


def stage_kernel(away, first, me_ref, *refs):
    pieces, held, old = refs[:2], refs[2:9], refs[9:-5]
    (new_sums, new_bridge), scratch = refs[-5:-3], refs[-3:]
    products, bridge = add_stage(away, me_ref, pieces, held, read_sums(old) if old else (), scratch)
    for i in range(SUMS):
        new_sums[:, i * LANES : (i + 1) * LANES] = products[i]
    new_bridge[...] = bridge


def feature_kernel(width, counts_ref, *refs):
    old, local_ref, expand_ref, sketch_ref, out_ref = refs[:2], *refs[2:]
    products, bridge = read_sums(old)
    local = [local_ref[:, i * LANES : (i + 1) * LANES] for i in range(LOCAL_SUMS)]
    tokens = local_ref.shape[0]
    half = LANES // 2
    inverse = local[INVERSE]
    returned = products[VALUES].astype(BF16)
    back = mm(returned, jnp.concatenate([bridge.astype(BF16), sketch_ref[...]], axis=1))
    right_one = ALPHA * back[:, 2 * LANES :]
    reduced = inverse * products[X_DOWN]
    expand = expand_ref[...]
    left_two = mm_rows(reduced.astype(BF16), jnp.concatenate([expand, expand], axis=0))
    along = (ALPHA / width) * jnp.sum(returned.astype(F32) * reduced, axis=1, keepdims=True)
    along = along * inverse
    right_three = products[J_LOW] + inverse * (ALPHA * back[:, :LANES] - along * products[X_LOW])
    right_four = products[J_TARGET] + inverse * (ALPHA * back[:, LANES : 2 * LANES] - along * local[X_TARGET])
    rights = (right_one, ALPHA * products[V_TARGET], ALPHA * right_three, ALPHA * right_four)
    lefts = (local[LEFT_ONE], left_two, products[M_SOURCE], products[M_DOWN])
    place = lax.broadcasted_iota(jnp.int32, (tokens, LANES), 0)
    one, two = counts_ref[0, 0], counts_ref[0, 1]
    lower = half_lanes((tokens, LANES))
    member = (place >= jnp.where(lower, 0, one)) & (place < jnp.where(lower, one, one + two))
    feats = jnp.zeros((LANES, LANES), F32)
    for left, right in zip(lefts, rights):
        feats = feats + mm_cols(jnp.where(member, left, 0.0).astype(BF16), right.astype(BF16))
    for e in range(2):
        own = feats[e * half : (e + 1) * half]
        squares = jnp.sum(own * own, keepdims=True)
        out_ref[pl.ds(e * half, half), :] = (own * lax.rsqrt(squares + 1e-06)).astype(BF16).astype(F32)


def split_kernel(block_ref, *refs):
    head_ref, tail_ref = refs[-2:]
    cut, tail = head_ref.shape[0], block_ref.shape[0] - head_ref.shape[0]
    head_ref[...] = block_ref[pl.ds(0, cut), :]
    if len(refs) == 3:
        tail_ref[pl.ds(0, refs[0].shape[0]), :] = refs[0][...]
    tail_ref[pl.ds(tail_ref.shape[0] - tail, tail), :] = block_ref[pl.ds(cut, tail), :]


def score_kernel(spans, count, unit_ref, *refs):
    block_refs, (out_ref, mean_ref) = refs[:-2], refs[-2:]
    half = LANES // 2
    scale = float(half * LANES) ** 0.5
    shape = (count, LANES)
    totals = [[jnp.zeros(shape, F32) for _ in range(2)] for _ in spans]
    for i in range(0, half, 2):
        units = [
            [jnp.broadcast_to(unit_ref[pl.ds(e * half + i + k, 1), :], shape) for k in range(2)]
            for e in range(2)
        ]
        for b, (parts, _) in enumerate(spans):
            ref, row, low, _ = next(part for part in parts if part[2] <= i < part[3])
            wide = block_refs[ref][pl.ds(row + (i - low) * count, 2 * count), :].astype(F32)
            for e in range(2):
                totals[b][e] = totals[b][e] + (wide[:count] * units[e][0] + wide[count:] * units[e][1])
    best = [[jnp.full(shape, -2.0 * scale, F32) for _ in range(TASKS)] for _ in range(2)]
    for b, (_, (ref, row)) in enumerate(spans):
        labels = block_refs[ref][pl.ds(row, 2 * count), :].astype(F32)[:count]
        for e in range(2):
            similar = scale * jnp.sum(totals[b][e], axis=1, keepdims=True)
            for t in range(TASKS):
                best[e][t] = jnp.maximum(best[e][t], jnp.where(labels == float(t), similar, -2.0 * scale))
    lane = lax.broadcasted_iota(jnp.int32, (1, LANES), 1)
    means = []
    for e in range(2):
        values = [jnp.max(best[e][t], axis=0, keepdims=True) for t in range(TASKS)]
        row = jnp.where(lane == 0, values[0], jnp.where(lane == 1, values[1], values[2]))
        out_ref[pl.ds(e, 1), :] = row[:, :TASKS]
        means.append((values[0] + values[1] + values[2]) * (1.0 / TASKS))
    mean_ref[...] = jnp.where(lane == 0, means[0], means[1])[:, :2]


VMEM = pl.BlockSpec(memory_space=pltpu.VMEM)
SMEM = pl.BlockSpec(memory_space=pltpu.SMEM)
ANY = pl.BlockSpec(memory_space=pl.ANY)
HBM = pl.BlockSpec(memory_space=pltpu.HBM)


def in_hbm(arrays):
    return [pltpu.with_memory_space_constraint(a, pltpu.HBM) for a in arrays]


def params(mib):
    return pltpu.CompilerParams(vmem_limit_bytes=mib * MIB)


def cost(flops, nbytes):
    return pl.CostEstimate(flops=flops, bytes_accessed=nbytes, transcendentals=0)


def shards(
    hidden_state_input,
    attention_mixed_state,
    hidden_state_adjoint,
    attention_values_adjoint,
    sequence_token_counts,
    heldout_sketched_signals,
    benchmark_labels,
    top_rmsnorm_weights,
    top_reducer_matrix,
    top_expander_matrix,
    bottom_reducer_matrix,
    bottom_expander_matrix,
    source_sketch,
    top_reducer_sketch,
    top_expander_sketch,
    top_target_sketch,
    bottom_reducer_sketch,
    bottom_expander_sketch,
    bottom_target_sketch,
):
    me = lax.axis_index("dp").astype(jnp.int32)
    x, mixed, adjoint, values = (
        hidden_state_input,
        attention_mixed_state,
        hidden_state_adjoint,
        attention_values_adjoint,
    )
    tokens, width = x.shape
    rows = top_reducer_matrix.shape[0]
    count = heldout_sketched_signals.shape[0]

    inputs = (
        top_expander_matrix.T,
        heldout_sketched_signals,
        top_reducer_matrix,
        bottom_expander_matrix.T,
        bottom_reducer_matrix,
        top_rmsnorm_weights.reshape(width // LANES, LANES),
        bottom_reducer_sketch,
        bottom_expander_sketch.T,
        benchmark_labels.T,
    )
    own = pl.pallas_call(
        pack_kernel,
        out_shape=jax.ShapeDtypeStruct((3 * rows + (LANES // 2 + 2) * count, LANES), BF16),
        in_specs=[SMEM] + [HBM] * len(inputs),
        out_specs=VMEM,
        scratch_shapes=[pltpu.VMEM(a.shape, a.dtype) for a in inputs[1:]]
        + [pltpu.SemaphoreType.DMA((len(inputs),))],
        compiler_params=params(8),
        name="pack",
    )(me.reshape(1), *in_hbm(inputs))

    inputs = (
        x,
        mixed,
        adjoint,
        values,
        bottom_target_sketch,
        top_target_sketch,
        top_expander_sketch.T,
        top_reducer_sketch,
        top_rmsnorm_weights.reshape(1, width),
        source_sketch.T,
    )
    *activations, local = pl.pallas_call(
        local_kernel,
        out_shape=[jax.ShapeDtypeStruct(a.shape, a.dtype) for a in inputs[:8]]
        + [
            jax.ShapeDtypeStruct((width, LANES), BF16),
            jax.ShapeDtypeStruct((tokens, LOCAL_SUMS * LANES), F32),
        ],
        in_specs=[HBM] * len(inputs),
        out_specs=[VMEM] * 10,
        scratch_shapes=[pltpu.VMEM(a.shape, a.dtype) for a in inputs[8:]]
        + [pltpu.SemaphoreType.DMA((STEPS + 1, 6))],
        compiler_params=params(24),
        cost_estimate=cost(tokens * width * LANES * 6, 14 * MIB),
        name="local_products",
    )(*in_hbm(inputs))
    activations, small = [*activations[:6], activations[8]], activations[6:8]

    stage_scratch = [
        pltpu.VMEM((2 * rows, 2 * LANES), BF16),
        pltpu.VMEM((rows + LANES // 2, 2 * LANES), BF16),
        pltpu.VMEM((2 * rows, LANES), BF16),
    ]

    def stage(away, pieces, sums):
        first = not sums
        start = 1 + len(pieces) + len(activations)
        return pl.pallas_call(
            functools.partial(stage_kernel, away, first),
            out_shape=[
                jax.ShapeDtypeStruct((tokens, SUMS * LANES), F32),
                jax.ShapeDtypeStruct((LANES, 2 * LANES), F32),
            ],
            in_specs=[SMEM] + [VMEM] * (len(pieces) + len(activations) + len(sums)),
            out_specs=[VMEM, VMEM],
            scratch_shapes=stage_scratch,
            input_output_aliases={} if first else {start: 0, start + 1: 1},
            compiler_params=params(16),
            cost_estimate=cost(tokens * rows * LANES * 16, 2 * MIB),
            name="stage",
        )(me.reshape(1), *pieces, *activations, *sums)

    def split(block, cut, *tails):
        tail = block.shape[0] - cut
        size = tail + sum(t.shape[0] for t in tails)
        return pl.pallas_call(
            split_kernel,
            out_shape=[
                jax.ShapeDtypeStruct((cut, LANES), BF16),
                jax.ShapeDtypeStruct((size, LANES), BF16),
            ],
            in_specs=[VMEM] * (1 + len(tails)),
            out_specs=[VMEM, VMEM],
            compiler_params=params(8),
            name="split",
        )(block, *tails)

    tie = lax.optimization_barrier
    half = RING_CHIPS // 2
    factor_rows, features = 3 * rows, LANES // 2
    early = 10
    held = [own, other_core(own)]
    blocks = list(held)
    first, second = hop(held[0]), hop(held[1])
    first, activations = tie((first, activations))
    sums = stage(0, held, [])
    second, sums = tie((second, sums))
    for k in range(1, half):
        held = [first, second]
        crossed = [other_core(first), other_core(second)]
        blocks += [first, crossed[0], second, crossed[1]]
        if k == half - 1:
            first, tails = split(first, 3 * rows, tail)
            tails, sums = tie((tails, sums))
        first = hop(first)
        sums = stage(k, held, sums)
        first, sums = tie((first, sums))
        if k == half - 2:
            second, tail = split(second, 3 * rows + early * count)
        if k < half - 1:
            second = hop(second)
        if k < half - 1:
            sums = stage(-k, crossed, sums)
            second, sums = tie((second, sums))
    tails = hop(tails)
    half_scratch = [
        pltpu.VMEM((rows + LANES // 2, 3 * LANES), BF16),
        pltpu.VMEM((rows + LANES // 2, 2 * LANES), BF16),
        pltpu.VMEM((rows + LANES // 2, 2 * LANES), BF16),
    ]
    start = 4 + len(activations)
    sums = pl.pallas_call(
        functools.partial(stage_and_half_kernel, 1 - half, half),
        out_shape=[jax.ShapeDtypeStruct(a.shape, a.dtype) for a in sums],
        in_specs=[SMEM] + [VMEM] * (3 + len(activations) + 2),
        out_specs=[VMEM, VMEM],
        scratch_shapes=stage_scratch + half_scratch,
        input_output_aliases={start: 0, start + 1: 1},
        compiler_params=params(16),
        cost_estimate=cost(1, 1),
        name="stage_and_half",
    )(me.reshape(1), *crossed, first, *activations, *sums)
    crossed = other_core(first)
    start = 2 + len(activations)
    sums = pl.pallas_call(
        functools.partial(half_kernel, half),
        out_shape=[jax.ShapeDtypeStruct(a.shape, a.dtype) for a in sums],
        in_specs=[SMEM] + [VMEM] * (1 + len(activations) + 2),
        out_specs=[VMEM, VMEM],
        scratch_shapes=half_scratch,
        input_output_aliases={start: 0, start + 1: 1},
        compiler_params=params(16),
        cost_estimate=cost(1, 1),
        name="half_stage",
    )(me.reshape(1), crossed, *activations, *sums)
    tails, sums = tie((tails, sums))
    blocks += [tails, other_core(tails)]
    unit = pl.pallas_call(
        functools.partial(feature_kernel, width),
        out_shape=jax.ShapeDtypeStruct((LANES, LANES), F32),
        in_specs=[SMEM] + [VMEM] * 5,
        out_specs=VMEM,
        compiler_params=params(16),
        cost_estimate=cost(1, 1),
        name="features",
    )(sequence_token_counts, *sums, local, *small)
    spans, rest = [], (features - early) * count
    for b, block in enumerate(blocks[:-2]):
        if block.shape == own.shape:
            parts = ((b, factor_rows, 0, features),)
            spans.append((parts, (b, factor_rows + features * count)))
        else:
            tail = len(blocks) - 2 + (b + 2 == len(blocks) - 1)
            parts = ((b, factor_rows, 0, early), (tail, 0, early, features))
            spans.append((parts, (tail, rest)))
    for tail in (len(blocks) - 2, len(blocks) - 1):
        first_row = rest + 2 * count
        spans.append((((tail, first_row, 0, features),), (tail, first_row + features * count)))
    task_best, scores = pl.pallas_call(
        functools.partial(score_kernel, spans, count),
        out_shape=(jax.ShapeDtypeStruct((2, TASKS), F32), jax.ShapeDtypeStruct((1, 2), F32)),
        in_specs=[VMEM] * (1 + len(blocks)),
        out_specs=(VMEM, VMEM),
        compiler_params=params(16),
        cost_estimate=cost(4 * MIB, 2 * MIB),
        name="scores",
    )(unit, *blocks)
    return (scores.reshape(2), task_best)


def shards_of_any_slice(
    hidden_state_input,
    attention_mixed_state,
    hidden_state_adjoint,
    attention_values_adjoint,
    sequence_token_counts,
    heldout_sketched_signals,
    benchmark_labels,
    top_rmsnorm_weights,
    top_reducer_matrix,
    top_expander_matrix,
    bottom_reducer_matrix,
    bottom_expander_matrix,
    source_sketch,
    top_reducer_sketch,
    top_expander_sketch,
    top_target_sketch,
    bottom_reducer_sketch,
    bottom_expander_sketch,
    bottom_target_sketch,
    n,
):
    me = lax.axis_index("dp")
    x, mixed, adjoint, values = (
        hidden_state_input,
        attention_mixed_state,
        hidden_state_adjoint,
        attention_values_adjoint,
    )
    tokens, width = x.shape
    rows = top_reducer_matrix.shape[0]
    up_rows = top_expander_matrix.shape[1]
    rank = top_reducer_matrix.shape[1]
    k1 = source_sketch.shape[1]
    gain = top_rmsnorm_weights
    own_gain = lax.dynamic_slice_in_dim(gain, me * rows, rows)

    down_upper = (own_gain[:, None] * top_reducer_matrix.astype(F32)).astype(BF16)
    up_lower = mm(bottom_expander_matrix.T, bottom_reducer_sketch).astype(BF16)
    down_lower = mm(bottom_reducer_matrix, bottom_expander_sketch).astype(BF16)
    packed_lower = jnp.concatenate([down_lower[: rows // 2], down_lower[rows // 2 :]], axis=1)
    factors = jnp.concatenate([down_upper, up_lower, top_expander_matrix.T, packed_lower], axis=0)
    factors = lax.all_gather(factors, "dp")

    val_wide = heldout_sketched_signals.astype(F32)
    val_unit = (
        val_wide * lax.rsqrt(jnp.sum(val_wide * val_wide, axis=1, keepdims=True) + 1e-06)
    ).astype(BF16)
    labels = jnp.broadcast_to(benchmark_labels.astype(BF16), (val_unit.shape[0], 128))
    panel = jnp.concatenate([val_unit.reshape(-1, 128), labels], axis=0)
    panel = lax.all_gather(panel, "dp")
    val_rows = val_unit.shape[0]
    cut = panel.shape[1] - val_rows
    panel_tasks = panel[:, cut:, 0].reshape(n * val_rows, 1).astype(jnp.int32)
    panel = panel[:, :cut].reshape(n * val_rows, val_unit.shape[1])

    wide = x.astype(F32)
    inverse = lax.rsqrt(jnp.mean(wide * wide, axis=1, keepdims=True) + 1e-05)
    gained_sketch = (gain[:, None] * source_sketch.astype(F32)).astype(BF16)
    left_one = inverse * mm(x, gained_sketch)
    left_three = mm(mixed, source_sketch)
    right_two = ALPHA * mm(values, top_target_sketch)

    at = 0
    down_upper = factors[:, at : at + rows].reshape(width, rank)
    at += rows
    up_lower = factors[:, at : at + rows].reshape(width, -1)
    at += rows
    up_upper = factors[:, at : at + up_rows].reshape(-1, rank)
    at += up_rows
    down_lower = factors[:, at:]
    down_lower = jnp.concatenate([down_lower[:, :, :k1], down_lower[:, :, k1:]], axis=1)
    down_lower = down_lower.reshape(width, k1)

    reduced = inverse * mm(x, down_upper)
    left_two = mm(reduced.astype(BF16), top_expander_sketch)
    left_four = mm(mixed, down_lower)
    returned = mm(values, up_upper).astype(BF16)
    right_one = ALPHA * mm(returned, top_reducer_sketch)
    along = (ALPHA / width) * jnp.sum(returned.astype(F32) * reduced, axis=1, keepdims=True)
    targets = jnp.concatenate([up_lower, bottom_target_sketch], axis=1)
    bridge = mm_cols(down_upper, targets).astype(BF16)
    rights_low = mm(adjoint, targets) + inverse * (
        ALPHA * mm(returned, bridge) - (along * inverse) * mm(x, targets)
    )
    rights_low = ALPHA * rights_low
    k2 = up_lower.shape[1]
    lefts = (left_one, left_two, left_three, left_four)
    rights = (right_one, right_two, rights_low[:, :k2], rights_low[:, k2:])

    counts = sequence_token_counts[0]
    ends = jnp.cumsum(counts)
    starts = ends - counts
    places = jnp.arange(tokens, dtype=jnp.int32)[:, None]
    member = (places >= starts[None, :]) & (places < ends[None, :])
    count_ex = counts.shape[0]
    spread = jnp.concatenate(lefts, axis=0).astype(BF16)
    member = jnp.tile(member, (4, 1))
    spread = jnp.concatenate(
        [jnp.where(member[:, e : e + 1], spread, 0) for e in range(count_ex)], axis=1
    )
    feats = mm_cols(spread, jnp.concatenate(rights, axis=0).astype(BF16))
    feats = feats.reshape(count_ex, -1)
    squares = jnp.sum(feats * feats, axis=1, keepdims=True)
    unit_rows = (feats * lax.rsqrt(squares + 1e-06)).astype(BF16)

    score_scale = float(unit_rows.shape[1]) ** 0.5
    similar = score_scale * mm_rows(unit_rows, panel)
    task_mask = panel_tasks == jnp.arange(TASKS, dtype=jnp.int32)[None, :]
    task_best = jnp.max(
        jnp.where(task_mask[None, :, :], similar[:, :, None], -2.0 * score_scale), axis=1
    )
    return (jnp.mean(task_best, axis=1), task_best)


def solution(mesh):
    n = mesh.shape["dp"]
    split = P(("parts", "dp"), None)
    by_row, by_column, whole = P("dp", None), P(None, "dp"), P()
    placed = (
        (split,) * 5
        + (by_row, by_row, whole)
        + (by_row, by_column, by_row, by_column)
        + (whole,) * 7
    )
    ours = shards if n == 2 * RING_CHIPS else functools.partial(shards_of_any_slice, n=n)
    return jax.shard_map(
        ours,
        mesh=mesh,
        in_specs=placed,
        out_specs=(P(("parts", "dp")), split),
        check_vma=False,
    )
```

```python
import functools

import jax
import jax.numpy as jnp
from jax import lax
from jax.experimental import pallas as pl
from jax.experimental.pallas import tpu as pltpu
from jax.sharding import PartitionSpec as P

TASKS = 3
ALPHA = 4.0
F32 = jnp.float32
BF16 = jnp.bfloat16
RING_CHIPS = 8
LANES = 128
STEPS = 4
VALUES, V_TARGET, X_DOWN, X_LOW, J_LOW, J_TARGET, M_DOWN, M_SOURCE, SUMS = range(9)
INVERSE, LEFT_ONE, X_TARGET, LOCAL_SUMS = range(4)
MIB = 1 << 20


def mm(a, b):
    return jnp.dot(a, b, preferred_element_type=F32)


def mm_rows(a, b):
    return lax.dot_general(a, b, (((1,), (1,)), ((), ())), preferred_element_type=F32)


def mm_cols(a, b):
    return lax.dot_general(a, b, (((0,), (0,)), ((), ())), preferred_element_type=F32)


def ring_chip(pos):
    half = RING_CHIPS // 2
    return jnp.where(pos < half, 2 * pos, 2 * (RING_CHIPS - 1 - pos) + 1)


def ring_pos(chip):
    row, side = chip // 2, chip % 2
    return jnp.where(side == 0, row, RING_CHIPS - 1 - row)


def hop(value):
    half = RING_CHIPS // 2
    place = [2 * q if q < half else 2 * (RING_CHIPS - 1 - q) + 1 for q in range(RING_CHIPS)]
    pairs = []
    for q in range(RING_CHIPS):
        pairs.append((2 * place[q], 2 * place[(q - 1) % RING_CHIPS]))
        pairs.append((2 * place[q] + 1, 2 * place[(q + 1) % RING_CHIPS] + 1))
    return lax.ppermute(value, "dp", pairs)


def other_core(value):
    return lax.ppermute(value, "dp", [(d, d ^ 1) for d in range(2 * RING_CHIPS)])


def half_lanes(shape):
    return lax.broadcasted_iota(jnp.int32, shape, 1) < LANES // 2


def diagonal_column(row, first, count):
    shape = (count, row.shape[1])
    lane = lax.broadcasted_iota(jnp.int32, shape, 1)
    at = lax.broadcasted_iota(jnp.int32, shape, 0)
    return jnp.sum(jnp.where(lane == at + first, row, 0.0), axis=1, keepdims=True)


def load(pairs, sems):
    copies = [pltpu.make_async_copy(src, dst, sems.at[i]) for i, (src, dst) in enumerate(pairs)]
    for copy in copies:
        copy.start()
    return copies


def pack_kernel(me_ref, *refs):
    up_up_hbm, hbm, out_ref, held, sems = refs[0], refs[1:9], refs[9], refs[10:18], refs[18]
    val_ref, down_up_ref, up_low_ref, down_low_ref, gain_ref, sketch_ref, expand_ref, label_ref = held
    rows = down_up_ref.shape[0]
    half = LANES // 2
    direct = (up_up_hbm, out_ref.at[pl.ds(2 * rows, rows // 2)])
    for copy in load((*zip(hbm, held), direct), sems):
        copy.wait()
    for b in range(rows // half):
        place = me_ref[0] * (rows // half) + b
        row = gain_ref[pl.ds(place // 2, 1), :]
        column = diagonal_column(row, (place % 2) * half, half)
        part = down_up_ref[pl.ds(b * half, half), :].astype(F32)
        out_ref[pl.ds(b * half, half), :] = (column * part).astype(BF16)
    at = rows
    out_ref[pl.ds(at, rows), :] = mm(up_low_ref[...], sketch_ref[...]).astype(BF16)
    at += rows + rows // 2
    expand = expand_ref[...]
    low = mm_rows(down_low_ref[...], jnp.concatenate([expand, expand], axis=0))
    first, second = low[: rows // 2], low[rows // 2 :]
    out_ref[pl.ds(at, rows // 2), :] = jnp.where(half_lanes(first.shape), first, second).astype(BF16)
    at += rows // 2
    wide = val_ref[...].astype(F32)
    count, width = wide.shape
    scale = lax.rsqrt(jnp.sum(wide * wide, axis=1, keepdims=True) + 1e-06)
    unit = wide * scale
    blocks = [unit[:, i * LANES : (i + 1) * LANES] for i in range(width // LANES)]
    row = label_ref[...].astype(F32)
    labels = jnp.broadcast_to(diagonal_column(row, 0, count), (count, LANES))
    blocks += [labels, labels]
    for i in range(0, len(blocks), 2):
        pair = jnp.concatenate(blocks[i : i + 2], axis=0)
        out_ref[pl.ds(at + i * count, 2 * count), :] = pair.astype(BF16)


def local_kernel(*refs):
    x_hbm, mixed_hbm, adjoint_hbm, values_hbm, target_hbm, top_target_hbm = refs[:6]
    small_hbm, gain_hbm, source_hbm = refs[6:8], refs[8], refs[9]
    x_ref, mixed_ref, adjoint_ref, values_ref, target_ref, top_target_ref = refs[10:16]
    small_refs, turned_ref, sums_ref = refs[16:18], refs[18], refs[19]
    gain_ref, source_ref, sems = refs[20:]
    tokens, width = x_ref.shape
    span = width // STEPS
    copies = []
    for j in range(STEPS):
        part = pl.ds(j * span, span)
        pairs = (
            (gain_hbm.at[:, part], gain_ref.at[:, part]),
            (source_hbm.at[:, part], source_ref.at[:, part]),
            (x_hbm.at[:, part], x_ref.at[:, part]),
            (target_hbm.at[part], target_ref.at[part]),
        )
        copies.append(load(pairs, sems.at[j]))
    pairs = (
        (adjoint_hbm, adjoint_ref),
        (mixed_hbm, mixed_ref),
        (values_hbm, values_ref),
        (top_target_hbm, top_target_ref),
        *zip(small_hbm, small_refs),
    )
    later = load(pairs, sems.at[STEPS])
    products = jnp.zeros((tokens, 2 * LANES), F32)
    squares = jnp.zeros((tokens, LANES), F32)
    for j in range(STEPS):
        for copy in copies[j]:
            copy.wait()
        part = slice(j * span, (j + 1) * span)
        x, source = x_ref[:, part], source_ref[:, part].astype(F32)
        gained = source * gain_ref[:, part]
        turned_ref[part, :] = jnp.concatenate([source, source], axis=0).T.astype(BF16)
        gained = jnp.concatenate([gained, gained], axis=0).T.astype(BF16)
        products = products + mm(x, jnp.concatenate([gained, target_ref[part, :]], axis=1))
        for i in range(span // LANES):
            wide = x[:, i * LANES : (i + 1) * LANES].astype(F32)
            squares = squares + wide * wide
    mean = jnp.sum(squares, axis=1, keepdims=True) * (1.0 / width)
    inverse = jnp.broadcast_to(lax.rsqrt(mean + 1e-05), (tokens, LANES))
    for i, value in enumerate((inverse, inverse * products[:, :LANES], products[:, LANES:])):
        sums_ref[:, i * LANES : (i + 1) * LANES] = value
    for copy in later:
        copy.wait()


def add_stage(away, me_ref, pieces, held, old, scratch):
    x_ref, mixed_ref, adjoint_ref, values_ref, target_ref, top_target_ref, source_ref = held
    both, up, down = scratch
    rows = both.shape[0] // 2
    half, pad = rows // 2, LANES // 2
    span = 2 * rows
    me = me_ref[0]
    pos, core = ring_pos(me // 2), me % 2
    chip = ring_chip((pos + away * (1 - 2 * core) + RING_CHIPS) % RING_CHIPS)
    odd = chip % 2
    mine = pl.ds(pl.multiple_of(chip * span, LANES), span)
    values_start = (chip // 2) * span + odd * (rows - pad)
    values_part = pl.ds(pl.multiple_of(values_start, LANES), rows + pad)
    side = core if away >= 0 else 1 - core
    up[pl.ds(pl.multiple_of((1 - odd) * rows, 16), pad), :] = jnp.zeros((pad, 2 * LANES), BF16)
    up[pl.ds(pl.multiple_of(odd * pad, 16), rows), pl.ds(LANES, LANES)] = top_target_ref[
        pl.ds(pl.multiple_of(chip * rows, 16), rows), :
    ]
    for piece, c in ((pieces[0], side), (pieces[1], 1 - side)):
        one = pl.ds(pl.multiple_of(c * rows, 16), rows)
        both[one, pl.ds(0, LANES)] = piece[pl.ds(0, rows), :]
        both[one, pl.ds(LANES, LANES)] = piece[pl.ds(rows, rows), :]
        up[pl.ds(pl.multiple_of(odd * pad + c * half, 16), half), pl.ds(0, LANES)] = piece[
            pl.ds(2 * rows, half), :
        ]
        packed = piece[pl.ds(2 * rows + half, half), :].astype(F32)
        turned = pltpu.roll(packed, pad, 1)
        lower = half_lanes(packed.shape)
        down[pl.ds(pl.multiple_of(c * rows, 16), half), :] = jnp.where(lower, packed, turned).astype(BF16)
        down[pl.ds(pl.multiple_of(c * rows + half, 16), half), :] = jnp.where(lower, turned, packed).astype(BF16)

    weights = both[...]
    down_up = weights[:, :LANES]
    lows = jnp.concatenate([weights[:, LANES:], target_ref[mine, :]], axis=1)
    bridge = mm_cols(down_up, lows)
    products = []
    for activation, factor in (
        (values_ref[:, values_part], up[...]),
        (x_ref[:, mine], weights),
        (adjoint_ref[:, mine], lows),
        (mixed_ref[:, mine], jnp.concatenate([down[...], source_ref[mine, :]], axis=1)),
    ):
        product = mm(activation, factor)
        products += [product[:, :LANES], product[:, LANES:]]
    if old:
        products = [p + q for p, q in zip(products, old[0])]
        bridge = bridge + old[1]
    return products, bridge


def read_sums(refs):
    return [refs[0][:, i * LANES : (i + 1) * LANES] for i in range(SUMS)], refs[1][...]


def add_half(away, other, me_ref, piece, held, old, scratch):
    x_ref, mixed_ref, adjoint_ref, values_ref, target_ref, top_target_ref, source_ref = held
    wide, down, up = scratch
    pad = LANES // 2
    rows = wide.shape[0] - pad
    half, span = rows // 2, 2 * rows
    me = me_ref[0]
    pos, core = ring_pos(me // 2), me % 2
    chip = ring_chip((pos + away * (1 - 2 * core) + RING_CHIPS) % RING_CHIPS)
    side = 1 - core if other else core
    odd = chip % 2
    mine = pl.ds(pl.multiple_of(chip * span + side * (rows - pad), LANES), rows + pad)
    inside = pl.ds(pl.multiple_of(side * pad, 16), rows)
    outside = pl.ds(pl.multiple_of((1 - side) * rows, 16), pad)
    block = pl.ds(pl.multiple_of(chip * span + side * rows, 16), rows)
    values_start = (chip // 2) * span + odd * (rows - pad)
    values_part = pl.ds(pl.multiple_of(values_start, LANES), rows + pad)
    values_inside = pl.ds(pl.multiple_of(odd * pad + side * half, 16), half)
    values_block = pl.ds(pl.multiple_of(chip * rows + side * half, 16), half)
    wide[outside, :] = jnp.zeros((pad, wide.shape[1]), BF16)
    down[outside, :] = jnp.zeros((pad, down.shape[1]), BF16)
    up[...] = jnp.zeros(up.shape, BF16)
    wide[inside, pl.ds(0, LANES)] = piece[pl.ds(0, rows), :]
    wide[inside, pl.ds(LANES, LANES)] = piece[pl.ds(rows, rows), :]
    wide[inside, pl.ds(2 * LANES, LANES)] = target_ref[block, :]
    up[values_inside, pl.ds(0, LANES)] = piece[pl.ds(2 * rows, half), :]
    up[values_inside, pl.ds(LANES, LANES)] = top_target_ref[values_block, :]
    packed = piece[pl.ds(2 * rows + half, half), :].astype(F32)
    turned = pltpu.roll(packed, pad, 1)
    lower = half_lanes(packed.shape)
    at = side * pad
    down[pl.ds(pl.multiple_of(at, 16), half), pl.ds(0, LANES)] = jnp.where(lower, packed, turned).astype(BF16)
    down[pl.ds(pl.multiple_of(at + half, 16), half), pl.ds(0, LANES)] = jnp.where(lower, turned, packed).astype(BF16)
    down[inside, pl.ds(LANES, LANES)] = source_ref[block, :]

    weights = wide[...]
    bridge = mm_cols(weights[:, :LANES], weights[:, LANES:])
    products = []
    for activation, factor in (
        (values_ref[:, values_part], up[...]),
        (x_ref[:, mine], weights[:, : 2 * LANES]),
        (adjoint_ref[:, mine], weights[:, LANES:]),
        (mixed_ref[:, mine], down[...]),
    ):
        product = mm(activation, factor)
        products += [product[:, :LANES], product[:, LANES:]]
    return [p + q for p, q in zip(products, old[0])], bridge + old[1]


def stage_and_half_kernel(away, half_away, me_ref, *refs):
    pieces, piece, held, old = refs[:2], refs[2], refs[3:10], refs[10:12]
    (new_sums, new_bridge), scratch, half_scratch = refs[12:14], refs[14:17], refs[17:]
    sums = add_stage(away, me_ref, pieces, held, read_sums(old), scratch)
    products, bridge = add_half(half_away, False, me_ref, piece, held, sums, half_scratch)
    for i in range(SUMS):
        new_sums[:, i * LANES : (i + 1) * LANES] = products[i]
    new_bridge[...] = bridge


def stage_kernel(away, first, me_ref, *refs):
    pieces, held, old = refs[:2], refs[2:9], refs[9:-5]
    (new_sums, new_bridge), scratch = refs[-5:-3], refs[-3:]
    products, bridge = add_stage(away, me_ref, pieces, held, read_sums(old) if old else (), scratch)
    for i in range(SUMS):
        new_sums[:, i * LANES : (i + 1) * LANES] = products[i]
    new_bridge[...] = bridge


def feature_kernel(away, me_ref, counts_ref, *refs):
    piece, held, old, local_ref, expand_ref, sketch_ref = refs[0], refs[1:8], refs[8:10], *refs[10:13]
    out_ref, scratch = refs[13], refs[14:]
    products, bridge = add_half(away, True, me_ref, piece, held, read_sums(old), scratch)
    local = [local_ref[:, i * LANES : (i + 1) * LANES] for i in range(LOCAL_SUMS)]
    tokens, width = held[0].shape
    half = LANES // 2
    inverse = local[INVERSE]
    returned = products[VALUES].astype(BF16)
    back = mm(returned, jnp.concatenate([bridge.astype(BF16), sketch_ref[...]], axis=1))
    right_one = ALPHA * back[:, 2 * LANES :]
    reduced = inverse * products[X_DOWN]
    expand = expand_ref[...]
    left_two = mm_rows(reduced.astype(BF16), jnp.concatenate([expand, expand], axis=0))
    along = (ALPHA / width) * jnp.sum(returned.astype(F32) * reduced, axis=1, keepdims=True)
    along = along * inverse
    right_three = products[J_LOW] + inverse * (ALPHA * back[:, :LANES] - along * products[X_LOW])
    right_four = products[J_TARGET] + inverse * (ALPHA * back[:, LANES : 2 * LANES] - along * local[X_TARGET])
    rights = (right_one, ALPHA * products[V_TARGET], ALPHA * right_three, ALPHA * right_four)
    lefts = (local[LEFT_ONE], left_two, products[M_SOURCE], products[M_DOWN])
    place = lax.broadcasted_iota(jnp.int32, (tokens, LANES), 0)
    one, two = counts_ref[0, 0], counts_ref[0, 1]
    lower = half_lanes((tokens, LANES))
    member = (place >= jnp.where(lower, 0, one)) & (place < jnp.where(lower, one, one + two))
    feats = jnp.zeros((LANES, LANES), F32)
    for left, right in zip(lefts, rights):
        feats = feats + mm_cols(jnp.where(member, left, 0.0).astype(BF16), right.astype(BF16))
    for e in range(2):
        own = feats[e * half : (e + 1) * half]
        squares = jnp.sum(own * own, keepdims=True)
        out_ref[pl.ds(e * half, half), :] = (own * lax.rsqrt(squares + 1e-06)).astype(BF16).astype(F32)


def split_kernel(block_ref, *refs):
    head_ref, tail_ref = refs[-2:]
    cut, tail = head_ref.shape[0], block_ref.shape[0] - head_ref.shape[0]
    head_ref[...] = block_ref[pl.ds(0, cut), :]
    if len(refs) == 3:
        tail_ref[pl.ds(0, tail), :] = refs[0][...]
    tail_ref[pl.ds(tail_ref.shape[0] - tail, tail), :] = block_ref[pl.ds(cut, tail), :]


def best_of(places, count, unit_ref, best):
    half = LANES // 2
    scale = float(half * LANES) ** 0.5
    shape = (count, LANES)
    totals = [[jnp.zeros(shape, F32) for _ in range(2)] for _ in places]
    for i in range(0, half, 2):
        units = [
            [jnp.broadcast_to(unit_ref[pl.ds(e * half + i + k, 1), :], shape) for k in range(2)]
            for e in range(2)
        ]
        for b, (block, start) in enumerate(places):
            wide = block[pl.ds(start + i * count, 2 * count), :].astype(F32)
            for e in range(2):
                totals[b][e] = totals[b][e] + (wide[:count] * units[e][0] + wide[count:] * units[e][1])
    for b, (block, start) in enumerate(places):
        labels = block[pl.ds(start + half * count, 2 * count), :].astype(F32)[:count]
        for e in range(2):
            similar = scale * jnp.sum(totals[b][e], axis=1, keepdims=True)
            for t in range(TASKS):
                best[e][t] = jnp.maximum(best[e][t], jnp.where(labels == float(t), similar, -2.0 * scale))


def places_of(blocks, count):
    size = (LANES // 2 + 2) * count
    places = []
    for block in blocks:
        total = block.shape[0]
        firsts = range(0, total, size) if total % size == 0 else [total - size]
        places += [(block, first) for first in firsts]
    return places


def score_kernel(blocks, count, unit_ref, *refs):
    block_refs, best_ref = refs[:blocks], refs[blocks]
    lowest = -2.0 * float(LANES // 2 * LANES) ** 0.5
    best = [[jnp.full((count, LANES), lowest, F32) for _ in range(TASKS)] for _ in range(2)]
    best_of(places_of(block_refs, count), count, unit_ref, best)
    for e in range(2):
        for t in range(TASKS):
            best_ref[e, t] = best[e][t]


def last_score_kernel(count, unit_ref, block_ref, best_ref, out_ref, mean_ref):
    best = [[best_ref[e, t] for t in range(TASKS)] for e in range(2)]
    best_of(places_of([block_ref], count), count, unit_ref, best)
    lane = lax.broadcasted_iota(jnp.int32, (1, LANES), 1)
    means = []
    for e in range(2):
        values = [jnp.max(best[e][t], axis=0, keepdims=True) for t in range(TASKS)]
        row = jnp.where(lane == 0, values[0], jnp.where(lane == 1, values[1], values[2]))
        out_ref[pl.ds(e, 1), :] = row[:, :TASKS]
        means.append((values[0] + values[1] + values[2]) * (1.0 / TASKS))
    mean_ref[...] = jnp.where(lane == 0, means[0], means[1])[:, :2]


VMEM = pl.BlockSpec(memory_space=pltpu.VMEM)
SMEM = pl.BlockSpec(memory_space=pltpu.SMEM)
ANY = pl.BlockSpec(memory_space=pl.ANY)
HBM = pl.BlockSpec(memory_space=pltpu.HBM)


def in_hbm(arrays):
    return [pltpu.with_memory_space_constraint(a, pltpu.HBM) for a in arrays]


def params(mib):
    return pltpu.CompilerParams(vmem_limit_bytes=mib * MIB)


def cost(flops, nbytes):
    return pl.CostEstimate(flops=flops, bytes_accessed=nbytes, transcendentals=0)


def shards(
    hidden_state_input,
    attention_mixed_state,
    hidden_state_adjoint,
    attention_values_adjoint,
    sequence_token_counts,
    heldout_sketched_signals,
    benchmark_labels,
    top_rmsnorm_weights,
    top_reducer_matrix,
    top_expander_matrix,
    bottom_reducer_matrix,
    bottom_expander_matrix,
    source_sketch,
    top_reducer_sketch,
    top_expander_sketch,
    top_target_sketch,
    bottom_reducer_sketch,
    bottom_expander_sketch,
    bottom_target_sketch,
):
    me = lax.axis_index("dp").astype(jnp.int32)
    x, mixed, adjoint, values = (
        hidden_state_input,
        attention_mixed_state,
        hidden_state_adjoint,
        attention_values_adjoint,
    )
    tokens, width = x.shape
    rows = top_reducer_matrix.shape[0]
    count = heldout_sketched_signals.shape[0]

    inputs = (
        top_expander_matrix.T,
        heldout_sketched_signals,
        top_reducer_matrix,
        bottom_expander_matrix.T,
        bottom_reducer_matrix,
        top_rmsnorm_weights.reshape(width // LANES, LANES),
        bottom_reducer_sketch,
        bottom_expander_sketch.T,
        benchmark_labels.T,
    )
    own = pl.pallas_call(
        pack_kernel,
        out_shape=jax.ShapeDtypeStruct((3 * rows + (LANES // 2 + 2) * count, LANES), BF16),
        in_specs=[SMEM] + [HBM] * len(inputs),
        out_specs=VMEM,
        scratch_shapes=[pltpu.VMEM(a.shape, a.dtype) for a in inputs[1:]]
        + [pltpu.SemaphoreType.DMA((len(inputs),))],
        compiler_params=params(8),
        name="pack",
    )(me.reshape(1), *in_hbm(inputs))

    inputs = (
        x,
        mixed,
        adjoint,
        values,
        bottom_target_sketch,
        top_target_sketch,
        top_expander_sketch.T,
        top_reducer_sketch,
        top_rmsnorm_weights.reshape(1, width),
        source_sketch.T,
    )
    *activations, local = pl.pallas_call(
        local_kernel,
        out_shape=[jax.ShapeDtypeStruct(a.shape, a.dtype) for a in inputs[:8]]
        + [
            jax.ShapeDtypeStruct((width, LANES), BF16),
            jax.ShapeDtypeStruct((tokens, LOCAL_SUMS * LANES), F32),
        ],
        in_specs=[HBM] * len(inputs),
        out_specs=[VMEM] * 10,
        scratch_shapes=[pltpu.VMEM(a.shape, a.dtype) for a in inputs[8:]]
        + [pltpu.SemaphoreType.DMA((STEPS + 1, 6))],
        compiler_params=params(24),
        cost_estimate=cost(tokens * width * LANES * 6, 14 * MIB),
        name="local_products",
    )(*in_hbm(inputs))
    activations, small = [*activations[:6], activations[8]], activations[6:8]

    stage_scratch = [
        pltpu.VMEM((2 * rows, 2 * LANES), BF16),
        pltpu.VMEM((rows + LANES // 2, 2 * LANES), BF16),
        pltpu.VMEM((2 * rows, LANES), BF16),
    ]

    def stage(away, pieces, sums):
        first = not sums
        start = 1 + len(pieces) + len(activations)
        return pl.pallas_call(
            functools.partial(stage_kernel, away, first),
            out_shape=[
                jax.ShapeDtypeStruct((tokens, SUMS * LANES), F32),
                jax.ShapeDtypeStruct((LANES, 2 * LANES), F32),
            ],
            in_specs=[SMEM] + [VMEM] * (len(pieces) + len(activations) + len(sums)),
            out_specs=[VMEM, VMEM],
            scratch_shapes=stage_scratch,
            input_output_aliases={} if first else {start: 0, start + 1: 1},
            compiler_params=params(16),
            cost_estimate=cost(tokens * rows * LANES * 16, 2 * MIB),
            name="stage",
        )(me.reshape(1), *pieces, *activations, *sums)

    def split(block, *tails):
        tail = block.shape[0] - 3 * rows
        shapes = (3 * rows, LANES), ((1 + len(tails)) * tail, LANES)
        return pl.pallas_call(
            split_kernel,
            out_shape=[jax.ShapeDtypeStruct(shape, BF16) for shape in shapes],
            in_specs=[VMEM] * (1 + len(tails)),
            out_specs=[VMEM, VMEM],
            compiler_params=params(8),
            name="split",
        )(block, *tails)

    tie = lax.optimization_barrier
    half = RING_CHIPS // 2
    held = [own, other_core(own)]
    blocks = list(held)
    first, second = hop(held[0]), hop(held[1])
    first, activations = tie((first, activations))
    sums = stage(0, held, [])
    second, sums = tie((second, sums))
    for k in range(1, half):
        held = [first, second]
        crossed = [other_core(first), other_core(second)]
        blocks += [first, crossed[0]]
        if k < half - 1:
            blocks += [second, crossed[1]]
        else:
            first, tails = split(first, tail)
            tails, sums = tie((tails, sums))
        first = hop(first)
        sums = stage(k, held, sums)
        first, sums = tie((first, sums))
        if k == half - 2:
            second, tail = split(second)
        if k < half - 1:
            second = hop(second)
        if k < half - 1:
            sums = stage(-k, crossed, sums)
            second, sums = tie((second, sums))
    tails = hop(tails)
    half_scratch = [
        pltpu.VMEM((rows + LANES // 2, 3 * LANES), BF16),
        pltpu.VMEM((rows + LANES // 2, 2 * LANES), BF16),
        pltpu.VMEM((rows + LANES // 2, 2 * LANES), BF16),
    ]
    start = 4 + len(activations)
    sums = pl.pallas_call(
        functools.partial(stage_and_half_kernel, 1 - half, half),
        out_shape=[jax.ShapeDtypeStruct(a.shape, a.dtype) for a in sums],
        in_specs=[SMEM] + [VMEM] * (3 + len(activations) + 2),
        out_specs=[VMEM, VMEM],
        scratch_shapes=stage_scratch + half_scratch,
        input_output_aliases={start: 0, start + 1: 1},
        compiler_params=params(16),
        cost_estimate=cost(tokens * rows * LANES * 24, 3 * MIB),
        name="stage_and_half",
    )(me.reshape(1), *crossed, first, *activations, *sums)
    crossed = other_core(first)
    unit = pl.pallas_call(
        functools.partial(feature_kernel, half),
        out_shape=jax.ShapeDtypeStruct((LANES, LANES), F32),
        in_specs=[SMEM] * 2 + [VMEM] * (1 + len(activations) + 5),
        out_specs=VMEM,
        scratch_shapes=half_scratch,
        compiler_params=params(16),
        cost_estimate=cost(1, 1),
        name="features",
    )(me.reshape(1), sequence_token_counts, crossed, *activations, *sums, local, *small)
    tails, unit = tie((tails, unit))
    blocks.append(tails)
    best = pl.pallas_call(
        functools.partial(score_kernel, len(blocks), count),
        out_shape=jax.ShapeDtypeStruct((2, TASKS, count, LANES), F32),
        in_specs=[VMEM] * (1 + len(blocks)),
        out_specs=VMEM,
        compiler_params=params(16),
        cost_estimate=cost(4 * MIB, 2 * MIB),
        name="scores",
    )(unit, *blocks)
    task_best, scores = pl.pallas_call(
        functools.partial(last_score_kernel, count),
        out_shape=(jax.ShapeDtypeStruct((2, TASKS), F32), jax.ShapeDtypeStruct((1, 2), F32)),
        in_specs=[VMEM] * 3,
        out_specs=(VMEM, VMEM),
        compiler_params=params(8),
        name="last_scores",
    )(unit, other_core(tails), best)
    return (scores.reshape(2), task_best)


def shards_of_any_slice(
    hidden_state_input,
    attention_mixed_state,
    hidden_state_adjoint,
    attention_values_adjoint,
    sequence_token_counts,
    heldout_sketched_signals,
    benchmark_labels,
    top_rmsnorm_weights,
    top_reducer_matrix,
    top_expander_matrix,
    bottom_reducer_matrix,
    bottom_expander_matrix,
    source_sketch,
    top_reducer_sketch,
    top_expander_sketch,
    top_target_sketch,
    bottom_reducer_sketch,
    bottom_expander_sketch,
    bottom_target_sketch,
    n,
):
    me = lax.axis_index("dp")
    x, mixed, adjoint, values = (
        hidden_state_input,
        attention_mixed_state,
        hidden_state_adjoint,
        attention_values_adjoint,
    )
    tokens, width = x.shape
    rows = top_reducer_matrix.shape[0]
    up_rows = top_expander_matrix.shape[1]
    rank = top_reducer_matrix.shape[1]
    k1 = source_sketch.shape[1]
    gain = top_rmsnorm_weights
    own_gain = lax.dynamic_slice_in_dim(gain, me * rows, rows)

    down_upper = (own_gain[:, None] * top_reducer_matrix.astype(F32)).astype(BF16)
    up_lower = mm(bottom_expander_matrix.T, bottom_reducer_sketch).astype(BF16)
    down_lower = mm(bottom_reducer_matrix, bottom_expander_sketch).astype(BF16)
    packed_lower = jnp.concatenate([down_lower[: rows // 2], down_lower[rows // 2 :]], axis=1)
    factors = jnp.concatenate([down_upper, up_lower, top_expander_matrix.T, packed_lower], axis=0)
    factors = lax.all_gather(factors, "dp")

    val_wide = heldout_sketched_signals.astype(F32)
    val_unit = (
        val_wide * lax.rsqrt(jnp.sum(val_wide * val_wide, axis=1, keepdims=True) + 1e-06)
    ).astype(BF16)
    labels = jnp.broadcast_to(benchmark_labels.astype(BF16), (val_unit.shape[0], 128))
    panel = jnp.concatenate([val_unit.reshape(-1, 128), labels], axis=0)
    panel = lax.all_gather(panel, "dp")
    val_rows = val_unit.shape[0]
    cut = panel.shape[1] - val_rows
    panel_tasks = panel[:, cut:, 0].reshape(n * val_rows, 1).astype(jnp.int32)
    panel = panel[:, :cut].reshape(n * val_rows, val_unit.shape[1])

    wide = x.astype(F32)
    inverse = lax.rsqrt(jnp.mean(wide * wide, axis=1, keepdims=True) + 1e-05)
    gained_sketch = (gain[:, None] * source_sketch.astype(F32)).astype(BF16)
    left_one = inverse * mm(x, gained_sketch)
    left_three = mm(mixed, source_sketch)
    right_two = ALPHA * mm(values, top_target_sketch)

    at = 0
    down_upper = factors[:, at : at + rows].reshape(width, rank)
    at += rows
    up_lower = factors[:, at : at + rows].reshape(width, -1)
    at += rows
    up_upper = factors[:, at : at + up_rows].reshape(-1, rank)
    at += up_rows
    down_lower = factors[:, at:]
    down_lower = jnp.concatenate([down_lower[:, :, :k1], down_lower[:, :, k1:]], axis=1)
    down_lower = down_lower.reshape(width, k1)

    reduced = inverse * mm(x, down_upper)
    left_two = mm(reduced.astype(BF16), top_expander_sketch)
    left_four = mm(mixed, down_lower)
    returned = mm(values, up_upper).astype(BF16)
    right_one = ALPHA * mm(returned, top_reducer_sketch)
    along = (ALPHA / width) * jnp.sum(returned.astype(F32) * reduced, axis=1, keepdims=True)
    targets = jnp.concatenate([up_lower, bottom_target_sketch], axis=1)
    bridge = mm_cols(down_upper, targets).astype(BF16)
    rights_low = mm(adjoint, targets) + inverse * (
        ALPHA * mm(returned, bridge) - (along * inverse) * mm(x, targets)
    )
    rights_low = ALPHA * rights_low
    k2 = up_lower.shape[1]
    lefts = (left_one, left_two, left_three, left_four)
    rights = (right_one, right_two, rights_low[:, :k2], rights_low[:, k2:])

    counts = sequence_token_counts[0]
    ends = jnp.cumsum(counts)
    starts = ends - counts
    places = jnp.arange(tokens, dtype=jnp.int32)[:, None]
    member = (places >= starts[None, :]) & (places < ends[None, :])
    count_ex = counts.shape[0]
    spread = jnp.concatenate(lefts, axis=0).astype(BF16)
    member = jnp.tile(member, (4, 1))
    spread = jnp.concatenate(
        [jnp.where(member[:, e : e + 1], spread, 0) for e in range(count_ex)], axis=1
    )
    feats = mm_cols(spread, jnp.concatenate(rights, axis=0).astype(BF16))
    feats = feats.reshape(count_ex, -1)
    squares = jnp.sum(feats * feats, axis=1, keepdims=True)
    unit_rows = (feats * lax.rsqrt(squares + 1e-06)).astype(BF16)

    score_scale = float(unit_rows.shape[1]) ** 0.5
    similar = score_scale * mm_rows(unit_rows, panel)
    task_mask = panel_tasks == jnp.arange(TASKS, dtype=jnp.int32)[None, :]
    task_best = jnp.max(
        jnp.where(task_mask[None, :, :], similar[:, :, None], -2.0 * score_scale), axis=1
    )
    return (jnp.mean(task_best, axis=1), task_best)


def solution(mesh):
    n = mesh.shape["dp"]
    split = P(("parts", "dp"), None)
    by_row, by_column, whole = P("dp", None), P(None, "dp"), P()
    placed = (
        (split,) * 5
        + (by_row, by_row, whole)
        + (by_row, by_column, by_row, by_column)
        + (whole,) * 7
    )
    ours = shards if n == 2 * RING_CHIPS else functools.partial(shards_of_any_slice, n=n)
    return jax.shard_map(
        ours,
        mesh=mesh,
        in_specs=placed,
        out_specs=(P(("parts", "dp")), split),
        check_vma=False,
    )
```

```python
import functools

import jax
import jax.numpy as jnp
from jax import lax
from jax.experimental import pallas as pl
from jax.experimental.pallas import tpu as pltpu
from jax.sharding import PartitionSpec as P

TASKS = 3
ALPHA = 4.0
F32 = jnp.float32
BF16 = jnp.bfloat16
RING_CHIPS = 8
LANES = 128
STEPS = 4
VALUES, V_TARGET, X_DOWN, X_LOW, J_LOW, J_TARGET, M_DOWN, M_SOURCE, SUMS = range(9)
INVERSE, LEFT_ONE, X_TARGET, LOCAL_SUMS = range(4)
MIB = 1 << 20


def mm(a, b):
    return jnp.dot(a, b, preferred_element_type=F32)


def mm_rows(a, b):
    return lax.dot_general(a, b, (((1,), (1,)), ((), ())), preferred_element_type=F32)


def mm_cols(a, b):
    return lax.dot_general(a, b, (((0,), (0,)), ((), ())), preferred_element_type=F32)


def ring_chip(pos):
    half = RING_CHIPS // 2
    return jnp.where(pos < half, 2 * pos, 2 * (RING_CHIPS - 1 - pos) + 1)


def ring_pos(chip):
    row, side = chip // 2, chip % 2
    return jnp.where(side == 0, row, RING_CHIPS - 1 - row)


def hop(value):
    half = RING_CHIPS // 2
    place = [2 * q if q < half else 2 * (RING_CHIPS - 1 - q) + 1 for q in range(RING_CHIPS)]
    pairs = []
    for q in range(RING_CHIPS):
        pairs.append((2 * place[q], 2 * place[(q - 1) % RING_CHIPS]))
        pairs.append((2 * place[q] + 1, 2 * place[(q + 1) % RING_CHIPS] + 1))
    return lax.ppermute(value, "dp", pairs)


def other_core(value):
    return lax.ppermute(value, "dp", [(d, d ^ 1) for d in range(2 * RING_CHIPS)])


def half_lanes(shape):
    return lax.broadcasted_iota(jnp.int32, shape, 1) < LANES // 2


def diagonal_column(row, first, count):
    shape = (count, row.shape[1])
    lane = lax.broadcasted_iota(jnp.int32, shape, 1)
    at = lax.broadcasted_iota(jnp.int32, shape, 0)
    return jnp.sum(jnp.where(lane == at + first, row, 0.0), axis=1, keepdims=True)


def load(pairs, sems):
    copies = [pltpu.make_async_copy(src, dst, sems.at[i]) for i, (src, dst) in enumerate(pairs)]
    for copy in copies:
        copy.start()
    return copies


def pack_kernel(me_ref, *refs):
    up_up_hbm, hbm, out_ref, held, sems = refs[0], refs[1:9], refs[9], refs[10:18], refs[18]
    val_ref, down_up_ref, up_low_ref, down_low_ref, gain_ref, sketch_ref, expand_ref, label_ref = held
    rows = down_up_ref.shape[0]
    half = LANES // 2
    direct = (up_up_hbm, out_ref.at[pl.ds(2 * rows, rows // 2)])
    for copy in load((*zip(hbm, held), direct), sems):
        copy.wait()
    for b in range(rows // half):
        place = me_ref[0] * (rows // half) + b
        row = gain_ref[pl.ds(place // 2, 1), :]
        column = diagonal_column(row, (place % 2) * half, half)
        part = down_up_ref[pl.ds(b * half, half), :].astype(F32)
        out_ref[pl.ds(b * half, half), :] = (column * part).astype(BF16)
    at = rows
    out_ref[pl.ds(at, rows), :] = mm(up_low_ref[...], sketch_ref[...]).astype(BF16)
    at += rows + rows // 2
    expand = expand_ref[...]
    low = mm_rows(down_low_ref[...], jnp.concatenate([expand, expand], axis=0))
    first, second = low[: rows // 2], low[rows // 2 :]
    out_ref[pl.ds(at, rows // 2), :] = jnp.where(half_lanes(first.shape), first, second).astype(BF16)
    at += rows // 2
    wide = val_ref[...].astype(F32)
    count, width = wide.shape
    scale = lax.rsqrt(jnp.sum(wide * wide, axis=1, keepdims=True) + 1e-06)
    unit = wide * scale
    blocks = [unit[:, i * LANES : (i + 1) * LANES] for i in range(width // LANES)]
    row = label_ref[...].astype(F32)
    labels = jnp.broadcast_to(diagonal_column(row, 0, count), (count, LANES))
    blocks += [labels, labels]
    for i in range(0, len(blocks), 2):
        pair = jnp.concatenate(blocks[i : i + 2], axis=0)
        out_ref[pl.ds(at + i * count, 2 * count), :] = pair.astype(BF16)


def local_kernel(*refs):
    x_hbm, mixed_hbm, adjoint_hbm, values_hbm, target_hbm, top_target_hbm = refs[:6]
    small_hbm, gain_hbm, source_hbm = refs[6:8], refs[8], refs[9]
    x_ref, mixed_ref, adjoint_ref, values_ref, target_ref, top_target_ref = refs[10:16]
    small_refs, turned_ref, sums_ref = refs[16:18], refs[18], refs[19]
    gain_ref, source_ref, sems = refs[20:]
    tokens, width = x_ref.shape
    span = width // STEPS
    copies = []
    for j in range(STEPS):
        part = pl.ds(j * span, span)
        pairs = (
            (gain_hbm.at[:, part], gain_ref.at[:, part]),
            (source_hbm.at[:, part], source_ref.at[:, part]),
            (x_hbm.at[:, part], x_ref.at[:, part]),
            (target_hbm.at[part], target_ref.at[part]),
        )
        copies.append(load(pairs, sems.at[j]))
    pairs = (
        (adjoint_hbm, adjoint_ref),
        (mixed_hbm, mixed_ref),
        (values_hbm, values_ref),
        (top_target_hbm, top_target_ref),
        *zip(small_hbm, small_refs),
    )
    later = load(pairs, sems.at[STEPS])
    products = jnp.zeros((tokens, 2 * LANES), F32)
    squares = jnp.zeros((tokens, LANES), F32)
    for j in range(STEPS):
        for copy in copies[j]:
            copy.wait()
        part = slice(j * span, (j + 1) * span)
        x, source = x_ref[:, part], source_ref[:, part].astype(F32)
        gained = source * gain_ref[:, part]
        turned_ref[part, :] = jnp.concatenate([source, source], axis=0).T.astype(BF16)
        gained = jnp.concatenate([gained, gained], axis=0).T.astype(BF16)
        products = products + mm(x, jnp.concatenate([gained, target_ref[part, :]], axis=1))
        for i in range(span // LANES):
            wide = x[:, i * LANES : (i + 1) * LANES].astype(F32)
            squares = squares + wide * wide
    mean = jnp.sum(squares, axis=1, keepdims=True) * (1.0 / width)
    inverse = jnp.broadcast_to(lax.rsqrt(mean + 1e-05), (tokens, LANES))
    for i, value in enumerate((inverse, inverse * products[:, :LANES], products[:, LANES:])):
        sums_ref[:, i * LANES : (i + 1) * LANES] = value
    for copy in later:
        copy.wait()


def add_stage(away, me_ref, pieces, held, old, scratch):
    x_ref, mixed_ref, adjoint_ref, values_ref, target_ref, top_target_ref, source_ref = held
    both, up, down = scratch
    rows = both.shape[0] // 2
    half, pad = rows // 2, LANES // 2
    span = 2 * rows
    me = me_ref[0]
    pos, core = ring_pos(me // 2), me % 2
    chip = ring_chip((pos + away * (1 - 2 * core) + RING_CHIPS) % RING_CHIPS)
    odd = chip % 2
    mine = pl.ds(pl.multiple_of(chip * span, LANES), span)
    values_start = (chip // 2) * span + odd * (rows - pad)
    values_part = pl.ds(pl.multiple_of(values_start, LANES), rows + pad)
    side = core if away >= 0 else 1 - core
    up[pl.ds(pl.multiple_of((1 - odd) * rows, 16), pad), :] = jnp.zeros((pad, 2 * LANES), BF16)
    up[pl.ds(pl.multiple_of(odd * pad, 16), rows), pl.ds(LANES, LANES)] = top_target_ref[
        pl.ds(pl.multiple_of(chip * rows, 16), rows), :
    ]
    for piece, c in ((pieces[0], side), (pieces[1], 1 - side)):
        one = pl.ds(pl.multiple_of(c * rows, 16), rows)
        both[one, pl.ds(0, LANES)] = piece[pl.ds(0, rows), :]
        both[one, pl.ds(LANES, LANES)] = piece[pl.ds(rows, rows), :]
        up[pl.ds(pl.multiple_of(odd * pad + c * half, 16), half), pl.ds(0, LANES)] = piece[
            pl.ds(2 * rows, half), :
        ]
        packed = piece[pl.ds(2 * rows + half, half), :].astype(F32)
        turned = pltpu.roll(packed, pad, 1)
        lower = half_lanes(packed.shape)
        down[pl.ds(pl.multiple_of(c * rows, 16), half), :] = jnp.where(lower, packed, turned).astype(BF16)
        down[pl.ds(pl.multiple_of(c * rows + half, 16), half), :] = jnp.where(lower, turned, packed).astype(BF16)

    weights = both[...]
    down_up = weights[:, :LANES]
    lows = jnp.concatenate([weights[:, LANES:], target_ref[mine, :]], axis=1)
    bridge = mm_cols(down_up, lows)
    products = []
    for activation, factor in (
        (values_ref[:, values_part], up[...]),
        (x_ref[:, mine], weights),
        (adjoint_ref[:, mine], lows),
        (mixed_ref[:, mine], jnp.concatenate([down[...], source_ref[mine, :]], axis=1)),
    ):
        product = mm(activation, factor)
        products += [product[:, :LANES], product[:, LANES:]]
    if old:
        products = [p + q for p, q in zip(products, old[0])]
        bridge = bridge + old[1]
    return products, bridge


def read_sums(refs):
    return [refs[0][:, i * LANES : (i + 1) * LANES] for i in range(SUMS)], refs[1][...]


def add_half(away, other, me_ref, piece, held, old, scratch):
    x_ref, mixed_ref, adjoint_ref, values_ref, target_ref, top_target_ref, source_ref = held
    wide, down, up = scratch
    pad = LANES // 2
    rows = wide.shape[0] - pad
    half, span = rows // 2, 2 * rows
    me = me_ref[0]
    pos, core = ring_pos(me // 2), me % 2
    chip = ring_chip((pos + away * (1 - 2 * core) + RING_CHIPS) % RING_CHIPS)
    side = 1 - core if other else core
    odd = chip % 2
    mine = pl.ds(pl.multiple_of(chip * span + side * (rows - pad), LANES), rows + pad)
    inside = pl.ds(pl.multiple_of(side * pad, 16), rows)
    outside = pl.ds(pl.multiple_of((1 - side) * rows, 16), pad)
    block = pl.ds(pl.multiple_of(chip * span + side * rows, 16), rows)
    values_start = (chip // 2) * span + odd * (rows - pad)
    values_part = pl.ds(pl.multiple_of(values_start, LANES), rows + pad)
    values_inside = pl.ds(pl.multiple_of(odd * pad + side * half, 16), half)
    values_block = pl.ds(pl.multiple_of(chip * rows + side * half, 16), half)
    wide[outside, :] = jnp.zeros((pad, wide.shape[1]), BF16)
    down[outside, :] = jnp.zeros((pad, down.shape[1]), BF16)
    up[...] = jnp.zeros(up.shape, BF16)
    wide[inside, pl.ds(0, LANES)] = piece[pl.ds(0, rows), :]
    wide[inside, pl.ds(LANES, LANES)] = piece[pl.ds(rows, rows), :]
    wide[inside, pl.ds(2 * LANES, LANES)] = target_ref[block, :]
    up[values_inside, pl.ds(0, LANES)] = piece[pl.ds(2 * rows, half), :]
    up[values_inside, pl.ds(LANES, LANES)] = top_target_ref[values_block, :]
    packed = piece[pl.ds(2 * rows + half, half), :].astype(F32)
    turned = pltpu.roll(packed, pad, 1)
    lower = half_lanes(packed.shape)
    at = side * pad
    down[pl.ds(pl.multiple_of(at, 16), half), pl.ds(0, LANES)] = jnp.where(lower, packed, turned).astype(BF16)
    down[pl.ds(pl.multiple_of(at + half, 16), half), pl.ds(0, LANES)] = jnp.where(lower, turned, packed).astype(BF16)
    down[inside, pl.ds(LANES, LANES)] = source_ref[block, :]

    weights = wide[...]
    bridge = mm_cols(weights[:, :LANES], weights[:, LANES:])
    products = []
    for activation, factor in (
        (values_ref[:, values_part], up[...]),
        (x_ref[:, mine], weights[:, : 2 * LANES]),
        (adjoint_ref[:, mine], weights[:, LANES:]),
        (mixed_ref[:, mine], down[...]),
    ):
        product = mm(activation, factor)
        products += [product[:, :LANES], product[:, LANES:]]
    return [p + q for p, q in zip(products, old[0])], bridge + old[1]


def stage_and_half_kernel(away, half_away, me_ref, *refs):
    pieces, piece, held, old = refs[:2], refs[2], refs[3:10], refs[10:12]
    (new_sums, new_bridge), scratch, half_scratch = refs[12:14], refs[14:17], refs[17:]
    sums = add_stage(away, me_ref, pieces, held, read_sums(old), scratch)
    products, bridge = add_half(half_away, False, me_ref, piece, held, sums, half_scratch)
    for i in range(SUMS):
        new_sums[:, i * LANES : (i + 1) * LANES] = products[i]
    new_bridge[...] = bridge


def stage_kernel(away, first, me_ref, *refs):
    pieces, held, old = refs[:2], refs[2:9], refs[9:-5]
    (new_sums, new_bridge), scratch = refs[-5:-3], refs[-3:]
    products, bridge = add_stage(away, me_ref, pieces, held, read_sums(old) if old else (), scratch)
    for i in range(SUMS):
        new_sums[:, i * LANES : (i + 1) * LANES] = products[i]
    new_bridge[...] = bridge


def feature_kernel(away, me_ref, counts_ref, *refs):
    piece, held, old, local_ref, expand_ref, sketch_ref = refs[0], refs[1:8], refs[8:10], *refs[10:13]
    out_ref, scratch = refs[13], refs[14:]
    products, bridge = add_half(away, True, me_ref, piece, held, read_sums(old), scratch)
    local = [local_ref[:, i * LANES : (i + 1) * LANES] for i in range(LOCAL_SUMS)]
    tokens, width = held[0].shape
    half = LANES // 2
    inverse = local[INVERSE]
    returned = products[VALUES].astype(BF16)
    back = mm(returned, jnp.concatenate([bridge.astype(BF16), sketch_ref[...]], axis=1))
    right_one = ALPHA * back[:, 2 * LANES :]
    reduced = inverse * products[X_DOWN]
    expand = expand_ref[...]
    left_two = mm_rows(reduced.astype(BF16), jnp.concatenate([expand, expand], axis=0))
    along = (ALPHA / width) * jnp.sum(returned.astype(F32) * reduced, axis=1, keepdims=True)
    along = along * inverse
    right_three = products[J_LOW] + inverse * (ALPHA * back[:, :LANES] - along * products[X_LOW])
    right_four = products[J_TARGET] + inverse * (ALPHA * back[:, LANES : 2 * LANES] - along * local[X_TARGET])
    rights = (right_one, ALPHA * products[V_TARGET], ALPHA * right_three, ALPHA * right_four)
    lefts = (local[LEFT_ONE], left_two, products[M_SOURCE], products[M_DOWN])
    place = lax.broadcasted_iota(jnp.int32, (tokens, LANES), 0)
    one, two = counts_ref[0, 0], counts_ref[0, 1]
    lower = half_lanes((tokens, LANES))
    member = (place >= jnp.where(lower, 0, one)) & (place < jnp.where(lower, one, one + two))
    feats = jnp.zeros((LANES, LANES), F32)
    for left, right in zip(lefts, rights):
        feats = feats + mm_cols(jnp.where(member, left, 0.0).astype(BF16), right.astype(BF16))
    for e in range(2):
        own = feats[e * half : (e + 1) * half]
        squares = jnp.sum(own * own, keepdims=True)
        out_ref[pl.ds(e * half, half), :] = (own * lax.rsqrt(squares + 1e-06)).astype(BF16).astype(F32)


def split_kernel(block_ref, *refs):
    head_ref, tail_ref = refs[-2:]
    cut, tail = head_ref.shape[0], block_ref.shape[0] - head_ref.shape[0]
    head_ref[...] = block_ref[pl.ds(0, cut), :]
    if len(refs) == 3:
        tail_ref[pl.ds(0, tail), :] = refs[0][...]
    tail_ref[pl.ds(tail_ref.shape[0] - tail, tail), :] = block_ref[pl.ds(cut, tail), :]


def best_of(places, count, unit_ref, best):
    half = LANES // 2
    scale = float(half * LANES) ** 0.5
    shape = (count, LANES)
    chains = 4 if len(places) <= 4 else 1
    partial = [[[None] * chains for _ in range(2)] for _ in places]
    for i in range(0, half, 2):
        units = [
            [jnp.broadcast_to(unit_ref[pl.ds(e * half + i + k, 1), :], shape) for k in range(2)]
            for e in range(2)
        ]
        c = i // 2 % chains
        for b, (block, start) in enumerate(places):
            wide = block[pl.ds(start + i * count, 2 * count), :].astype(F32)
            for e in range(2):
                pair = wide[:count] * units[e][0] + wide[count:] * units[e][1]
                partial[b][e][c] = pair if partial[b][e][c] is None else partial[b][e][c] + pair
    totals = [[functools.reduce(jnp.add, parts) for parts in block] for block in partial]
    for b, (block, start) in enumerate(places):
        labels = block[pl.ds(start + half * count, 2 * count), :].astype(F32)[:count]
        for e in range(2):
            similar = scale * jnp.sum(totals[b][e], axis=1, keepdims=True)
            for t in range(TASKS):
                best[e][t] = jnp.maximum(best[e][t], jnp.where(labels == float(t), similar, -2.0 * scale))


def places_of(blocks, count):
    size = (LANES // 2 + 2) * count
    places = []
    for block in blocks:
        total = block.shape[0]
        firsts = range(0, total, size) if total % size == 0 else [total - size]
        places += [(block, first) for first in firsts]
    return places


def score_kernel(blocks, count, unit_ref, *refs):
    block_refs, best_ref = refs[:blocks], refs[blocks]
    lowest = -2.0 * float(LANES // 2 * LANES) ** 0.5
    best = [[jnp.full((count, LANES), lowest, F32) for _ in range(TASKS)] for _ in range(2)]
    best_of(places_of(block_refs, count), count, unit_ref, best)
    for e in range(2):
        for t in range(TASKS):
            best_ref[e, t] = best[e][t]


def last_score_kernel(count, unit_ref, block_ref, best_ref, out_ref, mean_ref):
    best = [[best_ref[e, t] for t in range(TASKS)] for e in range(2)]
    best_of(places_of([block_ref], count), count, unit_ref, best)
    lane = lax.broadcasted_iota(jnp.int32, (1, LANES), 1)
    means = []
    for e in range(2):
        values = [jnp.max(best[e][t], axis=0, keepdims=True) for t in range(TASKS)]
        row = jnp.where(lane == 0, values[0], jnp.where(lane == 1, values[1], values[2]))
        out_ref[pl.ds(e, 1), :] = row[:, :TASKS]
        means.append((values[0] + values[1] + values[2]) * (1.0 / TASKS))
    mean_ref[...] = jnp.where(lane == 0, means[0], means[1])[:, :2]


VMEM = pl.BlockSpec(memory_space=pltpu.VMEM)
SMEM = pl.BlockSpec(memory_space=pltpu.SMEM)
ANY = pl.BlockSpec(memory_space=pl.ANY)
HBM = pl.BlockSpec(memory_space=pltpu.HBM)


def in_hbm(arrays):
    return [pltpu.with_memory_space_constraint(a, pltpu.HBM) for a in arrays]


def params(mib):
    return pltpu.CompilerParams(vmem_limit_bytes=mib * MIB)


def cost(flops, nbytes):
    return pl.CostEstimate(flops=flops, bytes_accessed=nbytes, transcendentals=0)


def shards(
    hidden_state_input,
    attention_mixed_state,
    hidden_state_adjoint,
    attention_values_adjoint,
    sequence_token_counts,
    heldout_sketched_signals,
    benchmark_labels,
    top_rmsnorm_weights,
    top_reducer_matrix,
    top_expander_matrix,
    bottom_reducer_matrix,
    bottom_expander_matrix,
    source_sketch,
    top_reducer_sketch,
    top_expander_sketch,
    top_target_sketch,
    bottom_reducer_sketch,
    bottom_expander_sketch,
    bottom_target_sketch,
):
    me = lax.axis_index("dp").astype(jnp.int32)
    x, mixed, adjoint, values = (
        hidden_state_input,
        attention_mixed_state,
        hidden_state_adjoint,
        attention_values_adjoint,
    )
    tokens, width = x.shape
    rows = top_reducer_matrix.shape[0]
    count = heldout_sketched_signals.shape[0]

    inputs = (
        top_expander_matrix.T,
        heldout_sketched_signals,
        top_reducer_matrix,
        bottom_expander_matrix.T,
        bottom_reducer_matrix,
        top_rmsnorm_weights.reshape(width // LANES, LANES),
        bottom_reducer_sketch,
        bottom_expander_sketch.T,
        benchmark_labels.T,
    )
    own = pl.pallas_call(
        pack_kernel,
        out_shape=jax.ShapeDtypeStruct((3 * rows + (LANES // 2 + 2) * count, LANES), BF16),
        in_specs=[SMEM] + [HBM] * len(inputs),
        out_specs=VMEM,
        scratch_shapes=[pltpu.VMEM(a.shape, a.dtype) for a in inputs[1:]]
        + [pltpu.SemaphoreType.DMA((len(inputs),))],
        compiler_params=params(8),
        name="pack",
    )(me.reshape(1), *in_hbm(inputs))

    inputs = (
        x,
        mixed,
        adjoint,
        values,
        bottom_target_sketch,
        top_target_sketch,
        top_expander_sketch.T,
        top_reducer_sketch,
        top_rmsnorm_weights.reshape(1, width),
        source_sketch.T,
    )
    *activations, local = pl.pallas_call(
        local_kernel,
        out_shape=[jax.ShapeDtypeStruct(a.shape, a.dtype) for a in inputs[:8]]
        + [
            jax.ShapeDtypeStruct((width, LANES), BF16),
            jax.ShapeDtypeStruct((tokens, LOCAL_SUMS * LANES), F32),
        ],
        in_specs=[HBM] * len(inputs),
        out_specs=[VMEM] * 10,
        scratch_shapes=[pltpu.VMEM(a.shape, a.dtype) for a in inputs[8:]]
        + [pltpu.SemaphoreType.DMA((STEPS + 1, 6))],
        compiler_params=params(24),
        cost_estimate=cost(tokens * width * LANES * 6, 14 * MIB),
        name="local_products",
    )(*in_hbm(inputs))
    activations, small = [*activations[:6], activations[8]], activations[6:8]

    stage_scratch = [
        pltpu.VMEM((2 * rows, 2 * LANES), BF16),
        pltpu.VMEM((rows + LANES // 2, 2 * LANES), BF16),
        pltpu.VMEM((2 * rows, LANES), BF16),
    ]

    def stage(away, pieces, sums):
        first = not sums
        start = 1 + len(pieces) + len(activations)
        return pl.pallas_call(
            functools.partial(stage_kernel, away, first),
            out_shape=[
                jax.ShapeDtypeStruct((tokens, SUMS * LANES), F32),
                jax.ShapeDtypeStruct((LANES, 2 * LANES), F32),
            ],
            in_specs=[SMEM] + [VMEM] * (len(pieces) + len(activations) + len(sums)),
            out_specs=[VMEM, VMEM],
            scratch_shapes=stage_scratch,
            input_output_aliases={} if first else {start: 0, start + 1: 1},
            compiler_params=params(16),
            cost_estimate=cost(tokens * rows * LANES * 16, 2 * MIB),
            name="stage",
        )(me.reshape(1), *pieces, *activations, *sums)

    def split(block, *tails):
        tail = block.shape[0] - 3 * rows
        shapes = (3 * rows, LANES), ((1 + len(tails)) * tail, LANES)
        return pl.pallas_call(
            split_kernel,
            out_shape=[jax.ShapeDtypeStruct(shape, BF16) for shape in shapes],
            in_specs=[VMEM] * (1 + len(tails)),
            out_specs=[VMEM, VMEM],
            compiler_params=params(8),
            name="split",
        )(block, *tails)

    tie = lax.optimization_barrier
    half = RING_CHIPS // 2
    held = [own, other_core(own)]
    blocks = list(held)
    first, second = hop(held[0]), hop(held[1])
    first, activations = tie((first, activations))
    sums = stage(0, held, [])
    second, sums = tie((second, sums))
    for k in range(1, half):
        held = [first, second]
        crossed = [other_core(first), other_core(second)]
        blocks += [first, crossed[0]]
        if k < half - 1:
            blocks += [second, crossed[1]]
        else:
            first, tails = split(first, tail)
            tails, sums = tie((tails, sums))
        first = hop(first)
        sums = stage(k, held, sums)
        first, sums = tie((first, sums))
        if k == half - 2:
            second, tail = split(second)
        if k < half - 1:
            second = hop(second)
        if k < half - 1:
            sums = stage(-k, crossed, sums)
            second, sums = tie((second, sums))
    tails = hop(tails)
    half_scratch = [
        pltpu.VMEM((rows + LANES // 2, 3 * LANES), BF16),
        pltpu.VMEM((rows + LANES // 2, 2 * LANES), BF16),
        pltpu.VMEM((rows + LANES // 2, 2 * LANES), BF16),
    ]
    start = 4 + len(activations)
    sums = pl.pallas_call(
        functools.partial(stage_and_half_kernel, 1 - half, half),
        out_shape=[jax.ShapeDtypeStruct(a.shape, a.dtype) for a in sums],
        in_specs=[SMEM] + [VMEM] * (3 + len(activations) + 2),
        out_specs=[VMEM, VMEM],
        scratch_shapes=stage_scratch + half_scratch,
        input_output_aliases={start: 0, start + 1: 1},
        compiler_params=params(16),
        cost_estimate=cost(tokens * rows * LANES * 24, 3 * MIB),
        name="stage_and_half",
    )(me.reshape(1), *crossed, first, *activations, *sums)
    crossed = other_core(first)
    unit = pl.pallas_call(
        functools.partial(feature_kernel, half),
        out_shape=jax.ShapeDtypeStruct((LANES, LANES), F32),
        in_specs=[SMEM] * 2 + [VMEM] * (1 + len(activations) + 5),
        out_specs=VMEM,
        scratch_shapes=half_scratch,
        compiler_params=params(16),
        cost_estimate=cost(1, 1),
        name="features",
    )(me.reshape(1), sequence_token_counts, crossed, *activations, *sums, local, *small)
    tails, unit = tie((tails, unit))
    blocks.append(tails)
    best = pl.pallas_call(
        functools.partial(score_kernel, len(blocks), count),
        out_shape=jax.ShapeDtypeStruct((2, TASKS, count, LANES), F32),
        in_specs=[VMEM] * (1 + len(blocks)),
        out_specs=VMEM,
        compiler_params=params(16),
        cost_estimate=cost(4 * MIB, 2 * MIB),
        name="scores",
    )(unit, *blocks)
    task_best, scores = pl.pallas_call(
        functools.partial(last_score_kernel, count),
        out_shape=(jax.ShapeDtypeStruct((2, TASKS), F32), jax.ShapeDtypeStruct((1, 2), F32)),
        in_specs=[VMEM] * 3,
        out_specs=(VMEM, VMEM),
        compiler_params=params(8),
        name="last_scores",
    )(unit, other_core(tails), best)
    return (scores.reshape(2), task_best)


def shards_of_any_slice(
    hidden_state_input,
    attention_mixed_state,
    hidden_state_adjoint,
    attention_values_adjoint,
    sequence_token_counts,
    heldout_sketched_signals,
    benchmark_labels,
    top_rmsnorm_weights,
    top_reducer_matrix,
    top_expander_matrix,
    bottom_reducer_matrix,
    bottom_expander_matrix,
    source_sketch,
    top_reducer_sketch,
    top_expander_sketch,
    top_target_sketch,
    bottom_reducer_sketch,
    bottom_expander_sketch,
    bottom_target_sketch,
    n,
):
    me = lax.axis_index("dp")
    x, mixed, adjoint, values = (
        hidden_state_input,
        attention_mixed_state,
        hidden_state_adjoint,
        attention_values_adjoint,
    )
    tokens, width = x.shape
    rows = top_reducer_matrix.shape[0]
    up_rows = top_expander_matrix.shape[1]
    rank = top_reducer_matrix.shape[1]
    k1 = source_sketch.shape[1]
    gain = top_rmsnorm_weights
    own_gain = lax.dynamic_slice_in_dim(gain, me * rows, rows)

    down_upper = (own_gain[:, None] * top_reducer_matrix.astype(F32)).astype(BF16)
    up_lower = mm(bottom_expander_matrix.T, bottom_reducer_sketch).astype(BF16)
    down_lower = mm(bottom_reducer_matrix, bottom_expander_sketch).astype(BF16)
    packed_lower = jnp.concatenate([down_lower[: rows // 2], down_lower[rows // 2 :]], axis=1)
    factors = jnp.concatenate([down_upper, up_lower, top_expander_matrix.T, packed_lower], axis=0)
    factors = lax.all_gather(factors, "dp")

    val_wide = heldout_sketched_signals.astype(F32)
    val_unit = (
        val_wide * lax.rsqrt(jnp.sum(val_wide * val_wide, axis=1, keepdims=True) + 1e-06)
    ).astype(BF16)
    labels = jnp.broadcast_to(benchmark_labels.astype(BF16), (val_unit.shape[0], 128))
    panel = jnp.concatenate([val_unit.reshape(-1, 128), labels], axis=0)
    panel = lax.all_gather(panel, "dp")
    val_rows = val_unit.shape[0]
    cut = panel.shape[1] - val_rows
    panel_tasks = panel[:, cut:, 0].reshape(n * val_rows, 1).astype(jnp.int32)
    panel = panel[:, :cut].reshape(n * val_rows, val_unit.shape[1])

    wide = x.astype(F32)
    inverse = lax.rsqrt(jnp.mean(wide * wide, axis=1, keepdims=True) + 1e-05)
    gained_sketch = (gain[:, None] * source_sketch.astype(F32)).astype(BF16)
    left_one = inverse * mm(x, gained_sketch)
    left_three = mm(mixed, source_sketch)
    right_two = ALPHA * mm(values, top_target_sketch)

    at = 0
    down_upper = factors[:, at : at + rows].reshape(width, rank)
    at += rows
    up_lower = factors[:, at : at + rows].reshape(width, -1)
    at += rows
    up_upper = factors[:, at : at + up_rows].reshape(-1, rank)
    at += up_rows
    down_lower = factors[:, at:]
    down_lower = jnp.concatenate([down_lower[:, :, :k1], down_lower[:, :, k1:]], axis=1)
    down_lower = down_lower.reshape(width, k1)

    reduced = inverse * mm(x, down_upper)
    left_two = mm(reduced.astype(BF16), top_expander_sketch)
    left_four = mm(mixed, down_lower)
    returned = mm(values, up_upper).astype(BF16)
    right_one = ALPHA * mm(returned, top_reducer_sketch)
    along = (ALPHA / width) * jnp.sum(returned.astype(F32) * reduced, axis=1, keepdims=True)
    targets = jnp.concatenate([up_lower, bottom_target_sketch], axis=1)
    bridge = mm_cols(down_upper, targets).astype(BF16)
    rights_low = mm(adjoint, targets) + inverse * (
        ALPHA * mm(returned, bridge) - (along * inverse) * mm(x, targets)
    )
    rights_low = ALPHA * rights_low
    k2 = up_lower.shape[1]
    lefts = (left_one, left_two, left_three, left_four)
    rights = (right_one, right_two, rights_low[:, :k2], rights_low[:, k2:])

    counts = sequence_token_counts[0]
    ends = jnp.cumsum(counts)
    starts = ends - counts
    places = jnp.arange(tokens, dtype=jnp.int32)[:, None]
    member = (places >= starts[None, :]) & (places < ends[None, :])
    count_ex = counts.shape[0]
    spread = jnp.concatenate(lefts, axis=0).astype(BF16)
    member = jnp.tile(member, (4, 1))
    spread = jnp.concatenate(
        [jnp.where(member[:, e : e + 1], spread, 0) for e in range(count_ex)], axis=1
    )
    feats = mm_cols(spread, jnp.concatenate(rights, axis=0).astype(BF16))
    feats = feats.reshape(count_ex, -1)
    squares = jnp.sum(feats * feats, axis=1, keepdims=True)
    unit_rows = (feats * lax.rsqrt(squares + 1e-06)).astype(BF16)

    score_scale = float(unit_rows.shape[1]) ** 0.5
    similar = score_scale * mm_rows(unit_rows, panel)
    task_mask = panel_tasks == jnp.arange(TASKS, dtype=jnp.int32)[None, :]
    task_best = jnp.max(
        jnp.where(task_mask[None, :, :], similar[:, :, None], -2.0 * score_scale), axis=1
    )
    return (jnp.mean(task_best, axis=1), task_best)


def solution(mesh):
    n = mesh.shape["dp"]
    split = P(("parts", "dp"), None)
    by_row, by_column, whole = P("dp", None), P(None, "dp"), P()
    placed = (
        (split,) * 5
        + (by_row, by_row, whole)
        + (by_row, by_column, by_row, by_column)
        + (whole,) * 7
    )
    ours = shards if n == 2 * RING_CHIPS else functools.partial(shards_of_any_slice, n=n)
    return jax.shard_map(
        ours,
        mesh=mesh,
        in_specs=placed,
        out_specs=(P(("parts", "dp")), split),
        check_vma=False,
    )
```

```python
import functools

import jax
import jax.numpy as jnp
from jax import lax
from jax.experimental import pallas as pl
from jax.experimental.pallas import tpu as pltpu
from jax.sharding import PartitionSpec as P

TASKS = 3
ALPHA = 4.0
F32 = jnp.float32
BF16 = jnp.bfloat16
RING_CHIPS = 8
LANES = 128
STEPS = 4
VALUES, V_TARGET, X_DOWN, X_LOW, J_LOW, J_TARGET, M_DOWN, M_SOURCE, SUMS = range(9)
INVERSE, LEFT_ONE, X_TARGET, LOCAL_SUMS = range(4)
MIB = 1 << 20


def mm(a, b):
    return jnp.dot(a, b, preferred_element_type=F32)


def mm_rows(a, b):
    return lax.dot_general(a, b, (((1,), (1,)), ((), ())), preferred_element_type=F32)


def mm_cols(a, b):
    return lax.dot_general(a, b, (((0,), (0,)), ((), ())), preferred_element_type=F32)


def ring_chip(pos):
    half = RING_CHIPS // 2
    return jnp.where(pos < half, 2 * pos, 2 * (RING_CHIPS - 1 - pos) + 1)


def ring_pos(chip):
    row, side = chip // 2, chip % 2
    return jnp.where(side == 0, row, RING_CHIPS - 1 - row)


def hop(value):
    half = RING_CHIPS // 2
    place = [2 * q if q < half else 2 * (RING_CHIPS - 1 - q) + 1 for q in range(RING_CHIPS)]
    pairs = []
    for q in range(RING_CHIPS):
        pairs.append((2 * place[q], 2 * place[(q - 1) % RING_CHIPS]))
        pairs.append((2 * place[q] + 1, 2 * place[(q + 1) % RING_CHIPS] + 1))
    return lax.ppermute(value, "dp", pairs)


def other_core(value):
    return lax.ppermute(value, "dp", [(d, d ^ 1) for d in range(2 * RING_CHIPS)])


def half_lanes(shape):
    return lax.broadcasted_iota(jnp.int32, shape, 1) < LANES // 2


def diagonal_column(row, first, count):
    shape = (count, row.shape[1])
    lane = lax.broadcasted_iota(jnp.int32, shape, 1)
    at = lax.broadcasted_iota(jnp.int32, shape, 0)
    return jnp.sum(jnp.where(lane == at + first, row, 0.0), axis=1, keepdims=True)


def load(pairs, sems):
    copies = [pltpu.make_async_copy(src, dst, sems.at[i]) for i, (src, dst) in enumerate(pairs)]
    for copy in copies:
        copy.start()
    return copies


def pack_kernel(me_ref, *refs):
    up_up_hbm, hbm, out_ref, held, sems = refs[0], refs[1:9], refs[9], refs[10:18], refs[18]
    val_ref, down_up_ref, up_low_ref, down_low_ref, gain_ref, sketch_ref, expand_ref, label_ref = held
    rows = down_up_ref.shape[0]
    half = LANES // 2
    direct = (up_up_hbm, out_ref.at[pl.ds(2 * rows, rows // 2)])
    for copy in load((*zip(hbm, held), direct), sems):
        copy.wait()
    for b in range(rows // half):
        place = me_ref[0] * (rows // half) + b
        row = gain_ref[pl.ds(place // 2, 1), :]
        column = diagonal_column(row, (place % 2) * half, half)
        part = down_up_ref[pl.ds(b * half, half), :].astype(F32)
        out_ref[pl.ds(b * half, half), :] = (column * part).astype(BF16)
    at = rows
    out_ref[pl.ds(at, rows), :] = mm(up_low_ref[...], sketch_ref[...]).astype(BF16)
    at += rows + rows // 2
    expand = expand_ref[...]
    low = mm_rows(down_low_ref[...], jnp.concatenate([expand, expand], axis=0))
    first, second = low[: rows // 2], low[rows // 2 :]
    out_ref[pl.ds(at, rows // 2), :] = jnp.where(half_lanes(first.shape), first, second).astype(BF16)
    at += rows // 2
    wide = val_ref[...].astype(F32)
    count, width = wide.shape
    scale = lax.rsqrt(jnp.sum(wide * wide, axis=1, keepdims=True) + 1e-06)
    unit = wide * scale
    blocks = [unit[:, i * LANES : (i + 1) * LANES] for i in range(width // LANES)]
    row = label_ref[...].astype(F32)
    labels = jnp.broadcast_to(diagonal_column(row, 0, count), (count, LANES))
    blocks += [labels, labels]
    for i in range(0, len(blocks), 2):
        pair = jnp.concatenate(blocks[i : i + 2], axis=0)
        out_ref[pl.ds(at + i * count, 2 * count), :] = pair.astype(BF16)


def local_kernel(*refs):
    x_hbm, mixed_hbm, adjoint_hbm, values_hbm, target_hbm, top_target_hbm = refs[:6]
    small_hbm, gain_hbm, source_hbm = refs[6:8], refs[8], refs[9]
    x_ref, mixed_ref, adjoint_ref, values_ref, target_ref, top_target_ref = refs[10:16]
    small_refs, turned_ref, sums_ref = refs[16:18], refs[18], refs[19]
    gain_ref, source_ref, sems = refs[20:]
    tokens, width = x_ref.shape
    span = width // STEPS
    copies = []
    for j in range(STEPS):
        part = pl.ds(j * span, span)
        pairs = (
            (gain_hbm.at[:, part], gain_ref.at[:, part]),
            (source_hbm.at[:, part], source_ref.at[:, part]),
            (x_hbm.at[:, part], x_ref.at[:, part]),
            (target_hbm.at[part], target_ref.at[part]),
        )
        copies.append(load(pairs, sems.at[j]))
    pairs = (
        (adjoint_hbm, adjoint_ref),
        (mixed_hbm, mixed_ref),
        (values_hbm, values_ref),
        (top_target_hbm, top_target_ref),
        *zip(small_hbm, small_refs),
    )
    later = load(pairs, sems.at[STEPS])
    products = jnp.zeros((tokens, 2 * LANES), F32)
    squares = jnp.zeros((tokens, LANES), F32)
    for j in range(STEPS):
        for copy in copies[j]:
            copy.wait()
        part = slice(j * span, (j + 1) * span)
        x, source = x_ref[:, part], source_ref[:, part].astype(F32)
        gained = source * gain_ref[:, part]
        turned_ref[part, :] = jnp.concatenate([source, source], axis=0).T.astype(BF16)
        gained = jnp.concatenate([gained, gained], axis=0).T.astype(BF16)
        products = products + mm(x, jnp.concatenate([gained, target_ref[part, :]], axis=1))
        for i in range(span // LANES):
            wide = x[:, i * LANES : (i + 1) * LANES].astype(F32)
            squares = squares + wide * wide
    mean = jnp.sum(squares, axis=1, keepdims=True) * (1.0 / width)
    inverse = jnp.broadcast_to(lax.rsqrt(mean + 1e-05), (tokens, LANES))
    for i, value in enumerate((inverse, inverse * products[:, :LANES], products[:, LANES:])):
        sums_ref[:, i * LANES : (i + 1) * LANES] = value
    for copy in later:
        copy.wait()


def add_stage(away, me_ref, pieces, held, old, scratch):
    x_ref, mixed_ref, adjoint_ref, values_ref, target_ref, top_target_ref, source_ref = held
    both, up, down = scratch
    rows = both.shape[0] // 2
    half, pad = rows // 2, LANES // 2
    span = 2 * rows
    me = me_ref[0]
    pos, core = ring_pos(me // 2), me % 2
    chip = ring_chip((pos + away * (1 - 2 * core) + RING_CHIPS) % RING_CHIPS)
    odd = chip % 2
    mine = pl.ds(pl.multiple_of(chip * span, LANES), span)
    values_start = (chip // 2) * span + odd * (rows - pad)
    values_part = pl.ds(pl.multiple_of(values_start, LANES), rows + pad)
    side = core if away >= 0 else 1 - core
    up[pl.ds(pl.multiple_of((1 - odd) * rows, 16), pad), :] = jnp.zeros((pad, 2 * LANES), BF16)
    up[pl.ds(pl.multiple_of(odd * pad, 16), rows), pl.ds(LANES, LANES)] = top_target_ref[
        pl.ds(pl.multiple_of(chip * rows, 16), rows), :
    ]
    for piece, c in ((pieces[0], side), (pieces[1], 1 - side)):
        one = pl.ds(pl.multiple_of(c * rows, 16), rows)
        both[one, pl.ds(0, LANES)] = piece[pl.ds(0, rows), :]
        both[one, pl.ds(LANES, LANES)] = piece[pl.ds(rows, rows), :]
        up[pl.ds(pl.multiple_of(odd * pad + c * half, 16), half), pl.ds(0, LANES)] = piece[
            pl.ds(2 * rows, half), :
        ]
        packed = piece[pl.ds(2 * rows + half, half), :].astype(F32)
        turned = pltpu.roll(packed, pad, 1)
        lower = half_lanes(packed.shape)
        down[pl.ds(pl.multiple_of(c * rows, 16), half), :] = jnp.where(lower, packed, turned).astype(BF16)
        down[pl.ds(pl.multiple_of(c * rows + half, 16), half), :] = jnp.where(lower, turned, packed).astype(BF16)

    weights = both[...]
    down_up = weights[:, :LANES]
    lows = jnp.concatenate([weights[:, LANES:], target_ref[mine, :]], axis=1)
    bridge = mm_cols(down_up, lows)
    products = []
    for activation, factor in (
        (values_ref[:, values_part], up[...]),
        (x_ref[:, mine], weights),
        (adjoint_ref[:, mine], lows),
        (mixed_ref[:, mine], jnp.concatenate([down[...], source_ref[mine, :]], axis=1)),
    ):
        product = mm(activation, factor)
        products += [product[:, :LANES], product[:, LANES:]]
    if old:
        products = [p + q for p, q in zip(products, old[0])]
        bridge = bridge + old[1]
    return products, bridge


def read_sums(refs):
    return [refs[0][:, i * LANES : (i + 1) * LANES] for i in range(SUMS)], refs[1][...]


def add_half(away, other, me_ref, piece, held, old, scratch):
    x_ref, mixed_ref, adjoint_ref, values_ref, target_ref, top_target_ref, source_ref = held
    wide, down, up = scratch
    pad = LANES // 2
    rows = wide.shape[0] - pad
    half, span = rows // 2, 2 * rows
    me = me_ref[0]
    pos, core = ring_pos(me // 2), me % 2
    chip = ring_chip((pos + away * (1 - 2 * core) + RING_CHIPS) % RING_CHIPS)
    side = 1 - core if other else core
    odd = chip % 2
    mine = pl.ds(pl.multiple_of(chip * span + side * (rows - pad), LANES), rows + pad)
    inside = pl.ds(pl.multiple_of(side * pad, 16), rows)
    outside = pl.ds(pl.multiple_of((1 - side) * rows, 16), pad)
    block = pl.ds(pl.multiple_of(chip * span + side * rows, 16), rows)
    values_start = (chip // 2) * span + odd * (rows - pad)
    values_part = pl.ds(pl.multiple_of(values_start, LANES), rows + pad)
    values_inside = pl.ds(pl.multiple_of(odd * pad + side * half, 16), half)
    values_block = pl.ds(pl.multiple_of(chip * rows + side * half, 16), half)
    wide[outside, :] = jnp.zeros((pad, wide.shape[1]), BF16)
    down[outside, :] = jnp.zeros((pad, down.shape[1]), BF16)
    up[...] = jnp.zeros(up.shape, BF16)
    wide[inside, pl.ds(0, LANES)] = piece[pl.ds(0, rows), :]
    wide[inside, pl.ds(LANES, LANES)] = piece[pl.ds(rows, rows), :]
    wide[inside, pl.ds(2 * LANES, LANES)] = target_ref[block, :]
    up[values_inside, pl.ds(0, LANES)] = piece[pl.ds(2 * rows, half), :]
    up[values_inside, pl.ds(LANES, LANES)] = top_target_ref[values_block, :]
    packed = piece[pl.ds(2 * rows + half, half), :].astype(F32)
    turned = pltpu.roll(packed, pad, 1)
    lower = half_lanes(packed.shape)
    at = side * pad
    down[pl.ds(pl.multiple_of(at, 16), half), pl.ds(0, LANES)] = jnp.where(lower, packed, turned).astype(BF16)
    down[pl.ds(pl.multiple_of(at + half, 16), half), pl.ds(0, LANES)] = jnp.where(lower, turned, packed).astype(BF16)
    down[inside, pl.ds(LANES, LANES)] = source_ref[block, :]

    weights = wide[...]
    bridge = mm_cols(weights[:, :LANES], weights[:, LANES:])
    products = []
    for activation, factor in (
        (values_ref[:, values_part], up[...]),
        (x_ref[:, mine], weights[:, : 2 * LANES]),
        (adjoint_ref[:, mine], weights[:, LANES:]),
        (mixed_ref[:, mine], down[...]),
    ):
        product = mm(activation, factor)
        products += [product[:, :LANES], product[:, LANES:]]
    return [p + q for p, q in zip(products, old[0])], bridge + old[1]


def stage_and_half_kernel(away, half_away, me_ref, *refs):
    pieces, piece, held, old = refs[:2], refs[2], refs[3:10], refs[10:12]
    (new_sums, new_bridge), scratch, half_scratch = refs[12:14], refs[14:17], refs[17:]
    sums = add_stage(away, me_ref, pieces, held, read_sums(old), scratch)
    products, bridge = add_half(half_away, False, me_ref, piece, held, sums, half_scratch)
    for i in range(SUMS):
        new_sums[:, i * LANES : (i + 1) * LANES] = products[i]
    new_bridge[...] = bridge


def stage_kernel(away, first, me_ref, *refs):
    pieces, held, old = refs[:2], refs[2:9], refs[9:-5]
    (new_sums, new_bridge), scratch = refs[-5:-3], refs[-3:]
    products, bridge = add_stage(away, me_ref, pieces, held, read_sums(old) if old else (), scratch)
    for i in range(SUMS):
        new_sums[:, i * LANES : (i + 1) * LANES] = products[i]
    new_bridge[...] = bridge


def feature_kernel(away, me_ref, counts_ref, *refs):
    piece, held, old, local_ref, expand_ref, sketch_ref = refs[0], refs[1:8], refs[8:10], *refs[10:13]
    out_ref, scratch = refs[13], refs[14:]
    products, bridge = add_half(away, True, me_ref, piece, held, read_sums(old), scratch)
    local = [local_ref[:, i * LANES : (i + 1) * LANES] for i in range(LOCAL_SUMS)]
    tokens, width = held[0].shape
    half = LANES // 2
    inverse = local[INVERSE]
    returned = products[VALUES].astype(BF16)
    back = mm(returned, jnp.concatenate([bridge.astype(BF16), sketch_ref[...]], axis=1))
    right_one = ALPHA * back[:, 2 * LANES :]
    reduced = inverse * products[X_DOWN]
    expand = expand_ref[...]
    left_two = mm_rows(reduced.astype(BF16), jnp.concatenate([expand, expand], axis=0))
    along = (ALPHA / width) * jnp.sum(returned.astype(F32) * reduced, axis=1, keepdims=True)
    along = along * inverse
    right_three = products[J_LOW] + inverse * (ALPHA * back[:, :LANES] - along * products[X_LOW])
    right_four = products[J_TARGET] + inverse * (ALPHA * back[:, LANES : 2 * LANES] - along * local[X_TARGET])
    rights = (right_one, ALPHA * products[V_TARGET], ALPHA * right_three, ALPHA * right_four)
    lefts = (local[LEFT_ONE], left_two, products[M_SOURCE], products[M_DOWN])
    place = lax.broadcasted_iota(jnp.int32, (tokens, LANES), 0)
    one, two = counts_ref[0, 0], counts_ref[0, 1]
    lower = half_lanes((tokens, LANES))
    member = (place >= jnp.where(lower, 0, one)) & (place < jnp.where(lower, one, one + two))
    feats = jnp.zeros((LANES, LANES), F32)
    for left, right in zip(lefts, rights):
        feats = feats + mm_cols(jnp.where(member, left, 0.0).astype(BF16), right.astype(BF16))
    for e in range(2):
        own = feats[e * half : (e + 1) * half]
        squares = jnp.sum(own * own, keepdims=True)
        out_ref[pl.ds(e * half, half), :] = own * lax.rsqrt(squares + 1e-06)


def split_kernel(block_ref, *refs):
    head_ref, tail_ref = refs[-2:]
    cut, tail = head_ref.shape[0], block_ref.shape[0] - head_ref.shape[0]
    head_ref[...] = block_ref[pl.ds(0, cut), :]
    if len(refs) == 3:
        tail_ref[pl.ds(0, tail), :] = refs[0][...]
    tail_ref[pl.ds(tail_ref.shape[0] - tail, tail), :] = block_ref[pl.ds(cut, tail), :]


def best_of(places, count, unit_ref, best):
    half = LANES // 2
    scale = float(half * LANES) ** 0.5
    shape = (count, LANES)
    chains = 4 if len(places) <= 4 else 1
    partial = [[[None] * chains for _ in range(2)] for _ in places]
    for i in range(0, half, 2):
        units = [
            [jnp.broadcast_to(unit_ref[pl.ds(e * half + i + k, 1), :], shape) for k in range(2)]
            for e in range(2)
        ]
        c = i // 2 % chains
        for b, (block, start) in enumerate(places):
            wide = block[pl.ds(start + i * count, 2 * count), :].astype(F32)
            for e in range(2):
                pair = wide[:count] * units[e][0] + wide[count:] * units[e][1]
                partial[b][e][c] = pair if partial[b][e][c] is None else partial[b][e][c] + pair
    totals = [[functools.reduce(jnp.add, parts) for parts in block] for block in partial]
    for b, (block, start) in enumerate(places):
        labels = block[pl.ds(start + half * count, 2 * count), :].astype(F32)[:count]
        for e in range(2):
            similar = scale * jnp.sum(totals[b][e], axis=1, keepdims=True)
            for t in range(TASKS):
                best[e][t] = jnp.maximum(best[e][t], jnp.where(labels == float(t), similar, -2.0 * scale))


def places_of(blocks, count):
    size = (LANES // 2 + 2) * count
    places = []
    for block in blocks:
        total = block.shape[0]
        firsts = range(0, total, size) if total % size == 0 else [total - size]
        places += [(block, first) for first in firsts]
    return places


def score_kernel(blocks, count, unit_ref, *refs):
    block_refs, best_ref = refs[:blocks], refs[blocks]
    lowest = -2.0 * float(LANES // 2 * LANES) ** 0.5
    best = [[jnp.full((count, LANES), lowest, F32) for _ in range(TASKS)] for _ in range(2)]
    best_of(places_of(block_refs, count), count, unit_ref, best)
    for e in range(2):
        for t in range(TASKS):
            best_ref[e, t] = best[e][t]


def last_score_kernel(count, unit_ref, block_ref, best_ref, out_ref, mean_ref):
    best = [[best_ref[e, t] for t in range(TASKS)] for e in range(2)]
    best_of(places_of([block_ref], count), count, unit_ref, best)
    lane = lax.broadcasted_iota(jnp.int32, (1, LANES), 1)
    means = []
    for e in range(2):
        values = [jnp.max(best[e][t], axis=0, keepdims=True) for t in range(TASKS)]
        row = jnp.where(lane == 0, values[0], jnp.where(lane == 1, values[1], values[2]))
        out_ref[pl.ds(e, 1), :] = row[:, :TASKS]
        means.append((values[0] + values[1] + values[2]) * (1.0 / TASKS))
    mean_ref[...] = jnp.where(lane == 0, means[0], means[1])[:, :2]


VMEM = pl.BlockSpec(memory_space=pltpu.VMEM)
SMEM = pl.BlockSpec(memory_space=pltpu.SMEM)
ANY = pl.BlockSpec(memory_space=pl.ANY)
HBM = pl.BlockSpec(memory_space=pltpu.HBM)


def in_hbm(arrays):
    return [pltpu.with_memory_space_constraint(a, pltpu.HBM) for a in arrays]


def params(mib):
    return pltpu.CompilerParams(vmem_limit_bytes=mib * MIB)


def cost(flops, nbytes):
    return pl.CostEstimate(flops=flops, bytes_accessed=nbytes, transcendentals=0)


def shards(
    hidden_state_input,
    attention_mixed_state,
    hidden_state_adjoint,
    attention_values_adjoint,
    sequence_token_counts,
    heldout_sketched_signals,
    benchmark_labels,
    top_rmsnorm_weights,
    top_reducer_matrix,
    top_expander_matrix,
    bottom_reducer_matrix,
    bottom_expander_matrix,
    source_sketch,
    top_reducer_sketch,
    top_expander_sketch,
    top_target_sketch,
    bottom_reducer_sketch,
    bottom_expander_sketch,
    bottom_target_sketch,
):
    me = lax.axis_index("dp").astype(jnp.int32)
    x, mixed, adjoint, values = (
        hidden_state_input,
        attention_mixed_state,
        hidden_state_adjoint,
        attention_values_adjoint,
    )
    tokens, width = x.shape
    rows = top_reducer_matrix.shape[0]
    count = heldout_sketched_signals.shape[0]

    inputs = (
        top_expander_matrix.T,
        heldout_sketched_signals,
        top_reducer_matrix,
        bottom_expander_matrix.T,
        bottom_reducer_matrix,
        top_rmsnorm_weights.reshape(width // LANES, LANES),
        bottom_reducer_sketch,
        bottom_expander_sketch.T,
        benchmark_labels.T,
    )
    own = pl.pallas_call(
        pack_kernel,
        out_shape=jax.ShapeDtypeStruct((3 * rows + (LANES // 2 + 2) * count, LANES), BF16),
        in_specs=[SMEM] + [HBM] * len(inputs),
        out_specs=VMEM,
        scratch_shapes=[pltpu.VMEM(a.shape, a.dtype) for a in inputs[1:]]
        + [pltpu.SemaphoreType.DMA((len(inputs),))],
        compiler_params=params(8),
        name="pack",
    )(me.reshape(1), *in_hbm(inputs))

    inputs = (
        x,
        mixed,
        adjoint,
        values,
        bottom_target_sketch,
        top_target_sketch,
        top_expander_sketch.T,
        top_reducer_sketch,
        top_rmsnorm_weights.reshape(1, width),
        source_sketch.T,
    )
    *activations, local = pl.pallas_call(
        local_kernel,
        out_shape=[jax.ShapeDtypeStruct(a.shape, a.dtype) for a in inputs[:8]]
        + [
            jax.ShapeDtypeStruct((width, LANES), BF16),
            jax.ShapeDtypeStruct((tokens, LOCAL_SUMS * LANES), F32),
        ],
        in_specs=[HBM] * len(inputs),
        out_specs=[VMEM] * 10,
        scratch_shapes=[pltpu.VMEM(a.shape, a.dtype) for a in inputs[8:]]
        + [pltpu.SemaphoreType.DMA((STEPS + 1, 6))],
        compiler_params=params(24),
        cost_estimate=cost(tokens * width * LANES * 6, 14 * MIB),
        name="local_products",
    )(*in_hbm(inputs))
    activations, small = [*activations[:6], activations[8]], activations[6:8]

    stage_scratch = [
        pltpu.VMEM((2 * rows, 2 * LANES), BF16),
        pltpu.VMEM((rows + LANES // 2, 2 * LANES), BF16),
        pltpu.VMEM((2 * rows, LANES), BF16),
    ]

    def stage(away, pieces, sums):
        first = not sums
        start = 1 + len(pieces) + len(activations)
        return pl.pallas_call(
            functools.partial(stage_kernel, away, first),
            out_shape=[
                jax.ShapeDtypeStruct((tokens, SUMS * LANES), F32),
                jax.ShapeDtypeStruct((LANES, 2 * LANES), F32),
            ],
            in_specs=[SMEM] + [VMEM] * (len(pieces) + len(activations) + len(sums)),
            out_specs=[VMEM, VMEM],
            scratch_shapes=stage_scratch,
            input_output_aliases={} if first else {start: 0, start + 1: 1},
            compiler_params=params(16),
            cost_estimate=cost(tokens * rows * LANES * 16, 2 * MIB),
            name="stage",
        )(me.reshape(1), *pieces, *activations, *sums)

    def split(block, *tails):
        tail = block.shape[0] - 3 * rows
        shapes = (3 * rows, LANES), ((1 + len(tails)) * tail, LANES)
        return pl.pallas_call(
            split_kernel,
            out_shape=[jax.ShapeDtypeStruct(shape, BF16) for shape in shapes],
            in_specs=[VMEM] * (1 + len(tails)),
            out_specs=[VMEM, VMEM],
            compiler_params=params(8),
            name="split",
        )(block, *tails)

    tie = lax.optimization_barrier
    half = RING_CHIPS // 2
    held = [own, other_core(own)]
    blocks = list(held)
    first, second = hop(held[0]), hop(held[1])
    first, activations = tie((first, activations))
    sums = stage(0, held, [])
    second, sums = tie((second, sums))
    for k in range(1, half):
        held = [first, second]
        crossed = [other_core(first), other_core(second)]
        blocks += [first, crossed[0]]
        if k < half - 1:
            blocks += [second, crossed[1]]
        else:
            first, tails = split(first, tail)
            tails, sums = tie((tails, sums))
        first = hop(first)
        sums = stage(k, held, sums)
        first, sums = tie((first, sums))
        if k == half - 2:
            second, tail = split(second)
        if k < half - 1:
            second = hop(second)
        if k < half - 1:
            sums = stage(-k, crossed, sums)
            second, sums = tie((second, sums))
    tails = hop(tails)
    half_scratch = [
        pltpu.VMEM((rows + LANES // 2, 3 * LANES), BF16),
        pltpu.VMEM((rows + LANES // 2, 2 * LANES), BF16),
        pltpu.VMEM((rows + LANES // 2, 2 * LANES), BF16),
    ]
    start = 4 + len(activations)
    sums = pl.pallas_call(
        functools.partial(stage_and_half_kernel, 1 - half, half),
        out_shape=[jax.ShapeDtypeStruct(a.shape, a.dtype) for a in sums],
        in_specs=[SMEM] + [VMEM] * (3 + len(activations) + 2),
        out_specs=[VMEM, VMEM],
        scratch_shapes=stage_scratch + half_scratch,
        input_output_aliases={start: 0, start + 1: 1},
        compiler_params=params(16),
        cost_estimate=cost(tokens * rows * LANES * 24, 3 * MIB),
        name="stage_and_half",
    )(me.reshape(1), *crossed, first, *activations, *sums)
    crossed = other_core(first)
    unit = pl.pallas_call(
        functools.partial(feature_kernel, half),
        out_shape=jax.ShapeDtypeStruct((LANES, LANES), F32),
        in_specs=[SMEM] * 2 + [VMEM] * (1 + len(activations) + 5),
        out_specs=VMEM,
        scratch_shapes=half_scratch,
        compiler_params=params(16),
        cost_estimate=cost(1, 1),
        name="features",
    )(me.reshape(1), sequence_token_counts, crossed, *activations, *sums, local, *small)
    tails, unit = tie((tails, unit))
    blocks.append(tails)
    best = pl.pallas_call(
        functools.partial(score_kernel, len(blocks), count),
        out_shape=jax.ShapeDtypeStruct((2, TASKS, count, LANES), F32),
        in_specs=[VMEM] * (1 + len(blocks)),
        out_specs=VMEM,
        compiler_params=params(16),
        cost_estimate=cost(4 * MIB, 2 * MIB),
        name="scores",
    )(unit, *blocks)
    task_best, scores = pl.pallas_call(
        functools.partial(last_score_kernel, count),
        out_shape=(jax.ShapeDtypeStruct((2, TASKS), F32), jax.ShapeDtypeStruct((1, 2), F32)),
        in_specs=[VMEM] * 3,
        out_specs=(VMEM, VMEM),
        compiler_params=params(8),
        name="last_scores",
    )(unit, other_core(tails), best)
    return (scores.reshape(2), task_best)


def shards_of_any_slice(
    hidden_state_input,
    attention_mixed_state,
    hidden_state_adjoint,
    attention_values_adjoint,
    sequence_token_counts,
    heldout_sketched_signals,
    benchmark_labels,
    top_rmsnorm_weights,
    top_reducer_matrix,
    top_expander_matrix,
    bottom_reducer_matrix,
    bottom_expander_matrix,
    source_sketch,
    top_reducer_sketch,
    top_expander_sketch,
    top_target_sketch,
    bottom_reducer_sketch,
    bottom_expander_sketch,
    bottom_target_sketch,
    n,
):
    me = lax.axis_index("dp")
    x, mixed, adjoint, values = (
        hidden_state_input,
        attention_mixed_state,
        hidden_state_adjoint,
        attention_values_adjoint,
    )
    tokens, width = x.shape
    rows = top_reducer_matrix.shape[0]
    up_rows = top_expander_matrix.shape[1]
    rank = top_reducer_matrix.shape[1]
    k1 = source_sketch.shape[1]
    gain = top_rmsnorm_weights
    own_gain = lax.dynamic_slice_in_dim(gain, me * rows, rows)

    down_upper = (own_gain[:, None] * top_reducer_matrix.astype(F32)).astype(BF16)
    up_lower = mm(bottom_expander_matrix.T, bottom_reducer_sketch).astype(BF16)
    down_lower = mm(bottom_reducer_matrix, bottom_expander_sketch).astype(BF16)
    packed_lower = jnp.concatenate([down_lower[: rows // 2], down_lower[rows // 2 :]], axis=1)
    factors = jnp.concatenate([down_upper, up_lower, top_expander_matrix.T, packed_lower], axis=0)
    factors = lax.all_gather(factors, "dp")

    val_wide = heldout_sketched_signals.astype(F32)
    val_unit = (
        val_wide * lax.rsqrt(jnp.sum(val_wide * val_wide, axis=1, keepdims=True) + 1e-06)
    ).astype(BF16)
    labels = jnp.broadcast_to(benchmark_labels.astype(BF16), (val_unit.shape[0], 128))
    panel = jnp.concatenate([val_unit.reshape(-1, 128), labels], axis=0)
    panel = lax.all_gather(panel, "dp")
    val_rows = val_unit.shape[0]
    cut = panel.shape[1] - val_rows
    panel_tasks = panel[:, cut:, 0].reshape(n * val_rows, 1).astype(jnp.int32)
    panel = panel[:, :cut].reshape(n * val_rows, val_unit.shape[1])

    wide = x.astype(F32)
    inverse = lax.rsqrt(jnp.mean(wide * wide, axis=1, keepdims=True) + 1e-05)
    gained_sketch = (gain[:, None] * source_sketch.astype(F32)).astype(BF16)
    left_one = inverse * mm(x, gained_sketch)
    left_three = mm(mixed, source_sketch)
    right_two = ALPHA * mm(values, top_target_sketch)

    at = 0
    down_upper = factors[:, at : at + rows].reshape(width, rank)
    at += rows
    up_lower = factors[:, at : at + rows].reshape(width, -1)
    at += rows
    up_upper = factors[:, at : at + up_rows].reshape(-1, rank)
    at += up_rows
    down_lower = factors[:, at:]
    down_lower = jnp.concatenate([down_lower[:, :, :k1], down_lower[:, :, k1:]], axis=1)
    down_lower = down_lower.reshape(width, k1)

    reduced = inverse * mm(x, down_upper)
    left_two = mm(reduced.astype(BF16), top_expander_sketch)
    left_four = mm(mixed, down_lower)
    returned = mm(values, up_upper).astype(BF16)
    right_one = ALPHA * mm(returned, top_reducer_sketch)
    along = (ALPHA / width) * jnp.sum(returned.astype(F32) * reduced, axis=1, keepdims=True)
    targets = jnp.concatenate([up_lower, bottom_target_sketch], axis=1)
    bridge = mm_cols(down_upper, targets).astype(BF16)
    rights_low = mm(adjoint, targets) + inverse * (
        ALPHA * mm(returned, bridge) - (along * inverse) * mm(x, targets)
    )
    rights_low = ALPHA * rights_low
    k2 = up_lower.shape[1]
    lefts = (left_one, left_two, left_three, left_four)
    rights = (right_one, right_two, rights_low[:, :k2], rights_low[:, k2:])

    counts = sequence_token_counts[0]
    ends = jnp.cumsum(counts)
    starts = ends - counts
    places = jnp.arange(tokens, dtype=jnp.int32)[:, None]
    member = (places >= starts[None, :]) & (places < ends[None, :])
    count_ex = counts.shape[0]
    spread = jnp.concatenate(lefts, axis=0).astype(BF16)
    member = jnp.tile(member, (4, 1))
    spread = jnp.concatenate(
        [jnp.where(member[:, e : e + 1], spread, 0) for e in range(count_ex)], axis=1
    )
    feats = mm_cols(spread, jnp.concatenate(rights, axis=0).astype(BF16))
    feats = feats.reshape(count_ex, -1)
    squares = jnp.sum(feats * feats, axis=1, keepdims=True)
    unit_rows = (feats * lax.rsqrt(squares + 1e-06)).astype(BF16)

    score_scale = float(unit_rows.shape[1]) ** 0.5
    similar = score_scale * mm_rows(unit_rows, panel)
    task_mask = panel_tasks == jnp.arange(TASKS, dtype=jnp.int32)[None, :]
    task_best = jnp.max(
        jnp.where(task_mask[None, :, :], similar[:, :, None], -2.0 * score_scale), axis=1
    )
    return (jnp.mean(task_best, axis=1), task_best)


def solution(mesh):
    n = mesh.shape["dp"]
    split = P(("parts", "dp"), None)
    by_row, by_column, whole = P("dp", None), P(None, "dp"), P()
    placed = (
        (split,) * 5
        + (by_row, by_row, whole)
        + (by_row, by_column, by_row, by_column)
        + (whole,) * 7
    )
    ours = shards if n == 2 * RING_CHIPS else functools.partial(shards_of_any_slice, n=n)
    return jax.shard_map(
        ours,
        mesh=mesh,
        in_specs=placed,
        out_specs=(P(("parts", "dp")), split),
        check_vma=False,
    )
```
